32 devices in a mesh: rows: 4 (over y, core), cols: 8 (over z, x).
Axes of the slice: x: 2, y: 2, z: 4, core: 2. Of those that a mesh axis runs over, the one named last changes fastest.
Arguments:
- displacement: float32 [2048, 288], P(('rows', 'cols')), may hold values from -6 to 6
- positions: float32 [2048, 288], P(('rows', 'cols')), as said below
- cluster_basis: bfloat16 [2048, 288, 64], P(('rows', 'cols')), may hold values from -0.375 to 0.375
- near_pairs: int32 [8192, 2], P(('rows', 'cols')), may hold values from 0 to 67, as said below
- near_count: int32 [32], P(('rows', 'cols')), may hold values from 64 to 256, as said below
- far_pairs: int32 [32768, 2], P(('rows', 'cols')), may hold values from 0 to 511, as said below
- far_count: int32 [32], P(('rows', 'cols')), may hold values from 256 to 1024, as said below
- far_blocks: bfloat16 [32768, 64, 64], P(('rows', 'cols')), may hold values from -0.75 to 0.75
- intact: int32 [2048, 96], P(('rows', 'cols')), may hold values 0 or 1
- stiffness: float32 [2048, 96], P(('rows', 'cols')), may hold values from 0.5 to 2
Outputs:
- net_traction: float32 [2048, 288], P(('rows', 'cols'))
- damage: float32 [2048, 96], P(('rows', 'cols'))
The draws below stay inside these ranges and needn't reach their ends.
Inputs may be any that keep to these rules, and one draw needn't show every extreme that they name: `positions`: centroids of the elements of each cluster. `near_pairs`: column 0 is a cluster of the device's own 64; column 1 counts from 2 clusters before the device's first cluster and names a cluster at most 2 away from the target in the cluster order. Dead slots hold valid entries too. `near_count`: loads differ from device to device. `far_pairs`: column 0 is a target cluster of the device's index along rows (0 to 511); column 1 a source cluster of its index along cols (0 to 255), numbered through the devices of that column in the order of rows. Dead slots hold valid entries too. `far_count`: loads differ from device to device.
All inputs are finite; a program needn't handle non-finite values. No bound on the sum of `intact` on one device may be relied on, other than what follows from the above.
Results may differ from the reference program's by a relative error of at most 0.0014.
Values may be sent and summed in bfloat16 or wider, within the bound.
No kernel may reach another device: no remote copies, remote signals or barrier semaphores. Data moves between devices by JAX's collectives and lax.ppermute only.
A program may use at most 128 MiB of HBM per device.

```python
import math
import jax
import jax.numpy as jnp
from jax import lax

ELEMS = 96
RANK = 64
HALO = 2
CLUSTERS_DEV = 64
NEAR_MAX = 256
FAR_MAX = 1024
CLUSTERS = 2048
ROW_BLOCK = 512
COL_BLOCK = 256
N_ROWS = 4
N_COLS = 8
DEVICES = 32


def draw_positions(key, part):
    unit_key = jax.random.fold_in(key, 31)
    unit = jax.random.uniform(unit_key, (CLUSTERS, 3, ELEMS), jnp.float32, -1.0, 1.0)
    order = (jnp.arange(CLUSTERS, dtype=jnp.int32) % 4096).astype(jnp.float32)
    along_x = 0.6 * order[:, None] + 0.9 * unit[:, 0]
    along_y = 2.5 * unit[:, 1]
    along_z = 0.4 * unit[:, 2]
    return jnp.stack([along_x, along_y, along_z], axis=1).reshape(CLUSTERS, 3 * ELEMS)


def skewed_counts(key, largest):
    smallest = largest // 4
    spread_key, pick_key = jax.random.split(key)
    spread = jax.random.randint(spread_key, (DEVICES,), 0, largest - smallest + 1)
    counts = smallest + spread * spread // (largest - smallest)
    chosen = jax.random.randint(pick_key, (), 0, DEVICES)
    return jnp.where(jnp.arange(DEVICES, dtype=jnp.int32) == chosen, largest, counts).astype(jnp.int32)


def draw_near_count(key, part):
    return skewed_counts(jax.random.fold_in(key, 11), NEAR_MAX)


def draw_far_count(key, part):
    return skewed_counts(jax.random.fold_in(key, 12), FAR_MAX)


def draw_near_pairs(key, part):
    base_key = jax.random.fold_in(key, 21)
    target_key, shift_key, rim_key, reach_key = jax.random.split(base_key, 4)
    targets = jax.random.randint(target_key, (DEVICES, NEAR_MAX), 0, CLUSTERS_DEV)
    shifts = jax.random.randint(shift_key, (DEVICES, NEAR_MAX), -HALO, HALO + 1)
    rim = jax.random.randint(rim_key, (DEVICES, 4), 0, 2)
    raw_reach = jax.random.randint(reach_key, (DEVICES, 4), 0, 1024)
    reach = raw_reach % (HALO - rim)
    is_upper = jnp.arange(4, dtype=jnp.int32)[None, :] >= 2
    edge_targets = jnp.where(is_upper, CLUSTERS_DEV - 1 - rim, rim)
    edge_shifts = jnp.where(is_upper, HALO - reach, -HALO + reach)
    targets = targets.at[:, :4].set(edge_targets)
    shifts = shifts.at[:, :4].set(edge_shifts)
    sources = targets + HALO + shifts
    return jnp.stack([targets, sources], axis=-1).reshape(DEVICES * NEAR_MAX, 2).astype(jnp.int32)


def draw_far_pairs(key, part):
    base_key = jax.random.fold_in(key, 22)
    target_key, source_key = jax.random.split(base_key)
    targets = jax.random.randint(target_key, (DEVICES, FAR_MAX), 0, ROW_BLOCK)
    sources = jax.random.randint(source_key, (DEVICES, FAR_MAX), 0, COL_BLOCK)
    return jnp.stack([targets, sources], axis=-1).reshape(DEVICES * FAR_MAX, 2).astype(jnp.int32)


def plant(entries, stream_key, low, high):
    longest = entries.shape.index(max(entries.shape))
    spots = []
    for shift in (0, 1):
        where = [jax.random.randint(jax.random.fold_in(stream_key, axis), (), 0, length) for axis, length in enumerate(entries.shape)]
        where[longest] = (where[longest] + shift) % entries.shape[longest]
        spots.append(tuple(where))
    return entries.at[spots[0]].set(low).at[spots[1]].set(high)


def block_levels(rng, shape, cuts, low, high):
    gain = 1.0
    for position, blocks in cuts:
        steps = jax.random.uniform(jax.random.fold_in(jax.random.fold_in(rng, 6), position), (blocks,), jnp.float32, low / len(cuts), high / len(cuts))
        gain = gain * jnp.repeat(jnp.exp(steps), shape[position] // blocks).reshape((-1,) + (1,) * (len(shape) - 1 - position))
    return gain


def gaussian(rng, shape, scale, most, shards=(), kind=jnp.bfloat16):
    gain = block_levels(rng, shape, shards, -0.22, 0.18) if shards else 1.0
    values = jax.random.normal(rng, shape, jnp.float32) * scale * gain
    return jnp.minimum(jnp.maximum(values, -most), most).astype(kind)


def setup_inputs(seed: int = 0) -> dict:
    key_of = jax.random.split(jax.random.key(seed), 11)
    displacement = gaussian(key_of[0], (CLUSTERS, 3 * ELEMS), 1.0, 6.0, ((0, 32),), jnp.float32)
    positions = draw_positions(jax.random.fold_in(key_of[10], 71), 0)
    cluster_basis = gaussian(key_of[2], (CLUSTERS, 3 * ELEMS, RANK), (3 * ELEMS) ** -0.5, 0.375, ((0, 32),))
    near_pairs = draw_near_pairs(jax.random.fold_in(key_of[10], 71), 0)
    near_count = draw_near_count(jax.random.fold_in(key_of[10], 71), 0)
    far_pairs = draw_far_pairs(jax.random.fold_in(key_of[10], 71), 0)
    far_count = draw_far_count(jax.random.fold_in(key_of[10], 71), 0)
    far_blocks = gaussian(key_of[7], (N_ROWS * N_COLS * FAR_MAX, RANK, RANK), RANK ** -0.5, 0.75, ((0, 32),))
    intact = plant((jax.random.randint(key_of[8], (CLUSTERS, ELEMS), 0, 4) < 3).astype(jnp.int32), jax.random.fold_in(key_of[8], 1), 0, 1)
    stiffness = jnp.clip(jnp.exp(math.log(2.0) - 1.3862944 * jax.random.uniform(key_of[9], (CLUSTERS, ELEMS), jnp.float32) ** block_levels(key_of[9], (CLUSTERS, ELEMS), ((0, 32),), -0.2, 0.2)), 0.5, 2.0)
    return dict(displacement=displacement, positions=positions, cluster_basis=cluster_basis, near_pairs=near_pairs, near_count=near_count, far_pairs=far_pairs, far_count=far_count, far_blocks=far_blocks, intact=intact, stiffness=stiffness)


core_square = 0.25
softening = 1.5

def kernel_block(target_pos, source_pos, source_disp):
    offsets = target_pos[:, :, :, None] - source_pos[:, :, None, :]
    distance = lax.optimization_barrier(jnp.sum(offsets * offsets, axis=1)) + core_square
    inverse = lax.rsqrt(distance)
    inverse = inverse * inverse * inverse
    along = lax.optimization_barrier(jnp.sum(offsets * source_disp[:, :, None, :], axis=1))
    direct = lax.optimization_barrier(jnp.sum(inverse[:, None, :, :] * source_disp[:, :, None, :], axis=3))
    second = lax.optimization_barrier(jnp.sum(offsets * (along * inverse / distance)[:, None, :, :], axis=3))
    return direct - 3.0 * second

def reference(displacement, positions, cluster_basis, near_pairs, near_count, far_pairs, far_count, far_blocks, intact, stiffness):
    devices = N_ROWS * N_COLS
    clusters = CLUSTERS_DEV * devices
    row_width = 3 * ELEMS
    row_clusters = CLUSTERS_DEV * N_COLS
    padding = jnp.zeros((HALO, row_width), jnp.float32)
    ext_disp = jnp.concatenate([padding, displacement, padding], axis=0)
    ext_pos = jnp.concatenate([padding, positions, padding], axis=0)
    device_ids = jnp.arange(devices, dtype=jnp.int32)
    near_lists = near_pairs.reshape(devices, NEAR_MAX, 2)
    near_slots = jnp.arange(NEAR_MAX, dtype=jnp.int32)

    def near_device(summed, inputs):
        pair_list, slot_count, device = inputs
        first_cluster = device * CLUSTERS_DEV
        targets = first_cluster + pair_list[:, 0]
        sources = first_cluster + pair_list[:, 1]
        active = (near_slots < slot_count).astype(jnp.float32)
        target_pos = positions[targets].reshape(NEAR_MAX, 3, ELEMS)
        source_pos = ext_pos[sources].reshape(NEAR_MAX, 3, ELEMS)
        source_disp = ext_disp[sources].reshape(NEAR_MAX, 3, ELEMS)
        contrib = kernel_block(target_pos, source_pos, source_disp) * active[:, None, None]
        return (summed.at[targets].add(contrib.reshape(NEAR_MAX, row_width)), None)
    near_sum = lax.scan(near_device, jnp.zeros((clusters, row_width), jnp.float32), (near_lists, near_count, device_ids))[0]
    basis_dev = cluster_basis.reshape(devices, CLUSTERS_DEV, row_width, RANK)
    disp_dev = displacement.astype(jnp.bfloat16).reshape(devices, CLUSTERS_DEV, row_width)

    def project(inputs):
        local_basis, local_disp = inputs
        result = jnp.einsum('kf,kfr->kr', local_disp.astype(jnp.float32), local_basis.astype(jnp.float32))
        return result.astype(jnp.bfloat16)
    coeff_bf = lax.map(project, (basis_dev, disp_dev)).reshape(clusters, RANK)
    far_lists = far_pairs.reshape(devices, FAR_MAX, 2)
    blocks_dev = far_blocks.reshape(devices, FAR_MAX, RANK, RANK)
    far_slots = jnp.arange(FAR_MAX, dtype=jnp.int32)

    def far_device(summed, inputs):
        pair_list, slot_count, blocks, device = inputs
        row_index = device // N_COLS
        col_index = device % N_COLS
        targets = row_index * row_clusters + pair_list[:, 0]
        local = pair_list[:, 1]
        sources = local // CLUSTERS_DEV * row_clusters + col_index * CLUSTERS_DEV + local % CLUSTERS_DEV
        active = (far_slots < slot_count).astype(jnp.float32)
        coupled = jnp.einsum('prs,ps->pr', blocks.astype(jnp.float32), coeff_bf[sources].astype(jnp.float32))
        return (summed.at[targets].add(coupled * active[:, None]), None)
    coupled_sum = lax.scan(far_device, jnp.zeros((clusters, RANK), jnp.float32), (far_lists, far_count, blocks_dev, device_ids))[0]
    coupled_dev = coupled_sum.astype(jnp.bfloat16).reshape(devices, CLUSTERS_DEV, RANK)

    def expand(inputs):
        local_basis, local_coupled = inputs
        return jnp.einsum('kfr,kr->kf', local_basis.astype(jnp.float32), local_coupled.astype(jnp.float32))
    far_part = lax.map(expand, (basis_dev, coupled_dev)).reshape(clusters, row_width)
    traction = near_sum + far_part
    disp3 = displacement.reshape(clusters, 3, ELEMS)
    separation = jnp.sqrt(1.0 + lax.optimization_barrier(jnp.sum(disp3 * disp3, axis=1)))
    softened = 1.0 - jnp.exp(-(separation - 1.0) / softening)
    intact_float = intact.astype(jnp.float32)
    damage = intact_float * softened + (1.0 - intact_float)
    holding = ((1.0 - damage) * stiffness)[:, None, :] * disp3
    net_traction = traction - holding.reshape(clusters, row_width)
    return (net_traction, damage)
```

```python
import functools

import jax
import jax.numpy as jnp
from jax import lax
from jax.experimental import pallas as pl
from jax.experimental.pallas import tpu as pltpu
from jax.sharding import PartitionSpec as P

HALO = 2
LANES = 128
SUBLANES = 8
CHUNK = 32
GROUPS = LANES // CHUNK
core_square = 0.25
softening = 1.5
UNROLL = 2
VMEM = 56 * 1024 * 1024


def near_kernel(
    pairs_ref,
    count_ref,
    disp_ref,
    pos_ref,
    before_ref,
    after_ref,
    intact_ref,
    stiff_ref,
    out_ref,
    damage_ref,
    ext_scr,
    src_scr,
    tgt_scr,
    acc_scr,
):
    clusters, width = disp_ref.shape
    elems = width // 3
    chunks = elems // CHUNK
    steps = elems // (GROUPS * SUBLANES)
    spread = elems // GROUPS
    halo = before_ref.shape[0] // 2
    sources = clusters + 2 * halo
    tiles = ext_scr.shape[2] // LANES
    lane = lax.broadcasted_iota(jnp.int32, (SUBLANES, LANES), 1)
    group = lane // CHUNK
    group_start = group * CHUNK

    for k, own in enumerate((disp_ref, pos_ref)):
        ext_scr[k, 0:halo, 0:width] = before_ref[k * halo : (k + 1) * halo, :]
        ext_scr[k, halo : halo + clusters, 0:width] = own[...]
        ext_scr[k, halo + clusters : sources, 0:width] = after_ref[k * halo : (k + 1) * halo, :]

    flipped = [
        jnp.concatenate(
            [ext_scr[k, :, t * LANES : (t + 1) * LANES].T for t in range(tiles)], axis=0
        )
        for k in range(2)
    ]
    for block in range(pl.cdiv(sources, CHUNK)):
        packed = []
        for k in (1, 0):
            for c in range(3):
                for f in range(steps):
                    merged = None
                    for g in range(GROUPS):
                        row = c * elems + g * spread + f * SUBLANES
                        piece = flipped[k][row : row + SUBLANES, :]
                        shift = (g * CHUNK - block * CHUNK) % LANES
                        if shift:
                            piece = pltpu.roll(piece, shift, 1)
                        merged = piece if merged is None else jnp.where(group == g, piece, merged)
                    packed.append(merged)
        for i in range(min(CHUNK, sources - block * CHUNK)):
            index = group_start + i
            for n, item in enumerate(packed):
                value = jnp.take_along_axis(item, index, axis=1, mode="promise_in_bounds")
                src_scr[block * CHUNK + i, n] = value
                if n >= 3 * steps:
                    src_scr[block * CHUNK + i, n + 3 * steps] = 3.0 * value

    within = lax.broadcasted_iota(jnp.int32, (clusters, LANES), 1) % CHUNK
    for m in range(3 * chunks):
        tile = m // GROUPS
        own = ext_scr[1, halo : halo + clusters, tile * LANES : (tile + 1) * LANES]
        tgt_scr[:, m, :] = jnp.take_along_axis(
            own, within + (m % GROUPS) * CHUNK, axis=1, mode="promise_in_bounds"
        )

    acc_scr[...] = jnp.zeros_like(acc_scr)
    count = count_ref[0]

    def one_pair(slot):
        target = pairs_ref[0, slot]
        source = pairs_ref[1, slot]
        into = jnp.where(slot < count, target, clusters) * SUBLANES
        into = pl.multiple_of(into, SUBLANES)
        tgt = [
            jnp.broadcast_to(tgt_scr[target, m : m + 1, :], (SUBLANES, LANES))
            for m in range(3 * chunks)
        ]
        sums = [None] * (3 * chunks)
        for f in range(steps):
            y = [src_scr[source, c * steps + f] for c in range(3)]
            u = [src_scr[source, (3 + c) * steps + f] for c in range(3)]
            v = [src_scr[source, (6 + c) * steps + f] for c in range(3)]
            for h in range(chunks):
                r = [tgt[c * chunks + h] - y[c] for c in range(3)]
                q = (r[0] * r[0] + core_square) + (r[1] * r[1] + r[2] * r[2])
                s = r[0] * v[0] + (r[1] * v[1] + r[2] * v[2])
                inverse = lax.rsqrt(q)
                square = inverse * inverse
                weight = square * inverse
                s = s * square
                for c in range(3):
                    term = weight * (u[c] - s * r[c])
                    m = c * chunks + h
                    sums[m] = term if sums[m] is None else sums[m] + term
        for m in range(3 * chunks):
            acc_scr[m, pl.ds(into, SUBLANES), :] += sums[m]

    def step(it, carry):
        for k in range(UNROLL):
            one_pair(it * UNROLL + k)
        return carry

    lax.fori_loop(0, (count + UNROLL - 1) // UNROLL, step, 0)

    own_group = lax.broadcasted_iota(jnp.int32, (clusters, LANES), 1) // CHUNK
    for t in range(tiles):
        merged = None
        for g in range(GROUPS):
            m = t * GROUPS + g
            if m >= 3 * chunks:
                break
            total = acc_scr[m, pl.ds(0, clusters, stride=SUBLANES), :]
            for s in range(1, SUBLANES):
                total = total + acc_scr[m, pl.ds(s, clusters, stride=SUBLANES), :]
            total = total + pltpu.roll(total, 2 * CHUNK, 1)
            total = total + pltpu.roll(total, CHUNK, 1)
            merged = total if merged is None else jnp.where(own_group == g, total, merged)
        ext_scr[0, 0:clusters, t * LANES : (t + 1) * LANES] = merged

    disp = [disp_ref[:, c * elems : (c + 1) * elems] for c in range(3)]
    separation = jnp.sqrt(1.0 + (disp[0] * disp[0] + disp[1] * disp[1] + disp[2] * disp[2]))
    softened = 1.0 - jnp.exp(-(separation - 1.0) / softening)
    intact = intact_ref[...].astype(jnp.float32)
    damage = intact * softened + (1.0 - intact)
    damage_ref[...] = damage
    hold = (1.0 - damage) * stiff_ref[...]
    for c in range(3):
        near = ext_scr[0, 0:clusters, c * elems : (c + 1) * elems]
        out_ref[:, c * elems : (c + 1) * elems] = near - hold * disp[c]


def near_field(pairs, count, disp, pos, before, after, intact, stiffness):
    clusters, width = disp.shape
    elems = width // 3
    chunks = elems // CHUNK
    steps = elems // (GROUPS * SUBLANES)
    halo = before.shape[0] // 2
    sources = clusters + 2 * halo
    padded = pl.cdiv(width, LANES) * LANES
    slots = pairs.shape[1]
    vmem = pl.BlockSpec(memory_space=pltpu.VMEM)
    smem = pl.BlockSpec(memory_space=pltpu.SMEM)
    return pl.pallas_call(
        near_kernel,
        out_shape=(
            jax.ShapeDtypeStruct((clusters, width), jnp.float32),
            jax.ShapeDtypeStruct((clusters, elems), jnp.float32),
        ),
        in_specs=[smem, smem] + [vmem] * 6,
        out_specs=(vmem, vmem),
        scratch_shapes=[
            pltpu.VMEM((2, LANES, padded), jnp.float32),
            pltpu.VMEM((sources, 9 * steps, SUBLANES, LANES), jnp.float32),
            pltpu.VMEM((clusters, 3 * chunks, LANES), jnp.float32),
            pltpu.VMEM((3 * chunks, (clusters + 1) * SUBLANES, LANES), jnp.float32),
        ],
        compiler_params=pltpu.CompilerParams(vmem_limit_bytes=VMEM),
        cost_estimate=pl.CostEstimate(
            flops=30 * slots * elems * elems,
            bytes_accessed=4 * clusters * width * 6,
            transcendentals=slots * elems * elems,
        ),
        name="near_field",
    )(pairs, count, disp, pos, before, after, intact, stiffness)


def far_kernel(
    count_ref, column_ref, pairs_ref, blocks_ref, out_ref, coeff_scr, sum_scr, *, steps
):
    step = pl.program_id(0)
    rows, rank, slots = blocks_ref.shape
    sources = column_ref.shape[0]
    targets = out_ref.shape[0]

    @pl.when(step == 0)
    def _():
        chosen = pairs_ref[1:2, :]
        index = lax.broadcasted_iota(jnp.int32, (sources, slots), 0)
        pick = jnp.where(index == chosen, 1.0, 0.0).astype(jnp.bfloat16)
        coeff_scr[...] = lax.dot_general(
            column_ref[...], pick, (((0,), (0,)), ((), ())), preferred_element_type=jnp.float32
        )

    for t in range(slots // LANES):
        lanes = slice(t * LANES, (t + 1) * LANES)
        coeff = coeff_scr[:, lanes]
        for r in range(rows):
            product = blocks_ref[r, :, lanes].astype(jnp.float32) * coeff
            folded = product[0:SUBLANES]
            for s in range(1, rank // SUBLANES):
                folded = folded + product[s * SUBLANES : (s + 1) * SUBLANES]
            start = pl.multiple_of((step * rows + r) * SUBLANES, SUBLANES)
            sum_scr[t, pl.ds(start, SUBLANES), :] = folded

    @pl.when(step == steps - 1)
    def _():
        parts = []
        for t in range(slots // LANES):
            total = sum_scr[t, pl.ds(0, rank, stride=SUBLANES), :]
            for s in range(1, SUBLANES):
                total = total + sum_scr[t, pl.ds(s, rank, stride=SUBLANES), :]
            parts.append(total)
        coupled = jnp.concatenate(parts, axis=1)
        high = coupled.astype(jnp.bfloat16)
        low = (coupled - high.astype(jnp.float32)).astype(jnp.bfloat16)
        both = jnp.concatenate([high, low], axis=0)
        slot = lax.broadcasted_iota(jnp.int32, (1, slots), 1)
        wanted = jnp.where(slot < count_ref[0], pairs_ref[0:1, :], -1)
        index = lax.broadcasted_iota(jnp.int32, (targets, slots), 0)
        place = jnp.where(index == wanted, 1.0, 0.0).astype(jnp.bfloat16)
        summed = lax.dot_general(
            place, both, (((1,), (1,)), ((), ())), preferred_element_type=jnp.float32
        )
        out_ref[...] = (summed[:, 0:rank] + summed[:, rank:]).astype(out_ref.dtype)


def far_field(count, column, pairs, blocks, targets):
    rank, _, slots = blocks.shape
    sources = column.shape[0]
    rows = SUBLANES
    steps = rank // rows
    vmem = pl.BlockSpec(memory_space=pltpu.VMEM)
    smem = pl.BlockSpec(memory_space=pltpu.SMEM)
    return pl.pallas_call(
        functools.partial(far_kernel, steps=steps),
        grid=(steps,),
        out_shape=jax.ShapeDtypeStruct((targets, rank), jnp.bfloat16),
        in_specs=[
            smem,
            vmem,
            vmem,
            pl.BlockSpec((rows, rank, slots), lambda i: (i, 0, 0)),
        ],
        out_specs=pl.BlockSpec((targets, rank), lambda i: (0, 0)),
        scratch_shapes=[
            pltpu.VMEM((rank, slots), jnp.float32),
            pltpu.VMEM((slots // LANES, rank * SUBLANES, LANES), jnp.float32),
        ],
        compiler_params=pltpu.CompilerParams(vmem_limit_bytes=VMEM),
        cost_estimate=pl.CostEstimate(
            flops=2 * rank * rank * slots,
            bytes_accessed=2 * rank * rank * slots,
            transcendentals=0,
        ),
        name="far_field",
    )(count, column, pairs, blocks)


def local(
    displacement,
    positions,
    cluster_basis,
    near_pairs,
    near_count,
    far_pairs,
    far_count,
    far_blocks,
    intact,
    stiffness,
):
    clusters = displacement.shape[0]
    rank = cluster_basis.shape[2]
    cols = lax.axis_size("cols")
    devices = lax.axis_size("rows") * cols
    axes = ("rows", "cols")

    up = [(i, i + 1) for i in range(devices - 1)]
    down = [(i + 1, i) for i in range(devices - 1)]
    last = jnp.concatenate([displacement[clusters - HALO :], positions[clusters - HALO :]], axis=0)
    first = jnp.concatenate([displacement[:HALO], positions[:HALO]], axis=0)
    before = lax.ppermute(last, axes, up)
    after = lax.ppermute(first, axes, down)

    disp_bf = displacement.astype(jnp.bfloat16)
    coeff = jnp.einsum("kf,kfr->kr", disp_bf, cluster_basis, preferred_element_type=jnp.float32)
    column = lax.all_gather(coeff.astype(jnp.bfloat16), "rows", axis=0, tiled=True)
    partial = far_field(
        far_count, column, far_pairs.T, far_blocks.transpose(1, 2, 0), clusters * cols
    )
    received = lax.all_to_all(
        partial.reshape(cols, clusters, rank), "cols", split_axis=0, concat_axis=0
    )

    near, damage = near_field(
        near_pairs.T, near_count, displacement, positions, before, after, intact, stiffness
    )
    owned = jnp.sum(received.astype(jnp.float32), axis=0).astype(jnp.bfloat16)
    far_part = jnp.einsum("kfr,kr->kf", cluster_basis, owned, preferred_element_type=jnp.float32)
    return (near + far_part, damage)


def solution(mesh):
    both = ("rows", "cols")
    in_specs = (
        P(both, None),
        P(both, None),
        P(both, None, None),
        P(both, None),
        P(both),
        P(both, None),
        P(both),
        P(both, None, None),
        P(both, None),
        P(both, None),
    )
    out_specs = (P(both, None), P(both, None))
    return jax.shard_map(local, mesh=mesh, in_specs=in_specs, out_specs=out_specs, check_vma=False)
```

```python
import functools

import jax
import jax.numpy as jnp
from jax import lax
from jax.experimental import pallas as pl
from jax.experimental.pallas import tpu as pltpu
from jax.sharding import PartitionSpec as P

HALO = 2
LANES = 128
SUBLANES = 8
CHUNK = 32
GROUPS = LANES // CHUNK
core_square = 0.25
softening = 1.5
UNROLL = 4
SPREAD = 8
FOLD = 256
PIECES = 3
VMEM = 32 * 1024 * 1024


def split_rows(width, lanes):
    return pl.cdiv(width, lanes)


def project_kernel(disp_ref, pos_ref, basis_ref, out_ref, stage_scr):
    clusters, rank, width = basis_ref.shape
    spare = LANES - rank
    segments = split_rows(width, spare)
    rows = 2 * HALO
    stage_scr[...] = jnp.zeros_like(stage_scr)

    for side, start in enumerate((0, clusters - HALO)):
        block = jnp.concatenate(
            [disp_ref[start : start + HALO, :], pos_ref[start : start + HALO, :]], axis=0
        )
        for n in range(PIECES):
            piece = block.astype(jnp.bfloat16).astype(jnp.float32)
            block = block - piece
            for g in range(segments):
                size = min(spare, width - g * spare)
                row = side * clusters + (n * segments + g) * rows
                stage_scr[row : row + rows, rank : rank + size] = piece[
                    :, g * spare : g * spare + size
                ]

    disp_bf = disp_ref[...].astype(jnp.bfloat16)
    for k in range(clusters // SUBLANES):
        group = slice(k * SUBLANES, (k + 1) * SUBLANES)
        basis = basis_ref[group].reshape(SUBLANES * rank, width)
        product = lax.dot_general(
            disp_bf[group, :],
            basis,
            (((1,), (1,)), ((), ())),
            preferred_element_type=jnp.float32,
        )
        row = lax.broadcasted_iota(jnp.int32, (SUBLANES, rank), 0)
        coeff = jnp.zeros((SUBLANES, rank), jnp.float32)
        for i in range(SUBLANES):
            coeff = jnp.where(row == i, product[:, i * rank : (i + 1) * rank], coeff)
        stage_scr[group, 0:rank] = coeff
    out_ref[...] = stage_scr[...].astype(out_ref.dtype)


def project(disp, pos, basis):
    clusters, rank, width = basis.shape
    vmem = pl.BlockSpec(memory_space=pltpu.VMEM)
    return pl.pallas_call(
        project_kernel,
        out_shape=jax.ShapeDtypeStruct((2 * clusters, LANES), jnp.bfloat16),
        in_specs=[vmem] * 3,
        out_specs=vmem,
        scratch_shapes=[pltpu.VMEM((2 * clusters, LANES), jnp.float32)],
        compiler_params=pltpu.CompilerParams(vmem_limit_bytes=VMEM),
        cost_estimate=pl.CostEstimate(
            flops=2 * clusters * rank * width,
            bytes_accessed=2 * clusters * rank * width,
            transcendentals=0,
        ),
        name="project",
    )(disp, pos, basis)


def far_kernel(
    count_ref,
    pairs_ref,
    gathered_ref,
    blocks_ref,
    out_ref,
    buffer,
    coeff_scr,
    sum_scr,
    place_scr,
    summed_scr,
    sems,
):
    rank, _, slots = buffer.shape
    cols, clusters, _ = out_ref.shape
    targets = cols * clusters
    rows = gathered_ref.shape[0] // (2 * clusters)
    sources = rows * clusters
    steps = sems.shape[0]
    part = rank // steps

    def fetch(step):
        here = pl.ds(step * part, part)
        return pltpu.make_async_copy(blocks_ref.at[here], buffer.at[here], sems.at[step])

    for step in range(steps):
        fetch(step).start()

    column = jnp.concatenate(
        [gathered_ref[2 * i * clusters : (2 * i + 1) * clusters, :] for i in range(rows)], axis=0
    )
    index = lax.broadcasted_iota(jnp.int32, (sources, slots), 0)
    pick = jnp.where(index == pairs_ref[1:2, :], 1.0, 0.0).astype(jnp.bfloat16)
    coeff = lax.dot_general(
        column, pick, (((0,), (0,)), ((), ())), preferred_element_type=jnp.float32
    )
    coeff_scr[...] = coeff[0:rank, :]

    slot = lax.broadcasted_iota(jnp.int32, (1, slots), 1)
    wanted = jnp.where(slot < count_ref[0], pairs_ref[0:1, :], -1)
    index = lax.broadcasted_iota(jnp.int32, (targets, slots), 0)
    place_scr[...] = jnp.where(index == wanted, 1.0, 0.0).astype(jnp.bfloat16)

    def multiply(step, carry):
        fetch(step).wait()
        for t in range(slots // FOLD):
            lanes = slice(t * FOLD, (t + 1) * FOLD)
            coeff = coeff_scr[:, lanes]
            for r in range(part):
                product = buffer[step * part + r, :, lanes].astype(jnp.float32) * coeff
                folded = product[0:SUBLANES]
                for s in range(1, rank // SUBLANES):
                    folded = folded + product[s * SUBLANES : (s + 1) * SUBLANES]
                start = pl.multiple_of((step * part + r) * SUBLANES, SUBLANES)
                for h in range(FOLD // LANES):
                    sum_scr[t * (FOLD // LANES) + h, pl.ds(start, SUBLANES), :] = folded[
                        :, h * LANES : (h + 1) * LANES
                    ]
        return carry

    lax.fori_loop(0, steps, multiply, 0)

    parts = []
    for t in range(slots // LANES):
        total = sum_scr[t, pl.ds(0, rank, stride=SUBLANES), :]
        for s in range(1, SUBLANES):
            total = total + sum_scr[t, pl.ds(s, rank, stride=SUBLANES), :]
        parts.append(total)
    coupled = jnp.concatenate(parts, axis=1)
    high = coupled.astype(jnp.bfloat16)
    low = (coupled - high.astype(jnp.float32)).astype(jnp.bfloat16)
    both = jnp.concatenate([high, low], axis=0)
    summed = lax.dot_general(
        place_scr[...], both, (((1,), (1,)), ((), ())), preferred_element_type=jnp.float32
    )
    summed_scr[...] = summed + pltpu.roll(summed, rank, 1)

    i = lax.axis_index("rows")
    j = lax.axis_index("cols")
    from_last = jnp.where(j < cols - 1, i, i - 1)
    from_first = jnp.where(j > 0, i, i + 1)
    start = pl.multiple_of((2 * jnp.maximum(from_last, 0) + 1) * clusters, clusters)
    last = gathered_ref[pl.ds(start, clusters), :].astype(jnp.float32)
    last = jnp.where(from_last >= 0, last, 0.0)
    start = pl.multiple_of(2 * jnp.minimum(from_first, rows - 1) * clusters, clusters)
    first = gathered_ref[pl.ds(start, clusters), :].astype(jnp.float32)
    first = jnp.where(from_first < rows, first, 0.0)
    after = jnp.where(j < cols - 1, j + 1, 0)
    lane = lax.broadcasted_iota(jnp.int32, (clusters, LANES), 1)
    for d in range(cols):
        halo = jnp.where(after == d, last, first)
        mine = summed_scr[d * clusters : (d + 1) * clusters, :]
        out_ref[d] = jnp.where(lane < rank, mine, halo).astype(out_ref.dtype)


def far_field(count, pairs, gathered, blocks, cols):
    rank, _, slots = blocks.shape
    rows = lax.axis_size("rows")
    clusters = gathered.shape[0] // (2 * rows)
    steps = SUBLANES
    vmem = pl.BlockSpec(memory_space=pltpu.VMEM)
    smem = pl.BlockSpec(memory_space=pltpu.SMEM)
    return pl.pallas_call(
        far_kernel,
        out_shape=jax.ShapeDtypeStruct((cols, clusters, LANES), jnp.bfloat16),
        in_specs=[smem, vmem, vmem, pl.BlockSpec(memory_space=pl.ANY)],
        out_specs=vmem,
        scratch_shapes=[
            pltpu.VMEM((rank, rank, slots), jnp.bfloat16),
            pltpu.VMEM((rank, slots), jnp.float32),
            pltpu.VMEM((slots // LANES, rank * SUBLANES, LANES), jnp.float32),
            pltpu.VMEM((cols * clusters, slots), jnp.bfloat16),
            pltpu.VMEM((cols * clusters, LANES), jnp.float32),
            pltpu.SemaphoreType.DMA((steps,)),
        ],
        compiler_params=pltpu.CompilerParams(vmem_limit_bytes=VMEM),
        cost_estimate=pl.CostEstimate(
            flops=2 * rank * rank * slots,
            bytes_accessed=2 * rank * rank * slots,
            transcendentals=0,
        ),
        name="far_field",
    )(count, pairs, gathered, blocks)


def traction_kernel(
    pairs_ref,
    count_ref,
    disp_ref,
    pos_ref,
    received_ref,
    intact_ref,
    stiff_ref,
    basis_ref,
    out_ref,
    damage_ref,
    basis_scr,
    ext_scr,
    halo_scr,
    packed_scr,
    src_scr,
    tgt_scr,
    acc_scr,
    sem,
):
    clusters, width = disp_ref.shape
    cols, _, lanes = received_ref.shape
    rank = basis_ref.shape[1]
    elems = width // 3
    chunks = elems // CHUNK
    steps = elems // (GROUPS * SUBLANES)
    spread = elems // GROUPS
    sources = clusters + 2 * HALO
    tiles = ext_scr.shape[2] // LANES
    spare = LANES - rank
    segments = split_rows(width, spare)
    lane = lax.broadcasted_iota(jnp.int32, (SUBLANES, LANES), 1)
    group = lane // CHUNK
    group_start = group * CHUNK

    fetch = pltpu.make_async_copy(basis_ref, basis_scr, sem)
    fetch.start()

    for k, own in enumerate((disp_ref, pos_ref)):
        ext_scr[k, HALO : HALO + clusters, 0:width] = own[...]
    j = lax.axis_index("cols")
    before = jnp.where(j > 0, j - 1, cols - 1)
    after = jnp.where(j < cols - 1, j + 1, 0)
    for start, sender in ((0, before), (HALO + clusters, after)):
        halo_scr[...] = received_ref[sender].astype(jnp.float32)
        size = 2 * HALO * segments
        whole = halo_scr[0:size, :]
        for n in range(1, PIECES):
            whole = whole + halo_scr[n * size : (n + 1) * size, :]
        for g in range(segments):
            count = min(spare, width - g * spare)
            for k in range(2):
                row = (2 * g + k) * HALO
                ext_scr[k, start : start + HALO, g * spare : g * spare + count] = whole[
                    row : row + HALO, rank : rank + count
                ]

    for k in range(2):
        flipped = jnp.concatenate(
            [ext_scr[k, :, t * LANES : (t + 1) * LANES].T for t in range(tiles)], axis=0
        )
        for block in range(packed_scr.shape[0]):
            for c in range(3):
                for f in range(steps):
                    merged = None
                    for g in range(GROUPS):
                        row = c * elems + g * spread + f * SUBLANES
                        piece = flipped[row : row + SUBLANES, :]
                        shift = (g * CHUNK - block * CHUNK) % LANES
                        if shift:
                            piece = pltpu.roll(piece, shift, 1)
                        merged = piece if merged is None else jnp.where(group == g, piece, merged)
                    packed_scr[block, ((1 - k) * 3 + c) * steps + f] = merged

    def spread_sources(it, carry):
        block = it // (CHUNK // SPREAD)
        offset = (it % (CHUNK // SPREAD)) * SPREAD
        for n in range(6 * steps):
            item = packed_scr[block, n]
            for i in range(SPREAD):
                value = jnp.take_along_axis(
                    item, group_start + (offset + i), axis=1, mode="promise_in_bounds"
                )
                src_scr[it * SPREAD + i, n] = value
                if n >= 3 * steps:
                    src_scr[it * SPREAD + i, n + 3 * steps] = 3.0 * value
        return carry

    lax.fori_loop(0, pl.cdiv(sources, SPREAD), spread_sources, 0)

    within = lax.broadcasted_iota(jnp.int32, (clusters, LANES), 1) % CHUNK
    for m in range(3 * chunks):
        tile = m // GROUPS
        own = ext_scr[1, HALO : HALO + clusters, tile * LANES : (tile + 1) * LANES]
        tgt_scr[:, m, :] = jnp.take_along_axis(
            own, within + (m % GROUPS) * CHUNK, axis=1, mode="promise_in_bounds"
        )

    acc_scr[...] = jnp.zeros_like(acc_scr)
    count = count_ref[0]

    def one_pair(slot):
        target = pairs_ref[0, slot]
        source = pairs_ref[1, slot]
        into = jnp.where(slot < count, target, clusters) * SUBLANES
        into = pl.multiple_of(into, SUBLANES)
        tgt = [
            jnp.broadcast_to(tgt_scr[target, m : m + 1, :], (SUBLANES, LANES))
            for m in range(3 * chunks)
        ]
        sums = [None] * (3 * chunks)
        for f in range(steps):
            y = [src_scr[source, c * steps + f] for c in range(3)]
            u = [src_scr[source, (3 + c) * steps + f] for c in range(3)]
            v = [src_scr[source, (6 + c) * steps + f] for c in range(3)]
            for h in range(chunks):
                r = [tgt[c * chunks + h] - y[c] for c in range(3)]
                q = (r[0] * r[0] + core_square) + (r[1] * r[1] + r[2] * r[2])
                s = r[0] * v[0] + (r[1] * v[1] + r[2] * v[2])
                inverse = lax.rsqrt(q)
                square = inverse * inverse
                weight = square * inverse
                s = s * square
                for c in range(3):
                    term = weight * (u[c] - s * r[c])
                    m = c * chunks + h
                    sums[m] = term if sums[m] is None else sums[m] + term
        for m in range(3 * chunks):
            acc_scr[m, pl.ds(into, SUBLANES), :] += sums[m]

    def step(it, carry):
        for k in range(UNROLL):
            one_pair(it * UNROLL + k)
        return carry

    lax.fori_loop(0, (count + UNROLL - 1) // UNROLL, step, 0)

    owned = received_ref[0].astype(jnp.float32)
    for d in range(1, cols):
        owned = owned + received_ref[d].astype(jnp.float32)
    fetch.wait()
    wide = lax.broadcasted_iota(jnp.int32, (SUBLANES, SUBLANES * rank), 1) // rank
    wide = wide == lax.broadcasted_iota(jnp.int32, (SUBLANES, SUBLANES * rank), 0)
    for k in range(clusters // SUBLANES):
        some = slice(k * SUBLANES, (k + 1) * SUBLANES)
        tiled = jnp.concatenate([owned[some, 0:rank]] * SUBLANES, axis=1)
        diagonal = jnp.where(wide, tiled, 0.0).astype(jnp.bfloat16)
        ext_scr[1, some, 0:width] = jnp.dot(
            diagonal,
            basis_scr[some].reshape(SUBLANES * rank, width),
            preferred_element_type=jnp.float32,
        )

    own_group = lax.broadcasted_iota(jnp.int32, (clusters, LANES), 1) // CHUNK
    for t in range(tiles):
        merged = None
        for g in range(GROUPS):
            m = t * GROUPS + g
            if m >= 3 * chunks:
                break
            total = acc_scr[m, pl.ds(0, clusters, stride=SUBLANES), :]
            for s in range(1, SUBLANES):
                total = total + acc_scr[m, pl.ds(s, clusters, stride=SUBLANES), :]
            total = total + pltpu.roll(total, 2 * CHUNK, 1)
            total = total + pltpu.roll(total, CHUNK, 1)
            merged = total if merged is None else jnp.where(own_group == g, total, merged)
        ext_scr[0, 0:clusters, t * LANES : (t + 1) * LANES] = merged

    disp = [disp_ref[:, c * elems : (c + 1) * elems] for c in range(3)]
    separation = jnp.sqrt(1.0 + (disp[0] * disp[0] + disp[1] * disp[1] + disp[2] * disp[2]))
    softened = 1.0 - jnp.exp(-(separation - 1.0) / softening)
    intact = intact_ref[...].astype(jnp.float32)
    damage = intact * softened + (1.0 - intact)
    damage_ref[...] = damage
    hold = (1.0 - damage) * stiff_ref[...]
    for c in range(3):
        here = slice(c * elems, (c + 1) * elems)
        elastic = ext_scr[0, 0:clusters, here] + ext_scr[1, 0:clusters, here]
        out_ref[:, here] = elastic - hold * disp[c]


def traction_field(pairs, count, disp, pos, received, intact, stiffness, basis):
    clusters, width = disp.shape
    rank = basis.shape[1]
    elems = width // 3
    chunks = elems // CHUNK
    steps = elems // (GROUPS * SUBLANES)
    sources = clusters + 2 * HALO
    padded = pl.cdiv(width, LANES) * LANES
    slots = pairs.shape[1]
    vmem = pl.BlockSpec(memory_space=pltpu.VMEM)
    smem = pl.BlockSpec(memory_space=pltpu.SMEM)
    return pl.pallas_call(
        traction_kernel,
        out_shape=(
            jax.ShapeDtypeStruct((clusters, width), jnp.float32),
            jax.ShapeDtypeStruct((clusters, elems), jnp.float32),
        ),
        in_specs=[smem, smem] + [vmem] * 5 + [pl.BlockSpec(memory_space=pl.ANY)],
        out_specs=(vmem, vmem),
        scratch_shapes=[
            pltpu.VMEM(basis.shape, basis.dtype),
            pltpu.VMEM((2, LANES, padded), jnp.float32),
            pltpu.VMEM((clusters, LANES), jnp.float32),
            pltpu.VMEM((pl.cdiv(sources, CHUNK), 6 * steps, SUBLANES, LANES), jnp.float32),
            pltpu.VMEM(
                (pl.cdiv(sources, SPREAD) * SPREAD, 9 * steps, SUBLANES, LANES), jnp.float32
            ),
            pltpu.VMEM((clusters, 3 * chunks, LANES), jnp.float32),
            pltpu.VMEM((3 * chunks, (clusters + 1) * SUBLANES, LANES), jnp.float32),
            pltpu.SemaphoreType.DMA(()),
        ],
        compiler_params=pltpu.CompilerParams(vmem_limit_bytes=VMEM),
        cost_estimate=pl.CostEstimate(
            flops=30 * slots * elems * elems,
            bytes_accessed=4 * clusters * width * 6 + 2 * clusters * rank * width,
            transcendentals=slots * elems * elems,
        ),
        name="traction",
    )(pairs, count, disp, pos, received, intact, stiffness, basis)


def local(
    displacement,
    positions,
    cluster_basis,
    near_pairs,
    near_count,
    far_pairs,
    far_count,
    far_blocks,
    intact,
    stiffness,
):
    cols = lax.axis_size("cols")
    basis = cluster_basis.transpose(0, 2, 1)
    payload = project(displacement, positions, basis)
    gathered = lax.all_gather(payload, "rows", axis=0, tiled=True)
    partial = far_field(far_count, far_pairs.T, gathered, far_blocks.transpose(1, 2, 0), cols)
    received = lax.all_to_all(partial, "cols", split_axis=0, concat_axis=0)
    return traction_field(
        near_pairs.T, near_count, displacement, positions, received, intact, stiffness, basis
    )


def solution(mesh):
    both = ("rows", "cols")
    in_specs = (
        P(both, None),
        P(both, None),
        P(both, None, None),
        P(both, None),
        P(both),
        P(both, None),
        P(both),
        P(both, None, None),
        P(both, None),
        P(both, None),
    )
    out_specs = (P(both, None), P(both, None))
    return jax.shard_map(local, mesh=mesh, in_specs=in_specs, out_specs=out_specs, check_vma=False)
```

```python
import functools

import jax
import jax.numpy as jnp
from jax import lax
from jax.experimental import pallas as pl
from jax.experimental.pallas import tpu as pltpu
from jax.sharding import PartitionSpec as P

HALO = 2
LANES = 128
SUBLANES = 8
CHUNK = 32
GROUPS = LANES // CHUNK
core_square = 0.25
softening = 1.5
UNROLL = 4
FOLD = 256
PIECES = 3
VMEM = 60 * 1024 * 1024


def split_rows(width, lanes):
    return pl.cdiv(width, lanes)


def project_kernel(disp_ref, pos_ref, basis_ref, out_ref, stage_scr, basis_scr, sems):
    clusters, rank, width = basis_ref.shape
    spare = LANES - rank
    segments = split_rows(width, spare)
    rows = 2 * HALO
    fetches = sems.shape[0]
    part = clusters // fetches

    def fetch(k):
        here = pl.ds(k * part, part)
        return pltpu.make_async_copy(basis_ref.at[here], basis_scr.at[here], sems.at[k])

    for k in range(fetches):
        fetch(k).start()
    stage_scr[...] = jnp.zeros_like(stage_scr)

    for side, start in enumerate((0, clusters - HALO)):
        block = jnp.concatenate(
            [disp_ref[start : start + HALO, :], pos_ref[start : start + HALO, :]], axis=0
        )
        for n in range(PIECES):
            piece = block.astype(jnp.bfloat16).astype(jnp.float32)
            block = block - piece
            for g in range(segments):
                size = min(spare, width - g * spare)
                row = side * clusters + (n * segments + g) * rows
                stage_scr[row : row + rows, rank : rank + size] = piece[
                    :, g * spare : g * spare + size
                ]

    disp_bf = disp_ref[...].astype(jnp.bfloat16)
    for k in range(clusters // SUBLANES):
        group = slice(k * SUBLANES, (k + 1) * SUBLANES)
        if (k * SUBLANES) % part == 0:
            fetch(k * SUBLANES // part).wait()
        basis = basis_scr[group].reshape(SUBLANES * rank, width)
        product = lax.dot_general(
            disp_bf[group, :],
            basis,
            (((1,), (1,)), ((), ())),
            preferred_element_type=jnp.float32,
        )
        row = lax.broadcasted_iota(jnp.int32, (SUBLANES, rank), 0)
        coeff = jnp.zeros((SUBLANES, rank), jnp.float32)
        for i in range(SUBLANES):
            coeff = jnp.where(row == i, product[:, i * rank : (i + 1) * rank], coeff)
        stage_scr[group, 0:rank] = coeff
    out_ref[...] = stage_scr[...].astype(out_ref.dtype)


def project(disp, pos, basis):
    clusters, rank, width = basis.shape
    vmem = pl.BlockSpec(memory_space=pltpu.VMEM)
    return pl.pallas_call(
        project_kernel,
        out_shape=jax.ShapeDtypeStruct((2 * clusters, LANES), jnp.bfloat16),
        in_specs=[vmem] * 2 + [pl.BlockSpec(memory_space=pl.ANY)],
        out_specs=vmem,
        scratch_shapes=[
            pltpu.VMEM((2 * clusters, LANES), jnp.float32),
            pltpu.VMEM(basis.shape, basis.dtype),
            pltpu.SemaphoreType.DMA((4,)),
        ],
        compiler_params=pltpu.CompilerParams(vmem_limit_bytes=VMEM),
        cost_estimate=pl.CostEstimate(
            flops=2 * clusters * rank * width,
            bytes_accessed=2 * clusters * rank * width,
            transcendentals=0,
        ),
        name="project",
    )(disp, pos, basis)


def far_kernel(
    count_ref,
    pairs_ref,
    gathered_ref,
    blocks_ref,
    out_ref,
    buffer,
    coeff_scr,
    sum_scr,
    place_scr,
    summed_scr,
    sems,
):
    rank, _, slots = buffer.shape
    cols, clusters, _ = out_ref.shape
    targets = cols * clusters
    rows = gathered_ref.shape[0] // (2 * clusters)
    sources = rows * clusters
    steps = sems.shape[0]
    part = rank // steps

    def fetch(step):
        here = pl.ds(step * part, part)
        return pltpu.make_async_copy(blocks_ref.at[here], buffer.at[here], sems.at[step])

    for step in range(steps):
        fetch(step).start()

    column = jnp.concatenate(
        [gathered_ref[2 * i * clusters : (2 * i + 1) * clusters, :] for i in range(rows)], axis=0
    )
    index = lax.broadcasted_iota(jnp.int32, (sources, slots), 0)
    pick = jnp.where(index == pairs_ref[1:2, :], 1.0, 0.0).astype(jnp.bfloat16)
    coeff = lax.dot_general(
        column, pick, (((0,), (0,)), ((), ())), preferred_element_type=jnp.float32
    )
    coeff_scr[...] = coeff[0:rank, :]

    slot = lax.broadcasted_iota(jnp.int32, (1, slots), 1)
    wanted = jnp.where(slot < count_ref[0], pairs_ref[0:1, :], -1)
    index = lax.broadcasted_iota(jnp.int32, (targets, slots), 0)
    place_scr[...] = jnp.where(index == wanted, 1.0, 0.0).astype(jnp.bfloat16)

    def multiply(step, carry):
        fetch(step).wait()
        for t in range(slots // FOLD):
            lanes = slice(t * FOLD, (t + 1) * FOLD)
            coeff = coeff_scr[:, lanes]
            for r in range(part):
                product = buffer[step * part + r, :, lanes].astype(jnp.float32) * coeff
                folded = product[0:SUBLANES]
                for s in range(1, rank // SUBLANES):
                    folded = folded + product[s * SUBLANES : (s + 1) * SUBLANES]
                start = pl.multiple_of((step * part + r) * SUBLANES, SUBLANES)
                for h in range(FOLD // LANES):
                    sum_scr[t * (FOLD // LANES) + h, pl.ds(start, SUBLANES), :] = folded[
                        :, h * LANES : (h + 1) * LANES
                    ]
        return carry

    lax.fori_loop(0, steps, multiply, 0)

    parts = []
    for t in range(slots // LANES):
        total = sum_scr[t, pl.ds(0, rank, stride=SUBLANES), :]
        for s in range(1, SUBLANES):
            total = total + sum_scr[t, pl.ds(s, rank, stride=SUBLANES), :]
        parts.append(total)
    coupled = jnp.concatenate(parts, axis=1)
    high = coupled.astype(jnp.bfloat16)
    low = (coupled - high.astype(jnp.float32)).astype(jnp.bfloat16)
    both = jnp.concatenate([high, low], axis=0)
    summed = lax.dot_general(
        place_scr[...], both, (((1,), (1,)), ((), ())), preferred_element_type=jnp.float32
    )
    summed_scr[...] = summed + pltpu.roll(summed, rank, 1)

    i = lax.axis_index("rows")
    j = lax.axis_index("cols")
    from_last = jnp.where(j < cols - 1, i, i - 1)
    from_first = jnp.where(j > 0, i, i + 1)
    start = pl.multiple_of((2 * jnp.maximum(from_last, 0) + 1) * clusters, clusters)
    last = gathered_ref[pl.ds(start, clusters), :].astype(jnp.float32)
    last = jnp.where(from_last >= 0, last, 0.0)
    start = pl.multiple_of(2 * jnp.minimum(from_first, rows - 1) * clusters, clusters)
    first = gathered_ref[pl.ds(start, clusters), :].astype(jnp.float32)
    first = jnp.where(from_first < rows, first, 0.0)
    after = jnp.where(j < cols - 1, j + 1, 0)
    lane = lax.broadcasted_iota(jnp.int32, (clusters, LANES), 1)
    for d in range(cols):
        halo = jnp.where(after == d, last, first)
        mine = summed_scr[d * clusters : (d + 1) * clusters, :]
        out_ref[d] = jnp.where(lane < rank, mine, halo).astype(out_ref.dtype)


def far_field(count, pairs, gathered, blocks, cols):
    rank, _, slots = blocks.shape
    rows = lax.axis_size("rows")
    clusters = gathered.shape[0] // (2 * rows)
    steps = SUBLANES
    vmem = pl.BlockSpec(memory_space=pltpu.VMEM)
    smem = pl.BlockSpec(memory_space=pltpu.SMEM)
    return pl.pallas_call(
        far_kernel,
        out_shape=jax.ShapeDtypeStruct((cols, clusters, LANES), jnp.bfloat16),
        in_specs=[smem, vmem, vmem, pl.BlockSpec(memory_space=pl.ANY)],
        out_specs=vmem,
        scratch_shapes=[
            pltpu.VMEM((rank, rank, slots), jnp.bfloat16),
            pltpu.VMEM((rank, slots), jnp.float32),
            pltpu.VMEM((slots // LANES, rank * SUBLANES, LANES), jnp.float32),
            pltpu.VMEM((cols * clusters, slots), jnp.bfloat16),
            pltpu.VMEM((cols * clusters, LANES), jnp.float32),
            pltpu.SemaphoreType.DMA((steps,)),
        ],
        compiler_params=pltpu.CompilerParams(vmem_limit_bytes=VMEM),
        cost_estimate=pl.CostEstimate(
            flops=2 * rank * rank * slots,
            bytes_accessed=2 * rank * rank * slots,
            transcendentals=0,
        ),
        name="far_field",
    )(count, pairs, gathered, blocks)


def replicate(rows, chunks, store):
    within = lax.broadcasted_iota(jnp.int32, (rows.shape[0], LANES), 1) % CHUNK
    for m in range(3 * chunks):
        tile = m // GROUPS
        store(
            m,
            jnp.take_along_axis(
                rows[:, tile * LANES : (tile + 1) * LANES],
                within + (m % GROUPS) * CHUNK,
                axis=1,
                mode="promise_in_bounds",
            ),
        )


def turn(row, index):
    wide = jnp.broadcast_to(row, (SUBLANES, LANES))
    return jnp.take_along_axis(wide, index, axis=1, mode="promise_in_bounds")


def turn_index():
    lane = lax.broadcasted_iota(jnp.int32, (SUBLANES, LANES), 1)
    sublane = lax.broadcasted_iota(jnp.int32, (SUBLANES, LANES), 0)
    group = lane // CHUNK
    return group * CHUNK + (lane + group * SUBLANES + sublane) % CHUNK


def pair_sums(tgt, src, chunks):
    sums = [None] * (3 * chunks)
    size = 3 * chunks
    for f in range(chunks):
        y = [src(c * chunks + f) for c in range(3)]
        u = [src(size + c * chunks + f) for c in range(3)]
        v = [src(2 * size + c * chunks + f) for c in range(3)]
        for h in range(chunks):
            r = [tgt[c * chunks + h] - y[c] for c in range(3)]
            q = (r[0] * r[0] + core_square) + (r[1] * r[1] + r[2] * r[2])
            s = r[0] * v[0] + (r[1] * v[1] + r[2] * v[2])
            inverse = lax.rsqrt(q)
            square = inverse * inverse
            weight = square * inverse
            s = s * square
            for c in range(3):
                term = weight * (u[c] - s * r[c])
                m = c * chunks + h
                sums[m] = term if sums[m] is None else sums[m] + term
    return sums


def gather_sums(acc_scr, clusters, chunks, store):
    own_group = lax.broadcasted_iota(jnp.int32, (clusters, LANES), 1) // CHUNK
    for t in range(pl.cdiv(3 * chunks, GROUPS)):
        merged = None
        for g in range(GROUPS):
            m = t * GROUPS + g
            if m >= 3 * chunks:
                break
            total = acc_scr[m, pl.ds(0, clusters, stride=SUBLANES), :]
            for s in range(1, SUBLANES):
                total = total + acc_scr[m, pl.ds(s, clusters, stride=SUBLANES), :]
            total = total + pltpu.roll(total, 2 * CHUNK, 1)
            total = total + pltpu.roll(total, CHUNK, 1)
            merged = total if merged is None else jnp.where(own_group == g, total, merged)
        store(t, merged)


def near_kernel(
    pairs_ref,
    count_ref,
    disp_ref,
    pos_ref,
    intact_ref,
    stiff_ref,
    out_ref,
    damage_ref,
    rest_ref,
    wide_scr,
    row_scr,
    src_a,
    src_b,
    acc_scr,
):
    clusters, width = disp_ref.shape
    elems = width // 3
    chunks = elems // CHUNK
    size = 3 * chunks
    slots = pairs_ref.shape[1]
    index = turn_index()

    for k, own in enumerate((pos_ref, disp_ref)):
        wide_scr[:, 0:width] = own[...]

        def store(m, value, k=k):
            row_scr[k * size + m] = value
            if k == 1:
                row_scr[2 * size + m] = 3.0 * value

        replicate(wide_scr[...], chunks, store)

    acc_scr[...] = jnp.zeros_like(acc_scr)
    count = count_ref[0]

    def place_sources(scr, first):
        for k in range(UNROLL):
            slot = jnp.minimum(first + k, slots - 1)
            source = jnp.clip(pairs_ref[1, slot] - HALO, 0, clusters - 1)
            for n in range(3 * size):
                scr[k, n] = turn(row_scr[n, pl.ds(source, 1), :], index)

    def one_pair(scr, k, slot, rest):
        target = pairs_ref[0, slot]
        source = pairs_ref[1, slot]
        live = slot < count
        own = jnp.logical_and(source >= HALO, source < clusters + HALO)
        into = jnp.where(jnp.logical_and(live, own), target, clusters) * SUBLANES
        into = pl.multiple_of(into, SUBLANES)
        rest_ref[1 + 2 * rest] = target
        rest_ref[2 + 2 * rest] = source
        rest = rest + jnp.where(jnp.logical_and(live, jnp.logical_not(own)), 1, 0)
        tgt = [
            jnp.broadcast_to(row_scr[m, pl.ds(target, 1), :], (SUBLANES, LANES))
            for m in range(size)
        ]
        sums = pair_sums(tgt, lambda n: scr[k, n], chunks)
        for m in range(size):
            acc_scr[m, pl.ds(into, SUBLANES), :] += sums[m]
        return rest

    def step(it, rest):
        first = it * 2 * UNROLL
        for this, other, start in (
            (src_a, src_b, first),
            (src_b, src_a, first + UNROLL),
        ):
            place_sources(other, start + UNROLL)
            for k in range(UNROLL):
                rest = one_pair(this, k, start + k, rest)
        return rest

    place_sources(src_a, 0)
    rest_ref[0] = lax.fori_loop(0, (count + 2 * UNROLL - 1) // (2 * UNROLL), step, 0)

    def store_sum(t, value):
        wide_scr[:, t * LANES : (t + 1) * LANES] = value

    gather_sums(acc_scr, clusters, chunks, store_sum)

    disp = [disp_ref[:, c * elems : (c + 1) * elems] for c in range(3)]
    separation = jnp.sqrt(1.0 + (disp[0] * disp[0] + disp[1] * disp[1] + disp[2] * disp[2]))
    softened = 1.0 - jnp.exp(-(separation - 1.0) / softening)
    intact = intact_ref[...].astype(jnp.float32)
    damage = intact * softened + (1.0 - intact)
    damage_ref[...] = damage
    hold = (1.0 - damage) * stiff_ref[...]
    for c in range(3):
        here = slice(c * elems, (c + 1) * elems)
        out_ref[:, here] = wide_scr[:, here] - hold * disp[c]


def near_field(pairs, count, disp, pos, intact, stiffness):
    clusters, width = disp.shape
    elems = width // 3
    chunks = elems // CHUNK
    padded = pl.cdiv(width, LANES) * LANES
    slots = pairs.shape[1]
    vmem = pl.BlockSpec(memory_space=pltpu.VMEM)
    smem = pl.BlockSpec(memory_space=pltpu.SMEM)
    return pl.pallas_call(
        near_kernel,
        out_shape=(
            jax.ShapeDtypeStruct((clusters, width), jnp.float32),
            jax.ShapeDtypeStruct((clusters, elems), jnp.float32),
            jax.ShapeDtypeStruct((2 * slots + 4,), jnp.int32),
        ),
        in_specs=[smem, smem] + [vmem] * 4,
        out_specs=(vmem, vmem, smem),
        scratch_shapes=[
            pltpu.VMEM((clusters, padded), jnp.float32),
            pltpu.VMEM((9 * chunks, clusters, LANES), jnp.float32),
            pltpu.VMEM((UNROLL, 9 * chunks, SUBLANES, LANES), jnp.float32),
            pltpu.VMEM((UNROLL, 9 * chunks, SUBLANES, LANES), jnp.float32),
            pltpu.VMEM((3 * chunks, (clusters + 1) * SUBLANES, LANES), jnp.float32),
        ],
        compiler_params=pltpu.CompilerParams(vmem_limit_bytes=VMEM),
        cost_estimate=pl.CostEstimate(
            flops=30 * slots * elems * elems,
            bytes_accessed=4 * clusters * width * 6,
            transcendentals=slots * elems * elems,
        ),
        name="near_field",
    )(pairs, count, disp, pos, intact, stiffness)


def finish_kernel(
    rest_ref,
    pos_ref,
    received_ref,
    near_ref,
    basis_ref,
    out_ref,
    basis_scr,
    ext_scr,
    halo_scr,
    row_scr,
    acc_scr,
    sem,
):
    clusters, width = pos_ref.shape
    cols = received_ref.shape[0]
    rank = basis_ref.shape[1]
    elems = width // 3
    chunks = elems // CHUNK
    size = 3 * chunks
    spare = LANES - rank
    segments = split_rows(width, spare)
    edge = 2 * HALO
    index = turn_index()

    fetch = pltpu.make_async_copy(basis_ref, basis_scr, sem)
    fetch.start()

    j = lax.axis_index("cols")
    before = jnp.where(j > 0, j - 1, cols - 1)
    after = jnp.where(j < cols - 1, j + 1, 0)
    for start, sender in ((0, before), (HALO, after)):
        halo_scr[...] = received_ref[sender].astype(jnp.float32)
        rows = edge * segments
        whole = halo_scr[0:rows, :]
        for n in range(1, PIECES):
            whole = whole + halo_scr[n * rows : (n + 1) * rows, :]
        for g in range(segments):
            count = min(spare, width - g * spare)
            for k in range(2):
                row = (2 * g + k) * HALO
                ext_scr[k, start : start + HALO, g * spare : g * spare + count] = whole[
                    row : row + HALO, rank : rank + count
                ]
    ext_scr[1, edge : edge + HALO, 0:width] = pos_ref[0:HALO, :]
    ext_scr[1, edge + HALO : 2 * edge, 0:width] = pos_ref[clusters - HALO :, :]
    for k in range(2):

        def store(m, value, k=k):
            row_scr[(1 - k) * size + m] = value
            if k == 0:
                row_scr[2 * size + m] = 3.0 * value

        replicate(ext_scr[k], chunks, store)

    acc_scr[...] = jnp.zeros_like(acc_scr)

    def step(n, carry):
        target = rest_ref[1 + 2 * n]
        source = rest_ref[2 + 2 * n]
        target = jnp.where(target < HALO, target, target - (clusters - edge))
        source = jnp.where(source < HALO, source, source - clusters)
        into = pl.multiple_of(target * SUBLANES, SUBLANES)
        tgt = [
            jnp.broadcast_to(row_scr[m, pl.ds(edge + target, 1), :], (SUBLANES, LANES))
            for m in range(size)
        ]
        sums = pair_sums(
            tgt, lambda k: turn(row_scr[k, pl.ds(source, 1), :], index), chunks
        )
        for m in range(size):
            acc_scr[m, pl.ds(into, SUBLANES), :] += sums[m]
        return carry

    lax.fori_loop(0, rest_ref[0], step, 0)

    def store_sum(t, value):
        ext_scr[0, :, t * LANES : (t + 1) * LANES] = value

    gather_sums(acc_scr, 2 * edge, chunks, store_sum)

    owned = received_ref[0].astype(jnp.float32)
    for d in range(1, cols):
        owned = owned + received_ref[d].astype(jnp.float32)
    fetch.wait()
    wide = lax.broadcasted_iota(jnp.int32, (SUBLANES, SUBLANES * rank), 1) // rank
    wide = wide == lax.broadcasted_iota(jnp.int32, (SUBLANES, SUBLANES * rank), 0)
    for k in range(clusters // SUBLANES):
        some = slice(k * SUBLANES, (k + 1) * SUBLANES)
        tiled = jnp.concatenate([owned[some, 0:rank]] * SUBLANES, axis=1)
        diagonal = jnp.where(wide, tiled, 0.0).astype(jnp.bfloat16)
        out_ref[some, :] = near_ref[some, :] + jnp.dot(
            diagonal,
            basis_scr[some].reshape(SUBLANES * rank, width),
            preferred_element_type=jnp.float32,
        )
    out_ref[0:HALO, :] += ext_scr[0, 0:HALO, 0:width]
    out_ref[clusters - HALO :, :] += ext_scr[0, HALO:edge, 0:width]


def finish(rest, pos, received, near, basis):
    clusters, width = pos.shape
    rank = basis.shape[1]
    chunks = width // 3 // CHUNK
    padded = pl.cdiv(width, LANES) * LANES
    edge = 2 * HALO
    vmem = pl.BlockSpec(memory_space=pltpu.VMEM)
    smem = pl.BlockSpec(memory_space=pltpu.SMEM)
    return pl.pallas_call(
        finish_kernel,
        out_shape=jax.ShapeDtypeStruct((clusters, width), jnp.float32),
        in_specs=[smem] + [vmem] * 3 + [pl.BlockSpec(memory_space=pl.ANY)],
        out_specs=vmem,
        scratch_shapes=[
            pltpu.VMEM(basis.shape, basis.dtype),
            pltpu.VMEM((2, 2 * edge, padded), jnp.float32),
            pltpu.VMEM((clusters, LANES), jnp.float32),
            pltpu.VMEM((9 * chunks, 2 * edge, LANES), jnp.float32),
            pltpu.VMEM((3 * chunks, 2 * edge * SUBLANES, LANES), jnp.float32),
            pltpu.SemaphoreType.DMA(()),
        ],
        compiler_params=pltpu.CompilerParams(vmem_limit_bytes=VMEM),
        cost_estimate=pl.CostEstimate(
            flops=2 * clusters * rank * width,
            bytes_accessed=2 * clusters * rank * width,
            transcendentals=0,
        ),
        name="finish",
    )(rest, pos, received, near, basis)


def local(
    displacement,
    positions,
    cluster_basis,
    near_pairs,
    near_count,
    far_pairs,
    far_count,
    far_blocks,
    intact,
    stiffness,
):
    cols = lax.axis_size("cols")
    basis = cluster_basis.transpose(0, 2, 1)
    payload = project(displacement, positions, basis)
    gathered = lax.all_gather(payload, "rows", axis=0, tiled=True)
    partial = far_field(far_count, far_pairs.T, gathered, far_blocks.transpose(1, 2, 0), cols)
    received = lax.all_to_all(partial, "cols", split_axis=0, concat_axis=0)
    near, damage, rest = near_field(
        near_pairs.T, near_count, displacement, positions, intact, stiffness
    )
    return finish(rest, positions, received, near, basis), damage


def solution(mesh):
    both = ("rows", "cols")
    in_specs = (
        P(both, None),
        P(both, None),
        P(both, None, None),
        P(both, None),
        P(both),
        P(both, None),
        P(both),
        P(both, None, None),
        P(both, None),
        P(both, None),
    )
    out_specs = (P(both, None), P(both, None))
    return jax.shard_map(local, mesh=mesh, in_specs=in_specs, out_specs=out_specs, check_vma=False)
```

```python
import functools

import jax
import jax.numpy as jnp
from jax import lax
from jax.experimental import pallas as pl
from jax.experimental.pallas import tpu as pltpu
from jax.sharding import PartitionSpec as P

HALO = 2
LANES = 128
SUBLANES = 8
CHUNK = 32
GROUPS = LANES // CHUNK
core_square = 0.25
softening = 1.5
UNROLL = 4
FOLD = 256
PIECES = 3
VMEM = 60 * 1024 * 1024


def split_rows(width, lanes):
    return pl.cdiv(width, lanes)


def in_hbm(count):
    return [pl.BlockSpec(memory_space=pltpu.HBM)] * count


def start_all(sems, moves):
    copies = [
        pltpu.make_async_copy(source, target, sems.at[n])
        for n, (source, target) in enumerate(moves)
    ]
    for copy in copies:
        copy.start()
    return copies


def project_kernel(
    disp_hbm, pos_hbm, basis_ref, out_ref, disp_ref, pos_ref, stage_scr, basis_scr, sems, basis_sems
):
    clusters, rank, width = basis_ref.shape
    spare = LANES - rank
    segments = split_rows(width, spare)
    rows = 2 * HALO
    fetches = basis_sems.shape[0]
    part = clusters // fetches

    def fetch(k):
        here = pl.ds(k * part, part)
        return pltpu.make_async_copy(basis_ref.at[here], basis_scr.at[here], basis_sems.at[k])

    inputs = start_all(sems, ((disp_hbm, disp_ref), (pos_hbm, pos_ref)))
    for k in range(fetches):
        fetch(k).start()
    stage_scr[...] = jnp.zeros_like(stage_scr)
    for copy in inputs:
        copy.wait()

    for side, start in enumerate((0, clusters - HALO)):
        block = jnp.concatenate(
            [disp_ref[start : start + HALO, :], pos_ref[start : start + HALO, :]], axis=0
        )
        for n in range(PIECES):
            piece = block.astype(jnp.bfloat16).astype(jnp.float32)
            block = block - piece
            for g in range(segments):
                size = min(spare, width - g * spare)
                row = side * clusters + (n * segments + g) * rows
                stage_scr[row : row + rows, rank : rank + size] = piece[
                    :, g * spare : g * spare + size
                ]

    disp_bf = disp_ref[...].astype(jnp.bfloat16)
    for k in range(clusters // SUBLANES):
        group = slice(k * SUBLANES, (k + 1) * SUBLANES)
        if (k * SUBLANES) % part == 0:
            fetch(k * SUBLANES // part).wait()
        basis = basis_scr[group].reshape(SUBLANES * rank, width)
        product = lax.dot_general(
            disp_bf[group, :],
            basis,
            (((1,), (1,)), ((), ())),
            preferred_element_type=jnp.float32,
        )
        row = lax.broadcasted_iota(jnp.int32, (SUBLANES, rank), 0)
        coeff = jnp.zeros((SUBLANES, rank), jnp.float32)
        for i in range(SUBLANES):
            coeff = jnp.where(row == i, product[:, i * rank : (i + 1) * rank], coeff)
        stage_scr[group, 0:rank] = coeff
    out_ref[...] = stage_scr[...].astype(out_ref.dtype)


def project(disp, pos, basis):
    clusters, rank, width = basis.shape
    vmem = pl.BlockSpec(memory_space=pltpu.VMEM)
    return pl.pallas_call(
        project_kernel,
        out_shape=jax.ShapeDtypeStruct((2 * clusters, LANES), jnp.bfloat16),
        in_specs=in_hbm(3),
        out_specs=vmem,
        scratch_shapes=[
            pltpu.VMEM(disp.shape, disp.dtype),
            pltpu.VMEM(pos.shape, pos.dtype),
            pltpu.VMEM((2 * clusters, LANES), jnp.float32),
            pltpu.VMEM(basis.shape, basis.dtype),
            pltpu.SemaphoreType.DMA((2,)),
            pltpu.SemaphoreType.DMA((4,)),
        ],
        compiler_params=pltpu.CompilerParams(vmem_limit_bytes=VMEM),
        cost_estimate=pl.CostEstimate(
            flops=2 * clusters * rank * width,
            bytes_accessed=2 * clusters * rank * width,
            transcendentals=0,
        ),
        name="project",
    )(disp, pos, basis)


def far_kernel(
    count_hbm,
    pairs_hbm,
    gathered_hbm,
    blocks_ref,
    out_ref,
    count_ref,
    pairs_ref,
    gathered_ref,
    buffer,
    column_scr,
    coeff_scr,
    place_scr,
    sum_scr,
    summed_scr,
    sems,
    block_sems,
):
    rank, _, slots = buffer.shape
    cols, clusters, _ = out_ref.shape
    targets = cols * clusters
    rows = gathered_ref.shape[0] // (2 * clusters)
    sources = rows * clusters
    tiles = slots // FOLD

    def fetch(t):
        here = pl.ds(pl.multiple_of(t * FOLD, FOLD), FOLD)
        return pltpu.make_async_copy(
            blocks_ref.at[:, :, here], buffer.at[:, :, here], block_sems.at[t]
        )

    inputs = start_all(
        sems, ((count_hbm, count_ref), (pairs_hbm, pairs_ref), (gathered_hbm, gathered_ref))
    )
    fetch(0).start()
    summed_scr[...] = jnp.zeros_like(summed_scr)
    inputs[0].wait()
    count = count_ref[0]
    live = (count + FOLD - 1) // FOLD
    for t in range(1, tiles):

        @pl.when(t < live)
        def _(t=t):
            fetch(t).start()

    inputs[1].wait()
    inputs[2].wait()
    for i in range(rows):
        column_scr[i * clusters : (i + 1) * clusters, :] = gathered_ref[
            2 * i * clusters : (2 * i + 1) * clusters, :
        ]

    def multiply(t, carry):
        start = pl.multiple_of(t * FOLD, FOLD)
        lanes = pl.ds(start, FOLD)
        index = lax.broadcasted_iota(jnp.int32, (sources, FOLD), 0)
        pick = jnp.where(index == pairs_ref[1:2, lanes], 1.0, 0.0).astype(jnp.bfloat16)
        coeff = lax.dot_general(
            column_scr[...], pick, (((0,), (0,)), ((), ())), preferred_element_type=jnp.float32
        )
        coeff_scr[...] = coeff[0:rank, :]
        slot = lax.broadcasted_iota(jnp.int32, (1, FOLD), 1) + start
        wanted = jnp.where(slot < count, pairs_ref[0:1, lanes], -1)
        index = lax.broadcasted_iota(jnp.int32, (targets, FOLD), 0)
        place_scr[...] = jnp.where(index == wanted, 1.0, 0.0).astype(jnp.bfloat16)
        fetch(t).wait()

        def some_rows(k, carry):
            coeff = coeff_scr[...]
            for i in range(SUBLANES):
                r = k * SUBLANES + i
                product = buffer[r, :, lanes].astype(jnp.float32) * coeff
                folded = product[0:SUBLANES]
                for s in range(1, rank // SUBLANES):
                    folded = folded + product[s * SUBLANES : (s + 1) * SUBLANES]
                here = pl.ds(pl.multiple_of(r * SUBLANES, SUBLANES), SUBLANES)
                for h in range(FOLD // LANES):
                    sum_scr[h, here, :] = folded[:, h * LANES : (h + 1) * LANES]
            return carry

        lax.fori_loop(0, rank // SUBLANES, some_rows, 0)
        parts = []
        for h in range(FOLD // LANES):
            total = sum_scr[h, pl.ds(0, rank, stride=SUBLANES), :]
            for s in range(1, SUBLANES):
                total = total + sum_scr[h, pl.ds(s, rank, stride=SUBLANES), :]
            parts.append(total)
        coupled = jnp.concatenate(parts, axis=1)
        high = coupled.astype(jnp.bfloat16)
        low = (coupled - high.astype(jnp.float32)).astype(jnp.bfloat16)
        both = jnp.concatenate([high, low], axis=0)
        summed_scr[...] += lax.dot_general(
            place_scr[...], both, (((1,), (1,)), ((), ())), preferred_element_type=jnp.float32
        )
        return carry

    lax.fori_loop(0, live, multiply, 0)

    i = lax.axis_index("rows")
    j = lax.axis_index("cols")
    from_last = jnp.where(j < cols - 1, i, i - 1)
    from_first = jnp.where(j > 0, i, i + 1)
    start = pl.multiple_of((2 * jnp.maximum(from_last, 0) + 1) * clusters, clusters)
    last = gathered_ref[pl.ds(start, clusters), :].astype(jnp.float32)
    last = jnp.where(from_last >= 0, last, 0.0)
    start = pl.multiple_of(2 * jnp.minimum(from_first, rows - 1) * clusters, clusters)
    first = gathered_ref[pl.ds(start, clusters), :].astype(jnp.float32)
    first = jnp.where(from_first < rows, first, 0.0)
    after = jnp.where(j < cols - 1, j + 1, 0)
    lane = lax.broadcasted_iota(jnp.int32, (clusters, LANES), 1)
    for d in range(cols):
        halo = jnp.where(after == d, last, first)
        mine = summed_scr[d * clusters : (d + 1) * clusters, :]
        mine = mine + pltpu.roll(mine, rank, 1)
        out_ref[d] = jnp.where(lane < rank, mine, halo).astype(out_ref.dtype)


def far_field(count, pairs, gathered, blocks, cols):
    rank, _, slots = blocks.shape
    rows = lax.axis_size("rows")
    clusters = gathered.shape[0] // (2 * rows)
    return pl.pallas_call(
        far_kernel,
        out_shape=jax.ShapeDtypeStruct((cols, clusters, LANES), jnp.bfloat16),
        in_specs=in_hbm(3) + [pl.BlockSpec(memory_space=pl.ANY)],
        out_specs=pl.BlockSpec(memory_space=pltpu.VMEM),
        scratch_shapes=[
            pltpu.SMEM(count.shape, count.dtype),
            pltpu.VMEM(pairs.shape, pairs.dtype),
            pltpu.VMEM(gathered.shape, gathered.dtype),
            pltpu.VMEM(blocks.shape, blocks.dtype),
            pltpu.VMEM((rows * clusters, LANES), jnp.bfloat16),
            pltpu.VMEM((rank, FOLD), jnp.float32),
            pltpu.VMEM((cols * clusters, FOLD), jnp.bfloat16),
            pltpu.VMEM((FOLD // LANES, rank * SUBLANES, LANES), jnp.float32),
            pltpu.VMEM((cols * clusters, LANES), jnp.float32),
            pltpu.SemaphoreType.DMA((3,)),
            pltpu.SemaphoreType.DMA((slots // FOLD,)),
        ],
        compiler_params=pltpu.CompilerParams(vmem_limit_bytes=VMEM),
        cost_estimate=pl.CostEstimate(
            flops=2 * rank * rank * slots,
            bytes_accessed=2 * rank * rank * slots,
            transcendentals=0,
        ),
        name="far_field",
    )(count, pairs, gathered, blocks)


def replicate(rows, chunks, store, turned):
    within = lax.broadcasted_iota(jnp.int32, (rows.shape[0], LANES), 1)
    if turned:
        within = within + (within // CHUNK) * SUBLANES
    within = within % CHUNK
    for m in range(3 * chunks):
        tile = m // GROUPS
        store(
            m,
            jnp.take_along_axis(
                rows[:, tile * LANES : (tile + 1) * LANES],
                within + (m % GROUPS) * CHUNK,
                axis=1,
                mode="promise_in_bounds",
            ),
        )


def turn(row):
    wide = jnp.broadcast_to(row, (SUBLANES, LANES))
    return pltpu.roll(wide, 0, 1, stride=1, stride_axis=0)


def pair_sums(tgt, src, chunks):
    sums = [None] * (3 * chunks)
    size = 3 * chunks
    for f in range(chunks):
        y = [src(c * chunks + f) for c in range(3)]
        u = [src(size + c * chunks + f) for c in range(3)]
        v = [src(2 * size + c * chunks + f) for c in range(3)]
        for h in range(chunks):
            r = [tgt[c * chunks + h] - y[c] for c in range(3)]
            q = (r[0] * r[0] + core_square) + (r[1] * r[1] + r[2] * r[2])
            s = r[0] * v[0] + (r[1] * v[1] + r[2] * v[2])
            inverse = lax.rsqrt(q)
            square = inverse * inverse
            weight = square * inverse
            s = s * square
            for c in range(3):
                term = weight * (u[c] - s * r[c])
                m = c * chunks + h
                sums[m] = term if sums[m] is None else sums[m] + term
    return sums


def gather_sums(acc_scr, clusters, chunks, store):
    own_group = lax.broadcasted_iota(jnp.int32, (clusters, LANES), 1) // CHUNK
    for t in range(pl.cdiv(3 * chunks, GROUPS)):
        merged = None
        for g in range(GROUPS):
            m = t * GROUPS + g
            if m >= 3 * chunks:
                break
            total = acc_scr[m, pl.ds(0, clusters, stride=SUBLANES), :]
            for s in range(1, SUBLANES):
                total = total + acc_scr[m, pl.ds(s, clusters, stride=SUBLANES), :]
            total = total + pltpu.roll(total, 2 * CHUNK, 1)
            total = total + pltpu.roll(total, CHUNK, 1)
            merged = total if merged is None else jnp.where(own_group == g, total, merged)
        store(t, merged)


def near_kernel(
    pairs_hbm,
    count_hbm,
    disp_hbm,
    pos_hbm,
    intact_hbm,
    stiff_hbm,
    out_hbm,
    damage_hbm,
    rest_hbm,
    pairs_ref,
    count_ref,
    disp_ref,
    pos_ref,
    intact_ref,
    stiff_ref,
    out_ref,
    damage_ref,
    rest_ref,
    wide_scr,
    tgt_scr,
    row_scr,
    src_a,
    src_b,
    acc_scr,
    sems,
    out_sems,
):
    clusters, width = disp_ref.shape
    elems = width // 3
    chunks = elems // CHUNK
    size = 3 * chunks
    slots = pairs_ref.shape[1]

    inputs = start_all(
        sems,
        (
            (pos_hbm, pos_ref),
            (disp_hbm, disp_ref),
            (pairs_hbm, pairs_ref),
            (count_hbm, count_ref),
            (intact_hbm, intact_ref),
            (stiff_hbm, stiff_ref),
        ),
    )
    acc_scr[...] = jnp.zeros_like(acc_scr)
    for k, own in enumerate((pos_ref, disp_ref)):
        inputs[k].wait()
        wide_scr[k, :, 0:width] = own[...]

        def store(m, value, k=k):
            row_scr[k * size + m] = value
            if k == 1:
                row_scr[2 * size + m] = 3.0 * value

        replicate(wide_scr[k], chunks, store, True)

    def store_target(m, value):
        tgt_scr[m] = value

    replicate(wide_scr[0], chunks, store_target, False)
    for copy in inputs[2:]:
        copy.wait()
    count = count_ref[0]

    disp = [disp_ref[:, c * elems : (c + 1) * elems] for c in range(3)]
    separation = jnp.sqrt(1.0 + (disp[0] * disp[0] + disp[1] * disp[1] + disp[2] * disp[2]))
    softened = 1.0 - jnp.exp(-(separation - 1.0) / softening)
    intact = intact_ref[...].astype(jnp.float32)
    damage = intact * softened + (1.0 - intact)
    damage_ref[...] = damage
    damage_out = pltpu.make_async_copy(damage_ref, damage_hbm, out_sems.at[0])
    damage_out.start()
    hold = (1.0 - damage) * stiff_ref[...]
    for c in range(3):
        out_ref[:, c * elems : (c + 1) * elems] = -hold * disp[c]

    def place_sources(scr, first):
        for k in range(UNROLL):
            slot = jnp.minimum(first + k, slots - 1)
            source = jnp.clip(pairs_ref[1, slot] - HALO, 0, clusters - 1)
            for n in range(3 * size):
                scr[k, n] = turn(row_scr[n, pl.ds(source, 1), :])

    def one_pair(scr, k, slot, rest):
        target = pairs_ref[0, slot]
        source = pairs_ref[1, slot]
        live = slot < count
        own = jnp.logical_and(source >= HALO, source < clusters + HALO)
        into = jnp.where(jnp.logical_and(live, own), target, clusters) * SUBLANES
        into = pl.multiple_of(into, SUBLANES)
        rest_ref[1 + 2 * rest] = target
        rest_ref[2 + 2 * rest] = source
        rest = rest + jnp.where(jnp.logical_and(live, jnp.logical_not(own)), 1, 0)
        tgt = [
            jnp.broadcast_to(tgt_scr[m, pl.ds(target, 1), :], (SUBLANES, LANES))
            for m in range(size)
        ]
        sums = pair_sums(tgt, lambda n: scr[k, n], chunks)
        for m in range(size):
            acc_scr[m, pl.ds(into, SUBLANES), :] += sums[m]
        return rest

    def step(it, rest):
        first = it * 2 * UNROLL
        for this, other, start in (
            (src_a, src_b, first),
            (src_b, src_a, first + UNROLL),
        ):
            place_sources(other, start + UNROLL)
            for k in range(UNROLL):
                rest = one_pair(this, k, start + k, rest)
        return rest

    place_sources(src_a, 0)
    rest_ref[0] = lax.fori_loop(0, (count + 2 * UNROLL - 1) // (2 * UNROLL), step, 0)
    rest_out = pltpu.make_async_copy(rest_ref, rest_hbm, out_sems.at[1])
    rest_out.start()

    def store_sum(t, value):
        wide_scr[0, :, t * LANES : (t + 1) * LANES] = value

    gather_sums(acc_scr, clusters, chunks, store_sum)
    out_ref[...] += wide_scr[0, :, 0:width]
    near_out = pltpu.make_async_copy(out_ref, out_hbm, out_sems.at[2])
    near_out.start()
    for copy in (damage_out, rest_out, near_out):
        copy.wait()


def near_field(pairs, count, disp, pos, intact, stiffness):
    clusters, width = disp.shape
    elems = width // 3
    chunks = elems // CHUNK
    padded = pl.cdiv(width, LANES) * LANES
    slots = pairs.shape[1]
    return pl.pallas_call(
        near_kernel,
        out_shape=(
            jax.ShapeDtypeStruct((clusters, width), jnp.float32),
            jax.ShapeDtypeStruct((clusters, elems), jnp.float32),
            jax.ShapeDtypeStruct((2 * slots + 4,), jnp.int32),
        ),
        in_specs=in_hbm(6),
        out_specs=tuple(in_hbm(3)),
        scratch_shapes=[
            pltpu.SMEM(pairs.shape, pairs.dtype),
            pltpu.SMEM(count.shape, count.dtype),
            pltpu.VMEM(disp.shape, disp.dtype),
            pltpu.VMEM(pos.shape, pos.dtype),
            pltpu.VMEM(intact.shape, intact.dtype),
            pltpu.VMEM(stiffness.shape, stiffness.dtype),
            pltpu.VMEM((clusters, width), jnp.float32),
            pltpu.VMEM((clusters, elems), jnp.float32),
            pltpu.SMEM((2 * slots + 4,), jnp.int32),
            pltpu.VMEM((2, clusters, padded), jnp.float32),
            pltpu.VMEM((3 * chunks, clusters, LANES), jnp.float32),
            pltpu.VMEM((9 * chunks, clusters, LANES), jnp.float32),
            pltpu.VMEM((UNROLL, 9 * chunks, SUBLANES, LANES), jnp.float32),
            pltpu.VMEM((UNROLL, 9 * chunks, SUBLANES, LANES), jnp.float32),
            pltpu.VMEM((3 * chunks, (clusters + 1) * SUBLANES, LANES), jnp.float32),
            pltpu.SemaphoreType.DMA((6,)),
            pltpu.SemaphoreType.DMA((3,)),
        ],
        compiler_params=pltpu.CompilerParams(vmem_limit_bytes=VMEM),
        cost_estimate=pl.CostEstimate(
            flops=30 * slots * elems * elems,
            bytes_accessed=4 * clusters * width * 6,
            transcendentals=slots * elems * elems,
        ),
        name="near_field",
    )(pairs, count, disp, pos, intact, stiffness)


def finish_kernel(
    rest_hbm,
    pos_hbm,
    received_hbm,
    near_hbm,
    basis_hbm,
    out_ref,
    rest_ref,
    pos_ref,
    received_ref,
    near_ref,
    basis_scr,
    ext_scr,
    halo_scr,
    tgt_scr,
    row_scr,
    acc_scr,
    sems,
):
    clusters, width = pos_ref.shape
    cols = received_ref.shape[0]
    rank = basis_scr.shape[1]
    elems = width // 3
    chunks = elems // CHUNK
    size = 3 * chunks
    spare = LANES - rank
    segments = split_rows(width, spare)
    edge = 2 * HALO

    inputs = start_all(
        sems,
        (
            (received_hbm, received_ref),
            (pos_hbm, pos_ref),
            (rest_hbm, rest_ref),
            (near_hbm, near_ref),
            (basis_hbm, basis_scr),
        ),
    )
    acc_scr[...] = jnp.zeros_like(acc_scr)
    inputs[0].wait()
    inputs[1].wait()

    j = lax.axis_index("cols")
    before = jnp.where(j > 0, j - 1, cols - 1)
    after = jnp.where(j < cols - 1, j + 1, 0)
    for start, sender in ((0, before), (HALO, after)):
        halo_scr[...] = received_ref[sender].astype(jnp.float32)
        rows = edge * segments
        whole = halo_scr[0:rows, :]
        for n in range(1, PIECES):
            whole = whole + halo_scr[n * rows : (n + 1) * rows, :]
        for g in range(segments):
            count = min(spare, width - g * spare)
            for k in range(2):
                row = (2 * g + k) * HALO
                ext_scr[k, start : start + HALO, g * spare : g * spare + count] = whole[
                    row : row + HALO, rank : rank + count
                ]
    ext_scr[1, edge : edge + HALO, 0:width] = pos_ref[0:HALO, :]
    ext_scr[1, edge + HALO : 2 * edge, 0:width] = pos_ref[clusters - HALO :, :]
    for k in range(2):

        def store(m, value, k=k):
            row_scr[(1 - k) * size + m] = value
            if k == 0:
                row_scr[2 * size + m] = 3.0 * value

        replicate(ext_scr[k], chunks, store, True)

    def store_target(m, value):
        tgt_scr[m] = value

    replicate(ext_scr[1], chunks, store_target, False)
    inputs[2].wait()

    def step(n, carry):
        target = rest_ref[1 + 2 * n]
        source = rest_ref[2 + 2 * n]
        target = jnp.where(target < HALO, target, target - (clusters - edge))
        source = jnp.where(source < HALO, source, source - clusters)
        into = pl.multiple_of(target * SUBLANES, SUBLANES)
        tgt = [
            jnp.broadcast_to(tgt_scr[m, pl.ds(edge + target, 1), :], (SUBLANES, LANES))
            for m in range(size)
        ]
        sums = pair_sums(tgt, lambda k: turn(row_scr[k, pl.ds(source, 1), :]), chunks)
        for m in range(size):
            acc_scr[m, pl.ds(into, SUBLANES), :] += sums[m]
        return carry

    lax.fori_loop(0, rest_ref[0], step, 0)

    def store_sum(t, value):
        ext_scr[0, :, t * LANES : (t + 1) * LANES] = value

    gather_sums(acc_scr, 2 * edge, chunks, store_sum)

    owned = received_ref[0].astype(jnp.float32)
    for d in range(1, cols):
        owned = owned + received_ref[d].astype(jnp.float32)
    inputs[3].wait()
    inputs[4].wait()
    wide = lax.broadcasted_iota(jnp.int32, (SUBLANES, SUBLANES * rank), 1) // rank
    wide = wide == lax.broadcasted_iota(jnp.int32, (SUBLANES, SUBLANES * rank), 0)
    for k in range(clusters // SUBLANES):
        some = slice(k * SUBLANES, (k + 1) * SUBLANES)
        tiled = jnp.concatenate([owned[some, 0:rank]] * SUBLANES, axis=1)
        diagonal = jnp.where(wide, tiled, 0.0).astype(jnp.bfloat16)
        out_ref[some, :] = near_ref[some, :] + jnp.dot(
            diagonal,
            basis_scr[some].reshape(SUBLANES * rank, width),
            preferred_element_type=jnp.float32,
        )
    out_ref[0:HALO, :] += ext_scr[0, 0:HALO, 0:width]
    out_ref[clusters - HALO :, :] += ext_scr[0, HALO:edge, 0:width]


def finish(rest, pos, received, near, basis):
    clusters, width = pos.shape
    rank = basis.shape[1]
    chunks = width // 3 // CHUNK
    padded = pl.cdiv(width, LANES) * LANES
    edge = 2 * HALO
    return pl.pallas_call(
        finish_kernel,
        out_shape=jax.ShapeDtypeStruct((clusters, width), jnp.float32),
        in_specs=in_hbm(5),
        out_specs=pl.BlockSpec(memory_space=pltpu.VMEM),
        scratch_shapes=[
            pltpu.SMEM(rest.shape, rest.dtype),
            pltpu.VMEM(pos.shape, pos.dtype),
            pltpu.VMEM(received.shape, received.dtype),
            pltpu.VMEM(near.shape, near.dtype),
            pltpu.VMEM(basis.shape, basis.dtype),
            pltpu.VMEM((2, 2 * edge, padded), jnp.float32),
            pltpu.VMEM((clusters, LANES), jnp.float32),
            pltpu.VMEM((3 * chunks, 2 * edge, LANES), jnp.float32),
            pltpu.VMEM((9 * chunks, 2 * edge, LANES), jnp.float32),
            pltpu.VMEM((3 * chunks, 2 * edge * SUBLANES, LANES), jnp.float32),
            pltpu.SemaphoreType.DMA((5,)),
        ],
        compiler_params=pltpu.CompilerParams(vmem_limit_bytes=VMEM),
        cost_estimate=pl.CostEstimate(
            flops=2 * clusters * rank * width,
            bytes_accessed=2 * clusters * rank * width,
            transcendentals=0,
        ),
        name="finish",
    )(rest, pos, received, near, basis)


def local(
    displacement,
    positions,
    cluster_basis,
    near_pairs,
    near_count,
    far_pairs,
    far_count,
    far_blocks,
    intact,
    stiffness,
):
    cols = lax.axis_size("cols")
    basis = cluster_basis.transpose(0, 2, 1)
    payload = project(displacement, positions, basis)
    gathered = lax.all_gather(payload, "rows", axis=0, tiled=True)
    partial = far_field(far_count, far_pairs.T, gathered, far_blocks.transpose(1, 2, 0), cols)
    received = lax.all_to_all(partial, "cols", split_axis=0, concat_axis=0)
    near, damage, rest = near_field(
        near_pairs.T, near_count, displacement, positions, intact, stiffness
    )
    return finish(rest, positions, received, near, basis), damage


def solution(mesh):
    both = ("rows", "cols")
    in_specs = (
        P(both, None),
        P(both, None),
        P(both, None, None),
        P(both, None),
        P(both),
        P(both, None),
        P(both),
        P(both, None, None),
        P(both, None),
        P(both, None),
    )
    out_specs = (P(both, None), P(both, None))
    return jax.shard_map(local, mesh=mesh, in_specs=in_specs, out_specs=out_specs, check_vma=False)
```

```python
import functools

import jax
import jax.numpy as jnp
from jax import lax
from jax.experimental import pallas as pl
from jax.experimental.pallas import tpu as pltpu
from jax.sharding import PartitionSpec as P

HALO = 2
LANES = 128
SUBLANES = 8
CHUNK = 32
GROUPS = LANES // CHUNK
core_square = 0.25
softening = 1.5
UNROLL = 4
FOLD = 256
PIECES = 3
VMEM = 60 * 1024 * 1024


def split_rows(width, lanes):
    return pl.cdiv(width, lanes)


def in_hbm(count):
    return [pl.BlockSpec(memory_space=pltpu.HBM)] * count


def start_all(sems, moves):
    copies = [
        pltpu.make_async_copy(source, target, sems.at[n])
        for n, (source, target) in enumerate(moves)
    ]
    for copy in copies:
        copy.start()
    return copies


def project_kernel(disp_ref, pos_ref, basis_ref, out_ref, stage_scr):
    clusters, width = disp_ref.shape
    part, rank, _ = basis_ref.shape
    spare = LANES - rank
    segments = split_rows(width, spare)
    rows = 2 * HALO
    step = pl.program_id(0)

    @pl.when(step == 0)
    def _():
        stage_scr[...] = jnp.zeros_like(stage_scr)
        for side, start in enumerate((0, clusters - HALO)):
            block = jnp.concatenate(
                [disp_ref[start : start + HALO, :], pos_ref[start : start + HALO, :]], axis=0
            )
            for n in range(PIECES):
                piece = block.astype(jnp.bfloat16).astype(jnp.float32)
                block = block - piece
                for g in range(segments):
                    size = min(spare, width - g * spare)
                    row = side * clusters + (n * segments + g) * rows
                    stage_scr[row : row + rows, rank : rank + size] = piece[
                        :, g * spare : g * spare + size
                    ]

    for k in range(part // SUBLANES):
        here = pl.ds(pl.multiple_of(step * part + k * SUBLANES, SUBLANES), SUBLANES)
        basis = basis_ref[k * SUBLANES : (k + 1) * SUBLANES].reshape(SUBLANES * rank, width)
        product = lax.dot_general(
            disp_ref[here, :].astype(jnp.bfloat16),
            basis,
            (((1,), (1,)), ((), ())),
            preferred_element_type=jnp.float32,
        )
        row = lax.broadcasted_iota(jnp.int32, (SUBLANES, rank), 0)
        coeff = jnp.zeros((SUBLANES, rank), jnp.float32)
        for i in range(SUBLANES):
            coeff = jnp.where(row == i, product[:, i * rank : (i + 1) * rank], coeff)
        stage_scr[here, 0:rank] = coeff

    @pl.when(step == pl.num_programs(0) - 1)
    def _():
        out_ref[...] = stage_scr[...].astype(out_ref.dtype)


def project(disp, pos, basis):
    clusters, rank, width = basis.shape
    steps = 4
    whole = pl.BlockSpec((clusters, width), lambda k: (0, 0))
    return pl.pallas_call(
        project_kernel,
        grid=(steps,),
        out_shape=jax.ShapeDtypeStruct((2 * clusters, LANES), jnp.bfloat16),
        in_specs=[
            whole,
            whole,
            pl.BlockSpec((clusters // steps, rank, width), lambda k: (k, 0, 0)),
        ],
        out_specs=pl.BlockSpec((2 * clusters, LANES), lambda k: (0, 0)),
        scratch_shapes=[pltpu.VMEM((2 * clusters, LANES), jnp.float32)],
        compiler_params=pltpu.CompilerParams(vmem_limit_bytes=VMEM),
        cost_estimate=pl.CostEstimate(
            flops=2 * clusters * rank * width,
            bytes_accessed=2 * clusters * rank * width,
            transcendentals=0,
        ),
        name="project",
    )(disp, pos, basis)


def far_kernel(
    count_hbm,
    pairs_hbm,
    gathered_hbm,
    blocks_ref,
    out_ref,
    count_ref,
    pairs_ref,
    gathered_ref,
    buffer,
    column_scr,
    coeff_scr,
    place_scr,
    sum_scr,
    summed_scr,
    sems,
    block_sems,
):
    rank, _, slots = buffer.shape
    cols, clusters, _ = out_ref.shape
    targets = cols * clusters
    rows = gathered_ref.shape[0] // (2 * clusters)
    sources = rows * clusters
    tiles = slots // FOLD

    def fetch(t):
        here = pl.ds(pl.multiple_of(t * FOLD, FOLD), FOLD)
        return pltpu.make_async_copy(
            blocks_ref.at[:, :, here], buffer.at[:, :, here], block_sems.at[t]
        )

    inputs = start_all(
        sems, ((count_hbm, count_ref), (pairs_hbm, pairs_ref), (gathered_hbm, gathered_ref))
    )
    fetch(0).start()
    summed_scr[...] = jnp.zeros_like(summed_scr)
    inputs[0].wait()
    count = count_ref[0]
    live = (count + FOLD - 1) // FOLD
    for t in range(1, tiles):

        @pl.when(t < live)
        def _(t=t):
            fetch(t).start()

    inputs[1].wait()
    inputs[2].wait()
    for i in range(rows):
        column_scr[i * clusters : (i + 1) * clusters, :] = gathered_ref[
            2 * i * clusters : (2 * i + 1) * clusters, :
        ]

    def multiply(t, carry):
        start = pl.multiple_of(t * FOLD, FOLD)
        lanes = pl.ds(start, FOLD)
        index = lax.broadcasted_iota(jnp.int32, (sources, FOLD), 0)
        pick = jnp.where(index == pairs_ref[1:2, lanes], 1.0, 0.0).astype(jnp.bfloat16)
        coeff = lax.dot_general(
            column_scr[...], pick, (((0,), (0,)), ((), ())), preferred_element_type=jnp.float32
        )
        coeff_scr[...] = coeff[0:rank, :]
        slot = lax.broadcasted_iota(jnp.int32, (1, FOLD), 1) + start
        wanted = jnp.where(slot < count, pairs_ref[0:1, lanes], -1)
        index = lax.broadcasted_iota(jnp.int32, (targets, FOLD), 0)
        place_scr[...] = jnp.where(index == wanted, 1.0, 0.0).astype(jnp.bfloat16)
        fetch(t).wait()

        def some_rows(k, carry):
            coeff = coeff_scr[...]
            for i in range(SUBLANES):
                r = k * SUBLANES + i
                product = buffer[r, :, lanes].astype(jnp.float32) * coeff
                folded = product[0:SUBLANES]
                for s in range(1, rank // SUBLANES):
                    folded = folded + product[s * SUBLANES : (s + 1) * SUBLANES]
                here = pl.ds(pl.multiple_of(r * SUBLANES, SUBLANES), SUBLANES)
                for h in range(FOLD // LANES):
                    sum_scr[h, here, :] = folded[:, h * LANES : (h + 1) * LANES]
            return carry

        lax.fori_loop(0, rank // SUBLANES, some_rows, 0)
        parts = []
        for h in range(FOLD // LANES):
            total = sum_scr[h, pl.ds(0, rank, stride=SUBLANES), :]
            for s in range(1, SUBLANES):
                total = total + sum_scr[h, pl.ds(s, rank, stride=SUBLANES), :]
            parts.append(total)
        coupled = jnp.concatenate(parts, axis=1)
        high = coupled.astype(jnp.bfloat16)
        low = (coupled - high.astype(jnp.float32)).astype(jnp.bfloat16)
        both = jnp.concatenate([high, low], axis=0)
        summed_scr[...] += lax.dot_general(
            place_scr[...], both, (((1,), (1,)), ((), ())), preferred_element_type=jnp.float32
        )
        return carry

    lax.fori_loop(0, live, multiply, 0)

    i = lax.axis_index("rows")
    j = lax.axis_index("cols")
    from_last = jnp.where(j < cols - 1, i, i - 1)
    from_first = jnp.where(j > 0, i, i + 1)
    start = pl.multiple_of((2 * jnp.maximum(from_last, 0) + 1) * clusters, clusters)
    last = gathered_ref[pl.ds(start, clusters), :].astype(jnp.float32)
    last = jnp.where(from_last >= 0, last, 0.0)
    start = pl.multiple_of(2 * jnp.minimum(from_first, rows - 1) * clusters, clusters)
    first = gathered_ref[pl.ds(start, clusters), :].astype(jnp.float32)
    first = jnp.where(from_first < rows, first, 0.0)
    after = jnp.where(j < cols - 1, j + 1, 0)
    lane = lax.broadcasted_iota(jnp.int32, (clusters, LANES), 1)
    for d in range(cols):
        halo = jnp.where(after == d, last, first)
        mine = summed_scr[d * clusters : (d + 1) * clusters, :]
        mine = mine + pltpu.roll(mine, rank, 1)
        out_ref[d] = jnp.where(lane < rank, mine, halo).astype(out_ref.dtype)


def far_field(count, pairs, gathered, blocks, cols):
    rank, _, slots = blocks.shape
    rows = lax.axis_size("rows")
    clusters = gathered.shape[0] // (2 * rows)
    return pl.pallas_call(
        far_kernel,
        out_shape=jax.ShapeDtypeStruct((cols, clusters, LANES), jnp.bfloat16),
        in_specs=in_hbm(3) + [pl.BlockSpec(memory_space=pl.ANY)],
        out_specs=pl.BlockSpec(memory_space=pltpu.VMEM),
        scratch_shapes=[
            pltpu.SMEM(count.shape, count.dtype),
            pltpu.VMEM(pairs.shape, pairs.dtype),
            pltpu.VMEM(gathered.shape, gathered.dtype),
            pltpu.VMEM(blocks.shape, blocks.dtype),
            pltpu.VMEM((rows * clusters, LANES), jnp.bfloat16),
            pltpu.VMEM((rank, FOLD), jnp.float32),
            pltpu.VMEM((cols * clusters, FOLD), jnp.bfloat16),
            pltpu.VMEM((FOLD // LANES, rank * SUBLANES, LANES), jnp.float32),
            pltpu.VMEM((cols * clusters, LANES), jnp.float32),
            pltpu.SemaphoreType.DMA((3,)),
            pltpu.SemaphoreType.DMA((slots // FOLD,)),
        ],
        compiler_params=pltpu.CompilerParams(vmem_limit_bytes=VMEM),
        cost_estimate=pl.CostEstimate(
            flops=2 * rank * rank * slots,
            bytes_accessed=2 * rank * rank * slots,
            transcendentals=0,
        ),
        name="far_field",
    )(count, pairs, gathered, blocks)


def replicate(rows, chunks, store, turned):
    within = lax.broadcasted_iota(jnp.int32, (rows.shape[0], LANES), 1)
    if turned:
        within = within + (within // CHUNK) * SUBLANES
    within = within % CHUNK
    for m in range(3 * chunks):
        tile = m // GROUPS
        store(
            m,
            jnp.take_along_axis(
                rows[:, tile * LANES : (tile + 1) * LANES],
                within + (m % GROUPS) * CHUNK,
                axis=1,
                mode="promise_in_bounds",
            ),
        )


def row_of(ref, n, row):
    return ref[n, pl.ds(row, SUBLANES, stride=0), :]


def turn(wide):
    return pltpu.roll(wide, 0, 1, stride=1, stride_axis=0)


def pair_sums(tgt, src, chunks):
    sums = [None] * (3 * chunks)
    size = 3 * chunks
    for f in range(chunks):
        y = [src(c * chunks + f) for c in range(3)]
        u = [src(size + c * chunks + f) for c in range(3)]
        v = [src(2 * size + c * chunks + f) for c in range(3)]
        for h in range(chunks):
            r = [tgt[c * chunks + h] - y[c] for c in range(3)]
            q = (r[0] * r[0] + core_square) + (r[1] * r[1] + r[2] * r[2])
            s = r[0] * v[0] + (r[1] * v[1] + r[2] * v[2])
            inverse = lax.rsqrt(q)
            square = inverse * inverse
            weight = square * inverse
            s = s * square
            for c in range(3):
                term = weight * (u[c] - s * r[c])
                m = c * chunks + h
                sums[m] = term if sums[m] is None else sums[m] + term
    return sums


def gather_sums(acc_scr, clusters, chunks, store):
    own_group = lax.broadcasted_iota(jnp.int32, (clusters, LANES), 1) // CHUNK
    for t in range(pl.cdiv(3 * chunks, GROUPS)):
        merged = None
        for g in range(GROUPS):
            m = t * GROUPS + g
            if m >= 3 * chunks:
                break
            total = acc_scr[m, pl.ds(0, clusters, stride=SUBLANES), :]
            for s in range(1, SUBLANES):
                total = total + acc_scr[m, pl.ds(s, clusters, stride=SUBLANES), :]
            total = total + pltpu.roll(total, 2 * CHUNK, 1)
            total = total + pltpu.roll(total, CHUNK, 1)
            merged = total if merged is None else jnp.where(own_group == g, total, merged)
        store(t, merged)


def near_kernel(
    pairs_hbm,
    count_hbm,
    disp_hbm,
    pos_hbm,
    intact_hbm,
    stiff_hbm,
    out_hbm,
    damage_hbm,
    rest_hbm,
    pairs_ref,
    count_ref,
    disp_ref,
    pos_ref,
    intact_ref,
    stiff_ref,
    out_ref,
    damage_ref,
    rest_ref,
    wide_scr,
    tgt_scr,
    row_scr,
    src_a,
    src_b,
    acc_scr,
    sems,
    out_sems,
):
    clusters, width = disp_ref.shape
    elems = width // 3
    chunks = elems // CHUNK
    size = 3 * chunks
    slots = pairs_ref.shape[1]

    inputs = start_all(
        sems,
        (
            (pos_hbm, pos_ref),
            (disp_hbm, disp_ref),
            (pairs_hbm, pairs_ref),
            (count_hbm, count_ref),
            (intact_hbm, intact_ref),
            (stiff_hbm, stiff_ref),
        ),
    )
    acc_scr[...] = jnp.zeros_like(acc_scr)
    for k, own in enumerate((pos_ref, disp_ref)):
        inputs[k].wait()
        wide_scr[k, :, 0:width] = own[...]

        def store(m, value, k=k):
            row_scr[k * size + m] = value
            if k == 1:
                row_scr[2 * size + m] = 3.0 * value

        replicate(wide_scr[k], chunks, store, True)

    def store_target(m, value):
        tgt_scr[m] = value

    replicate(wide_scr[0], chunks, store_target, False)
    for copy in inputs[2:]:
        copy.wait()
    count = count_ref[0]

    disp = [disp_ref[:, c * elems : (c + 1) * elems] for c in range(3)]
    separation = jnp.sqrt(1.0 + (disp[0] * disp[0] + disp[1] * disp[1] + disp[2] * disp[2]))
    softened = 1.0 - jnp.exp(-(separation - 1.0) / softening)
    intact = intact_ref[...].astype(jnp.float32)
    damage = intact * softened + (1.0 - intact)
    damage_ref[...] = damage
    damage_out = pltpu.make_async_copy(damage_ref, damage_hbm, out_sems.at[0])
    damage_out.start()
    hold = (1.0 - damage) * stiff_ref[...]
    for c in range(3):
        out_ref[:, c * elems : (c + 1) * elems] = -hold * disp[c]

    def place_sources(scr, first):
        for k in range(UNROLL):
            slot = jnp.minimum(first + k, slots - 1)
            source = jnp.clip(pairs_ref[1, slot] - HALO, 0, clusters - 1)
            for n in range(3 * size):
                scr[k, n] = turn(row_of(row_scr, n, source))

    def one_pair(scr, k, slot, rest):
        target = pairs_ref[0, slot]
        source = pairs_ref[1, slot]
        live = slot < count
        own = jnp.logical_and(source >= HALO, source < clusters + HALO)
        into = jnp.where(jnp.logical_and(live, own), target, clusters) * SUBLANES
        into = pl.multiple_of(into, SUBLANES)
        rest_ref[1 + 2 * rest] = target
        rest_ref[2 + 2 * rest] = source
        rest = rest + jnp.where(jnp.logical_and(live, jnp.logical_not(own)), 1, 0)
        tgt = [row_of(tgt_scr, m, target) for m in range(size)]
        sums = pair_sums(tgt, lambda n: scr[k, n], chunks)
        for m in range(size):
            acc_scr[m, pl.ds(into, SUBLANES), :] += sums[m]
        return rest

    def step(it, rest):
        first = it * 2 * UNROLL
        for this, other, start in (
            (src_a, src_b, first),
            (src_b, src_a, first + UNROLL),
        ):
            place_sources(other, start + UNROLL)
            for k in range(UNROLL):
                rest = one_pair(this, k, start + k, rest)
        return rest

    place_sources(src_a, 0)
    rest_ref[0] = lax.fori_loop(0, (count + 2 * UNROLL - 1) // (2 * UNROLL), step, 0)
    rest_out = pltpu.make_async_copy(rest_ref, rest_hbm, out_sems.at[1])
    rest_out.start()

    def store_sum(t, value):
        wide_scr[0, :, t * LANES : (t + 1) * LANES] = value

    gather_sums(acc_scr, clusters, chunks, store_sum)
    out_ref[...] += wide_scr[0, :, 0:width]
    near_out = pltpu.make_async_copy(out_ref, out_hbm, out_sems.at[2])
    near_out.start()
    for copy in (damage_out, rest_out, near_out):
        copy.wait()


def near_field(pairs, count, disp, pos, intact, stiffness):
    clusters, width = disp.shape
    elems = width // 3
    chunks = elems // CHUNK
    padded = pl.cdiv(width, LANES) * LANES
    slots = pairs.shape[1]
    return pl.pallas_call(
        near_kernel,
        out_shape=(
            jax.ShapeDtypeStruct((clusters, width), jnp.float32),
            jax.ShapeDtypeStruct((clusters, elems), jnp.float32),
            jax.ShapeDtypeStruct((2 * slots + 4,), jnp.int32),
        ),
        in_specs=in_hbm(6),
        out_specs=tuple(in_hbm(3)),
        scratch_shapes=[
            pltpu.SMEM(pairs.shape, pairs.dtype),
            pltpu.SMEM(count.shape, count.dtype),
            pltpu.VMEM(disp.shape, disp.dtype),
            pltpu.VMEM(pos.shape, pos.dtype),
            pltpu.VMEM(intact.shape, intact.dtype),
            pltpu.VMEM(stiffness.shape, stiffness.dtype),
            pltpu.VMEM((clusters, width), jnp.float32),
            pltpu.VMEM((clusters, elems), jnp.float32),
            pltpu.SMEM((2 * slots + 4,), jnp.int32),
            pltpu.VMEM((2, clusters, padded), jnp.float32),
            pltpu.VMEM((3 * chunks, clusters, LANES), jnp.float32),
            pltpu.VMEM((9 * chunks, clusters, LANES), jnp.float32),
            pltpu.VMEM((UNROLL, 9 * chunks, SUBLANES, LANES), jnp.float32),
            pltpu.VMEM((UNROLL, 9 * chunks, SUBLANES, LANES), jnp.float32),
            pltpu.VMEM((3 * chunks, (clusters + 1) * SUBLANES, LANES), jnp.float32),
            pltpu.SemaphoreType.DMA((6,)),
            pltpu.SemaphoreType.DMA((3,)),
        ],
        compiler_params=pltpu.CompilerParams(vmem_limit_bytes=VMEM),
        cost_estimate=pl.CostEstimate(
            flops=30 * slots * elems * elems,
            bytes_accessed=4 * clusters * width * 6,
            transcendentals=slots * elems * elems,
        ),
        name="near_field",
    )(pairs, count, disp, pos, intact, stiffness)


def finish_kernel(
    rest_hbm,
    pos_hbm,
    received_hbm,
    near_hbm,
    basis_hbm,
    out_ref,
    rest_ref,
    pos_ref,
    received_ref,
    near_ref,
    basis_scr,
    ext_scr,
    halo_scr,
    tgt_scr,
    row_scr,
    acc_scr,
    sems,
):
    clusters, width = pos_ref.shape
    cols = received_ref.shape[0]
    rank = basis_scr.shape[1]
    elems = width // 3
    chunks = elems // CHUNK
    size = 3 * chunks
    spare = LANES - rank
    segments = split_rows(width, spare)
    edge = 2 * HALO

    inputs = start_all(
        sems,
        (
            (received_hbm, received_ref),
            (pos_hbm, pos_ref),
            (rest_hbm, rest_ref),
            (near_hbm, near_ref),
            (basis_hbm, basis_scr),
        ),
    )
    acc_scr[...] = jnp.zeros_like(acc_scr)
    inputs[0].wait()
    inputs[1].wait()

    j = lax.axis_index("cols")
    before = jnp.where(j > 0, j - 1, cols - 1)
    after = jnp.where(j < cols - 1, j + 1, 0)
    for start, sender in ((0, before), (HALO, after)):
        halo_scr[...] = received_ref[sender].astype(jnp.float32)
        rows = edge * segments
        whole = halo_scr[0:rows, :]
        for n in range(1, PIECES):
            whole = whole + halo_scr[n * rows : (n + 1) * rows, :]
        for g in range(segments):
            count = min(spare, width - g * spare)
            for k in range(2):
                row = (2 * g + k) * HALO
                ext_scr[k, start : start + HALO, g * spare : g * spare + count] = whole[
                    row : row + HALO, rank : rank + count
                ]
    ext_scr[1, edge : edge + HALO, 0:width] = pos_ref[0:HALO, :]
    ext_scr[1, edge + HALO : 2 * edge, 0:width] = pos_ref[clusters - HALO :, :]
    for k in range(2):

        def store(m, value, k=k):
            row_scr[(1 - k) * size + m] = value
            if k == 0:
                row_scr[2 * size + m] = 3.0 * value

        replicate(ext_scr[k], chunks, store, True)

    def store_target(m, value):
        tgt_scr[m] = value

    replicate(ext_scr[1], chunks, store_target, False)
    inputs[2].wait()

    def step(n, carry):
        target = rest_ref[1 + 2 * n]
        source = rest_ref[2 + 2 * n]
        target = jnp.where(target < HALO, target, target - (clusters - edge))
        source = jnp.where(source < HALO, source, source - clusters)
        into = pl.multiple_of(target * SUBLANES, SUBLANES)
        tgt = [row_of(tgt_scr, m, edge + target) for m in range(size)]
        sums = pair_sums(tgt, lambda k: turn(row_of(row_scr, k, source)), chunks)
        for m in range(size):
            acc_scr[m, pl.ds(into, SUBLANES), :] += sums[m]
        return carry

    lax.fori_loop(0, rest_ref[0], step, 0)

    def store_sum(t, value):
        ext_scr[0, :, t * LANES : (t + 1) * LANES] = value

    gather_sums(acc_scr, 2 * edge, chunks, store_sum)

    owned = received_ref[0].astype(jnp.float32)
    for d in range(1, cols):
        owned = owned + received_ref[d].astype(jnp.float32)
    inputs[3].wait()
    inputs[4].wait()
    wide = lax.broadcasted_iota(jnp.int32, (SUBLANES, SUBLANES * rank), 1) // rank
    wide = wide == lax.broadcasted_iota(jnp.int32, (SUBLANES, SUBLANES * rank), 0)
    for k in range(clusters // SUBLANES):
        some = slice(k * SUBLANES, (k + 1) * SUBLANES)
        tiled = jnp.concatenate([owned[some, 0:rank]] * SUBLANES, axis=1)
        diagonal = jnp.where(wide, tiled, 0.0).astype(jnp.bfloat16)
        out_ref[some, :] = near_ref[some, :] + jnp.dot(
            diagonal,
            basis_scr[some].reshape(SUBLANES * rank, width),
            preferred_element_type=jnp.float32,
        )
    out_ref[0:HALO, :] += ext_scr[0, 0:HALO, 0:width]
    out_ref[clusters - HALO :, :] += ext_scr[0, HALO:edge, 0:width]


def finish(rest, pos, received, near, basis):
    clusters, width = pos.shape
    rank = basis.shape[1]
    chunks = width // 3 // CHUNK
    padded = pl.cdiv(width, LANES) * LANES
    edge = 2 * HALO
    return pl.pallas_call(
        finish_kernel,
        out_shape=jax.ShapeDtypeStruct((clusters, width), jnp.float32),
        in_specs=in_hbm(5),
        out_specs=pl.BlockSpec(memory_space=pltpu.VMEM),
        scratch_shapes=[
            pltpu.SMEM(rest.shape, rest.dtype),
            pltpu.VMEM(pos.shape, pos.dtype),
            pltpu.VMEM(received.shape, received.dtype),
            pltpu.VMEM(near.shape, near.dtype),
            pltpu.VMEM(basis.shape, basis.dtype),
            pltpu.VMEM((2, 2 * edge, padded), jnp.float32),
            pltpu.VMEM((clusters, LANES), jnp.float32),
            pltpu.VMEM((3 * chunks, 2 * edge, LANES), jnp.float32),
            pltpu.VMEM((9 * chunks, 2 * edge, LANES), jnp.float32),
            pltpu.VMEM((3 * chunks, 2 * edge * SUBLANES, LANES), jnp.float32),
            pltpu.SemaphoreType.DMA((5,)),
        ],
        compiler_params=pltpu.CompilerParams(vmem_limit_bytes=VMEM),
        cost_estimate=pl.CostEstimate(
            flops=2 * clusters * rank * width,
            bytes_accessed=2 * clusters * rank * width,
            transcendentals=0,
        ),
        name="finish",
    )(rest, pos, received, near, basis)


def local(
    displacement,
    positions,
    cluster_basis,
    near_pairs,
    near_count,
    far_pairs,
    far_count,
    far_blocks,
    intact,
    stiffness,
):
    cols = lax.axis_size("cols")
    basis = cluster_basis.transpose(0, 2, 1)
    payload = project(displacement, positions, basis)
    gathered = lax.all_gather(payload, "rows", axis=0, tiled=True)
    partial = far_field(far_count, far_pairs.T, gathered, far_blocks.transpose(1, 2, 0), cols)
    received = lax.all_to_all(partial, "cols", split_axis=0, concat_axis=0)
    near, damage, rest = near_field(
        near_pairs.T, near_count, displacement, positions, intact, stiffness
    )
    return finish(rest, positions, received, near, basis), damage


def solution(mesh):
    both = ("rows", "cols")
    in_specs = (
        P(both, None),
        P(both, None),
        P(both, None, None),
        P(both, None),
        P(both),
        P(both, None),
        P(both),
        P(both, None, None),
        P(both, None),
        P(both, None),
    )
    out_specs = (P(both, None), P(both, None))
    return jax.shard_map(local, mesh=mesh, in_specs=in_specs, out_specs=out_specs, check_vma=False)
```

```python
import functools

import jax
import jax.numpy as jnp
from jax import lax
from jax.experimental import pallas as pl
from jax.experimental.pallas import tpu as pltpu
from jax.sharding import PartitionSpec as P

HALO = 2
LANES = 128
SUBLANES = 8
CHUNK = 32
GROUPS = LANES // CHUNK
core_square = 0.25
softening = 1.5
UNROLL = 4
FOLD = 256
PIECES = 3
VMEM = 60 * 1024 * 1024


def split_rows(width, lanes):
    return pl.cdiv(width, lanes)


def in_hbm(count):
    return [pl.BlockSpec(memory_space=pltpu.HBM)] * count


def start_all(sems, moves):
    copies = [
        pltpu.make_async_copy(source, target, sems.at[n])
        for n, (source, target) in enumerate(moves)
    ]
    for copy in copies:
        copy.start()
    return copies


def far_kernel(
    count_hbm,
    pairs_hbm,
    gathered_hbm,
    blocks_ref,
    out_ref,
    count_ref,
    pairs_ref,
    gathered_ref,
    buffer,
    column_scr,
    coeff_scr,
    place_scr,
    sum_scr,
    summed_scr,
    halo_scr,
    sems,
    block_sems,
    *,
    segments,
):
    rank, _, slots = buffer.shape
    cols, clusters, _ = out_ref.shape
    targets = cols * clusters
    rows = gathered_ref.shape[0] // clusters
    sources = rows * clusters
    tiles = slots // FOLD

    def fetch(t):
        here = pl.ds(pl.multiple_of(t * FOLD, FOLD), FOLD)
        return pltpu.make_async_copy(
            blocks_ref.at[:, :, here], buffer.at[:, :, here], block_sems.at[t]
        )

    inputs = start_all(
        sems, ((count_hbm, count_ref), (pairs_hbm, pairs_ref), (gathered_hbm, gathered_ref))
    )
    fetch(0).start()
    summed_scr[...] = jnp.zeros_like(summed_scr)
    inputs[0].wait()
    count = count_ref[0]
    live = (count + FOLD - 1) // FOLD
    for t in range(1, tiles):

        @pl.when(t < live)
        def _(t=t):
            fetch(t).start()

    inputs[1].wait()
    inputs[2].wait()
    column_scr[...] = gathered_ref[...].astype(jnp.bfloat16)

    def multiply(t, carry):
        start = pl.multiple_of(t * FOLD, FOLD)
        lanes = pl.ds(start, FOLD)
        index = lax.broadcasted_iota(jnp.int32, (sources, FOLD), 0)
        pick = jnp.where(index == pairs_ref[1:2, lanes], 1.0, 0.0).astype(jnp.bfloat16)
        coeff = lax.dot_general(
            column_scr[...], pick, (((0,), (0,)), ((), ())), preferred_element_type=jnp.float32
        )
        coeff_scr[...] = coeff[0:rank, :]
        slot = lax.broadcasted_iota(jnp.int32, (1, FOLD), 1) + start
        wanted = jnp.where(slot < count, pairs_ref[0:1, lanes], -1)
        index = lax.broadcasted_iota(jnp.int32, (targets, FOLD), 0)
        place_scr[...] = jnp.where(index == wanted, 1.0, 0.0).astype(jnp.bfloat16)
        fetch(t).wait()

        def some_rows(k, carry):
            coeff = coeff_scr[...]
            for i in range(SUBLANES):
                r = k * SUBLANES + i
                product = buffer[r, :, lanes].astype(jnp.float32) * coeff
                folded = product[0:SUBLANES]
                for s in range(1, rank // SUBLANES):
                    folded = folded + product[s * SUBLANES : (s + 1) * SUBLANES]
                here = pl.ds(pl.multiple_of(r * SUBLANES, SUBLANES), SUBLANES)
                for h in range(FOLD // LANES):
                    sum_scr[h, here, :] = folded[:, h * LANES : (h + 1) * LANES]
            return carry

        lax.fori_loop(0, rank // SUBLANES, some_rows, 0)
        parts = []
        for h in range(FOLD // LANES):
            total = sum_scr[h, pl.ds(0, rank, stride=SUBLANES), :]
            for s in range(1, SUBLANES):
                total = total + sum_scr[h, pl.ds(s, rank, stride=SUBLANES), :]
            parts.append(total)
        coupled = jnp.concatenate(parts, axis=1)
        high = coupled.astype(jnp.bfloat16)
        low = (coupled - high.astype(jnp.float32)).astype(jnp.bfloat16)
        both = jnp.concatenate([high, low], axis=0)
        summed_scr[...] += lax.dot_general(
            place_scr[...], both, (((1,), (1,)), ((), ())), preferred_element_type=jnp.float32
        )
        return carry

    lax.fori_loop(0, live, multiply, 0)

    i = lax.axis_index("rows")
    j = lax.axis_index("cols")
    from_last = jnp.where(j < cols - 1, i, i - 1)
    from_first = jnp.where(j > 0, i, i + 1)
    edge = 2 * HALO
    halo_scr[...] = jnp.zeros_like(halo_scr)
    sides = (
        (0, jnp.minimum(from_first, rows - 1), from_first < rows),
        (edge, jnp.maximum(from_last, 0), from_last >= 0),
    )
    for side, (row, owner, there) in enumerate(sides):
        start = pl.multiple_of(owner * clusters, clusters)
        whole = jnp.where(there, gathered_ref[pl.ds(start, clusters), :], 0.0)
        for n in range(PIECES):
            piece = whole.astype(jnp.bfloat16).astype(jnp.float32)
            whole = whole - piece
            for g in range(segments):
                to = (n * segments + g) * edge
                here = g * 2 * edge + row
                halo_scr[side, to : to + edge, :] = piece[here : here + edge, :]
    after = jnp.where(j < cols - 1, j + 1, 0)
    lane = lax.broadcasted_iota(jnp.int32, (clusters, LANES), 1)
    for d in range(cols):
        halo = halo_scr[jnp.where(after == d, 1, 0)]
        mine = summed_scr[d * clusters : (d + 1) * clusters, :]
        mine = mine + pltpu.roll(mine, rank, 1)
        out_ref[d] = jnp.where(lane < rank, mine, halo).astype(out_ref.dtype)


def far_field(count, pairs, gathered, blocks, cols, segments):
    rank, _, slots = blocks.shape
    rows = lax.axis_size("rows")
    clusters = gathered.shape[0] // rows
    return pl.pallas_call(
        functools.partial(far_kernel, segments=segments),
        out_shape=jax.ShapeDtypeStruct((cols, clusters, LANES), jnp.bfloat16),
        in_specs=in_hbm(3) + [pl.BlockSpec(memory_space=pl.ANY)],
        out_specs=pl.BlockSpec(memory_space=pltpu.VMEM),
        scratch_shapes=[
            pltpu.SMEM(count.shape, count.dtype),
            pltpu.VMEM(pairs.shape, pairs.dtype),
            pltpu.VMEM(gathered.shape, gathered.dtype),
            pltpu.VMEM(blocks.shape, blocks.dtype),
            pltpu.VMEM((rows * clusters, LANES), jnp.bfloat16),
            pltpu.VMEM((rank, FOLD), jnp.float32),
            pltpu.VMEM((cols * clusters, FOLD), jnp.bfloat16),
            pltpu.VMEM((FOLD // LANES, rank * SUBLANES, LANES), jnp.float32),
            pltpu.VMEM((cols * clusters, LANES), jnp.float32),
            pltpu.VMEM((2, clusters, LANES), jnp.float32),
            pltpu.SemaphoreType.DMA((3,)),
            pltpu.SemaphoreType.DMA((slots // FOLD,)),
        ],
        compiler_params=pltpu.CompilerParams(vmem_limit_bytes=VMEM),
        cost_estimate=pl.CostEstimate(
            flops=2 * rank * rank * slots,
            bytes_accessed=2 * rank * rank * slots,
            transcendentals=0,
        ),
        name="far_field",
    )(count, pairs, gathered, blocks)


def replicate(rows, chunks, store, turned):
    within = lax.broadcasted_iota(jnp.int32, (rows.shape[0], LANES), 1)
    if turned:
        within = within + (within // CHUNK) * SUBLANES
    within = within % CHUNK
    for m in range(3 * chunks):
        tile = m // GROUPS
        store(
            m,
            jnp.take_along_axis(
                rows[:, tile * LANES : (tile + 1) * LANES],
                within + (m % GROUPS) * CHUNK,
                axis=1,
                mode="promise_in_bounds",
            ),
        )


def row_of(ref, n, row):
    return ref[n, pl.ds(row, SUBLANES, stride=0), :]


def turn(wide):
    return pltpu.roll(wide, 0, 1, stride=1, stride_axis=0)


def pair_sums(tgt, src, chunks, between=None):
    sums = [None] * (3 * chunks)
    size = 3 * chunks
    for f in range(chunks):
        y = [src(c * chunks + f) for c in range(3)]
        u = [src(size + c * chunks + f) for c in range(3)]
        v = [src(2 * size + c * chunks + f) for c in range(3)]
        for h in range(chunks):
            if between is not None:
                between(f, h)
            r = [tgt[c * chunks + h] - y[c] for c in range(3)]
            q = (r[0] * r[0] + core_square) + (r[1] * r[1] + r[2] * r[2])
            s = r[0] * v[0] + (r[1] * v[1] + r[2] * v[2])
            inverse = lax.rsqrt(q)
            square = inverse * inverse
            weight = square * inverse
            s = s * square
            for c in range(3):
                term = weight * (u[c] - s * r[c])
                m = c * chunks + h
                sums[m] = term if sums[m] is None else sums[m] + term
    return sums


def gather_sums(acc_scr, clusters, chunks, store):
    own_group = lax.broadcasted_iota(jnp.int32, (clusters, LANES), 1) // CHUNK
    for t in range(pl.cdiv(3 * chunks, GROUPS)):
        merged = None
        for g in range(GROUPS):
            m = t * GROUPS + g
            if m >= 3 * chunks:
                break
            total = acc_scr[m, pl.ds(0, clusters, stride=SUBLANES), :]
            for s in range(1, SUBLANES):
                total = total + acc_scr[m, pl.ds(s, clusters, stride=SUBLANES), :]
            total = total + pltpu.roll(total, 2 * CHUNK, 1)
            total = total + pltpu.roll(total, CHUNK, 1)
            merged = total if merged is None else jnp.where(own_group == g, total, merged)
        store(t, merged)


def near_kernel(
    pairs_hbm,
    count_hbm,
    disp_hbm,
    pos_hbm,
    intact_hbm,
    stiff_hbm,
    out_hbm,
    damage_hbm,
    rest_hbm,
    pairs_ref,
    count_ref,
    disp_ref,
    pos_ref,
    intact_ref,
    stiff_ref,
    out_ref,
    damage_ref,
    rest_ref,
    wide_scr,
    tgt_scr,
    row_scr,
    src_a,
    src_b,
    acc_scr,
    sems,
    out_sems,
):
    clusters, width = disp_ref.shape
    elems = width // 3
    chunks = elems // CHUNK
    size = 3 * chunks
    slots = pairs_ref.shape[1]

    inputs = start_all(
        sems,
        (
            (pos_hbm, pos_ref),
            (disp_hbm, disp_ref),
            (pairs_hbm, pairs_ref),
            (count_hbm, count_ref),
            (intact_hbm, intact_ref),
            (stiff_hbm, stiff_ref),
        ),
    )
    acc_scr[...] = jnp.zeros_like(acc_scr)
    for k, own in enumerate((pos_ref, disp_ref)):
        inputs[k].wait()
        wide_scr[k, :, 0:width] = own[...]

        def store(m, value, k=k):
            row_scr[k * size + m] = value
            if k == 1:
                row_scr[2 * size + m] = 3.0 * value

        replicate(wide_scr[k], chunks, store, True)

    def store_target(m, value):
        tgt_scr[m] = value

    replicate(wide_scr[0], chunks, store_target, False)
    for copy in inputs[2:]:
        copy.wait()
    count = count_ref[0]

    disp = [disp_ref[:, c * elems : (c + 1) * elems] for c in range(3)]
    separation = jnp.sqrt(1.0 + (disp[0] * disp[0] + disp[1] * disp[1] + disp[2] * disp[2]))
    softened = 1.0 - jnp.exp(-(separation - 1.0) / softening)
    intact = intact_ref[...].astype(jnp.float32)
    damage = intact * softened + (1.0 - intact)
    damage_ref[...] = damage
    damage_out = pltpu.make_async_copy(damage_ref, damage_hbm, out_sems.at[0])
    damage_out.start()
    hold = (1.0 - damage) * stiff_ref[...]
    for c in range(3):
        out_ref[:, c * elems : (c + 1) * elems] = -hold * disp[c]

    def source_of(slot):
        slot = jnp.minimum(slot, slots - 1)
        return jnp.clip(pairs_ref[1, slot] - HALO, 0, clusters - 1)

    def place_source(scr, k, source, rows):
        for n in rows:
            scr[k, n] = turn(row_of(row_scr, n, source))

    def one_pair(scr, other, k, slot, rest):
        later = source_of(slot + UNROLL)
        target = pairs_ref[0, slot]
        source = pairs_ref[1, slot]
        live = slot < count
        own = jnp.logical_and(source >= HALO, source < clusters + HALO)
        into = jnp.where(jnp.logical_and(live, own), target, clusters) * SUBLANES
        into = pl.multiple_of(into, SUBLANES)
        rest_ref[1 + 2 * rest] = target
        rest_ref[2 + 2 * rest] = source
        rest = rest + jnp.where(jnp.logical_and(live, jnp.logical_not(own)), 1, 0)
        tgt = [row_of(tgt_scr, m, target) for m in range(size)]

        def between(f, h):
            first = (f * chunks + h) * 3
            place_source(other, k, later, range(first, first + 3))

        sums = pair_sums(tgt, lambda n: scr[k, n], chunks, between)
        for m in range(size):
            acc_scr[m, pl.ds(into, SUBLANES), :] += sums[m]
        return rest

    def step(it, rest):
        first = it * 2 * UNROLL
        for this, other, start in (
            (src_a, src_b, first),
            (src_b, src_a, first + UNROLL),
        ):
            for k in range(UNROLL):
                rest = one_pair(this, other, k, start + k, rest)
        return rest

    for k in range(UNROLL):
        place_source(src_a, k, source_of(k), range(3 * size))
    rest_ref[0] = lax.fori_loop(0, (count + 2 * UNROLL - 1) // (2 * UNROLL), step, 0)
    rest_out = pltpu.make_async_copy(rest_ref, rest_hbm, out_sems.at[1])
    rest_out.start()

    def store_sum(t, value):
        wide_scr[0, :, t * LANES : (t + 1) * LANES] = value

    gather_sums(acc_scr, clusters, chunks, store_sum)
    out_ref[...] += wide_scr[0, :, 0:width]
    near_out = pltpu.make_async_copy(out_ref, out_hbm, out_sems.at[2])
    near_out.start()
    for copy in (damage_out, rest_out, near_out):
        copy.wait()


def near_field(pairs, count, disp, pos, intact, stiffness):
    clusters, width = disp.shape
    elems = width // 3
    chunks = elems // CHUNK
    padded = pl.cdiv(width, LANES) * LANES
    slots = pairs.shape[1]
    return pl.pallas_call(
        near_kernel,
        out_shape=(
            jax.ShapeDtypeStruct((clusters, width), jnp.float32),
            jax.ShapeDtypeStruct((clusters, elems), jnp.float32),
            jax.ShapeDtypeStruct((2 * slots + 4,), jnp.int32),
        ),
        in_specs=in_hbm(6),
        out_specs=tuple(in_hbm(3)),
        scratch_shapes=[
            pltpu.SMEM(pairs.shape, pairs.dtype),
            pltpu.SMEM(count.shape, count.dtype),
            pltpu.VMEM(disp.shape, disp.dtype),
            pltpu.VMEM(pos.shape, pos.dtype),
            pltpu.VMEM(intact.shape, intact.dtype),
            pltpu.VMEM(stiffness.shape, stiffness.dtype),
            pltpu.VMEM((clusters, width), jnp.float32),
            pltpu.VMEM((clusters, elems), jnp.float32),
            pltpu.SMEM((2 * slots + 4,), jnp.int32),
            pltpu.VMEM((2, clusters, padded), jnp.float32),
            pltpu.VMEM((3 * chunks, clusters, LANES), jnp.float32),
            pltpu.VMEM((9 * chunks, clusters, LANES), jnp.float32),
            pltpu.VMEM((UNROLL, 9 * chunks, SUBLANES, LANES), jnp.float32),
            pltpu.VMEM((UNROLL, 9 * chunks, SUBLANES, LANES), jnp.float32),
            pltpu.VMEM((3 * chunks, (clusters + 1) * SUBLANES, LANES), jnp.float32),
            pltpu.SemaphoreType.DMA((6,)),
            pltpu.SemaphoreType.DMA((3,)),
        ],
        compiler_params=pltpu.CompilerParams(vmem_limit_bytes=VMEM),
        cost_estimate=pl.CostEstimate(
            flops=30 * slots * elems * elems,
            bytes_accessed=4 * clusters * width * 6,
            transcendentals=slots * elems * elems,
        ),
        name="near_field",
    )(pairs, count, disp, pos, intact, stiffness)


def finish_kernel(
    rest_hbm,
    pos_hbm,
    received_hbm,
    near_hbm,
    basis_hbm,
    out_ref,
    rest_ref,
    pos_ref,
    received_ref,
    near_ref,
    basis_scr,
    ext_scr,
    halo_scr,
    tgt_scr,
    row_scr,
    acc_scr,
    sems,
):
    clusters, width = pos_ref.shape
    cols = received_ref.shape[0]
    rank = basis_scr.shape[1]
    elems = width // 3
    chunks = elems // CHUNK
    size = 3 * chunks
    spare = LANES - rank
    segments = split_rows(width, spare)
    edge = 2 * HALO

    inputs = start_all(
        sems,
        (
            (received_hbm, received_ref),
            (pos_hbm, pos_ref),
            (rest_hbm, rest_ref),
            (near_hbm, near_ref),
            (basis_hbm, basis_scr),
        ),
    )
    acc_scr[...] = jnp.zeros_like(acc_scr)
    inputs[0].wait()
    inputs[1].wait()

    j = lax.axis_index("cols")
    before = jnp.where(j > 0, j - 1, cols - 1)
    after = jnp.where(j < cols - 1, j + 1, 0)
    for start, sender in ((0, before), (HALO, after)):
        halo_scr[...] = received_ref[sender].astype(jnp.float32)
        rows = edge * segments
        whole = halo_scr[0:rows, :]
        for n in range(1, PIECES):
            whole = whole + halo_scr[n * rows : (n + 1) * rows, :]
        for g in range(segments):
            count = min(spare, width - g * spare)
            for k in range(2):
                row = (2 * g + k) * HALO
                ext_scr[k, start : start + HALO, g * spare : g * spare + count] = whole[
                    row : row + HALO, rank : rank + count
                ]
    ext_scr[1, edge : edge + HALO, 0:width] = pos_ref[0:HALO, :]
    ext_scr[1, edge + HALO : 2 * edge, 0:width] = pos_ref[clusters - HALO :, :]
    for k in range(2):

        def store(m, value, k=k):
            row_scr[(1 - k) * size + m] = value
            if k == 0:
                row_scr[2 * size + m] = 3.0 * value

        replicate(ext_scr[k], chunks, store, True)

    def store_target(m, value):
        tgt_scr[m] = value

    replicate(ext_scr[1], chunks, store_target, False)
    inputs[2].wait()

    def step(n, carry):
        target = rest_ref[1 + 2 * n]
        source = rest_ref[2 + 2 * n]
        target = jnp.where(target < HALO, target, target - (clusters - edge))
        source = jnp.where(source < HALO, source, source - clusters)
        into = pl.multiple_of(target * SUBLANES, SUBLANES)
        tgt = [row_of(tgt_scr, m, edge + target) for m in range(size)]
        sums = pair_sums(tgt, lambda k: turn(row_of(row_scr, k, source)), chunks)
        for m in range(size):
            acc_scr[m, pl.ds(into, SUBLANES), :] += sums[m]
        return carry

    lax.fori_loop(0, rest_ref[0], step, 0)

    def store_sum(t, value):
        ext_scr[0, :, t * LANES : (t + 1) * LANES] = value

    gather_sums(acc_scr, 2 * edge, chunks, store_sum)

    owned = received_ref[0].astype(jnp.float32)
    for d in range(1, cols):
        owned = owned + received_ref[d].astype(jnp.float32)
    inputs[3].wait()
    inputs[4].wait()
    wide = lax.broadcasted_iota(jnp.int32, (SUBLANES, SUBLANES * rank), 1) // rank
    wide = wide == lax.broadcasted_iota(jnp.int32, (SUBLANES, SUBLANES * rank), 0)
    for k in range(clusters // SUBLANES):
        some = slice(k * SUBLANES, (k + 1) * SUBLANES)
        tiled = jnp.concatenate([owned[some, 0:rank]] * SUBLANES, axis=1)
        diagonal = jnp.where(wide, tiled, 0.0).astype(jnp.bfloat16)
        out_ref[some, :] = near_ref[some, :] + jnp.dot(
            diagonal,
            basis_scr[some].reshape(SUBLANES * rank, width),
            preferred_element_type=jnp.float32,
        )
    out_ref[0:HALO, :] += ext_scr[0, 0:HALO, 0:width]
    out_ref[clusters - HALO :, :] += ext_scr[0, HALO:edge, 0:width]


def finish(rest, pos, received, near, basis):
    clusters, width = pos.shape
    rank = basis.shape[1]
    chunks = width // 3 // CHUNK
    padded = pl.cdiv(width, LANES) * LANES
    edge = 2 * HALO
    return pl.pallas_call(
        finish_kernel,
        out_shape=jax.ShapeDtypeStruct((clusters, width), jnp.float32),
        in_specs=in_hbm(5),
        out_specs=pl.BlockSpec(memory_space=pltpu.VMEM),
        scratch_shapes=[
            pltpu.SMEM(rest.shape, rest.dtype),
            pltpu.VMEM(pos.shape, pos.dtype),
            pltpu.VMEM(received.shape, received.dtype),
            pltpu.VMEM(near.shape, near.dtype),
            pltpu.VMEM(basis.shape, basis.dtype),
            pltpu.VMEM((2, 2 * edge, padded), jnp.float32),
            pltpu.VMEM((clusters, LANES), jnp.float32),
            pltpu.VMEM((3 * chunks, 2 * edge, LANES), jnp.float32),
            pltpu.VMEM((9 * chunks, 2 * edge, LANES), jnp.float32),
            pltpu.VMEM((3 * chunks, 2 * edge * SUBLANES, LANES), jnp.float32),
            pltpu.SemaphoreType.DMA((5,)),
        ],
        compiler_params=pltpu.CompilerParams(vmem_limit_bytes=VMEM),
        cost_estimate=pl.CostEstimate(
            flops=2 * clusters * rank * width,
            bytes_accessed=2 * clusters * rank * width,
            transcendentals=0,
        ),
        name="finish",
    )(rest, pos, received, near, basis)


def local(
    displacement,
    positions,
    cluster_basis,
    near_pairs,
    near_count,
    far_pairs,
    far_count,
    far_blocks,
    intact,
    stiffness,
):
    cols = lax.axis_size("cols")
    basis = cluster_basis.transpose(0, 2, 1)
    clusters, rank, width = basis.shape
    disp_bf = displacement.astype(jnp.bfloat16)
    coeff = jnp.einsum("kf,kfr->kr", disp_bf, cluster_basis, preferred_element_type=jnp.float32)

    spare = LANES - rank
    segments = split_rows(width, spare)
    edge = jnp.concatenate(
        [rows[part] for part in (slice(0, HALO), slice(clusters - HALO, clusters)) for rows in (displacement, positions)],
        axis=0,
    )
    edge = jnp.pad(edge, ((0, 0), (0, segments * spare - width)))
    halo = jnp.concatenate([edge[:, g * spare : (g + 1) * spare] for g in range(segments)], axis=0)
    halo = jnp.pad(halo, ((0, clusters - halo.shape[0]), (0, 0)))
    payload = jnp.concatenate([coeff, halo], axis=1)
    gathered = lax.all_gather(payload, "rows", axis=0, tiled=True)
    partial = far_field(
        far_count, far_pairs.T, gathered, far_blocks.transpose(1, 2, 0), cols, segments
    )
    received = lax.all_to_all(partial, "cols", split_axis=0, concat_axis=0)
    near, damage, rest = near_field(
        near_pairs.T, near_count, displacement, positions, intact, stiffness
    )
    return finish(rest, positions, received, near, basis), damage


def solution(mesh):
    both = ("rows", "cols")
    in_specs = (
        P(both, None),
        P(both, None),
        P(both, None, None),
        P(both, None),
        P(both),
        P(both, None),
        P(both),
        P(both, None, None),
        P(both, None),
        P(both, None),
    )
    out_specs = (P(both, None), P(both, None))
    return jax.shard_map(local, mesh=mesh, in_specs=in_specs, out_specs=out_specs, check_vma=False)
```

```python
import functools

import jax
import jax.numpy as jnp
from jax import lax
from jax.experimental import pallas as pl
from jax.experimental.pallas import tpu as pltpu
from jax.sharding import PartitionSpec as P

HALO = 2
LANES = 128
SUBLANES = 8
CHUNK = 32
GROUPS = LANES // CHUNK
core_square = 0.25
softening = 1.5
UNROLL = 4
FOLD = 256
PIECES = 3
VMEM = 56 * 1024 * 1024


def split_rows(width, lanes):
    return pl.cdiv(width, lanes)


def in_hbm(count):
    return [pl.BlockSpec(memory_space=pltpu.HBM)] * count


def start_all(sems, moves):
    copies = [
        pltpu.make_async_copy(source, target, sems.at[n])
        for n, (source, target) in enumerate(moves)
    ]
    for copy in copies:
        copy.start()
    return copies


def far_kernel(
    count_hbm,
    pairs_hbm,
    gathered_hbm,
    blocks_ref,
    out_ref,
    count_ref,
    pairs_ref,
    gathered_ref,
    buffer,
    column_scr,
    coeff_scr,
    place_scr,
    sum_scr,
    summed_scr,
    halo_scr,
    sems,
    block_sems,
    *,
    segments,
):
    rank, _, slots = buffer.shape
    cols, clusters, _ = out_ref.shape
    targets = cols * clusters
    rows = gathered_ref.shape[0] // clusters
    sources = rows * clusters
    tiles = slots // FOLD

    def fetch(t):
        here = pl.ds(pl.multiple_of(t * FOLD, FOLD), FOLD)
        return pltpu.make_async_copy(
            blocks_ref.at[:, :, here], buffer.at[:, :, here], block_sems.at[t]
        )

    inputs = start_all(
        sems, ((count_hbm, count_ref), (pairs_hbm, pairs_ref), (gathered_hbm, gathered_ref))
    )
    fetch(0).start()
    summed_scr[...] = jnp.zeros_like(summed_scr)
    inputs[0].wait()
    count = count_ref[0]
    live = (count + FOLD - 1) // FOLD
    for t in range(1, tiles):

        @pl.when(t < live)
        def _(t=t):
            fetch(t).start()

    inputs[1].wait()
    inputs[2].wait()
    column_scr[...] = gathered_ref[...].astype(jnp.bfloat16)

    def multiply(t, carry):
        start = pl.multiple_of(t * FOLD, FOLD)
        lanes = pl.ds(start, FOLD)
        index = lax.broadcasted_iota(jnp.int32, (sources, FOLD), 0)
        pick = jnp.where(index == pairs_ref[1:2, lanes], 1.0, 0.0).astype(jnp.bfloat16)
        coeff = lax.dot_general(
            column_scr[...], pick, (((0,), (0,)), ((), ())), preferred_element_type=jnp.float32
        )
        coeff_scr[...] = coeff[0:rank, :]
        slot = lax.broadcasted_iota(jnp.int32, (1, FOLD), 1) + start
        wanted = jnp.where(slot < count, pairs_ref[0:1, lanes], -1)
        index = lax.broadcasted_iota(jnp.int32, (targets, FOLD), 0)
        place_scr[...] = jnp.where(index == wanted, 1.0, 0.0).astype(jnp.bfloat16)
        fetch(t).wait()

        def some_rows(k, carry):
            coeff = coeff_scr[...]
            for i in range(SUBLANES):
                r = k * SUBLANES + i
                product = buffer[r, :, lanes].astype(jnp.float32) * coeff
                folded = product[0:SUBLANES]
                for s in range(1, rank // SUBLANES):
                    folded = folded + product[s * SUBLANES : (s + 1) * SUBLANES]
                here = pl.ds(pl.multiple_of(r * SUBLANES, SUBLANES), SUBLANES)
                for h in range(FOLD // LANES):
                    sum_scr[h, here, :] = folded[:, h * LANES : (h + 1) * LANES]
            return carry

        lax.fori_loop(0, rank // SUBLANES, some_rows, 0)
        parts = []
        for h in range(FOLD // LANES):
            total = sum_scr[h, pl.ds(0, rank, stride=SUBLANES), :]
            for s in range(1, SUBLANES):
                total = total + sum_scr[h, pl.ds(s, rank, stride=SUBLANES), :]
            parts.append(total)
        coupled = jnp.concatenate(parts, axis=1)
        high = coupled.astype(jnp.bfloat16)
        low = (coupled - high.astype(jnp.float32)).astype(jnp.bfloat16)
        both = jnp.concatenate([high, low], axis=0)
        summed_scr[...] += lax.dot_general(
            place_scr[...], both, (((1,), (1,)), ((), ())), preferred_element_type=jnp.float32
        )
        return carry

    lax.fori_loop(0, live, multiply, 0)

    i = lax.axis_index("rows")
    j = lax.axis_index("cols")
    from_last = jnp.where(j < cols - 1, i, i - 1)
    from_first = jnp.where(j > 0, i, i + 1)
    edge = 2 * HALO
    halo_scr[...] = jnp.zeros_like(halo_scr)
    sides = (
        (0, jnp.minimum(from_first, rows - 1), from_first < rows),
        (edge, jnp.maximum(from_last, 0), from_last >= 0),
    )
    for side, (row, owner, there) in enumerate(sides):
        start = pl.multiple_of(owner * clusters, clusters)
        whole = jnp.where(there, gathered_ref[pl.ds(start, clusters), :], 0.0)
        for n in range(PIECES):
            piece = whole.astype(jnp.bfloat16).astype(jnp.float32)
            whole = whole - piece
            for g in range(segments):
                to = (n * segments + g) * edge
                here = g * 2 * edge + row
                halo_scr[side, to : to + edge, :] = piece[here : here + edge, :]
    after = jnp.where(j < cols - 1, j + 1, 0)
    lane = lax.broadcasted_iota(jnp.int32, (clusters, LANES), 1)
    for d in range(cols):
        halo = halo_scr[jnp.where(after == d, 1, 0)]
        mine = summed_scr[d * clusters : (d + 1) * clusters, :]
        mine = mine + pltpu.roll(mine, rank, 1)
        out_ref[d] = jnp.where(lane < rank, mine, halo).astype(out_ref.dtype)


def far_field(count, pairs, gathered, blocks, cols, segments):
    rank, _, slots = blocks.shape
    rows = lax.axis_size("rows")
    clusters = gathered.shape[0] // rows
    return pl.pallas_call(
        functools.partial(far_kernel, segments=segments),
        out_shape=jax.ShapeDtypeStruct((cols, clusters, LANES), jnp.bfloat16),
        in_specs=in_hbm(3) + [pl.BlockSpec(memory_space=pl.ANY)],
        out_specs=pl.BlockSpec(memory_space=pltpu.VMEM),
        scratch_shapes=[
            pltpu.SMEM(count.shape, count.dtype),
            pltpu.VMEM(pairs.shape, pairs.dtype),
            pltpu.VMEM(gathered.shape, gathered.dtype),
            pltpu.VMEM(blocks.shape, blocks.dtype),
            pltpu.VMEM((rows * clusters, LANES), jnp.bfloat16),
            pltpu.VMEM((rank, FOLD), jnp.float32),
            pltpu.VMEM((cols * clusters, FOLD), jnp.bfloat16),
            pltpu.VMEM((FOLD // LANES, rank * SUBLANES, LANES), jnp.float32),
            pltpu.VMEM((cols * clusters, LANES), jnp.float32),
            pltpu.VMEM((2, clusters, LANES), jnp.float32),
            pltpu.SemaphoreType.DMA((3,)),
            pltpu.SemaphoreType.DMA((slots // FOLD,)),
        ],
        compiler_params=pltpu.CompilerParams(vmem_limit_bytes=VMEM),
        cost_estimate=pl.CostEstimate(
            flops=2 * rank * rank * slots,
            bytes_accessed=2 * rank * rank * slots,
            transcendentals=0,
        ),
        name="far_field",
    )(count, pairs, gathered, blocks)


def replicate(rows, chunks, store, turned):
    within = lax.broadcasted_iota(jnp.int32, (rows.shape[0], LANES), 1)
    if turned:
        within = within + (within // CHUNK) * SUBLANES
    within = within % CHUNK
    for m in range(3 * chunks):
        tile = m // GROUPS
        store(
            m,
            jnp.take_along_axis(
                rows[:, tile * LANES : (tile + 1) * LANES],
                within + (m % GROUPS) * CHUNK,
                axis=1,
                mode="promise_in_bounds",
            ),
        )


def row_of(ref, n, row):
    return ref[n, pl.ds(row, SUBLANES, stride=0), :]


def turn(wide):
    return pltpu.roll(wide, 0, 1, stride=1, stride_axis=0)


def pair_sums(tgt, src, chunks, between=None):
    sums = [None] * (3 * chunks)
    size = 3 * chunks
    for f in range(chunks):
        y = [src(c * chunks + f) for c in range(3)]
        u = [src(size + c * chunks + f) for c in range(3)]
        v = [3.0 * x for x in u]
        for h in range(chunks):
            if between is not None:
                between(f, h)
            r = [tgt[c * chunks + h] - y[c] for c in range(3)]
            q = (r[0] * r[0] + core_square) + (r[1] * r[1] + r[2] * r[2])
            s = r[0] * v[0] + (r[1] * v[1] + r[2] * v[2])
            inverse = lax.rsqrt(q)
            square = inverse * inverse
            weight = square * inverse
            s = s * square
            for c in range(3):
                term = weight * (u[c] - s * r[c])
                m = c * chunks + h
                sums[m] = term if sums[m] is None else sums[m] + term
    return sums


def gather_sums(acc_scr, clusters, chunks, store):
    own_group = lax.broadcasted_iota(jnp.int32, (clusters, LANES), 1) // CHUNK
    for t in range(pl.cdiv(3 * chunks, GROUPS)):
        merged = None
        for g in range(GROUPS):
            m = t * GROUPS + g
            if m >= 3 * chunks:
                break
            total = acc_scr[m, pl.ds(0, clusters, stride=SUBLANES), :]
            for s in range(1, SUBLANES):
                total = total + acc_scr[m, pl.ds(s, clusters, stride=SUBLANES), :]
            total = total + pltpu.roll(total, 2 * CHUNK, 1)
            total = total + pltpu.roll(total, CHUNK, 1)
            merged = total if merged is None else jnp.where(own_group == g, total, merged)
        store(t, merged)


def near_kernel(
    pairs_hbm,
    count_hbm,
    disp_hbm,
    pos_hbm,
    intact_hbm,
    stiff_hbm,
    out_hbm,
    damage_hbm,
    rest_hbm,
    pairs_ref,
    count_ref,
    disp_ref,
    pos_ref,
    intact_ref,
    stiff_ref,
    out_ref,
    damage_ref,
    rest_ref,
    wide_scr,
    tgt_scr,
    row_scr,
    src_a,
    src_b,
    acc_scr,
    sems,
    out_sems,
):
    clusters, width = disp_ref.shape
    elems = width // 3
    chunks = elems // CHUNK
    size = 3 * chunks
    slots = pairs_ref.shape[1]

    inputs = start_all(
        sems,
        (
            (pos_hbm, pos_ref),
            (disp_hbm, disp_ref),
            (pairs_hbm, pairs_ref),
            (count_hbm, count_ref),
            (intact_hbm, intact_ref),
            (stiff_hbm, stiff_ref),
        ),
    )
    acc_scr[...] = jnp.zeros_like(acc_scr)
    for k, own in enumerate((pos_ref, disp_ref)):
        inputs[k].wait()
        wide_scr[k, :, 0:width] = own[...]

        def store(m, value, k=k):
            row_scr[k * size + m] = value
        replicate(wide_scr[k], chunks, store, True)

    def store_target(m, value):
        tgt_scr[m] = value

    replicate(wide_scr[0], chunks, store_target, False)
    for copy in inputs[2:]:
        copy.wait()
    count = count_ref[0]

    disp = [disp_ref[:, c * elems : (c + 1) * elems] for c in range(3)]
    separation = jnp.sqrt(1.0 + (disp[0] * disp[0] + disp[1] * disp[1] + disp[2] * disp[2]))
    softened = 1.0 - jnp.exp(-(separation - 1.0) / softening)
    intact = intact_ref[...].astype(jnp.float32)
    damage = intact * softened + (1.0 - intact)
    damage_ref[...] = damage
    damage_out = pltpu.make_async_copy(damage_ref, damage_hbm, out_sems.at[0])
    damage_out.start()
    hold = (1.0 - damage) * stiff_ref[...]
    for c in range(3):
        out_ref[:, c * elems : (c + 1) * elems] = -hold * disp[c]

    def source_of(slot):
        slot = jnp.minimum(slot, slots - 1)
        return jnp.clip(pairs_ref[1, slot] - HALO, 0, clusters - 1)

    def place_source(scr, k, source, rows):
        for n in rows:
            scr[k, n] = turn(row_of(row_scr, n, source))

    def one_pair(scr, other, k, slot, rest):
        later = source_of(slot + UNROLL)
        target = pairs_ref[0, slot]
        source = pairs_ref[1, slot]
        live = slot < count
        own = jnp.logical_and(source >= HALO, source < clusters + HALO)
        into = jnp.where(jnp.logical_and(live, own), target, clusters) * SUBLANES
        into = pl.multiple_of(into, SUBLANES)
        rest_ref[1 + 2 * rest] = target
        rest_ref[2 + 2 * rest] = source
        rest = rest + jnp.where(jnp.logical_and(live, jnp.logical_not(own)), 1, 0)
        tgt = [row_of(tgt_scr, m, target) for m in range(size)]

        def between(f, h):
            first = (f * chunks + h) * 2
            place_source(other, k, later, range(first, first + 2))

        sums = pair_sums(tgt, lambda n: scr[k, n], chunks, between)
        for m in range(size):
            acc_scr[m, pl.ds(into, SUBLANES), :] += sums[m]
        return rest

    def step(it, rest):
        first = it * 2 * UNROLL
        for this, other, start in (
            (src_a, src_b, first),
            (src_b, src_a, first + UNROLL),
        ):
            for k in range(UNROLL):
                rest = one_pair(this, other, k, start + k, rest)
        return rest

    for k in range(UNROLL):
        place_source(src_a, k, source_of(k), range(2 * size))
    rest_ref[0] = lax.fori_loop(0, (count + 2 * UNROLL - 1) // (2 * UNROLL), step, 0)
    rest_out = pltpu.make_async_copy(rest_ref, rest_hbm, out_sems.at[1])
    rest_out.start()

    def store_sum(t, value):
        wide_scr[0, :, t * LANES : (t + 1) * LANES] = value

    gather_sums(acc_scr, clusters, chunks, store_sum)
    out_ref[...] += wide_scr[0, :, 0:width]
    near_out = pltpu.make_async_copy(out_ref, out_hbm, out_sems.at[2])
    near_out.start()
    for copy in (damage_out, rest_out, near_out):
        copy.wait()


def near_field(pairs, count, disp, pos, intact, stiffness):
    clusters, width = disp.shape
    elems = width // 3
    chunks = elems // CHUNK
    padded = pl.cdiv(width, LANES) * LANES
    slots = pairs.shape[1]
    return pl.pallas_call(
        near_kernel,
        out_shape=(
            jax.ShapeDtypeStruct((clusters, width), jnp.float32),
            jax.ShapeDtypeStruct((clusters, elems), jnp.float32),
            jax.ShapeDtypeStruct((2 * slots + 4,), jnp.int32),
        ),
        in_specs=in_hbm(6),
        out_specs=tuple(in_hbm(3)),
        scratch_shapes=[
            pltpu.SMEM(pairs.shape, pairs.dtype),
            pltpu.SMEM(count.shape, count.dtype),
            pltpu.VMEM(disp.shape, disp.dtype),
            pltpu.VMEM(pos.shape, pos.dtype),
            pltpu.VMEM(intact.shape, intact.dtype),
            pltpu.VMEM(stiffness.shape, stiffness.dtype),
            pltpu.VMEM((clusters, width), jnp.float32),
            pltpu.VMEM((clusters, elems), jnp.float32),
            pltpu.SMEM((2 * slots + 4,), jnp.int32),
            pltpu.VMEM((2, clusters, padded), jnp.float32),
            pltpu.VMEM((3 * chunks, clusters, LANES), jnp.float32),
            pltpu.VMEM((6 * chunks, clusters, LANES), jnp.float32),
            pltpu.VMEM((UNROLL, 6 * chunks, SUBLANES, LANES), jnp.float32),
            pltpu.VMEM((UNROLL, 6 * chunks, SUBLANES, LANES), jnp.float32),
            pltpu.VMEM((3 * chunks, (clusters + 1) * SUBLANES, LANES), jnp.float32),
            pltpu.SemaphoreType.DMA((6,)),
            pltpu.SemaphoreType.DMA((3,)),
        ],
        compiler_params=pltpu.CompilerParams(vmem_limit_bytes=VMEM),
        cost_estimate=pl.CostEstimate(
            flops=30 * slots * elems * elems,
            bytes_accessed=4 * clusters * width * 6,
            transcendentals=slots * elems * elems,
        ),
        name="near_field",
    )(pairs, count, disp, pos, intact, stiffness)


def finish_kernel(
    rest_hbm,
    pos_hbm,
    received_hbm,
    near_hbm,
    basis_hbm,
    out_ref,
    rest_ref,
    pos_ref,
    received_ref,
    near_ref,
    basis_scr,
    ext_scr,
    halo_scr,
    tgt_scr,
    row_scr,
    acc_scr,
    sems,
):
    clusters, width = pos_ref.shape
    cols = received_ref.shape[0]
    rank = basis_scr.shape[1]
    elems = width // 3
    chunks = elems // CHUNK
    size = 3 * chunks
    spare = LANES - rank
    segments = split_rows(width, spare)
    edge = 2 * HALO

    inputs = start_all(
        sems,
        (
            (received_hbm, received_ref),
            (pos_hbm, pos_ref),
            (rest_hbm, rest_ref),
            (near_hbm, near_ref),
            (basis_hbm, basis_scr),
        ),
    )
    acc_scr[...] = jnp.zeros_like(acc_scr)
    inputs[0].wait()
    inputs[1].wait()

    j = lax.axis_index("cols")
    before = jnp.where(j > 0, j - 1, cols - 1)
    after = jnp.where(j < cols - 1, j + 1, 0)
    for start, sender in ((0, before), (HALO, after)):
        halo_scr[...] = received_ref[sender].astype(jnp.float32)
        rows = edge * segments
        whole = halo_scr[0:rows, :]
        for n in range(1, PIECES):
            whole = whole + halo_scr[n * rows : (n + 1) * rows, :]
        for g in range(segments):
            count = min(spare, width - g * spare)
            for k in range(2):
                row = (2 * g + k) * HALO
                ext_scr[k, start : start + HALO, g * spare : g * spare + count] = whole[
                    row : row + HALO, rank : rank + count
                ]
    ext_scr[1, edge : edge + HALO, 0:width] = pos_ref[0:HALO, :]
    ext_scr[1, edge + HALO : 2 * edge, 0:width] = pos_ref[clusters - HALO :, :]
    for k in range(2):

        def store(m, value, k=k):
            row_scr[(1 - k) * size + m] = value
        replicate(ext_scr[k], chunks, store, True)

    def store_target(m, value):
        tgt_scr[m] = value

    replicate(ext_scr[1], chunks, store_target, False)
    inputs[2].wait()

    def step(n, carry):
        target = rest_ref[1 + 2 * n]
        source = rest_ref[2 + 2 * n]
        target = jnp.where(target < HALO, target, target - (clusters - edge))
        source = jnp.where(source < HALO, source, source - clusters)
        into = pl.multiple_of(target * SUBLANES, SUBLANES)
        tgt = [row_of(tgt_scr, m, edge + target) for m in range(size)]
        sums = pair_sums(tgt, lambda k: turn(row_of(row_scr, k, source)), chunks)
        for m in range(size):
            acc_scr[m, pl.ds(into, SUBLANES), :] += sums[m]
        return carry

    lax.fori_loop(0, rest_ref[0], step, 0)

    def store_sum(t, value):
        ext_scr[0, :, t * LANES : (t + 1) * LANES] = value

    gather_sums(acc_scr, 2 * edge, chunks, store_sum)

    owned = received_ref[0].astype(jnp.float32)
    for d in range(1, cols):
        owned = owned + received_ref[d].astype(jnp.float32)
    inputs[3].wait()
    inputs[4].wait()
    wide = lax.broadcasted_iota(jnp.int32, (SUBLANES, SUBLANES * rank), 1) // rank
    wide = wide == lax.broadcasted_iota(jnp.int32, (SUBLANES, SUBLANES * rank), 0)
    for k in range(clusters // SUBLANES):
        some = slice(k * SUBLANES, (k + 1) * SUBLANES)
        tiled = jnp.concatenate([owned[some, 0:rank]] * SUBLANES, axis=1)
        diagonal = jnp.where(wide, tiled, 0.0).astype(jnp.bfloat16)
        out_ref[some, :] = near_ref[some, :] + jnp.dot(
            diagonal,
            basis_scr[some].reshape(SUBLANES * rank, width),
            preferred_element_type=jnp.float32,
        )
    out_ref[0:HALO, :] += ext_scr[0, 0:HALO, 0:width]
    out_ref[clusters - HALO :, :] += ext_scr[0, HALO:edge, 0:width]


def finish(rest, pos, received, near, basis):
    clusters, width = pos.shape
    rank = basis.shape[1]
    chunks = width // 3 // CHUNK
    padded = pl.cdiv(width, LANES) * LANES
    edge = 2 * HALO
    return pl.pallas_call(
        finish_kernel,
        out_shape=jax.ShapeDtypeStruct((clusters, width), jnp.float32),
        in_specs=in_hbm(5),
        out_specs=pl.BlockSpec(memory_space=pltpu.VMEM),
        scratch_shapes=[
            pltpu.SMEM(rest.shape, rest.dtype),
            pltpu.VMEM(pos.shape, pos.dtype),
            pltpu.VMEM(received.shape, received.dtype),
            pltpu.VMEM(near.shape, near.dtype),
            pltpu.VMEM(basis.shape, basis.dtype),
            pltpu.VMEM((2, 2 * edge, padded), jnp.float32),
            pltpu.VMEM((clusters, LANES), jnp.float32),
            pltpu.VMEM((3 * chunks, 2 * edge, LANES), jnp.float32),
            pltpu.VMEM((6 * chunks, 2 * edge, LANES), jnp.float32),
            pltpu.VMEM((3 * chunks, 2 * edge * SUBLANES, LANES), jnp.float32),
            pltpu.SemaphoreType.DMA((5,)),
        ],
        compiler_params=pltpu.CompilerParams(vmem_limit_bytes=VMEM),
        cost_estimate=pl.CostEstimate(
            flops=2 * clusters * rank * width,
            bytes_accessed=2 * clusters * rank * width,
            transcendentals=0,
        ),
        name="finish",
    )(rest, pos, received, near, basis)


def local(
    displacement,
    positions,
    cluster_basis,
    near_pairs,
    near_count,
    far_pairs,
    far_count,
    far_blocks,
    intact,
    stiffness,
):
    cols = lax.axis_size("cols")
    basis = cluster_basis.transpose(0, 2, 1)
    clusters, rank, width = basis.shape
    disp_bf = displacement.astype(jnp.bfloat16)
    coeff = jnp.einsum("kf,kfr->kr", disp_bf, cluster_basis, preferred_element_type=jnp.float32)

    spare = LANES - rank
    segments = split_rows(width, spare)
    edge = jnp.concatenate(
        [rows[part] for part in (slice(0, HALO), slice(clusters - HALO, clusters)) for rows in (displacement, positions)],
        axis=0,
    )
    edge = jnp.pad(edge, ((0, 0), (0, segments * spare - width)))
    halo = jnp.concatenate([edge[:, g * spare : (g + 1) * spare] for g in range(segments)], axis=0)
    halo = jnp.pad(halo, ((0, clusters - halo.shape[0]), (0, 0)))
    payload = jnp.concatenate([coeff, halo], axis=1)
    gathered = lax.all_gather(payload, "rows", axis=0, tiled=True)
    partial = far_field(
        far_count, far_pairs.T, gathered, far_blocks.transpose(1, 2, 0), cols, segments
    )
    received = lax.all_to_all(partial, "cols", split_axis=0, concat_axis=0)
    near, damage, rest = near_field(
        near_pairs.T, near_count, displacement, positions, intact, stiffness
    )
    return finish(rest, positions, received, near, basis), damage


def solution(mesh):
    both = ("rows", "cols")
    in_specs = (
        P(both, None),
        P(both, None),
        P(both, None, None),
        P(both, None),
        P(both),
        P(both, None),
        P(both),
        P(both, None, None),
        P(both, None),
        P(both, None),
    )
    out_specs = (P(both, None), P(both, None))
    return jax.shard_map(local, mesh=mesh, in_specs=in_specs, out_specs=out_specs, check_vma=False)
```

```python
import functools

import jax
import jax.numpy as jnp
from jax import lax
from jax.experimental import pallas as pl
from jax.experimental.pallas import tpu as pltpu
from jax.sharding import PartitionSpec as P

HALO = 2
LANES = 128
SUBLANES = 8
CHUNK = 32
GROUPS = LANES // CHUNK
core_square = 0.25
softening = 1.5
UNROLL = 8
FOLD = 256
PIECES = 3
VMEM = 60 * 1024 * 1024


def split_rows(width, lanes):
    return pl.cdiv(width, lanes)


def in_hbm(count):
    return [pl.BlockSpec(memory_space=pltpu.HBM)] * count


def start_all(sems, moves):
    copies = [
        pltpu.make_async_copy(source, target, sems.at[n])
        for n, (source, target) in enumerate(moves)
    ]
    for copy in copies:
        copy.start()
    return copies


def far_kernel(
    count_hbm,
    pairs_hbm,
    gathered_hbm,
    blocks_ref,
    out_ref,
    count_ref,
    pairs_ref,
    gathered_ref,
    buffer,
    column_scr,
    coeff_scr,
    place_scr,
    sum_scr,
    summed_scr,
    halo_scr,
    sems,
    block_sems,
    *,
    segments,
):
    rank, _, slots = buffer.shape
    cols, clusters, _ = out_ref.shape
    targets = cols * clusters
    rows = gathered_ref.shape[0] // clusters
    sources = rows * clusters
    tiles = slots // FOLD

    def fetch(t):
        here = pl.ds(pl.multiple_of(t * FOLD, FOLD), FOLD)
        return pltpu.make_async_copy(
            blocks_ref.at[:, :, here], buffer.at[:, :, here], block_sems.at[t]
        )

    inputs = start_all(
        sems, ((count_hbm, count_ref), (pairs_hbm, pairs_ref), (gathered_hbm, gathered_ref))
    )
    fetch(0).start()
    summed_scr[...] = jnp.zeros_like(summed_scr)
    inputs[0].wait()
    count = count_ref[0]
    live = (count + FOLD - 1) // FOLD
    for t in range(1, tiles):

        @pl.when(t < live)
        def _(t=t):
            fetch(t).start()

    inputs[1].wait()
    inputs[2].wait()
    column_scr[...] = gathered_ref[...].astype(jnp.bfloat16)

    def multiply(t, carry):
        start = pl.multiple_of(t * FOLD, FOLD)
        lanes = pl.ds(start, FOLD)
        index = lax.broadcasted_iota(jnp.int32, (sources, FOLD), 0)
        pick = jnp.where(index == pairs_ref[1:2, lanes], 1.0, 0.0).astype(jnp.bfloat16)
        coeff = lax.dot_general(
            column_scr[...], pick, (((0,), (0,)), ((), ())), preferred_element_type=jnp.float32
        )
        coeff_scr[...] = coeff[0:rank, :]
        slot = lax.broadcasted_iota(jnp.int32, (1, FOLD), 1) + start
        wanted = jnp.where(slot < count, pairs_ref[0:1, lanes], -1)
        index = lax.broadcasted_iota(jnp.int32, (targets, FOLD), 0)
        place_scr[...] = jnp.where(index == wanted, 1.0, 0.0).astype(jnp.bfloat16)
        fetch(t).wait()

        def some_rows(k, carry):
            coeff = coeff_scr[...]
            for i in range(SUBLANES):
                r = k * SUBLANES + i
                product = buffer[r, :, lanes].astype(jnp.float32) * coeff
                folded = product[0:SUBLANES]
                for s in range(1, rank // SUBLANES):
                    folded = folded + product[s * SUBLANES : (s + 1) * SUBLANES]
                here = pl.ds(pl.multiple_of(r * SUBLANES, SUBLANES), SUBLANES)
                for h in range(FOLD // LANES):
                    sum_scr[h, here, :] = folded[:, h * LANES : (h + 1) * LANES]
            return carry

        lax.fori_loop(0, rank // SUBLANES, some_rows, 0)
        parts = []
        for h in range(FOLD // LANES):
            total = sum_scr[h, pl.ds(0, rank, stride=SUBLANES), :]
            for s in range(1, SUBLANES):
                total = total + sum_scr[h, pl.ds(s, rank, stride=SUBLANES), :]
            parts.append(total)
        coupled = jnp.concatenate(parts, axis=1)
        high = coupled.astype(jnp.bfloat16)
        low = (coupled - high.astype(jnp.float32)).astype(jnp.bfloat16)
        both = jnp.concatenate([high, low], axis=0)
        summed_scr[...] += lax.dot_general(
            place_scr[...], both, (((1,), (1,)), ((), ())), preferred_element_type=jnp.float32
        )
        return carry

    lax.fori_loop(0, live, multiply, 0)

    i = lax.axis_index("rows")
    j = lax.axis_index("cols")
    from_last = jnp.where(j < cols - 1, i, i - 1)
    from_first = jnp.where(j > 0, i, i + 1)
    edge = 2 * HALO
    halo_scr[...] = jnp.zeros_like(halo_scr)
    sides = (
        (0, jnp.minimum(from_first, rows - 1), from_first < rows),
        (edge, jnp.maximum(from_last, 0), from_last >= 0),
    )
    for side, (row, owner, there) in enumerate(sides):
        start = pl.multiple_of(owner * clusters, clusters)
        whole = jnp.where(there, gathered_ref[pl.ds(start, clusters), :], 0.0)
        for n in range(PIECES):
            piece = whole.astype(jnp.bfloat16).astype(jnp.float32)
            whole = whole - piece
            for g in range(segments):
                to = (n * segments + g) * edge
                here = g * 2 * edge + row
                halo_scr[side, to : to + edge, :] = piece[here : here + edge, :]
    after = jnp.where(j < cols - 1, j + 1, 0)
    lane = lax.broadcasted_iota(jnp.int32, (clusters, LANES), 1)
    for d in range(cols):
        halo = halo_scr[jnp.where(after == d, 1, 0)]
        mine = summed_scr[d * clusters : (d + 1) * clusters, :]
        mine = mine + pltpu.roll(mine, rank, 1)
        out_ref[d] = jnp.where(lane < rank, mine, halo).astype(out_ref.dtype)


def far_field(count, pairs, gathered, blocks, cols, segments):
    rank, _, slots = blocks.shape
    rows = lax.axis_size("rows")
    clusters = gathered.shape[0] // rows
    return pl.pallas_call(
        functools.partial(far_kernel, segments=segments),
        out_shape=jax.ShapeDtypeStruct((cols, clusters, LANES), jnp.bfloat16),
        in_specs=in_hbm(3) + [pl.BlockSpec(memory_space=pl.ANY)],
        out_specs=pl.BlockSpec(memory_space=pltpu.VMEM),
        scratch_shapes=[
            pltpu.SMEM(count.shape, count.dtype),
            pltpu.VMEM(pairs.shape, pairs.dtype),
            pltpu.VMEM(gathered.shape, gathered.dtype),
            pltpu.VMEM(blocks.shape, blocks.dtype),
            pltpu.VMEM((rows * clusters, LANES), jnp.bfloat16),
            pltpu.VMEM((rank, FOLD), jnp.float32),
            pltpu.VMEM((cols * clusters, FOLD), jnp.bfloat16),
            pltpu.VMEM((FOLD // LANES, rank * SUBLANES, LANES), jnp.float32),
            pltpu.VMEM((cols * clusters, LANES), jnp.float32),
            pltpu.VMEM((2, clusters, LANES), jnp.float32),
            pltpu.SemaphoreType.DMA((3,)),
            pltpu.SemaphoreType.DMA((slots // FOLD,)),
        ],
        compiler_params=pltpu.CompilerParams(vmem_limit_bytes=VMEM),
        cost_estimate=pl.CostEstimate(
            flops=2 * rank * rank * slots,
            bytes_accessed=2 * rank * rank * slots,
            transcendentals=0,
        ),
        name="far_field",
    )(count, pairs, gathered, blocks)


def replicate(rows, chunks, store, turned=False):
    within = lax.broadcasted_iota(jnp.int32, (rows.shape[0], LANES), 1)
    if turned:
        within = within + (within // CHUNK) * SUBLANES
    within = within % CHUNK
    for m in range(3 * chunks):
        tile = m // GROUPS
        store(
            m,
            jnp.take_along_axis(
                rows[:, tile * LANES : (tile + 1) * LANES],
                within + (m % GROUPS) * CHUNK,
                axis=1,
                mode="promise_in_bounds",
            ),
        )


def row_of(ref, n, row):
    return ref[n, pl.ds(row, SUBLANES, stride=0), :]


def turn(wide):
    return pltpu.roll(wide, 0, 1, stride=1, stride_axis=0)


def pair_sums(tgt, src, chunks):
    sums = [None] * (3 * chunks)
    size = 3 * chunks
    for f in range(chunks):
        y = [src(c * chunks + f) for c in range(3)]
        u = [src(size + c * chunks + f) for c in range(3)]
        v = [3.0 * x for x in u]
        for h in range(chunks):
            r = [tgt[c * chunks + h] - y[c] for c in range(3)]
            q = (r[0] * r[0] + core_square) + (r[1] * r[1] + r[2] * r[2])
            s = r[0] * v[0] + (r[1] * v[1] + r[2] * v[2])
            inverse = lax.rsqrt(q)
            square = inverse * inverse
            weight = square * inverse
            s = s * square
            for c in range(3):
                term = weight * (u[c] - s * r[c])
                m = c * chunks + h
                sums[m] = term if sums[m] is None else sums[m] + term
    return sums


def gather_sums(acc_scr, clusters, chunks, store):
    own_group = lax.broadcasted_iota(jnp.int32, (clusters, LANES), 1) // CHUNK
    for t in range(pl.cdiv(3 * chunks, GROUPS)):
        merged = None
        for g in range(GROUPS):
            m = t * GROUPS + g
            if m >= 3 * chunks:
                break
            total = acc_scr[m, pl.ds(0, clusters, stride=SUBLANES), :]
            for s in range(1, SUBLANES):
                total = total + acc_scr[m, pl.ds(s, clusters, stride=SUBLANES), :]
            total = total + pltpu.roll(total, 2 * CHUNK, 1)
            total = total + pltpu.roll(total, CHUNK, 1)
            merged = total if merged is None else jnp.where(own_group == g, total, merged)
        store(t, merged)


def turn_matrix():
    shape = (PIECES * CHUNK, SUBLANES * LANES)
    column = lax.broadcasted_iota(jnp.int32, shape, 1)
    lane = column % LANES
    entry = (lane + (lane // CHUNK) * SUBLANES + column // LANES) % CHUNK
    row = lax.broadcasted_iota(jnp.int32, shape, 0) % CHUNK
    return jnp.where(entry == row, 1.0, 0.0).astype(jnp.bfloat16)


def exact_pieces(value):
    pieces = []
    for _ in range(PIECES):
        piece = value.astype(jnp.bfloat16)
        pieces.append(piece)
        value = value - piece.astype(jnp.float32)
    return pieces


def near_kernel(
    pairs_hbm,
    count_hbm,
    disp_hbm,
    pos_hbm,
    intact_hbm,
    stiff_hbm,
    out_hbm,
    damage_hbm,
    rest_hbm,
    pairs_ref,
    count_ref,
    disp_ref,
    pos_ref,
    intact_ref,
    stiff_ref,
    out_ref,
    damage_ref,
    rest_ref,
    plan_ref,
    plan_smem,
    wide_scr,
    piece_scr,
    turn_scr,
    tgt_scr,
    src_scr,
    acc_scr,
    sems,
    out_sems,
    plan_sem,
):
    clusters, width = disp_ref.shape
    elems = width // 3
    chunks = elems // CHUNK
    size = 3 * chunks
    slots = pairs_ref.shape[1]

    inputs = start_all(
        sems,
        (
            (pos_hbm, pos_ref),
            (disp_hbm, disp_ref),
            (pairs_hbm, pairs_ref),
            (count_hbm, count_ref),
            (intact_hbm, intact_ref),
            (stiff_hbm, stiff_ref),
        ),
    )
    acc_scr[...] = jnp.zeros_like(acc_scr)
    turn_scr[...] = turn_matrix()
    for copy in inputs[2:4]:
        copy.wait()
    count = count_ref[0]

    target = pairs_ref[0:1, :]
    source = pairs_ref[1:2, :]
    live = lax.broadcasted_iota(jnp.int32, (1, slots), 1) < count
    own = jnp.logical_and(source >= HALO, source < clusters + HALO)
    plan_ref[0:1, :] = target
    plan_ref[1:2, :] = jnp.clip(source - HALO, 0, clusters - 1)
    plan_ref[2:3, :] = jnp.where(jnp.logical_and(live, own), target, clusters) * SUBLANES
    plan = pltpu.make_async_copy(plan_ref, plan_smem, plan_sem)
    plan.start()

    others = jnp.where(jnp.logical_and(live, jnp.logical_not(own)), 1.0, 0.0)
    square = (slots, slots)
    upto = lax.broadcasted_iota(jnp.int32, square, 0) <= lax.broadcasted_iota(jnp.int32, square, 1)
    upto = jnp.where(upto, 1.0, 0.0).astype(jnp.bfloat16)
    order = jnp.dot(
        jnp.broadcast_to(others, (SUBLANES, slots)).astype(jnp.bfloat16),
        upto,
        preferred_element_type=jnp.float32,
    )
    place = jnp.where(others > 0.0, order[0:1, :] - 1.0, -1.0).astype(jnp.int32)
    place = lax.broadcasted_iota(jnp.int32, square, 0) == place
    place = jnp.where(place, 1.0, 0.0).astype(jnp.bfloat16)
    row = lax.broadcasted_iota(jnp.int32, (SUBLANES, slots), 0)
    listed = jnp.where(row == 0, target, source).astype(jnp.float32).astype(jnp.bfloat16)
    listed = lax.dot_general(
        listed, place, (((1,), (1,)), ((), ())), preferred_element_type=jnp.float32
    )
    number = jnp.sum(others, axis=1, keepdims=True)
    rest_ref[...] = jnp.where(row < 2, listed, number).astype(jnp.int32)
    rest_out = pltpu.make_async_copy(rest_ref, rest_hbm, out_sems.at[1])
    rest_out.start()

    for k, values in enumerate((pos_ref, disp_ref)):
        inputs[k].wait()
        wide_scr[k, :, 0:width] = values[...]
        for m in range(size):
            pieces = exact_pieces(values[:, m * CHUNK : (m + 1) * CHUNK])
            piece_scr[(k * size + m) * clusters : (k * size + m + 1) * clusters, :] = (
                jnp.concatenate(pieces, axis=1)
            )
    columns = 2 * LANES
    for t in range(SUBLANES * LANES // columns):
        for k in range(2):
            rows = size * clusters
            turned = jnp.dot(
                piece_scr[k * rows : (k + 1) * rows, :],
                turn_scr[:, t * columns : (t + 1) * columns],
                preferred_element_type=jnp.float32,
            )
            for m in range(size):
                for h in range(columns // LANES):
                    s = t * (columns // LANES) + h
                    src_scr[k * size + m, pl.ds(s, clusters, stride=SUBLANES), :] = turned[
                        m * clusters : (m + 1) * clusters, h * LANES : (h + 1) * LANES
                    ]

    def store_target(m, value):
        tgt_scr[m] = value

    replicate(wide_scr[0], chunks, store_target)
    for copy in inputs[4:]:
        copy.wait()

    disp = [disp_ref[:, c * elems : (c + 1) * elems] for c in range(3)]
    separation = jnp.sqrt(1.0 + (disp[0] * disp[0] + disp[1] * disp[1] + disp[2] * disp[2]))
    softened = 1.0 - jnp.exp(-(separation - 1.0) / softening)
    intact = intact_ref[...].astype(jnp.float32)
    damage = intact * softened + (1.0 - intact)
    damage_ref[...] = damage
    damage_out = pltpu.make_async_copy(damage_ref, damage_hbm, out_sems.at[0])
    damage_out.start()
    hold = (1.0 - damage) * stiff_ref[...]
    for c in range(3):
        out_ref[:, c * elems : (c + 1) * elems] = -hold * disp[c]
    plan.wait()

    def one_pair(slot):
        target = plan_smem[0, slot]
        source = pl.multiple_of(plan_smem[1, slot] * SUBLANES, SUBLANES)
        into = pl.multiple_of(plan_smem[2, slot], SUBLANES)
        tgt = [row_of(tgt_scr, m, target) for m in range(size)]
        sums = pair_sums(tgt, lambda n: src_scr[n, pl.ds(source, SUBLANES), :], chunks)
        for m in range(size):
            acc_scr[m, pl.ds(into, SUBLANES), :] += sums[m]

    def step(it, carry):
        for k in range(UNROLL):
            one_pair(it * UNROLL + k)
        return carry

    lax.fori_loop(0, (count + UNROLL - 1) // UNROLL, step, 0)

    def store_sum(t, value):
        wide_scr[0, :, t * LANES : (t + 1) * LANES] = value

    gather_sums(acc_scr, clusters, chunks, store_sum)
    out_ref[...] += wide_scr[0, :, 0:width]
    near_out = pltpu.make_async_copy(out_ref, out_hbm, out_sems.at[2])
    near_out.start()
    for copy in (damage_out, rest_out, near_out):
        copy.wait()


def near_field(pairs, count, disp, pos, intact, stiffness):
    clusters, width = disp.shape
    elems = width // 3
    chunks = elems // CHUNK
    padded = pl.cdiv(width, LANES) * LANES
    slots = pairs.shape[1]
    return pl.pallas_call(
        near_kernel,
        out_shape=(
            jax.ShapeDtypeStruct((clusters, width), jnp.float32),
            jax.ShapeDtypeStruct((clusters, elems), jnp.float32),
            jax.ShapeDtypeStruct((SUBLANES, slots), jnp.int32),
        ),
        in_specs=in_hbm(6),
        out_specs=tuple(in_hbm(3)),
        scratch_shapes=[
            pltpu.VMEM(pairs.shape, pairs.dtype),
            pltpu.SMEM(count.shape, count.dtype),
            pltpu.VMEM(disp.shape, disp.dtype),
            pltpu.VMEM(pos.shape, pos.dtype),
            pltpu.VMEM(intact.shape, intact.dtype),
            pltpu.VMEM(stiffness.shape, stiffness.dtype),
            pltpu.VMEM((clusters, width), jnp.float32),
            pltpu.VMEM((clusters, elems), jnp.float32),
            pltpu.VMEM((SUBLANES, slots), jnp.int32),
            pltpu.VMEM((SUBLANES, slots), jnp.int32),
            pltpu.SMEM((SUBLANES, slots), jnp.int32),
            pltpu.VMEM((2, clusters, padded), jnp.float32),
            pltpu.VMEM((6 * chunks * clusters, PIECES * CHUNK), jnp.bfloat16),
            pltpu.VMEM((PIECES * CHUNK, SUBLANES * LANES), jnp.bfloat16),
            pltpu.VMEM((3 * chunks, clusters, LANES), jnp.float32),
            pltpu.VMEM((6 * chunks, clusters * SUBLANES, LANES), jnp.float32),
            pltpu.VMEM((3 * chunks, (clusters + 1) * SUBLANES, LANES), jnp.float32),
            pltpu.SemaphoreType.DMA((6,)),
            pltpu.SemaphoreType.DMA((3,)),
            pltpu.SemaphoreType.DMA(()),
        ],
        compiler_params=pltpu.CompilerParams(vmem_limit_bytes=VMEM),
        cost_estimate=pl.CostEstimate(
            flops=30 * slots * elems * elems,
            bytes_accessed=4 * clusters * width * 6,
            transcendentals=slots * elems * elems,
        ),
        name="near_field",
    )(pairs, count, disp, pos, intact, stiffness)


def finish_kernel(
    rest_hbm,
    pos_hbm,
    received_hbm,
    near_hbm,
    basis_hbm,
    out_ref,
    rest_ref,
    pos_ref,
    received_ref,
    near_ref,
    basis_scr,
    ext_scr,
    halo_scr,
    tgt_scr,
    row_scr,
    acc_scr,
    sems,
):
    clusters, width = pos_ref.shape
    cols = received_ref.shape[0]
    rank = basis_scr.shape[1]
    elems = width // 3
    chunks = elems // CHUNK
    size = 3 * chunks
    spare = LANES - rank
    segments = split_rows(width, spare)
    edge = 2 * HALO

    inputs = start_all(
        sems,
        (
            (received_hbm, received_ref),
            (pos_hbm, pos_ref),
            (rest_hbm, rest_ref),
            (near_hbm, near_ref),
            (basis_hbm, basis_scr),
        ),
    )
    acc_scr[...] = jnp.zeros_like(acc_scr)
    inputs[0].wait()
    inputs[1].wait()

    j = lax.axis_index("cols")
    before = jnp.where(j > 0, j - 1, cols - 1)
    after = jnp.where(j < cols - 1, j + 1, 0)
    for start, sender in ((0, before), (HALO, after)):
        halo_scr[...] = received_ref[sender].astype(jnp.float32)
        rows = edge * segments
        whole = halo_scr[0:rows, :]
        for n in range(1, PIECES):
            whole = whole + halo_scr[n * rows : (n + 1) * rows, :]
        for g in range(segments):
            count = min(spare, width - g * spare)
            for k in range(2):
                row = (2 * g + k) * HALO
                ext_scr[k, start : start + HALO, g * spare : g * spare + count] = whole[
                    row : row + HALO, rank : rank + count
                ]
    ext_scr[1, edge : edge + HALO, 0:width] = pos_ref[0:HALO, :]
    ext_scr[1, edge + HALO : 2 * edge, 0:width] = pos_ref[clusters - HALO :, :]
    for k in range(2):

        def store(m, value, k=k):
            row_scr[(1 - k) * size + m] = value
        replicate(ext_scr[k], chunks, store, True)

    def store_target(m, value):
        tgt_scr[m] = value

    replicate(ext_scr[1], chunks, store_target)
    inputs[2].wait()

    def step(n, carry):
        target = rest_ref[0, n]
        source = rest_ref[1, n]
        target = jnp.where(target < HALO, target, target - (clusters - edge))
        source = jnp.where(source < HALO, source, source - clusters)
        into = pl.multiple_of(target * SUBLANES, SUBLANES)
        tgt = [row_of(tgt_scr, m, edge + target) for m in range(size)]
        sums = pair_sums(tgt, lambda k: turn(row_of(row_scr, k, source)), chunks)
        for m in range(size):
            acc_scr[m, pl.ds(into, SUBLANES), :] += sums[m]
        return carry

    lax.fori_loop(0, rest_ref[2, 0], step, 0)

    def store_sum(t, value):
        ext_scr[0, :, t * LANES : (t + 1) * LANES] = value

    gather_sums(acc_scr, 2 * edge, chunks, store_sum)

    owned = received_ref[0].astype(jnp.float32)
    for d in range(1, cols):
        owned = owned + received_ref[d].astype(jnp.float32)
    inputs[3].wait()
    inputs[4].wait()
    wide = lax.broadcasted_iota(jnp.int32, (SUBLANES, SUBLANES * rank), 1) // rank
    wide = wide == lax.broadcasted_iota(jnp.int32, (SUBLANES, SUBLANES * rank), 0)
    for k in range(clusters // SUBLANES):
        some = slice(k * SUBLANES, (k + 1) * SUBLANES)
        tiled = jnp.concatenate([owned[some, 0:rank]] * SUBLANES, axis=1)
        diagonal = jnp.where(wide, tiled, 0.0).astype(jnp.bfloat16)
        out_ref[some, :] = near_ref[some, :] + jnp.dot(
            diagonal,
            basis_scr[some].reshape(SUBLANES * rank, width),
            preferred_element_type=jnp.float32,
        )
    out_ref[0:HALO, :] += ext_scr[0, 0:HALO, 0:width]
    out_ref[clusters - HALO :, :] += ext_scr[0, HALO:edge, 0:width]


def finish(rest, pos, received, near, basis):
    clusters, width = pos.shape
    rank = basis.shape[1]
    chunks = width // 3 // CHUNK
    padded = pl.cdiv(width, LANES) * LANES
    edge = 2 * HALO
    return pl.pallas_call(
        finish_kernel,
        out_shape=jax.ShapeDtypeStruct((clusters, width), jnp.float32),
        in_specs=in_hbm(5),
        out_specs=pl.BlockSpec(memory_space=pltpu.VMEM),
        scratch_shapes=[
            pltpu.SMEM(rest.shape, rest.dtype),
            pltpu.VMEM(pos.shape, pos.dtype),
            pltpu.VMEM(received.shape, received.dtype),
            pltpu.VMEM(near.shape, near.dtype),
            pltpu.VMEM(basis.shape, basis.dtype),
            pltpu.VMEM((2, 2 * edge, padded), jnp.float32),
            pltpu.VMEM((clusters, LANES), jnp.float32),
            pltpu.VMEM((3 * chunks, 2 * edge, LANES), jnp.float32),
            pltpu.VMEM((6 * chunks, 2 * edge, LANES), jnp.float32),
            pltpu.VMEM((3 * chunks, 2 * edge * SUBLANES, LANES), jnp.float32),
            pltpu.SemaphoreType.DMA((5,)),
        ],
        compiler_params=pltpu.CompilerParams(vmem_limit_bytes=VMEM),
        cost_estimate=pl.CostEstimate(
            flops=2 * clusters * rank * width,
            bytes_accessed=2 * clusters * rank * width,
            transcendentals=0,
        ),
        name="finish",
    )(rest, pos, received, near, basis)


def local(
    displacement,
    positions,
    cluster_basis,
    near_pairs,
    near_count,
    far_pairs,
    far_count,
    far_blocks,
    intact,
    stiffness,
):
    cols = lax.axis_size("cols")
    basis = cluster_basis.transpose(0, 2, 1)
    clusters, rank, width = basis.shape
    disp_bf = displacement.astype(jnp.bfloat16)
    coeff = jnp.einsum("kf,kfr->kr", disp_bf, cluster_basis, preferred_element_type=jnp.float32)

    spare = LANES - rank
    segments = split_rows(width, spare)
    edge = jnp.concatenate(
        [rows[part] for part in (slice(0, HALO), slice(clusters - HALO, clusters)) for rows in (displacement, positions)],
        axis=0,
    )
    edge = jnp.pad(edge, ((0, 0), (0, segments * spare - width)))
    halo = jnp.concatenate([edge[:, g * spare : (g + 1) * spare] for g in range(segments)], axis=0)
    halo = jnp.pad(halo, ((0, clusters - halo.shape[0]), (0, 0)))
    payload = jnp.concatenate([coeff, halo], axis=1)
    gathered = lax.all_gather(payload, "rows", axis=0, tiled=True)
    partial = far_field(
        far_count, far_pairs.T, gathered, far_blocks.transpose(1, 2, 0), cols, segments
    )
    received = lax.all_to_all(partial, "cols", split_axis=0, concat_axis=0)
    near, damage, rest = near_field(
        near_pairs.T, near_count, displacement, positions, intact, stiffness
    )
    return finish(rest, positions, received, near, basis), damage


def solution(mesh):
    both = ("rows", "cols")
    in_specs = (
        P(both, None),
        P(both, None),
        P(both, None, None),
        P(both, None),
        P(both),
        P(both, None),
        P(both),
        P(both, None, None),
        P(both, None),
        P(both, None),
    )
    out_specs = (P(both, None), P(both, None))
    return jax.shard_map(local, mesh=mesh, in_specs=in_specs, out_specs=out_specs, check_vma=False)
```

```python
import functools

import jax
import jax.numpy as jnp
from jax import lax
from jax.experimental import pallas as pl
from jax.experimental.pallas import tpu as pltpu
from jax.sharding import PartitionSpec as P

HALO = 2
LANES = 128
SUBLANES = 8
CHUNK = 32
GROUPS = LANES // CHUNK
core_square = 0.25
softening = 1.5
UNROLL = 8
FOLD = 256
PIECES = 3
VMEM = 20 * 1024 * 1024


def split_rows(width, lanes):
    return pl.cdiv(width, lanes)


def in_hbm(count):
    return [pl.BlockSpec(memory_space=pltpu.HBM)] * count


def pinned(*arrays):
    return [pltpu.with_memory_space_constraint(x, pltpu.HBM) for x in arrays]


def start_all(sems, moves):
    copies = [
        pltpu.make_async_copy(source, target, sems.at[n])
        for n, (source, target) in enumerate(moves)
    ]
    for copy in copies:
        copy.start()
    return copies


def far_kernel(
    count_hbm,
    pairs_hbm,
    gathered_hbm,
    blocks_ref,
    out_ref,
    count_ref,
    pairs_ref,
    gathered_ref,
    buffer,
    column_scr,
    coeff_scr,
    place_scr,
    sum_scr,
    summed_scr,
    halo_scr,
    sems,
    block_sems,
    *,
    segments,
):
    rank, _, slots = buffer.shape
    cols, clusters, _ = out_ref.shape
    targets = cols * clusters
    rows = gathered_ref.shape[0] // clusters
    sources = rows * clusters
    tiles = slots // FOLD

    def fetch(t):
        here = pl.ds(pl.multiple_of(t * FOLD, FOLD), FOLD)
        return pltpu.make_async_copy(
            blocks_ref.at[:, :, here], buffer.at[:, :, here], block_sems.at[t]
        )

    inputs = start_all(
        sems, ((count_hbm, count_ref), (pairs_hbm, pairs_ref), (gathered_hbm, gathered_ref))
    )
    fetch(0).start()
    summed_scr[...] = jnp.zeros_like(summed_scr)
    inputs[0].wait()
    count = count_ref[0]
    live = (count + FOLD - 1) // FOLD
    for t in range(1, tiles):

        @pl.when(t < live)
        def _(t=t):
            fetch(t).start()

    inputs[1].wait()
    inputs[2].wait()
    column_scr[...] = gathered_ref[...].astype(jnp.bfloat16)

    def multiply(t, carry):
        start = pl.multiple_of(t * FOLD, FOLD)
        lanes = pl.ds(start, FOLD)
        index = lax.broadcasted_iota(jnp.int32, (sources, FOLD), 0)
        pick = jnp.where(index == pairs_ref[1:2, lanes], 1.0, 0.0).astype(jnp.bfloat16)
        coeff = lax.dot_general(
            column_scr[...], pick, (((0,), (0,)), ((), ())), preferred_element_type=jnp.float32
        )
        coeff_scr[...] = coeff[0:rank, :]
        slot = lax.broadcasted_iota(jnp.int32, (1, FOLD), 1) + start
        wanted = jnp.where(slot < count, pairs_ref[0:1, lanes], -1)
        index = lax.broadcasted_iota(jnp.int32, (targets, FOLD), 0)
        place_scr[...] = jnp.where(index == wanted, 1.0, 0.0).astype(jnp.bfloat16)
        fetch(t).wait()

        def some_rows(k, carry):
            coeff = coeff_scr[...]
            for i in range(SUBLANES):
                r = k * SUBLANES + i
                product = buffer[r, :, lanes].astype(jnp.float32) * coeff
                folded = product[0:SUBLANES]
                for s in range(1, rank // SUBLANES):
                    folded = folded + product[s * SUBLANES : (s + 1) * SUBLANES]
                here = pl.ds(pl.multiple_of(r * SUBLANES, SUBLANES), SUBLANES)
                for h in range(FOLD // LANES):
                    sum_scr[h, here, :] = folded[:, h * LANES : (h + 1) * LANES]
            return carry

        lax.fori_loop(0, rank // SUBLANES, some_rows, 0)
        parts = []
        for h in range(FOLD // LANES):
            total = sum_scr[h, pl.ds(0, rank, stride=SUBLANES), :]
            for s in range(1, SUBLANES):
                total = total + sum_scr[h, pl.ds(s, rank, stride=SUBLANES), :]
            parts.append(total)
        coupled = jnp.concatenate(parts, axis=1)
        high = coupled.astype(jnp.bfloat16)
        low = (coupled - high.astype(jnp.float32)).astype(jnp.bfloat16)
        both = jnp.concatenate([high, low], axis=0)
        summed_scr[...] += lax.dot_general(
            place_scr[...], both, (((1,), (1,)), ((), ())), preferred_element_type=jnp.float32
        )
        return carry

    lax.fori_loop(0, live, multiply, 0)

    i = lax.axis_index("rows")
    j = lax.axis_index("cols")
    from_last = jnp.where(j < cols - 1, i, i - 1)
    from_first = jnp.where(j > 0, i, i + 1)
    edge = 2 * HALO
    halo_scr[...] = jnp.zeros_like(halo_scr)
    sides = (
        (0, jnp.minimum(from_first, rows - 1), from_first < rows),
        (edge, jnp.maximum(from_last, 0), from_last >= 0),
    )
    for side, (row, owner, there) in enumerate(sides):
        start = pl.multiple_of(owner * clusters, clusters)
        whole = jnp.where(there, gathered_ref[pl.ds(start, clusters), :], 0.0)
        for n in range(PIECES):
            piece = whole.astype(jnp.bfloat16).astype(jnp.float32)
            whole = whole - piece
            for g in range(segments):
                to = (n * segments + g) * edge
                here = g * 2 * edge + row
                halo_scr[side, to : to + edge, :] = piece[here : here + edge, :]
    after = jnp.where(j < cols - 1, j + 1, 0)
    lane = lax.broadcasted_iota(jnp.int32, (clusters, LANES), 1)
    for d in range(cols):
        halo = halo_scr[jnp.where(after == d, 1, 0)]
        mine = summed_scr[d * clusters : (d + 1) * clusters, :]
        mine = mine + pltpu.roll(mine, rank, 1)
        out_ref[d] = jnp.where(lane < rank, mine, halo).astype(out_ref.dtype)


def far_field(count, pairs, gathered, blocks, cols, segments):
    rank, _, slots = blocks.shape
    rows = lax.axis_size("rows")
    clusters = gathered.shape[0] // rows
    return pl.pallas_call(
        functools.partial(far_kernel, segments=segments),
        out_shape=jax.ShapeDtypeStruct((cols, clusters, LANES), jnp.bfloat16),
        in_specs=in_hbm(3) + [pl.BlockSpec(memory_space=pl.ANY)],
        out_specs=pl.BlockSpec(memory_space=pltpu.VMEM),
        scratch_shapes=[
            pltpu.SMEM(count.shape, count.dtype),
            pltpu.VMEM(pairs.shape, pairs.dtype),
            pltpu.VMEM(gathered.shape, gathered.dtype),
            pltpu.VMEM(blocks.shape, blocks.dtype),
            pltpu.VMEM((rows * clusters, LANES), jnp.bfloat16),
            pltpu.VMEM((rank, FOLD), jnp.float32),
            pltpu.VMEM((cols * clusters, FOLD), jnp.bfloat16),
            pltpu.VMEM((FOLD // LANES, rank * SUBLANES, LANES), jnp.float32),
            pltpu.VMEM((cols * clusters, LANES), jnp.float32),
            pltpu.VMEM((2, clusters, LANES), jnp.float32),
            pltpu.SemaphoreType.DMA((3,)),
            pltpu.SemaphoreType.DMA((slots // FOLD,)),
        ],
        compiler_params=pltpu.CompilerParams(vmem_limit_bytes=VMEM),
        cost_estimate=pl.CostEstimate(
            flops=2 * rank * rank * slots,
            bytes_accessed=2 * rank * rank * slots,
            transcendentals=0,
        ),
        name="far_field",
    )(count, *pinned(pairs), gathered, *pinned(blocks))


def replicate(rows, chunks, store, turned=False):
    within = lax.broadcasted_iota(jnp.int32, (rows.shape[0], LANES), 1)
    if turned:
        within = within + (within // CHUNK) * SUBLANES
    within = within % CHUNK
    for m in range(3 * chunks):
        tile = m // GROUPS
        store(
            m,
            jnp.take_along_axis(
                rows[:, tile * LANES : (tile + 1) * LANES],
                within + (m % GROUPS) * CHUNK,
                axis=1,
                mode="promise_in_bounds",
            ),
        )


def row_of(ref, n, row):
    return ref[n, pl.ds(row, SUBLANES, stride=0), :]


def turn(wide):
    return pltpu.roll(wide, 0, 1, stride=1, stride_axis=0)


def pair_sums(tgt, src, chunks):
    sums = [None] * (3 * chunks)
    size = 3 * chunks
    for f in range(chunks):
        y = [src(c * chunks + f) for c in range(3)]
        u = [src(size + c * chunks + f) for c in range(3)]
        v = [3.0 * x for x in u]
        for h in range(chunks):
            r = [tgt[c * chunks + h] - y[c] for c in range(3)]
            q = (r[0] * r[0] + core_square) + (r[1] * r[1] + r[2] * r[2])
            s = r[0] * v[0] + (r[1] * v[1] + r[2] * v[2])
            inverse = lax.rsqrt(q)
            square = inverse * inverse
            weight = square * inverse
            s = s * square
            for c in range(3):
                term = weight * (u[c] - s * r[c])
                m = c * chunks + h
                sums[m] = term if sums[m] is None else sums[m] + term
    return sums


def gather_sums(acc_scr, clusters, chunks, store):
    own_group = lax.broadcasted_iota(jnp.int32, (clusters, LANES), 1) // CHUNK
    for t in range(pl.cdiv(3 * chunks, GROUPS)):
        merged = None
        for g in range(GROUPS):
            m = t * GROUPS + g
            if m >= 3 * chunks:
                break
            total = acc_scr[m, pl.ds(0, clusters, stride=SUBLANES), :]
            for s in range(1, SUBLANES):
                total = total + acc_scr[m, pl.ds(s, clusters, stride=SUBLANES), :]
            total = total + pltpu.roll(total, 2 * CHUNK, 1)
            total = total + pltpu.roll(total, CHUNK, 1)
            merged = total if merged is None else jnp.where(own_group == g, total, merged)
        store(t, merged)


def turn_matrix():
    shape = (PIECES * CHUNK, SUBLANES * LANES)
    column = lax.broadcasted_iota(jnp.int32, shape, 1)
    lane = column % LANES
    entry = (lane + (lane // CHUNK) * SUBLANES + column // LANES) % CHUNK
    row = lax.broadcasted_iota(jnp.int32, shape, 0) % CHUNK
    return jnp.where(entry == row, 1.0, 0.0).astype(jnp.bfloat16)


def exact_pieces(value):
    pieces = []
    for _ in range(PIECES):
        piece = value.astype(jnp.bfloat16)
        pieces.append(piece)
        value = value - piece.astype(jnp.float32)
    return pieces


def near_kernel(
    pairs_hbm,
    count_hbm,
    disp_hbm,
    pos_hbm,
    intact_hbm,
    stiff_hbm,
    out_hbm,
    damage_hbm,
    rest_hbm,
    pairs_ref,
    count_ref,
    disp_ref,
    pos_ref,
    intact_ref,
    stiff_ref,
    out_ref,
    damage_ref,
    rest_ref,
    plan_ref,
    plan_smem,
    wide_scr,
    piece_scr,
    turn_scr,
    tgt_scr,
    src_scr,
    acc_scr,
    sems,
    out_sems,
    plan_sem,
):
    clusters, width = disp_ref.shape
    elems = width // 3
    chunks = elems // CHUNK
    size = 3 * chunks
    slots = pairs_ref.shape[1]

    inputs = start_all(
        sems,
        (
            (pos_hbm, pos_ref),
            (disp_hbm, disp_ref),
            (pairs_hbm, pairs_ref),
            (count_hbm, count_ref),
            (intact_hbm, intact_ref),
            (stiff_hbm, stiff_ref),
        ),
    )
    acc_scr[...] = jnp.zeros_like(acc_scr)
    turn_scr[...] = turn_matrix()
    for copy in inputs[2:4]:
        copy.wait()
    count = count_ref[0]

    target = pairs_ref[0:1, :]
    source = pairs_ref[1:2, :]
    live = lax.broadcasted_iota(jnp.int32, (1, slots), 1) < count
    own = jnp.logical_and(source >= HALO, source < clusters + HALO)
    plan_ref[0:1, :] = target
    plan_ref[1:2, :] = jnp.clip(source - HALO, 0, clusters - 1)
    plan_ref[2:3, :] = jnp.where(jnp.logical_and(live, own), target, clusters) * SUBLANES
    plan = pltpu.make_async_copy(plan_ref, plan_smem, plan_sem)
    plan.start()

    others = jnp.where(jnp.logical_and(live, jnp.logical_not(own)), 1.0, 0.0)
    square = (slots, slots)
    upto = lax.broadcasted_iota(jnp.int32, square, 0) <= lax.broadcasted_iota(jnp.int32, square, 1)
    upto = jnp.where(upto, 1.0, 0.0).astype(jnp.bfloat16)
    order = jnp.dot(
        jnp.broadcast_to(others, (SUBLANES, slots)).astype(jnp.bfloat16),
        upto,
        preferred_element_type=jnp.float32,
    )
    place = jnp.where(others > 0.0, order[0:1, :] - 1.0, -1.0).astype(jnp.int32)
    place = lax.broadcasted_iota(jnp.int32, square, 0) == place
    place = jnp.where(place, 1.0, 0.0).astype(jnp.bfloat16)
    row = lax.broadcasted_iota(jnp.int32, (SUBLANES, slots), 0)
    listed = jnp.where(row == 0, target, source).astype(jnp.float32).astype(jnp.bfloat16)
    listed = lax.dot_general(
        listed, place, (((1,), (1,)), ((), ())), preferred_element_type=jnp.float32
    )
    number = jnp.sum(others, axis=1, keepdims=True)
    rest_ref[...] = jnp.where(row < 2, listed, number).astype(jnp.int32)
    rest_out = pltpu.make_async_copy(rest_ref, rest_hbm, out_sems.at[1])
    rest_out.start()

    for k, values in enumerate((pos_ref, disp_ref)):
        inputs[k].wait()
        wide_scr[k, :, 0:width] = values[...]
        for m in range(size):
            pieces = exact_pieces(values[:, m * CHUNK : (m + 1) * CHUNK])
            piece_scr[(k * size + m) * clusters : (k * size + m + 1) * clusters, :] = (
                jnp.concatenate(pieces, axis=1)
            )
    columns = 2 * LANES
    for t in range(SUBLANES * LANES // columns):
        for k in range(2):
            rows = size * clusters
            turned = jnp.dot(
                piece_scr[k * rows : (k + 1) * rows, :],
                turn_scr[:, t * columns : (t + 1) * columns],
                preferred_element_type=jnp.float32,
            )
            for m in range(size):
                for h in range(columns // LANES):
                    s = t * (columns // LANES) + h
                    src_scr[k * size + m, pl.ds(s, clusters, stride=SUBLANES), :] = turned[
                        m * clusters : (m + 1) * clusters, h * LANES : (h + 1) * LANES
                    ]

    def store_target(m, value):
        tgt_scr[m] = value

    replicate(wide_scr[0], chunks, store_target)
    for copy in inputs[4:]:
        copy.wait()

    disp = [disp_ref[:, c * elems : (c + 1) * elems] for c in range(3)]
    separation = jnp.sqrt(1.0 + (disp[0] * disp[0] + disp[1] * disp[1] + disp[2] * disp[2]))
    softened = 1.0 - jnp.exp(-(separation - 1.0) / softening)
    intact = intact_ref[...].astype(jnp.float32)
    damage = intact * softened + (1.0 - intact)
    damage_ref[...] = damage
    damage_out = pltpu.make_async_copy(damage_ref, damage_hbm, out_sems.at[0])
    damage_out.start()
    hold = (1.0 - damage) * stiff_ref[...]
    for c in range(3):
        out_ref[:, c * elems : (c + 1) * elems] = -hold * disp[c]
    plan.wait()

    def one_pair(slot):
        target = plan_smem[0, slot]
        source = pl.multiple_of(plan_smem[1, slot] * SUBLANES, SUBLANES)
        into = pl.multiple_of(plan_smem[2, slot], SUBLANES)
        tgt = [row_of(tgt_scr, m, target) for m in range(size)]
        sums = pair_sums(tgt, lambda n: src_scr[n, pl.ds(source, SUBLANES), :], chunks)
        for m in range(size):
            acc_scr[m, pl.ds(into, SUBLANES), :] += sums[m]

    def step(it, carry):
        for k in range(UNROLL):
            one_pair(it * UNROLL + k)
        return carry

    lax.fori_loop(0, (count + UNROLL - 1) // UNROLL, step, 0)

    def store_sum(t, value):
        wide_scr[0, :, t * LANES : (t + 1) * LANES] = value

    gather_sums(acc_scr, clusters, chunks, store_sum)
    out_ref[...] += wide_scr[0, :, 0:width]
    near_out = pltpu.make_async_copy(out_ref, out_hbm, out_sems.at[2])
    near_out.start()
    for copy in (damage_out, rest_out, near_out):
        copy.wait()


def near_field(pairs, count, disp, pos, intact, stiffness):
    clusters, width = disp.shape
    elems = width // 3
    chunks = elems // CHUNK
    padded = pl.cdiv(width, LANES) * LANES
    slots = pairs.shape[1]
    return pl.pallas_call(
        near_kernel,
        out_shape=(
            jax.ShapeDtypeStruct((clusters, width), jnp.float32),
            jax.ShapeDtypeStruct((clusters, elems), jnp.float32),
            jax.ShapeDtypeStruct((SUBLANES, slots), jnp.int32),
        ),
        in_specs=in_hbm(6),
        out_specs=tuple(in_hbm(3)),
        scratch_shapes=[
            pltpu.VMEM(pairs.shape, pairs.dtype),
            pltpu.SMEM(count.shape, count.dtype),
            pltpu.VMEM(disp.shape, disp.dtype),
            pltpu.VMEM(pos.shape, pos.dtype),
            pltpu.VMEM(intact.shape, intact.dtype),
            pltpu.VMEM(stiffness.shape, stiffness.dtype),
            pltpu.VMEM((clusters, width), jnp.float32),
            pltpu.VMEM((clusters, elems), jnp.float32),
            pltpu.VMEM((SUBLANES, slots), jnp.int32),
            pltpu.VMEM((SUBLANES, slots), jnp.int32),
            pltpu.SMEM((SUBLANES, slots), jnp.int32),
            pltpu.VMEM((2, clusters, padded), jnp.float32),
            pltpu.VMEM((6 * chunks * clusters, PIECES * CHUNK), jnp.bfloat16),
            pltpu.VMEM((PIECES * CHUNK, SUBLANES * LANES), jnp.bfloat16),
            pltpu.VMEM((3 * chunks, clusters, LANES), jnp.float32),
            pltpu.VMEM((6 * chunks, clusters * SUBLANES, LANES), jnp.float32),
            pltpu.VMEM((3 * chunks, (clusters + 1) * SUBLANES, LANES), jnp.float32),
            pltpu.SemaphoreType.DMA((6,)),
            pltpu.SemaphoreType.DMA((3,)),
            pltpu.SemaphoreType.DMA(()),
        ],
        compiler_params=pltpu.CompilerParams(vmem_limit_bytes=VMEM),
        cost_estimate=pl.CostEstimate(
            flops=30 * slots * elems * elems,
            bytes_accessed=4 * clusters * width * 6,
            transcendentals=slots * elems * elems,
        ),
        name="near_field",
    )(*pinned(pairs), count, *pinned(disp, pos, intact, stiffness))


def finish_kernel(
    rest_hbm,
    pos_hbm,
    received_hbm,
    near_hbm,
    far_hbm,
    out_ref,
    rest_ref,
    pos_ref,
    received_ref,
    near_ref,
    far_ref,
    ext_scr,
    halo_scr,
    tgt_scr,
    row_scr,
    acc_scr,
    sems,
    *,
    rank,
):
    clusters, width = pos_ref.shape
    cols = received_ref.shape[0]
    elems = width // 3
    chunks = elems // CHUNK
    size = 3 * chunks
    spare = LANES - rank
    segments = split_rows(width, spare)
    edge = 2 * HALO

    inputs = start_all(
        sems,
        (
            (received_hbm, received_ref),
            (pos_hbm, pos_ref),
            (rest_hbm, rest_ref),
            (near_hbm, near_ref),
            (far_hbm, far_ref),
        ),
    )
    acc_scr[...] = jnp.zeros_like(acc_scr)
    inputs[0].wait()
    inputs[1].wait()

    j = lax.axis_index("cols")
    before = jnp.where(j > 0, j - 1, cols - 1)
    after = jnp.where(j < cols - 1, j + 1, 0)
    for start, sender in ((0, before), (HALO, after)):
        halo_scr[...] = received_ref[sender].astype(jnp.float32)
        rows = edge * segments
        whole = halo_scr[0:rows, :]
        for n in range(1, PIECES):
            whole = whole + halo_scr[n * rows : (n + 1) * rows, :]
        for g in range(segments):
            count = min(spare, width - g * spare)
            for k in range(2):
                row = (2 * g + k) * HALO
                ext_scr[k, start : start + HALO, g * spare : g * spare + count] = whole[
                    row : row + HALO, rank : rank + count
                ]
    ext_scr[1, edge : edge + HALO, 0:width] = pos_ref[0:HALO, :]
    ext_scr[1, edge + HALO : 2 * edge, 0:width] = pos_ref[clusters - HALO :, :]
    for k in range(2):

        def store(m, value, k=k):
            row_scr[(1 - k) * size + m] = value
        replicate(ext_scr[k], chunks, store, True)

    def store_target(m, value):
        tgt_scr[m] = value

    replicate(ext_scr[1], chunks, store_target)
    inputs[2].wait()

    def step(n, carry):
        target = rest_ref[0, n]
        source = rest_ref[1, n]
        target = jnp.where(target < HALO, target, target - (clusters - edge))
        source = jnp.where(source < HALO, source, source - clusters)
        into = pl.multiple_of(target * SUBLANES, SUBLANES)
        tgt = [row_of(tgt_scr, m, edge + target) for m in range(size)]
        sums = pair_sums(tgt, lambda k: turn(row_of(row_scr, k, source)), chunks)
        for m in range(size):
            acc_scr[m, pl.ds(into, SUBLANES), :] += sums[m]
        return carry

    lax.fori_loop(0, rest_ref[2, 0], step, 0)

    def store_sum(t, value):
        ext_scr[0, :, t * LANES : (t + 1) * LANES] = value

    gather_sums(acc_scr, 2 * edge, chunks, store_sum)

    for copy in inputs[3:]:
        copy.wait()
    out_ref[...] = near_ref[...] + far_ref[...]
    out_ref[0:HALO, :] += ext_scr[0, 0:HALO, 0:width]
    out_ref[clusters - HALO :, :] += ext_scr[0, HALO:edge, 0:width]


def finish(rest, pos, received, near, far, rank):
    clusters, width = pos.shape
    chunks = width // 3 // CHUNK
    padded = pl.cdiv(width, LANES) * LANES
    edge = 2 * HALO
    return pl.pallas_call(
        functools.partial(finish_kernel, rank=rank),
        out_shape=jax.ShapeDtypeStruct((clusters, width), jnp.float32),
        in_specs=in_hbm(5),
        out_specs=pl.BlockSpec(memory_space=pltpu.VMEM),
        scratch_shapes=[
            pltpu.SMEM(rest.shape, rest.dtype),
            pltpu.VMEM(pos.shape, pos.dtype),
            pltpu.VMEM(received.shape, received.dtype),
            pltpu.VMEM(near.shape, near.dtype),
            pltpu.VMEM(far.shape, far.dtype),
            pltpu.VMEM((2, 2 * edge, padded), jnp.float32),
            pltpu.VMEM((clusters, LANES), jnp.float32),
            pltpu.VMEM((3 * chunks, 2 * edge, LANES), jnp.float32),
            pltpu.VMEM((6 * chunks, 2 * edge, LANES), jnp.float32),
            pltpu.VMEM((3 * chunks, 2 * edge * SUBLANES, LANES), jnp.float32),
            pltpu.SemaphoreType.DMA((5,)),
        ],
        compiler_params=pltpu.CompilerParams(vmem_limit_bytes=VMEM),
        cost_estimate=pl.CostEstimate(
            flops=2 * clusters * rank * width,
            bytes_accessed=16 * clusters * width,
            transcendentals=0,
        ),
        name="finish",
    )(rest, *pinned(pos), received, near, far)


def local(
    displacement,
    positions,
    cluster_basis,
    near_pairs,
    near_count,
    far_pairs,
    far_count,
    far_blocks,
    intact,
    stiffness,
):
    cols = lax.axis_size("cols")
    clusters, width, rank = cluster_basis.shape
    disp_bf = displacement.astype(jnp.bfloat16)
    coeff = jnp.einsum("kf,kfr->kr", disp_bf, cluster_basis, preferred_element_type=jnp.float32)

    spare = LANES - rank
    segments = split_rows(width, spare)
    edge = jnp.concatenate(
        [rows[part] for part in (slice(0, HALO), slice(clusters - HALO, clusters)) for rows in (displacement, positions)],
        axis=0,
    )
    edge = jnp.pad(edge, ((0, 0), (0, segments * spare - width)))
    halo = jnp.concatenate([edge[:, g * spare : (g + 1) * spare] for g in range(segments)], axis=0)
    halo = jnp.pad(halo, ((0, clusters - halo.shape[0]), (0, 0)))
    payload = jnp.concatenate([coeff, halo], axis=1)
    gathered = lax.all_gather(payload, "rows", axis=0, tiled=True)
    partial = far_field(
        far_count, far_pairs.T, gathered, far_blocks.transpose(1, 2, 0), cols, segments
    )
    received = lax.all_to_all(partial, "cols", split_axis=0, concat_axis=0)
    near, damage, rest = near_field(
        near_pairs.T, near_count, displacement, positions, intact, stiffness
    )
    owned = jnp.sum(received[:, :, :rank].astype(jnp.float32), axis=0).astype(jnp.bfloat16)
    far = jnp.einsum("kfr,kr->kf", cluster_basis, owned, preferred_element_type=jnp.float32)
    return finish(rest, positions, received, near, far, rank), damage


def solution(mesh):
    both = ("rows", "cols")
    in_specs = (
        P(both, None),
        P(both, None),
        P(both, None, None),
        P(both, None),
        P(both),
        P(both, None),
        P(both),
        P(both, None, None),
        P(both, None),
        P(both, None),
    )
    out_specs = (P(both, None), P(both, None))
    return jax.shard_map(local, mesh=mesh, in_specs=in_specs, out_specs=out_specs, check_vma=False)
```

```python
import functools

import jax
import jax.numpy as jnp
from jax import lax
from jax.experimental import pallas as pl
from jax.experimental.pallas import tpu as pltpu
from jax.sharding import PartitionSpec as P

HALO = 2
LANES = 128
SUBLANES = 8
CHUNK = 32
GROUPS = LANES // CHUNK
core_square = 0.25
softening = 1.5
UNROLL = 8
FEW = 4
FOLD = 256
PIECES = 3
VMEM = 20 * 1024 * 1024


def split_rows(width, lanes):
    return pl.cdiv(width, lanes)


def in_hbm(count):
    return [pl.BlockSpec(memory_space=pltpu.HBM)] * count


def pinned(*arrays):
    return [pltpu.with_memory_space_constraint(x, pltpu.HBM) for x in arrays]


def start_all(sems, moves):
    copies = [
        pltpu.make_async_copy(source, target, sems.at[n])
        for n, (source, target) in enumerate(moves)
    ]
    for copy in copies:
        copy.start()
    return copies


def prepare_kernel(disp_hbm, pos_hbm, out_ref, halo_ref, disp_ref, pos_ref, sems):
    clusters, width = disp_ref.shape
    spare = halo_ref.shape[1]
    segments = split_rows(width, spare)
    copies = start_all(sems, ((disp_hbm, disp_ref), (pos_hbm, pos_ref)))
    halo_ref[...] = jnp.zeros_like(halo_ref)
    for copy in copies:
        copy.wait()
    out_ref[...] = disp_ref[...].astype(out_ref.dtype)
    row = 0
    for g in range(segments):
        size = min(spare, width - g * spare)
        for start in (0, clusters - HALO):
            for ref in (disp_ref, pos_ref):
                halo_ref[row : row + HALO, 0:size] = ref[
                    start : start + HALO, g * spare : g * spare + size
                ]
                row += HALO


def prepare(disp, pos, spare):
    clusters, width = disp.shape
    vmem = pl.BlockSpec(memory_space=pltpu.VMEM)
    return pl.pallas_call(
        prepare_kernel,
        out_shape=(
            jax.ShapeDtypeStruct((clusters, width), jnp.bfloat16),
            jax.ShapeDtypeStruct((clusters, spare), jnp.float32),
        ),
        in_specs=in_hbm(2),
        out_specs=(vmem, vmem),
        scratch_shapes=[
            pltpu.VMEM(disp.shape, disp.dtype),
            pltpu.VMEM(pos.shape, pos.dtype),
            pltpu.SemaphoreType.DMA((2,)),
        ],
        compiler_params=pltpu.CompilerParams(vmem_limit_bytes=VMEM),
        cost_estimate=pl.CostEstimate(
            flops=clusters * width, bytes_accessed=12 * clusters * width, transcendentals=0
        ),
        name="prepare",
    )(*pinned(disp, pos))


def far_kernel(
    count_hbm,
    pairs_hbm,
    gathered_hbm,
    blocks_ref,
    out_ref,
    count_ref,
    pairs_ref,
    gathered_ref,
    buffer,
    column_scr,
    coeff_scr,
    place_scr,
    sum_scr,
    summed_scr,
    halo_scr,
    sems,
    block_sems,
    *,
    segments,
):
    rank, _, slots = buffer.shape
    cols, clusters, _ = out_ref.shape
    targets = cols * clusters
    rows = gathered_ref.shape[0] // clusters
    sources = rows * clusters
    tiles = slots // FOLD

    def fetch(t):
        here = pl.ds(pl.multiple_of(t * FOLD, FOLD), FOLD)
        return pltpu.make_async_copy(
            blocks_ref.at[:, :, here], buffer.at[:, :, here], block_sems.at[t]
        )

    inputs = start_all(
        sems, ((count_hbm, count_ref), (pairs_hbm, pairs_ref), (gathered_hbm, gathered_ref))
    )
    fetch(0).start()
    summed_scr[...] = jnp.zeros_like(summed_scr)
    inputs[0].wait()
    count = count_ref[0]
    live = (count + FOLD - 1) // FOLD
    for t in range(1, tiles):

        @pl.when(t < live)
        def _(t=t):
            fetch(t).start()

    inputs[1].wait()
    inputs[2].wait()
    column_scr[...] = gathered_ref[...].astype(jnp.bfloat16)

    index = lax.broadcasted_iota(jnp.int32, (sources, slots), 0)
    pick = jnp.where(index == pairs_ref[1:2, :], 1.0, 0.0).astype(jnp.bfloat16)
    coeff = lax.dot_general(
        column_scr[...], pick, (((0,), (0,)), ((), ())), preferred_element_type=jnp.float32
    )
    coeff_scr[...] = coeff[0:rank, :]
    slot = lax.broadcasted_iota(jnp.int32, (1, slots), 1)
    wanted = jnp.where(slot < count, pairs_ref[0:1, :], -1)
    index = lax.broadcasted_iota(jnp.int32, (targets, slots), 0)
    place_scr[...] = jnp.where(index == wanted, 1.0, 0.0).astype(jnp.bfloat16)

    def multiply(t, carry):
        start = pl.multiple_of(t * FOLD, FOLD)
        lanes = pl.ds(start, FOLD)
        fetch(t).wait()
        coeff = coeff_scr[:, lanes]
        for r in range(rank):
            product = buffer[r, :, lanes].astype(jnp.float32) * coeff
            folded = product[0:SUBLANES]
            for s in range(1, rank // SUBLANES):
                folded = folded + product[s * SUBLANES : (s + 1) * SUBLANES]
            for h in range(FOLD // LANES):
                sum_scr[h, r * SUBLANES : (r + 1) * SUBLANES, :] = folded[
                    :, h * LANES : (h + 1) * LANES
                ]
        parts = []
        for h in range(FOLD // LANES):
            total = sum_scr[h, pl.ds(0, rank, stride=SUBLANES), :]
            for s in range(1, SUBLANES):
                total = total + sum_scr[h, pl.ds(s, rank, stride=SUBLANES), :]
            parts.append(total)
        coupled = jnp.concatenate(parts, axis=1)
        high = coupled.astype(jnp.bfloat16)
        low = (coupled - high.astype(jnp.float32)).astype(jnp.bfloat16)
        both = jnp.concatenate([high, low], axis=0)
        summed_scr[...] += lax.dot_general(
            place_scr[:, lanes], both, (((1,), (1,)), ((), ())), preferred_element_type=jnp.float32
        )
        return carry

    lax.fori_loop(0, live, multiply, 0)

    i = lax.axis_index("rows")
    j = lax.axis_index("cols")
    from_last = jnp.where(j < cols - 1, i, i - 1)
    from_first = jnp.where(j > 0, i, i + 1)
    edge = 2 * HALO
    halo_scr[...] = jnp.zeros_like(halo_scr)
    sides = (
        (0, jnp.minimum(from_first, rows - 1), from_first < rows),
        (edge, jnp.maximum(from_last, 0), from_last >= 0),
    )
    for side, (row, owner, there) in enumerate(sides):
        start = pl.multiple_of(owner * clusters, clusters)
        whole = jnp.where(there, gathered_ref[pl.ds(start, clusters), :], 0.0)
        for n in range(PIECES):
            piece = whole.astype(jnp.bfloat16).astype(jnp.float32)
            whole = whole - piece
            for g in range(segments):
                to = (n * segments + g) * edge
                here = g * 2 * edge + row
                halo_scr[side, to : to + edge, :] = piece[here : here + edge, :]
    after = jnp.where(j < cols - 1, j + 1, 0)
    lane = lax.broadcasted_iota(jnp.int32, (clusters, LANES), 1)
    for d in range(cols):
        halo = halo_scr[jnp.where(after == d, 1, 0)]
        mine = summed_scr[d * clusters : (d + 1) * clusters, :]
        mine = mine + pltpu.roll(mine, rank, 1)
        out_ref[d] = jnp.where(lane < rank, mine, halo).astype(out_ref.dtype)


def far_field(count, pairs, gathered, blocks, cols, segments):
    rank, _, slots = blocks.shape
    rows = lax.axis_size("rows")
    clusters = gathered.shape[0] // rows
    return pl.pallas_call(
        functools.partial(far_kernel, segments=segments),
        out_shape=jax.ShapeDtypeStruct((cols, clusters, LANES), jnp.bfloat16),
        in_specs=in_hbm(3) + [pl.BlockSpec(memory_space=pl.ANY)],
        out_specs=pl.BlockSpec(memory_space=pltpu.VMEM),
        scratch_shapes=[
            pltpu.SMEM(count.shape, count.dtype),
            pltpu.VMEM(pairs.shape, pairs.dtype),
            pltpu.VMEM(gathered.shape, gathered.dtype),
            pltpu.VMEM(blocks.shape, blocks.dtype),
            pltpu.VMEM((rows * clusters, LANES), jnp.bfloat16),
            pltpu.VMEM((rank, slots), jnp.float32),
            pltpu.VMEM((cols * clusters, slots), jnp.bfloat16),
            pltpu.VMEM((FOLD // LANES, rank * SUBLANES, LANES), jnp.float32),
            pltpu.VMEM((cols * clusters, LANES), jnp.float32),
            pltpu.VMEM((2, clusters, LANES), jnp.float32),
            pltpu.SemaphoreType.DMA((3,)),
            pltpu.SemaphoreType.DMA((slots // FOLD,)),
        ],
        compiler_params=pltpu.CompilerParams(vmem_limit_bytes=VMEM),
        cost_estimate=pl.CostEstimate(
            flops=2 * rank * rank * slots,
            bytes_accessed=2 * rank * rank * slots,
            transcendentals=0,
        ),
        name="far_field",
    )(count, *pinned(pairs), gathered, *pinned(blocks))


def replicate(rows, chunks, store, turned=False):
    within = lax.broadcasted_iota(jnp.int32, (rows.shape[0], LANES), 1)
    if turned:
        within = within + (within // CHUNK) * SUBLANES
    within = within % CHUNK
    for m in range(3 * chunks):
        tile = m // GROUPS
        store(
            m,
            jnp.take_along_axis(
                rows[:, tile * LANES : (tile + 1) * LANES],
                within + (m % GROUPS) * CHUNK,
                axis=1,
                mode="promise_in_bounds",
            ),
        )


def row_of(ref, n, row):
    return ref[n, pl.ds(row, SUBLANES, stride=0), :]


def turn(wide):
    return pltpu.roll(wide, 0, 1, stride=1, stride_axis=0)


def pair_sums(tgt, src, chunks):
    sums = [None] * (3 * chunks)
    size = 3 * chunks
    for f in range(chunks):
        y = [src(c * chunks + f) for c in range(3)]
        u = [src(size + c * chunks + f) for c in range(3)]
        v = [3.0 * x for x in u]
        for h in range(chunks):
            r = [tgt[c * chunks + h] - y[c] for c in range(3)]
            q = (r[0] * r[0] + core_square) + (r[1] * r[1] + r[2] * r[2])
            s = r[0] * v[0] + (r[1] * v[1] + r[2] * v[2])
            inverse = lax.rsqrt(q)
            square = inverse * inverse
            weight = square * inverse
            s = s * square
            for c in range(3):
                term = weight * (u[c] - s * r[c])
                m = c * chunks + h
                sums[m] = term if sums[m] is None else sums[m] + term
    return sums


def gather_sums(acc_scr, clusters, chunks, store):
    own_group = lax.broadcasted_iota(jnp.int32, (clusters, LANES), 1) // CHUNK
    for t in range(pl.cdiv(3 * chunks, GROUPS)):
        merged = None
        for g in range(GROUPS):
            m = t * GROUPS + g
            if m >= 3 * chunks:
                break
            total = acc_scr[m, pl.ds(0, clusters, stride=SUBLANES), :]
            for s in range(1, SUBLANES):
                total = total + acc_scr[m, pl.ds(s, clusters, stride=SUBLANES), :]
            total = total + pltpu.roll(total, 2 * CHUNK, 1)
            total = total + pltpu.roll(total, CHUNK, 1)
            merged = total if merged is None else jnp.where(own_group == g, total, merged)
        store(t, merged)


def turn_matrix():
    shape = (PIECES * CHUNK, SUBLANES * LANES)
    column = lax.broadcasted_iota(jnp.int32, shape, 1)
    lane = column % LANES
    entry = (lane + (lane // CHUNK) * SUBLANES + column // LANES) % CHUNK
    row = lax.broadcasted_iota(jnp.int32, shape, 0) % CHUNK
    return jnp.where(entry == row, 1.0, 0.0).astype(jnp.bfloat16)


def exact_pieces(value):
    pieces = []
    for _ in range(PIECES):
        piece = value.astype(jnp.bfloat16)
        pieces.append(piece)
        value = value - piece.astype(jnp.float32)
    return pieces


def near_kernel(
    pairs_hbm,
    count_hbm,
    disp_hbm,
    pos_hbm,
    intact_hbm,
    stiff_hbm,
    out_hbm,
    damage_hbm,
    rest_hbm,
    pairs_ref,
    count_ref,
    disp_ref,
    pos_ref,
    intact_ref,
    stiff_ref,
    out_ref,
    damage_ref,
    rest_ref,
    plan_ref,
    plan_smem,
    wide_scr,
    piece_scr,
    turn_scr,
    tgt_scr,
    src_scr,
    acc_scr,
    sems,
    out_sems,
    plan_sem,
):
    clusters, width = disp_ref.shape
    elems = width // 3
    chunks = elems // CHUNK
    size = 3 * chunks
    slots = pairs_ref.shape[1]

    inputs = start_all(
        sems,
        (
            (pos_hbm, pos_ref),
            (disp_hbm, disp_ref),
            (pairs_hbm, pairs_ref),
            (count_hbm, count_ref),
            (intact_hbm, intact_ref),
            (stiff_hbm, stiff_ref),
        ),
    )
    acc_scr[...] = jnp.zeros_like(acc_scr)
    turn_scr[...] = turn_matrix()
    for copy in inputs[2:4]:
        copy.wait()
    count = count_ref[0]

    target = pairs_ref[0:1, :]
    source = pairs_ref[1:2, :]
    live = lax.broadcasted_iota(jnp.int32, (1, slots), 1) < count
    own = jnp.logical_and(source >= HALO, source < clusters + HALO)
    plan_ref[0:1, :] = target
    plan_ref[1:2, :] = jnp.clip(source - HALO, 0, clusters - 1)
    plan_ref[2:3, :] = jnp.where(jnp.logical_and(live, own), target, clusters) * SUBLANES
    plan = pltpu.make_async_copy(plan_ref, plan_smem, plan_sem)
    plan.start()

    others = jnp.where(jnp.logical_and(live, jnp.logical_not(own)), 1.0, 0.0)
    square = (slots, slots)
    upto = lax.broadcasted_iota(jnp.int32, square, 0) <= lax.broadcasted_iota(jnp.int32, square, 1)
    upto = jnp.where(upto, 1.0, 0.0).astype(jnp.bfloat16)
    order = jnp.dot(
        jnp.broadcast_to(others, (SUBLANES, slots)).astype(jnp.bfloat16),
        upto,
        preferred_element_type=jnp.float32,
    )
    place = jnp.where(others > 0.0, order[0:1, :] - 1.0, -1.0).astype(jnp.int32)
    place = lax.broadcasted_iota(jnp.int32, square, 0) == place
    place = jnp.where(place, 1.0, 0.0).astype(jnp.bfloat16)
    row = lax.broadcasted_iota(jnp.int32, (SUBLANES, slots), 0)
    listed = jnp.where(row == 0, target, source).astype(jnp.float32).astype(jnp.bfloat16)
    listed = lax.dot_general(
        listed, place, (((1,), (1,)), ((), ())), preferred_element_type=jnp.float32
    )
    number = jnp.sum(others, axis=1, keepdims=True)
    rest_ref[...] = jnp.where(row < 2, listed, number).astype(jnp.int32)
    rest_out = pltpu.make_async_copy(rest_ref, rest_hbm, out_sems.at[1])
    rest_out.start()

    for k, values in enumerate((pos_ref, disp_ref)):
        inputs[k].wait()
        wide_scr[k, :, 0:width] = values[...]
        for m in range(size):
            pieces = exact_pieces(values[:, m * CHUNK : (m + 1) * CHUNK])
            piece_scr[(k * size + m) * clusters : (k * size + m + 1) * clusters, :] = (
                jnp.concatenate(pieces, axis=1)
            )
    columns = 2 * LANES
    for t in range(SUBLANES * LANES // columns):
        for k in range(2):
            rows = size * clusters
            turned = jnp.dot(
                piece_scr[k * rows : (k + 1) * rows, :],
                turn_scr[:, t * columns : (t + 1) * columns],
                preferred_element_type=jnp.float32,
            )
            for m in range(size):
                for h in range(columns // LANES):
                    s = t * (columns // LANES) + h
                    src_scr[k * size + m, pl.ds(s, clusters, stride=SUBLANES), :] = turned[
                        m * clusters : (m + 1) * clusters, h * LANES : (h + 1) * LANES
                    ]

    def store_target(m, value):
        tgt_scr[m] = value

    replicate(wide_scr[0], chunks, store_target)
    for copy in inputs[4:]:
        copy.wait()

    disp = [disp_ref[:, c * elems : (c + 1) * elems] for c in range(3)]
    separation = jnp.sqrt(1.0 + (disp[0] * disp[0] + disp[1] * disp[1] + disp[2] * disp[2]))
    softened = 1.0 - jnp.exp(-(separation - 1.0) / softening)
    intact = intact_ref[...].astype(jnp.float32)
    damage = intact * softened + (1.0 - intact)
    damage_ref[...] = damage
    damage_out = pltpu.make_async_copy(damage_ref, damage_hbm, out_sems.at[0])
    damage_out.start()
    hold = (1.0 - damage) * stiff_ref[...]
    for c in range(3):
        out_ref[:, c * elems : (c + 1) * elems] = -hold * disp[c]
    plan.wait()

    def one_pair(slot):
        target = plan_smem[0, slot]
        source = pl.multiple_of(plan_smem[1, slot] * SUBLANES, SUBLANES)
        into = pl.multiple_of(plan_smem[2, slot], SUBLANES)
        tgt = [row_of(tgt_scr, m, target) for m in range(size)]
        sums = pair_sums(tgt, lambda n: src_scr[n, pl.ds(source, SUBLANES), :], chunks)
        for m in range(size):
            acc_scr[m, pl.ds(into, SUBLANES), :] += sums[m]

    def step(it, carry):
        for k in range(UNROLL):
            one_pair(it * UNROLL + k)
        return carry

    lax.fori_loop(0, (count + UNROLL - 1) // UNROLL, step, 0)

    def store_sum(t, value):
        wide_scr[0, :, t * LANES : (t + 1) * LANES] = value

    gather_sums(acc_scr, clusters, chunks, store_sum)
    out_ref[...] += wide_scr[0, :, 0:width]
    near_out = pltpu.make_async_copy(out_ref, out_hbm, out_sems.at[2])
    near_out.start()
    for copy in (damage_out, rest_out, near_out):
        copy.wait()


def near_field(pairs, count, disp, pos, intact, stiffness):
    clusters, width = disp.shape
    elems = width // 3
    chunks = elems // CHUNK
    padded = pl.cdiv(width, LANES) * LANES
    slots = pairs.shape[1]
    return pl.pallas_call(
        near_kernel,
        out_shape=(
            jax.ShapeDtypeStruct((clusters, width), jnp.float32),
            jax.ShapeDtypeStruct((clusters, elems), jnp.float32),
            jax.ShapeDtypeStruct((SUBLANES, slots), jnp.int32),
        ),
        in_specs=in_hbm(6),
        out_specs=tuple(in_hbm(3)),
        scratch_shapes=[
            pltpu.VMEM(pairs.shape, pairs.dtype),
            pltpu.SMEM(count.shape, count.dtype),
            pltpu.VMEM(disp.shape, disp.dtype),
            pltpu.VMEM(pos.shape, pos.dtype),
            pltpu.VMEM(intact.shape, intact.dtype),
            pltpu.VMEM(stiffness.shape, stiffness.dtype),
            pltpu.VMEM((clusters, width), jnp.float32),
            pltpu.VMEM((clusters, elems), jnp.float32),
            pltpu.VMEM((SUBLANES, slots), jnp.int32),
            pltpu.VMEM((SUBLANES, slots), jnp.int32),
            pltpu.SMEM((SUBLANES, slots), jnp.int32),
            pltpu.VMEM((2, clusters, padded), jnp.float32),
            pltpu.VMEM((6 * chunks * clusters, PIECES * CHUNK), jnp.bfloat16),
            pltpu.VMEM((PIECES * CHUNK, SUBLANES * LANES), jnp.bfloat16),
            pltpu.VMEM((3 * chunks, clusters, LANES), jnp.float32),
            pltpu.VMEM((6 * chunks, clusters * SUBLANES, LANES), jnp.float32),
            pltpu.VMEM((3 * chunks, (clusters + 1) * SUBLANES, LANES), jnp.float32),
            pltpu.SemaphoreType.DMA((6,)),
            pltpu.SemaphoreType.DMA((3,)),
            pltpu.SemaphoreType.DMA(()),
        ],
        compiler_params=pltpu.CompilerParams(vmem_limit_bytes=VMEM),
        cost_estimate=pl.CostEstimate(
            flops=30 * slots * elems * elems,
            bytes_accessed=4 * clusters * width * 6,
            transcendentals=slots * elems * elems,
        ),
        name="near_field",
    )(*pinned(pairs), count, *pinned(disp, pos, intact, stiffness))


def finish_kernel(
    rest_hbm,
    pos_hbm,
    received_ref,
    near_ref,
    far_ref,
    out_ref,
    rest_ref,
    pos_ref,
    ext_scr,
    halo_scr,
    tgt_scr,
    src_scr,
    acc_scr,
    sems,
    *,
    rank,
):
    clusters, width = near_ref.shape
    cols = received_ref.shape[0]
    elems = width // 3
    chunks = elems // CHUNK
    size = 3 * chunks
    spare = LANES - rank
    segments = split_rows(width, spare)
    edge = 2 * HALO
    tail = pl.ds(clusters - SUBLANES, SUBLANES)

    inputs = start_all(
        sems,
        (
            (rest_hbm, rest_ref),
            (pos_hbm.at[pl.ds(0, SUBLANES)], pos_ref.at[0]),
            (pos_hbm.at[tail], pos_ref.at[1]),
        ),
    )
    acc_scr[...] = jnp.zeros_like(acc_scr)

    j = lax.axis_index("cols")
    before = jnp.where(j > 0, j - 1, cols - 1)
    after = jnp.where(j < cols - 1, j + 1, 0)
    for start, sender in ((0, before), (HALO, after)):
        halo_scr[...] = received_ref[sender].astype(jnp.float32)
        rows = edge * segments
        whole = halo_scr[0:rows, :]
        for n in range(1, PIECES):
            whole = whole + halo_scr[n * rows : (n + 1) * rows, :]
        for g in range(segments):
            count = min(spare, width - g * spare)
            for k in range(2):
                row = (2 * g + k) * HALO
                ext_scr[k, start : start + HALO, g * spare : g * spare + count] = whole[
                    row : row + HALO, rank : rank + count
                ]
    inputs[1].wait()
    inputs[2].wait()
    ext_scr[1, edge : edge + HALO, 0:width] = pos_ref[0, 0:HALO, :]
    ext_scr[1, edge + HALO : 2 * edge, 0:width] = pos_ref[1, SUBLANES - HALO :, :]
    for k in range(2):

        def store(m, value, k=k):
            for b in range(edge):
                wide = jnp.broadcast_to(value[b : b + 1, :], (SUBLANES, LANES))
                src_scr[(1 - k) * size + m, b * SUBLANES : (b + 1) * SUBLANES, :] = turn(wide)

        replicate(ext_scr[k], chunks, store, True)

    def store_target(m, value):
        tgt_scr[m] = value

    replicate(ext_scr[1], chunks, store_target)
    inputs[0].wait()
    number = rest_ref[2, 0]

    def one_pair(n):
        target = rest_ref[0, n]
        source = rest_ref[1, n]
        target = jnp.where(target < HALO, target, target - (clusters - edge))
        source = jnp.where(source < HALO, source, source - clusters)
        live = n < number
        target = jnp.where(live, target, edge)
        source = pl.multiple_of(jnp.where(live, source, 0) * SUBLANES, SUBLANES)
        into = pl.multiple_of(target * SUBLANES, SUBLANES)
        row = edge + jnp.where(live, target, 0)
        tgt = [row_of(tgt_scr, m, row) for m in range(size)]
        sums = pair_sums(tgt, lambda k: src_scr[k, pl.ds(source, SUBLANES), :], chunks)
        for m in range(size):
            acc_scr[m, pl.ds(into, SUBLANES), :] += sums[m]

    def step(it, carry):
        for k in range(FEW):
            one_pair(it * FEW + k)
        return carry

    lax.fori_loop(0, (number + FEW - 1) // FEW, step, 0)

    def store_sum(t, value):
        ext_scr[0, :, t * LANES : (t + 1) * LANES] = value

    gather_sums(acc_scr, 2 * edge, chunks, store_sum)
    out_ref[...] = near_ref[...] + far_ref[...]
    out_ref[0:HALO, :] += ext_scr[0, 0:HALO, 0:width]
    out_ref[clusters - HALO :, :] += ext_scr[0, HALO:edge, 0:width]


def finish(rest, pos, received, near, far, rank):
    clusters, width = pos.shape
    chunks = width // 3 // CHUNK
    padded = pl.cdiv(width, LANES) * LANES
    edge = 2 * HALO
    vmem = pl.BlockSpec(memory_space=pltpu.VMEM)
    return pl.pallas_call(
        functools.partial(finish_kernel, rank=rank),
        out_shape=jax.ShapeDtypeStruct((clusters, width), jnp.float32),
        in_specs=in_hbm(2) + [vmem] * 3,
        out_specs=vmem,
        scratch_shapes=[
            pltpu.SMEM(rest.shape, rest.dtype),
            pltpu.VMEM((2, SUBLANES, width), pos.dtype),
            pltpu.VMEM((2, 2 * edge, padded), jnp.float32),
            pltpu.VMEM((clusters, LANES), jnp.float32),
            pltpu.VMEM((3 * chunks, 2 * edge, LANES), jnp.float32),
            pltpu.VMEM((6 * chunks, edge * SUBLANES, LANES), jnp.float32),
            pltpu.VMEM((3 * chunks, 2 * edge * SUBLANES, LANES), jnp.float32),
            pltpu.SemaphoreType.DMA((3,)),
        ],
        compiler_params=pltpu.CompilerParams(vmem_limit_bytes=VMEM),
        cost_estimate=pl.CostEstimate(
            flops=2 * clusters * width, bytes_accessed=16 * clusters * width, transcendentals=0
        ),
        name="finish",
    )(rest, *pinned(pos), received, near, far)


def local(
    displacement,
    positions,
    cluster_basis,
    near_pairs,
    near_count,
    far_pairs,
    far_count,
    far_blocks,
    intact,
    stiffness,
):
    cols = lax.axis_size("cols")
    clusters, width, rank = cluster_basis.shape
    spare = LANES - rank
    segments = split_rows(width, spare)
    disp_bf, halo = prepare(displacement, positions, spare)
    coeff = jnp.einsum("kf,kfr->kr", disp_bf, cluster_basis, preferred_element_type=jnp.float32)
    payload = jnp.concatenate([coeff, halo], axis=1)
    gathered = lax.all_gather(payload, "rows", axis=0, tiled=True)
    partial = far_field(
        far_count, far_pairs.T, gathered, far_blocks.transpose(1, 2, 0), cols, segments
    )
    received = lax.all_to_all(partial, "cols", split_axis=0, concat_axis=0)
    near, damage, rest = near_field(
        near_pairs.T, near_count, displacement, positions, intact, stiffness
    )
    owned = jnp.sum(received[:, :, :rank].astype(jnp.float32), axis=0).astype(jnp.bfloat16)
    far = jnp.einsum("kfr,kr->kf", cluster_basis, owned, preferred_element_type=jnp.float32)
    return finish(rest, positions, received, near, far, rank), damage


def solution(mesh):
    both = ("rows", "cols")
    in_specs = (
        P(both, None),
        P(both, None),
        P(both, None, None),
        P(both, None),
        P(both),
        P(both, None),
        P(both),
        P(both, None, None),
        P(both, None),
        P(both, None),
    )
    out_specs = (P(both, None), P(both, None))
    return jax.shard_map(local, mesh=mesh, in_specs=in_specs, out_specs=out_specs, check_vma=False)
```

```python
import functools

import jax
import jax.numpy as jnp
from jax import lax
from jax.experimental import pallas as pl
from jax.experimental.pallas import tpu as pltpu
from jax.sharding import PartitionSpec as P

HALO = 2
LANES = 128
SUBLANES = 8
CHUNK = 32
GROUPS = LANES // CHUNK
core_square = 0.25
softening = 1.5
UNROLL = 8
FEW = 4
FOLD = 256
PIECES = 3
VMEM = 20 * 1024 * 1024


def split_rows(width, lanes):
    return pl.cdiv(width, lanes)


def in_hbm(count):
    return [pl.BlockSpec(memory_space=pltpu.HBM)] * count


def pinned(*arrays):
    return [pltpu.with_memory_space_constraint(x, pltpu.HBM) for x in arrays]


def start_all(sems, moves):
    copies = [
        pltpu.make_async_copy(source, target, sems.at[n])
        for n, (source, target) in enumerate(moves)
    ]
    for copy in copies:
        copy.start()
    return copies


def prepare_kernel(
    near_count_ref,
    far_count_ref,
    pairs_hbm,
    disp_hbm,
    pos_hbm,
    intact_hbm,
    stiff_hbm,
    low_ref,
    halo_ref,
    disp_ref,
    pos_ref,
    base_ref,
    damage_ref,
    list_ref,
    pairs_ref,
    intact_ref,
    stiff_ref,
    sems,
):
    clusters, width = disp_ref.shape
    elems = width // 3
    spare = halo_ref.shape[1]
    segments = split_rows(width, spare)
    inputs = start_all(
        sems,
        (
            (pairs_hbm, pairs_ref),
            (disp_hbm, disp_ref),
            (pos_hbm, pos_ref),
            (intact_hbm, intact_ref),
            (stiff_hbm, stiff_ref),
        ),
    )
    halo_ref[...] = jnp.zeros_like(halo_ref)
    for copy in inputs:
        copy.wait()
    list_pairs(pairs_ref, near_count_ref[0], far_count_ref[0], list_ref, clusters)
    low_ref[...] = disp_ref[...].astype(low_ref.dtype)
    row = 0
    for g in range(segments):
        size = min(spare, width - g * spare)
        for start in (0, clusters - HALO):
            for ref in (disp_ref, pos_ref):
                halo_ref[row : row + HALO, 0:size] = ref[
                    start : start + HALO, g * spare : g * spare + size
                ]
                row += HALO

    disp = [disp_ref[:, c * elems : (c + 1) * elems] for c in range(3)]
    separation = jnp.sqrt(1.0 + (disp[0] * disp[0] + disp[1] * disp[1] + disp[2] * disp[2]))
    softened = 1.0 - jnp.exp(-(separation - 1.0) / softening)
    intact = intact_ref[...].astype(jnp.float32)
    damage = intact * softened + (1.0 - intact)
    damage_ref[...] = damage
    hold = (1.0 - damage) * stiff_ref[...]
    for c in range(3):
        base_ref[:, c * elems : (c + 1) * elems] = -hold * disp[c]


def list_pairs(pairs_ref, near_count, far_count, list_ref, clusters):
    slots = pairs_ref.shape[1]
    target = pairs_ref[0:1, :]
    source = pairs_ref[1:2, :]
    live = lax.broadcasted_iota(jnp.int32, (1, slots), 1) < near_count
    own = jnp.logical_and(source >= HALO, source < clusters + HALO)
    list_ref[0:1, :] = target
    list_ref[1:2, :] = jnp.clip(source - HALO, 0, clusters - 1)
    list_ref[2:3, :] = jnp.where(jnp.logical_and(live, own), target, clusters) * SUBLANES
    list_ref[3:4, :] = jnp.full((1, slots), near_count, jnp.int32)
    others = jnp.where(jnp.logical_and(live, jnp.logical_not(own)), 1.0, 0.0)
    square = (slots, slots)
    upto = lax.broadcasted_iota(jnp.int32, square, 0) <= lax.broadcasted_iota(jnp.int32, square, 1)
    upto = jnp.where(upto, 1.0, 0.0).astype(jnp.bfloat16)
    order = jnp.dot(
        jnp.broadcast_to(others, (SUBLANES, slots)).astype(jnp.bfloat16),
        upto,
        preferred_element_type=jnp.float32,
    )
    place = jnp.where(others > 0.0, order[0:1, :] - 1.0, -1.0).astype(jnp.int32)
    place = lax.broadcasted_iota(jnp.int32, square, 0) == place
    place = jnp.where(place, 1.0, 0.0).astype(jnp.bfloat16)
    row = lax.broadcasted_iota(jnp.int32, (SUBLANES, slots), 0)
    listed = jnp.where(row == 0, target, source).astype(jnp.float32).astype(jnp.bfloat16)
    listed = lax.dot_general(
        listed, place, (((1,), (1,)), ((), ())), preferred_element_type=jnp.float32
    ).astype(jnp.int32)
    list_ref[4:6, :] = listed[0:2, :]
    number = jnp.sum(others, axis=1, keepdims=True).astype(jnp.int32)
    list_ref[6:7, :] = jnp.broadcast_to(number, (1, slots))
    list_ref[7:8, :] = jnp.full((1, slots), far_count, jnp.int32)


def prepare(near_count, far_count, pairs, disp, pos, intact, stiffness, spare):
    clusters, width = disp.shape
    slots = pairs.shape[1]
    vmem = pl.BlockSpec(memory_space=pltpu.VMEM)
    smem = pl.BlockSpec(memory_space=pltpu.SMEM)
    return pl.pallas_call(
        prepare_kernel,
        out_shape=(
            jax.ShapeDtypeStruct((clusters, width), jnp.bfloat16),
            jax.ShapeDtypeStruct((clusters, spare), jnp.float32),
            jax.ShapeDtypeStruct((clusters, width), jnp.float32),
            jax.ShapeDtypeStruct((clusters, width), jnp.float32),
            jax.ShapeDtypeStruct((clusters, width), jnp.float32),
            jax.ShapeDtypeStruct(stiffness.shape, jnp.float32),
            jax.ShapeDtypeStruct((SUBLANES, slots), jnp.int32),
        ),
        in_specs=[smem] * 2 + in_hbm(5),
        out_specs=(vmem,) * 7,
        scratch_shapes=[
            pltpu.VMEM(pairs.shape, pairs.dtype),
            pltpu.VMEM(intact.shape, intact.dtype),
            pltpu.VMEM(stiffness.shape, stiffness.dtype),
            pltpu.SemaphoreType.DMA((5,)),
        ],
        compiler_params=pltpu.CompilerParams(vmem_limit_bytes=VMEM),
        cost_estimate=pl.CostEstimate(
            flops=20 * clusters * width, bytes_accessed=24 * clusters * width, transcendentals=0
        ),
        name="prepare",
    )(near_count, far_count, *pinned(pairs, disp, pos, intact, stiffness))


def far_kernel(
    list_hbm,
    pairs_hbm,
    gathered_hbm,
    blocks_ref,
    out_ref,
    list_ref,
    pairs_ref,
    gathered_ref,
    buffer,
    column_scr,
    coeff_scr,
    place_scr,
    sum_scr,
    summed_scr,
    halo_scr,
    sems,
    block_sems,
    *,
    segments,
):
    rank, _, slots = buffer.shape
    cols, clusters, _ = out_ref.shape
    targets = cols * clusters
    rows = gathered_ref.shape[0] // clusters
    sources = rows * clusters
    tiles = slots // FOLD

    def fetch(t):
        here = pl.ds(pl.multiple_of(t * FOLD, FOLD), FOLD)
        return pltpu.make_async_copy(
            blocks_ref.at[:, :, here], buffer.at[:, :, here], block_sems.at[t]
        )

    inputs = start_all(
        sems, ((list_hbm, list_ref), (pairs_hbm, pairs_ref), (gathered_hbm, gathered_ref))
    )
    fetch(0).start()
    summed_scr[...] = jnp.zeros_like(summed_scr)
    inputs[0].wait()
    count = list_ref[7, 0]
    live = (count + FOLD - 1) // FOLD
    for t in range(1, tiles):

        @pl.when(t < live)
        def _(t=t):
            fetch(t).start()

    inputs[1].wait()
    inputs[2].wait()
    column_scr[...] = gathered_ref[...].astype(jnp.bfloat16)

    index = lax.broadcasted_iota(jnp.int32, (sources, slots), 0)
    pick = jnp.where(index == pairs_ref[1:2, :], 1.0, 0.0).astype(jnp.bfloat16)
    coeff = lax.dot_general(
        column_scr[...], pick, (((0,), (0,)), ((), ())), preferred_element_type=jnp.float32
    )
    coeff_scr[...] = coeff[0:rank, :]
    slot = lax.broadcasted_iota(jnp.int32, (1, slots), 1)
    wanted = jnp.where(slot < count, pairs_ref[0:1, :], -1)
    index = lax.broadcasted_iota(jnp.int32, (targets, slots), 0)
    place_scr[...] = jnp.where(index == wanted, 1.0, 0.0).astype(jnp.bfloat16)

    def multiply(t, carry):
        start = pl.multiple_of(t * FOLD, FOLD)
        lanes = pl.ds(start, FOLD)
        fetch(t).wait()
        coeff = coeff_scr[:, lanes]
        for r in range(rank):
            product = buffer[r, :, lanes].astype(jnp.float32) * coeff
            folded = product[0:SUBLANES]
            for s in range(1, rank // SUBLANES):
                folded = folded + product[s * SUBLANES : (s + 1) * SUBLANES]
            for h in range(FOLD // LANES):
                sum_scr[h, r * SUBLANES : (r + 1) * SUBLANES, :] = folded[
                    :, h * LANES : (h + 1) * LANES
                ]
        parts = []
        for h in range(FOLD // LANES):
            total = sum_scr[h, pl.ds(0, rank, stride=SUBLANES), :]
            for s in range(1, SUBLANES):
                total = total + sum_scr[h, pl.ds(s, rank, stride=SUBLANES), :]
            parts.append(total)
        coupled = jnp.concatenate(parts, axis=1)
        high = coupled.astype(jnp.bfloat16)
        low = (coupled - high.astype(jnp.float32)).astype(jnp.bfloat16)
        both = jnp.concatenate([high, low], axis=0)
        summed_scr[...] += lax.dot_general(
            place_scr[:, lanes], both, (((1,), (1,)), ((), ())), preferred_element_type=jnp.float32
        )
        return carry

    lax.fori_loop(0, live, multiply, 0)

    i = lax.axis_index("rows")
    j = lax.axis_index("cols")
    from_last = jnp.where(j < cols - 1, i, i - 1)
    from_first = jnp.where(j > 0, i, i + 1)
    edge = 2 * HALO
    halo_scr[...] = jnp.zeros_like(halo_scr)
    sides = (
        (0, jnp.minimum(from_first, rows - 1), from_first < rows),
        (edge, jnp.maximum(from_last, 0), from_last >= 0),
    )
    for side, (row, owner, there) in enumerate(sides):
        start = pl.multiple_of(owner * clusters, clusters)
        whole = jnp.where(there, gathered_ref[pl.ds(start, clusters), :], 0.0)
        for n in range(PIECES):
            piece = whole.astype(jnp.bfloat16).astype(jnp.float32)
            whole = whole - piece
            for g in range(segments):
                to = (n * segments + g) * edge
                here = g * 2 * edge + row
                halo_scr[side, to : to + edge, :] = piece[here : here + edge, :]
    after = jnp.where(j < cols - 1, j + 1, 0)
    lane = lax.broadcasted_iota(jnp.int32, (clusters, LANES), 1)
    for d in range(cols):
        halo = halo_scr[jnp.where(after == d, 1, 0)]
        mine = summed_scr[d * clusters : (d + 1) * clusters, :]
        mine = mine + pltpu.roll(mine, rank, 1)
        out_ref[d] = jnp.where(lane < rank, mine, halo).astype(out_ref.dtype)


def far_field(listed, pairs, gathered, blocks, cols, segments):
    rank, _, slots = blocks.shape
    rows = lax.axis_size("rows")
    clusters = gathered.shape[0] // rows
    return pl.pallas_call(
        functools.partial(far_kernel, segments=segments),
        out_shape=jax.ShapeDtypeStruct((cols, clusters, LANES), jnp.bfloat16),
        in_specs=in_hbm(3) + [pl.BlockSpec(memory_space=pl.ANY)],
        out_specs=pl.BlockSpec(memory_space=pltpu.VMEM),
        scratch_shapes=[
            pltpu.SMEM(listed.shape, listed.dtype),
            pltpu.VMEM(pairs.shape, pairs.dtype),
            pltpu.VMEM(gathered.shape, gathered.dtype),
            pltpu.VMEM(blocks.shape, blocks.dtype),
            pltpu.VMEM((rows * clusters, LANES), jnp.bfloat16),
            pltpu.VMEM((rank, slots), jnp.float32),
            pltpu.VMEM((cols * clusters, slots), jnp.bfloat16),
            pltpu.VMEM((FOLD // LANES, rank * SUBLANES, LANES), jnp.float32),
            pltpu.VMEM((cols * clusters, LANES), jnp.float32),
            pltpu.VMEM((2, clusters, LANES), jnp.float32),
            pltpu.SemaphoreType.DMA((3,)),
            pltpu.SemaphoreType.DMA((slots // FOLD,)),
        ],
        compiler_params=pltpu.CompilerParams(vmem_limit_bytes=VMEM),
        cost_estimate=pl.CostEstimate(
            flops=2 * rank * rank * slots,
            bytes_accessed=2 * rank * rank * slots,
            transcendentals=0,
        ),
        name="far_field",
    )(listed, *pinned(pairs), gathered, *pinned(blocks))


def replicate(rows, chunks, store, turned=False):
    within = lax.broadcasted_iota(jnp.int32, (rows.shape[0], LANES), 1)
    if turned:
        within = within + (within // CHUNK) * SUBLANES
    within = within % CHUNK
    for m in range(3 * chunks):
        tile = m // GROUPS
        store(
            m,
            jnp.take_along_axis(
                rows[:, tile * LANES : (tile + 1) * LANES],
                within + (m % GROUPS) * CHUNK,
                axis=1,
                mode="promise_in_bounds",
            ),
        )


def row_of(ref, n, row):
    return ref[n, pl.ds(row, SUBLANES, stride=0), :]


def turn(wide):
    return pltpu.roll(wide, 0, 1, stride=1, stride_axis=0)


def pair_sums(tgt, src, chunks):
    sums = [None] * (3 * chunks)
    size = 3 * chunks
    for f in range(chunks):
        y = [src(c * chunks + f) for c in range(3)]
        u = [src(size + c * chunks + f) for c in range(3)]
        v = [3.0 * x for x in u]
        for h in range(chunks):
            r = [tgt[c * chunks + h] - y[c] for c in range(3)]
            q = (r[0] * r[0] + core_square) + (r[1] * r[1] + r[2] * r[2])
            s = r[0] * v[0] + (r[1] * v[1] + r[2] * v[2])
            inverse = lax.rsqrt(q)
            square = inverse * inverse
            weight = square * inverse
            s = s * square
            for c in range(3):
                term = weight * (u[c] - s * r[c])
                m = c * chunks + h
                sums[m] = term if sums[m] is None else sums[m] + term
    return sums


def gather_sums(acc_scr, clusters, chunks, store):
    own_group = lax.broadcasted_iota(jnp.int32, (clusters, LANES), 1) // CHUNK
    for t in range(pl.cdiv(3 * chunks, GROUPS)):
        merged = None
        for g in range(GROUPS):
            m = t * GROUPS + g
            if m >= 3 * chunks:
                break
            total = acc_scr[m, pl.ds(0, clusters, stride=SUBLANES), :]
            for s in range(1, SUBLANES):
                total = total + acc_scr[m, pl.ds(s, clusters, stride=SUBLANES), :]
            total = total + pltpu.roll(total, 2 * CHUNK, 1)
            total = total + pltpu.roll(total, CHUNK, 1)
            merged = total if merged is None else jnp.where(own_group == g, total, merged)
        store(t, merged)


def turn_matrix():
    shape = (PIECES * CHUNK, SUBLANES * LANES)
    column = lax.broadcasted_iota(jnp.int32, shape, 1)
    lane = column % LANES
    entry = (lane + (lane // CHUNK) * SUBLANES + column // LANES) % CHUNK
    row = lax.broadcasted_iota(jnp.int32, shape, 0) % CHUNK
    return jnp.where(entry == row, 1.0, 0.0).astype(jnp.bfloat16)


def exact_pieces(value):
    pieces = []
    for _ in range(PIECES):
        piece = value.astype(jnp.bfloat16)
        pieces.append(piece)
        value = value - piece.astype(jnp.float32)
    return pieces


def near_kernel(
    list_hbm,
    disp_ref,
    pos_ref,
    base_ref,
    damage_ref,
    out_ref,
    damage_hbm,
    list_ref,
    wide_scr,
    piece_scr,
    turn_scr,
    tgt_scr,
    src_scr,
    acc_scr,
    sems,
):
    clusters, width = disp_ref.shape
    elems = width // 3
    chunks = elems // CHUNK
    size = 3 * chunks

    moves = start_all(sems, ((list_hbm, list_ref), (damage_ref, damage_hbm)))
    acc_scr[...] = jnp.zeros_like(acc_scr)
    turn_scr[...] = turn_matrix()

    for k, values in enumerate((pos_ref, disp_ref)):
        wide_scr[k, :, 0:width] = values[...]
        for m in range(size):
            pieces = exact_pieces(values[:, m * CHUNK : (m + 1) * CHUNK])
            piece_scr[(k * size + m) * clusters : (k * size + m + 1) * clusters, :] = (
                jnp.concatenate(pieces, axis=1)
            )
    columns = 2 * LANES
    for t in range(SUBLANES * LANES // columns):
        for k in range(2):
            rows = size * clusters
            turned = jnp.dot(
                piece_scr[k * rows : (k + 1) * rows, :],
                turn_scr[:, t * columns : (t + 1) * columns],
                preferred_element_type=jnp.float32,
            )
            for m in range(size):
                for h in range(columns // LANES):
                    s = t * (columns // LANES) + h
                    src_scr[k * size + m, pl.ds(s, clusters, stride=SUBLANES), :] = turned[
                        m * clusters : (m + 1) * clusters, h * LANES : (h + 1) * LANES
                    ]

    def store_target(m, value):
        tgt_scr[m] = value

    replicate(wide_scr[0], chunks, store_target)
    moves[0].wait()
    count = list_ref[3, 0]

    def one_pair(slot):
        target = list_ref[0, slot]
        source = pl.multiple_of(list_ref[1, slot] * SUBLANES, SUBLANES)
        into = pl.multiple_of(list_ref[2, slot], SUBLANES)
        tgt = [row_of(tgt_scr, m, target) for m in range(size)]
        sums = pair_sums(tgt, lambda n: src_scr[n, pl.ds(source, SUBLANES), :], chunks)
        for m in range(size):
            acc_scr[m, pl.ds(into, SUBLANES), :] += sums[m]

    def step(it, carry):
        for k in range(UNROLL):
            one_pair(it * UNROLL + k)
        return carry

    lax.fori_loop(0, (count + UNROLL - 1) // UNROLL, step, 0)

    def store_sum(t, value):
        wide_scr[0, :, t * LANES : (t + 1) * LANES] = value

    gather_sums(acc_scr, clusters, chunks, store_sum)
    out_ref[...] = base_ref[...] + wide_scr[0, :, 0:width]
    moves[1].wait()


def near_field(listed, disp, pos, base, damage):
    clusters, width = disp.shape
    elems = width // 3
    chunks = elems // CHUNK
    padded = pl.cdiv(width, LANES) * LANES
    slots = listed.shape[1]
    vmem = pl.BlockSpec(memory_space=pltpu.VMEM)
    return pl.pallas_call(
        near_kernel,
        out_shape=(
            jax.ShapeDtypeStruct((clusters, width), jnp.float32),
            jax.ShapeDtypeStruct(damage.shape, jnp.float32),
        ),
        in_specs=in_hbm(1) + [vmem] * 4,
        out_specs=(vmem, *in_hbm(1)),
        scratch_shapes=[
            pltpu.SMEM(listed.shape, listed.dtype),
            pltpu.VMEM((2, clusters, padded), jnp.float32),
            pltpu.VMEM((6 * chunks * clusters, PIECES * CHUNK), jnp.bfloat16),
            pltpu.VMEM((PIECES * CHUNK, SUBLANES * LANES), jnp.bfloat16),
            pltpu.VMEM((3 * chunks, clusters, LANES), jnp.float32),
            pltpu.VMEM((6 * chunks, clusters * SUBLANES, LANES), jnp.float32),
            pltpu.VMEM((3 * chunks, (clusters + 1) * SUBLANES, LANES), jnp.float32),
            pltpu.SemaphoreType.DMA((2,)),
        ],
        compiler_params=pltpu.CompilerParams(vmem_limit_bytes=VMEM),
        cost_estimate=pl.CostEstimate(
            flops=30 * slots * elems * elems,
            bytes_accessed=4 * clusters * width * 6,
            transcendentals=slots * elems * elems,
        ),
        name="near_field",
    )(listed, disp, pos, base, damage)


def finish_kernel(
    rest_hbm,
    pos_hbm,
    received_ref,
    near_ref,
    far_ref,
    out_ref,
    rest_ref,
    pos_ref,
    ext_scr,
    halo_scr,
    tgt_scr,
    src_scr,
    acc_scr,
    sems,
    *,
    rank,
):
    clusters, width = near_ref.shape
    cols = received_ref.shape[0]
    elems = width // 3
    chunks = elems // CHUNK
    size = 3 * chunks
    spare = LANES - rank
    segments = split_rows(width, spare)
    edge = 2 * HALO
    tail = pl.ds(clusters - SUBLANES, SUBLANES)

    inputs = start_all(
        sems,
        (
            (rest_hbm, rest_ref),
            (pos_hbm.at[pl.ds(0, SUBLANES)], pos_ref.at[0]),
            (pos_hbm.at[tail], pos_ref.at[1]),
        ),
    )
    acc_scr[...] = jnp.zeros_like(acc_scr)

    j = lax.axis_index("cols")
    before = jnp.where(j > 0, j - 1, cols - 1)
    after = jnp.where(j < cols - 1, j + 1, 0)
    for start, sender in ((0, before), (HALO, after)):
        halo_scr[...] = received_ref[sender].astype(jnp.float32)
        rows = edge * segments
        whole = halo_scr[0:rows, :]
        for n in range(1, PIECES):
            whole = whole + halo_scr[n * rows : (n + 1) * rows, :]
        for g in range(segments):
            count = min(spare, width - g * spare)
            for k in range(2):
                row = (2 * g + k) * HALO
                ext_scr[k, start : start + HALO, g * spare : g * spare + count] = whole[
                    row : row + HALO, rank : rank + count
                ]
    inputs[1].wait()
    inputs[2].wait()
    ext_scr[1, edge : edge + HALO, 0:width] = pos_ref[0, 0:HALO, :]
    ext_scr[1, edge + HALO : 2 * edge, 0:width] = pos_ref[1, SUBLANES - HALO :, :]
    for k in range(2):

        def store(m, value, k=k):
            for b in range(edge):
                wide = jnp.broadcast_to(value[b : b + 1, :], (SUBLANES, LANES))
                src_scr[(1 - k) * size + m, b * SUBLANES : (b + 1) * SUBLANES, :] = turn(wide)

        replicate(ext_scr[k], chunks, store, True)

    def store_target(m, value):
        tgt_scr[m] = value

    replicate(ext_scr[1], chunks, store_target)
    inputs[0].wait()
    number = rest_ref[6, 0]

    def one_pair(n):
        target = rest_ref[4, n]
        source = rest_ref[5, n]
        target = jnp.where(target < HALO, target, target - (clusters - edge))
        source = jnp.where(source < HALO, source, source - clusters)
        live = n < number
        target = jnp.where(live, target, edge)
        source = pl.multiple_of(jnp.where(live, source, 0) * SUBLANES, SUBLANES)
        into = pl.multiple_of(target * SUBLANES, SUBLANES)
        row = edge + jnp.where(live, target, 0)
        tgt = [row_of(tgt_scr, m, row) for m in range(size)]
        sums = pair_sums(tgt, lambda k: src_scr[k, pl.ds(source, SUBLANES), :], chunks)
        for m in range(size):
            acc_scr[m, pl.ds(into, SUBLANES), :] += sums[m]

    def step(it, carry):
        for k in range(FEW):
            one_pair(it * FEW + k)
        return carry

    lax.fori_loop(0, (number + FEW - 1) // FEW, step, 0)

    def store_sum(t, value):
        ext_scr[0, :, t * LANES : (t + 1) * LANES] = value

    gather_sums(acc_scr, 2 * edge, chunks, store_sum)
    out_ref[...] = near_ref[...] + far_ref[...]
    out_ref[0:HALO, :] += ext_scr[0, 0:HALO, 0:width]
    out_ref[clusters - HALO :, :] += ext_scr[0, HALO:edge, 0:width]


def finish(rest, pos, received, near, far, rank):
    clusters, width = pos.shape
    chunks = width // 3 // CHUNK
    padded = pl.cdiv(width, LANES) * LANES
    edge = 2 * HALO
    vmem = pl.BlockSpec(memory_space=pltpu.VMEM)
    return pl.pallas_call(
        functools.partial(finish_kernel, rank=rank),
        out_shape=jax.ShapeDtypeStruct((clusters, width), jnp.float32),
        in_specs=in_hbm(2) + [vmem] * 3,
        out_specs=vmem,
        scratch_shapes=[
            pltpu.SMEM(rest.shape, rest.dtype),
            pltpu.VMEM((2, SUBLANES, width), pos.dtype),
            pltpu.VMEM((2, 2 * edge, padded), jnp.float32),
            pltpu.VMEM((clusters, LANES), jnp.float32),
            pltpu.VMEM((3 * chunks, 2 * edge, LANES), jnp.float32),
            pltpu.VMEM((6 * chunks, edge * SUBLANES, LANES), jnp.float32),
            pltpu.VMEM((3 * chunks, 2 * edge * SUBLANES, LANES), jnp.float32),
            pltpu.SemaphoreType.DMA((3,)),
        ],
        compiler_params=pltpu.CompilerParams(vmem_limit_bytes=VMEM),
        cost_estimate=pl.CostEstimate(
            flops=2 * clusters * width, bytes_accessed=16 * clusters * width, transcendentals=0
        ),
        name="finish",
    )(rest, *pinned(pos), received, near, far)


def local(
    displacement,
    positions,
    cluster_basis,
    near_pairs,
    near_count,
    far_pairs,
    far_count,
    far_blocks,
    intact,
    stiffness,
):
    cols = lax.axis_size("cols")
    clusters, width, rank = cluster_basis.shape
    spare = LANES - rank
    segments = split_rows(width, spare)
    disp_bf, halo, disp, pos, base, damage, listed = prepare(
        near_count, far_count, near_pairs.T, displacement, positions, intact, stiffness, spare
    )
    coeff = jnp.einsum("kf,kfr->kr", disp_bf, cluster_basis, preferred_element_type=jnp.float32)
    payload = jnp.concatenate([coeff, halo], axis=1)
    gathered = lax.all_gather(payload, "rows", axis=0, tiled=True)
    partial = far_field(
        listed, far_pairs.T, gathered, far_blocks.transpose(1, 2, 0), cols, segments
    )
    received = lax.all_to_all(partial, "cols", split_axis=0, concat_axis=0)
    near, damage = near_field(listed, disp, pos, base, damage)
    owned = jnp.sum(received[:, :, :rank].astype(jnp.float32), axis=0).astype(jnp.bfloat16)
    far = jnp.einsum("kfr,kr->kf", cluster_basis, owned, preferred_element_type=jnp.float32)
    return finish(listed, positions, received, near, far, rank), damage


def solution(mesh):
    both = ("rows", "cols")
    in_specs = (
        P(both, None),
        P(both, None),
        P(both, None, None),
        P(both, None),
        P(both),
        P(both, None),
        P(both),
        P(both, None, None),
        P(both, None),
        P(both, None),
    )
    out_specs = (P(both, None), P(both, None))
    return jax.shard_map(local, mesh=mesh, in_specs=in_specs, out_specs=out_specs, check_vma=False)
```

```python
import functools

import jax
import jax.numpy as jnp
from jax import lax
from jax.experimental import pallas as pl
from jax.experimental.pallas import tpu as pltpu
from jax.sharding import PartitionSpec as P

HALO = 2
LANES = 128
SUBLANES = 8
CHUNK = 32
GROUPS = LANES // CHUNK
core_square = 0.25
softening = 1.5
UNROLL = 8
FEW = 4
FOLD = 256
PIECES = 3
VMEM = 20 * 1024 * 1024


def split_rows(width, lanes):
    return pl.cdiv(width, lanes)


def in_hbm(count):
    return [pl.BlockSpec(memory_space=pltpu.HBM)] * count


def pinned(*arrays):
    return [pltpu.with_memory_space_constraint(x, pltpu.HBM) for x in arrays]


def start_all(sems, moves):
    copies = [
        pltpu.make_async_copy(source, target, sems.at[n])
        for n, (source, target) in enumerate(moves)
    ]
    for copy in copies:
        copy.start()
    return copies


def prepare_kernel(
    near_count_ref,
    far_count_ref,
    pairs_hbm,
    disp_hbm,
    pos_hbm,
    intact_hbm,
    stiff_hbm,
    low_ref,
    halo_ref,
    disp_ref,
    pos_ref,
    base_ref,
    damage_ref,
    list_ref,
    pairs_ref,
    intact_ref,
    stiff_ref,
    sems,
):
    clusters, width = disp_ref.shape
    elems = width // 3
    spare = halo_ref.shape[1]
    segments = split_rows(width, spare)
    inputs = start_all(
        sems,
        (
            (pairs_hbm, pairs_ref),
            (disp_hbm, disp_ref),
            (pos_hbm, pos_ref),
            (intact_hbm, intact_ref),
            (stiff_hbm, stiff_ref),
        ),
    )
    halo_ref[...] = jnp.zeros_like(halo_ref)
    for copy in inputs:
        copy.wait()
    list_pairs(pairs_ref, near_count_ref[0], far_count_ref[0], list_ref, clusters)
    low_ref[...] = disp_ref[...].astype(low_ref.dtype)
    row = 0
    for g in range(segments):
        size = min(spare, width - g * spare)
        for start in (0, clusters - HALO):
            for ref in (disp_ref, pos_ref):
                halo_ref[row : row + HALO, 0:size] = ref[
                    start : start + HALO, g * spare : g * spare + size
                ]
                row += HALO

    disp = [disp_ref[:, c * elems : (c + 1) * elems] for c in range(3)]
    separation = jnp.sqrt(1.0 + (disp[0] * disp[0] + disp[1] * disp[1] + disp[2] * disp[2]))
    softened = 1.0 - jnp.exp(-(separation - 1.0) / softening)
    intact = intact_ref[...].astype(jnp.float32)
    damage = intact * softened + (1.0 - intact)
    damage_ref[...] = damage
    hold = (1.0 - damage) * stiff_ref[...]
    for c in range(3):
        base_ref[:, c * elems : (c + 1) * elems] = -hold * disp[c]


def list_pairs(pairs_ref, near_count, far_count, list_ref, clusters):
    slots = pairs_ref.shape[1]
    target = pairs_ref[0:1, :]
    source = pairs_ref[1:2, :]
    live = lax.broadcasted_iota(jnp.int32, (1, slots), 1) < near_count
    own = jnp.logical_and(source >= HALO, source < clusters + HALO)
    list_ref[0:1, :] = target
    list_ref[1:2, :] = jnp.clip(source - HALO, 0, clusters - 1)
    list_ref[2:3, :] = jnp.where(jnp.logical_and(live, own), target, clusters) * SUBLANES
    list_ref[3:4, :] = jnp.full((1, slots), near_count, jnp.int32)
    others = jnp.where(jnp.logical_and(live, jnp.logical_not(own)), 1.0, 0.0)
    square = (slots, slots)
    upto = lax.broadcasted_iota(jnp.int32, square, 0) <= lax.broadcasted_iota(jnp.int32, square, 1)
    upto = jnp.where(upto, 1.0, 0.0).astype(jnp.bfloat16)
    order = jnp.dot(
        jnp.broadcast_to(others, (SUBLANES, slots)).astype(jnp.bfloat16),
        upto,
        preferred_element_type=jnp.float32,
    )
    place = jnp.where(others > 0.0, order[0:1, :] - 1.0, -1.0).astype(jnp.int32)
    place = lax.broadcasted_iota(jnp.int32, square, 0) == place
    place = jnp.where(place, 1.0, 0.0).astype(jnp.bfloat16)
    row = lax.broadcasted_iota(jnp.int32, (SUBLANES, slots), 0)
    listed = jnp.where(row == 0, target, source).astype(jnp.float32).astype(jnp.bfloat16)
    listed = lax.dot_general(
        listed, place, (((1,), (1,)), ((), ())), preferred_element_type=jnp.float32
    ).astype(jnp.int32)
    list_ref[4:6, :] = listed[0:2, :]
    number = jnp.sum(others, axis=1, keepdims=True).astype(jnp.int32)
    list_ref[6:7, :] = jnp.broadcast_to(number, (1, slots))
    list_ref[7:8, :] = jnp.full((1, slots), far_count, jnp.int32)


def prepare(near_count, far_count, pairs, disp, pos, intact, stiffness, spare):
    clusters, width = disp.shape
    slots = pairs.shape[1]
    vmem = pl.BlockSpec(memory_space=pltpu.VMEM)
    smem = pl.BlockSpec(memory_space=pltpu.SMEM)
    return pl.pallas_call(
        prepare_kernel,
        out_shape=(
            jax.ShapeDtypeStruct((clusters, width), jnp.bfloat16),
            jax.ShapeDtypeStruct((clusters, spare), jnp.float32),
            jax.ShapeDtypeStruct((clusters, width), jnp.float32),
            jax.ShapeDtypeStruct((clusters, width), jnp.float32),
            jax.ShapeDtypeStruct((clusters, width), jnp.float32),
            jax.ShapeDtypeStruct(stiffness.shape, jnp.float32),
            jax.ShapeDtypeStruct((SUBLANES, slots), jnp.int32),
        ),
        in_specs=[smem] * 2 + in_hbm(5),
        out_specs=(vmem,) * 7,
        scratch_shapes=[
            pltpu.VMEM(pairs.shape, pairs.dtype),
            pltpu.VMEM(intact.shape, intact.dtype),
            pltpu.VMEM(stiffness.shape, stiffness.dtype),
            pltpu.SemaphoreType.DMA((5,)),
        ],
        compiler_params=pltpu.CompilerParams(vmem_limit_bytes=VMEM),
        cost_estimate=pl.CostEstimate(
            flops=20 * clusters * width, bytes_accessed=24 * clusters * width, transcendentals=0
        ),
        name="prepare",
    )(near_count, far_count, *pinned(pairs, disp, pos, intact, stiffness))


def far_kernel(
    list_hbm,
    pairs_hbm,
    gathered_hbm,
    blocks_ref,
    out_ref,
    list_ref,
    pairs_ref,
    gathered_ref,
    buffer,
    column_scr,
    coeff_scr,
    place_scr,
    sum_scr,
    summed_scr,
    halo_scr,
    sems,
    block_sems,
    *,
    segments,
):
    rank, _, slots = buffer.shape
    cols, clusters, _ = out_ref.shape
    targets = cols * clusters
    rows = gathered_ref.shape[0] // clusters
    sources = rows * clusters
    tiles = slots // FOLD

    def fetch(t):
        here = pl.ds(pl.multiple_of(t * FOLD, FOLD), FOLD)
        return pltpu.make_async_copy(
            blocks_ref.at[:, :, here], buffer.at[:, :, here], block_sems.at[t]
        )

    inputs = start_all(
        sems, ((list_hbm, list_ref), (pairs_hbm, pairs_ref), (gathered_hbm, gathered_ref))
    )
    fetch(0).start()
    summed_scr[...] = jnp.zeros_like(summed_scr)
    inputs[0].wait()
    count = list_ref[7, 0]
    live = (count + FOLD - 1) // FOLD
    for t in range(1, tiles):

        @pl.when(t < live)
        def _(t=t):
            fetch(t).start()

    inputs[1].wait()
    inputs[2].wait()
    column_scr[...] = gathered_ref[...].astype(jnp.bfloat16)

    index = lax.broadcasted_iota(jnp.int32, (sources, slots), 0)
    pick = jnp.where(index == pairs_ref[1:2, :], 1.0, 0.0).astype(jnp.bfloat16)
    coeff = lax.dot_general(
        column_scr[...], pick, (((0,), (0,)), ((), ())), preferred_element_type=jnp.float32
    )
    coeff_scr[...] = coeff[0:rank, :]
    slot = lax.broadcasted_iota(jnp.int32, (1, slots), 1)
    wanted = jnp.where(slot < count, pairs_ref[0:1, :], -1)
    index = lax.broadcasted_iota(jnp.int32, (targets, slots), 0)
    place_scr[...] = jnp.where(index == wanted, 1.0, 0.0).astype(jnp.bfloat16)

    def multiply(t, carry):
        start = pl.multiple_of(t * FOLD, FOLD)
        lanes = pl.ds(start, FOLD)
        fetch(t).wait()
        coeff = coeff_scr[:, lanes]
        for r in range(rank):
            product = buffer[r, :, lanes].astype(jnp.float32) * coeff
            folded = product[0:SUBLANES]
            for s in range(1, rank // SUBLANES):
                folded = folded + product[s * SUBLANES : (s + 1) * SUBLANES]
            for h in range(FOLD // LANES):
                sum_scr[h, r * SUBLANES : (r + 1) * SUBLANES, :] = folded[
                    :, h * LANES : (h + 1) * LANES
                ]
        parts = []
        for h in range(FOLD // LANES):
            total = sum_scr[h, pl.ds(0, rank, stride=SUBLANES), :]
            for s in range(1, SUBLANES):
                total = total + sum_scr[h, pl.ds(s, rank, stride=SUBLANES), :]
            parts.append(total)
        coupled = jnp.concatenate(parts, axis=1)
        high = coupled.astype(jnp.bfloat16)
        low = (coupled - high.astype(jnp.float32)).astype(jnp.bfloat16)
        both = jnp.concatenate([high, low], axis=0)
        summed_scr[...] += lax.dot_general(
            place_scr[:, lanes], both, (((1,), (1,)), ((), ())), preferred_element_type=jnp.float32
        )
        return carry

    lax.fori_loop(0, live, multiply, 0)

    i = lax.axis_index("rows")
    j = lax.axis_index("cols")
    from_last = jnp.where(j < cols - 1, i, i - 1)
    from_first = jnp.where(j > 0, i, i + 1)
    edge = 2 * HALO
    halo_scr[...] = jnp.zeros_like(halo_scr)
    sides = (
        (0, jnp.minimum(from_first, rows - 1), from_first < rows),
        (edge, jnp.maximum(from_last, 0), from_last >= 0),
    )
    for side, (row, owner, there) in enumerate(sides):
        start = pl.multiple_of(owner * clusters, clusters)
        whole = jnp.where(there, gathered_ref[pl.ds(start, clusters), :], 0.0)
        for n in range(PIECES):
            piece = whole.astype(jnp.bfloat16).astype(jnp.float32)
            whole = whole - piece
            for g in range(segments):
                to = (n * segments + g) * edge
                here = g * 2 * edge + row
                halo_scr[side, to : to + edge, :] = piece[here : here + edge, :]
    after = jnp.where(j < cols - 1, j + 1, 0)
    lane = lax.broadcasted_iota(jnp.int32, (clusters, LANES), 1)
    for d in range(cols):
        halo = halo_scr[jnp.where(after == d, 1, 0)]
        mine = summed_scr[d * clusters : (d + 1) * clusters, :]
        mine = mine + pltpu.roll(mine, rank, 1)
        out_ref[d] = jnp.where(lane < rank, mine, halo).astype(out_ref.dtype)


def far_field(listed, pairs, gathered, blocks, cols, segments):
    rank, _, slots = blocks.shape
    rows = lax.axis_size("rows")
    clusters = gathered.shape[0] // rows
    return pl.pallas_call(
        functools.partial(far_kernel, segments=segments),
        out_shape=jax.ShapeDtypeStruct((cols, clusters, LANES), jnp.bfloat16),
        in_specs=in_hbm(3) + [pl.BlockSpec(memory_space=pl.ANY)],
        out_specs=pl.BlockSpec(memory_space=pltpu.VMEM),
        scratch_shapes=[
            pltpu.SMEM(listed.shape, listed.dtype),
            pltpu.VMEM(pairs.shape, pairs.dtype),
            pltpu.VMEM(gathered.shape, gathered.dtype),
            pltpu.VMEM(blocks.shape, blocks.dtype),
            pltpu.VMEM((rows * clusters, LANES), jnp.bfloat16),
            pltpu.VMEM((rank, slots), jnp.float32),
            pltpu.VMEM((cols * clusters, slots), jnp.bfloat16),
            pltpu.VMEM((FOLD // LANES, rank * SUBLANES, LANES), jnp.float32),
            pltpu.VMEM((cols * clusters, LANES), jnp.float32),
            pltpu.VMEM((2, clusters, LANES), jnp.float32),
            pltpu.SemaphoreType.DMA((3,)),
            pltpu.SemaphoreType.DMA((slots // FOLD,)),
        ],
        compiler_params=pltpu.CompilerParams(vmem_limit_bytes=VMEM),
        cost_estimate=pl.CostEstimate(flops=rank, bytes_accessed=rank, transcendentals=0),
        name="far_field",
    )(listed, *pinned(pairs), gathered, *pinned(blocks))


def replicate(rows, chunks, store, turned=False):
    within = lax.broadcasted_iota(jnp.int32, (rows.shape[0], LANES), 1)
    if turned:
        within = within + (within // CHUNK) * SUBLANES
    within = within % CHUNK
    for m in range(3 * chunks):
        tile = m // GROUPS
        store(
            m,
            jnp.take_along_axis(
                rows[:, tile * LANES : (tile + 1) * LANES],
                within + (m % GROUPS) * CHUNK,
                axis=1,
                mode="promise_in_bounds",
            ),
        )


def row_of(ref, n, row):
    return ref[n, pl.ds(row, SUBLANES, stride=0), :]


def turn(wide):
    return pltpu.roll(wide, 0, 1, stride=1, stride_axis=0)


def pair_sums(tgt, src, chunks):
    sums = [None] * (3 * chunks)
    size = 3 * chunks
    for f in range(chunks):
        y = [src(c * chunks + f) for c in range(3)]
        u = [src(size + c * chunks + f) for c in range(3)]
        v = [3.0 * x for x in u]
        for h in range(chunks):
            r = [tgt[c * chunks + h] - y[c] for c in range(3)]
            q = (r[0] * r[0] + core_square) + (r[1] * r[1] + r[2] * r[2])
            s = r[0] * v[0] + (r[1] * v[1] + r[2] * v[2])
            inverse = lax.rsqrt(q)
            square = inverse * inverse
            weight = square * inverse
            s = s * square
            for c in range(3):
                term = weight * (u[c] - s * r[c])
                m = c * chunks + h
                sums[m] = term if sums[m] is None else sums[m] + term
    return sums


def gather_sums(acc_scr, clusters, chunks, store):
    own_group = lax.broadcasted_iota(jnp.int32, (clusters, LANES), 1) // CHUNK
    for t in range(pl.cdiv(3 * chunks, GROUPS)):
        merged = None
        for g in range(GROUPS):
            m = t * GROUPS + g
            if m >= 3 * chunks:
                break
            total = acc_scr[m, pl.ds(0, clusters, stride=SUBLANES), :]
            for s in range(1, SUBLANES):
                total = total + acc_scr[m, pl.ds(s, clusters, stride=SUBLANES), :]
            total = total + pltpu.roll(total, 2 * CHUNK, 1)
            total = total + pltpu.roll(total, CHUNK, 1)
            merged = total if merged is None else jnp.where(own_group == g, total, merged)
        store(t, merged)


def turn_matrix():
    shape = (PIECES * CHUNK, SUBLANES * LANES)
    column = lax.broadcasted_iota(jnp.int32, shape, 1)
    lane = column % LANES
    entry = (lane + (lane // CHUNK) * SUBLANES + column // LANES) % CHUNK
    row = lax.broadcasted_iota(jnp.int32, shape, 0) % CHUNK
    return jnp.where(entry == row, 1.0, 0.0).astype(jnp.bfloat16)


def exact_pieces(value):
    pieces = []
    for _ in range(PIECES):
        piece = value.astype(jnp.bfloat16)
        pieces.append(piece)
        value = value - piece.astype(jnp.float32)
    return pieces


def near_kernel(
    list_hbm,
    disp_ref,
    pos_ref,
    base_ref,
    damage_ref,
    out_ref,
    damage_hbm,
    list_ref,
    wide_scr,
    piece_scr,
    turn_scr,
    tgt_scr,
    src_scr,
    acc_scr,
    sems,
):
    clusters, width = disp_ref.shape
    elems = width // 3
    chunks = elems // CHUNK
    size = 3 * chunks

    moves = start_all(sems, ((list_hbm, list_ref), (damage_ref, damage_hbm)))
    acc_scr[...] = jnp.zeros_like(acc_scr)
    turn_scr[...] = turn_matrix()

    for k, values in enumerate((pos_ref, disp_ref)):
        wide_scr[k, :, 0:width] = values[...]
        for m in range(size):
            pieces = exact_pieces(values[:, m * CHUNK : (m + 1) * CHUNK])
            piece_scr[(k * size + m) * clusters : (k * size + m + 1) * clusters, :] = (
                jnp.concatenate(pieces, axis=1)
            )
    columns = 2 * LANES
    for t in range(SUBLANES * LANES // columns):
        for k in range(2):
            rows = size * clusters
            turned = jnp.dot(
                piece_scr[k * rows : (k + 1) * rows, :],
                turn_scr[:, t * columns : (t + 1) * columns],
                preferred_element_type=jnp.float32,
            )
            for m in range(size):
                for h in range(columns // LANES):
                    s = t * (columns // LANES) + h
                    src_scr[k * size + m, pl.ds(s, clusters, stride=SUBLANES), :] = turned[
                        m * clusters : (m + 1) * clusters, h * LANES : (h + 1) * LANES
                    ]

    def store_target(m, value):
        tgt_scr[m] = value

    replicate(wide_scr[0], chunks, store_target)
    moves[0].wait()
    count = list_ref[3, 0]

    def one_pair(slot):
        target = list_ref[0, slot]
        source = pl.multiple_of(list_ref[1, slot] * SUBLANES, SUBLANES)
        into = pl.multiple_of(list_ref[2, slot], SUBLANES)
        tgt = [row_of(tgt_scr, m, target) for m in range(size)]
        sums = pair_sums(tgt, lambda n: src_scr[n, pl.ds(source, SUBLANES), :], chunks)
        for m in range(size):
            acc_scr[m, pl.ds(into, SUBLANES), :] += sums[m]

    def step(it, carry):
        for k in range(UNROLL):
            one_pair(it * UNROLL + k)
        return carry

    lax.fori_loop(0, (count + UNROLL - 1) // UNROLL, step, 0)

    def store_sum(t, value):
        wide_scr[0, :, t * LANES : (t + 1) * LANES] = value

    gather_sums(acc_scr, clusters, chunks, store_sum)
    out_ref[...] = base_ref[...] + wide_scr[0, :, 0:width]
    moves[1].wait()


def near_field(listed, disp, pos, base, damage):
    clusters, width = disp.shape
    elems = width // 3
    chunks = elems // CHUNK
    padded = pl.cdiv(width, LANES) * LANES
    slots = listed.shape[1]
    vmem = pl.BlockSpec(memory_space=pltpu.VMEM)
    return pl.pallas_call(
        near_kernel,
        out_shape=(
            jax.ShapeDtypeStruct((clusters, width), jnp.float32),
            jax.ShapeDtypeStruct(damage.shape, jnp.float32),
        ),
        in_specs=in_hbm(1) + [vmem] * 4,
        out_specs=(vmem, *in_hbm(1)),
        scratch_shapes=[
            pltpu.SMEM(listed.shape, listed.dtype),
            pltpu.VMEM((2, clusters, padded), jnp.float32),
            pltpu.VMEM((6 * chunks * clusters, PIECES * CHUNK), jnp.bfloat16),
            pltpu.VMEM((PIECES * CHUNK, SUBLANES * LANES), jnp.bfloat16),
            pltpu.VMEM((3 * chunks, clusters, LANES), jnp.float32),
            pltpu.VMEM((6 * chunks, clusters * SUBLANES, LANES), jnp.float32),
            pltpu.VMEM((3 * chunks, (clusters + 1) * SUBLANES, LANES), jnp.float32),
            pltpu.SemaphoreType.DMA((2,)),
        ],
        compiler_params=pltpu.CompilerParams(vmem_limit_bytes=VMEM),
        cost_estimate=pl.CostEstimate(
            flops=30 * slots * elems * elems,
            bytes_accessed=4 * clusters * width * 6,
            transcendentals=slots * elems * elems,
        ),
        name="near_field",
    )(listed, disp, pos, base, damage)


def finish_kernel(
    rest_hbm,
    pos_hbm,
    received_ref,
    near_ref,
    far_ref,
    out_ref,
    rest_ref,
    pos_ref,
    ext_scr,
    halo_scr,
    tgt_scr,
    src_scr,
    acc_scr,
    sems,
    *,
    rank,
):
    clusters, width = near_ref.shape
    cols = received_ref.shape[0]
    elems = width // 3
    chunks = elems // CHUNK
    size = 3 * chunks
    spare = LANES - rank
    segments = split_rows(width, spare)
    edge = 2 * HALO
    tail = pl.ds(clusters - SUBLANES, SUBLANES)

    inputs = start_all(
        sems,
        (
            (rest_hbm, rest_ref),
            (pos_hbm.at[pl.ds(0, SUBLANES)], pos_ref.at[0]),
            (pos_hbm.at[tail], pos_ref.at[1]),
        ),
    )
    acc_scr[...] = jnp.zeros_like(acc_scr)

    j = lax.axis_index("cols")
    before = jnp.where(j > 0, j - 1, cols - 1)
    after = jnp.where(j < cols - 1, j + 1, 0)
    for start, sender in ((0, before), (HALO, after)):
        halo_scr[...] = received_ref[sender].astype(jnp.float32)
        rows = edge * segments
        whole = halo_scr[0:rows, :]
        for n in range(1, PIECES):
            whole = whole + halo_scr[n * rows : (n + 1) * rows, :]
        for g in range(segments):
            count = min(spare, width - g * spare)
            for k in range(2):
                row = (2 * g + k) * HALO
                ext_scr[k, start : start + HALO, g * spare : g * spare + count] = whole[
                    row : row + HALO, rank : rank + count
                ]
    inputs[1].wait()
    inputs[2].wait()
    ext_scr[1, edge : edge + HALO, 0:width] = pos_ref[0, 0:HALO, :]
    ext_scr[1, edge + HALO : 2 * edge, 0:width] = pos_ref[1, SUBLANES - HALO :, :]
    for k in range(2):

        def store(m, value, k=k):
            for b in range(edge):
                wide = jnp.broadcast_to(value[b : b + 1, :], (SUBLANES, LANES))
                src_scr[(1 - k) * size + m, b * SUBLANES : (b + 1) * SUBLANES, :] = turn(wide)

        replicate(ext_scr[k], chunks, store, True)

    def store_target(m, value):
        tgt_scr[m] = value

    replicate(ext_scr[1], chunks, store_target)
    inputs[0].wait()
    number = rest_ref[6, 0]

    def one_pair(n):
        target = rest_ref[4, n]
        source = rest_ref[5, n]
        target = jnp.where(target < HALO, target, target - (clusters - edge))
        source = jnp.where(source < HALO, source, source - clusters)
        live = n < number
        target = jnp.where(live, target, edge)
        source = pl.multiple_of(jnp.where(live, source, 0) * SUBLANES, SUBLANES)
        into = pl.multiple_of(target * SUBLANES, SUBLANES)
        row = edge + jnp.where(live, target, 0)
        tgt = [row_of(tgt_scr, m, row) for m in range(size)]
        sums = pair_sums(tgt, lambda k: src_scr[k, pl.ds(source, SUBLANES), :], chunks)
        for m in range(size):
            acc_scr[m, pl.ds(into, SUBLANES), :] += sums[m]

    def step(it, carry):
        for k in range(FEW):
            one_pair(it * FEW + k)
        return carry

    lax.fori_loop(0, (number + FEW - 1) // FEW, step, 0)

    def store_sum(t, value):
        ext_scr[0, :, t * LANES : (t + 1) * LANES] = value

    gather_sums(acc_scr, 2 * edge, chunks, store_sum)
    out_ref[...] = near_ref[...] + far_ref[...]
    out_ref[0:HALO, :] += ext_scr[0, 0:HALO, 0:width]
    out_ref[clusters - HALO :, :] += ext_scr[0, HALO:edge, 0:width]


def finish(rest, pos, received, near, far, rank):
    clusters, width = pos.shape
    chunks = width // 3 // CHUNK
    padded = pl.cdiv(width, LANES) * LANES
    edge = 2 * HALO
    vmem = pl.BlockSpec(memory_space=pltpu.VMEM)
    return pl.pallas_call(
        functools.partial(finish_kernel, rank=rank),
        out_shape=jax.ShapeDtypeStruct((clusters, width), jnp.float32),
        in_specs=in_hbm(2) + [vmem] * 3,
        out_specs=vmem,
        scratch_shapes=[
            pltpu.SMEM(rest.shape, rest.dtype),
            pltpu.VMEM((2, SUBLANES, width), pos.dtype),
            pltpu.VMEM((2, 2 * edge, padded), jnp.float32),
            pltpu.VMEM((clusters, LANES), jnp.float32),
            pltpu.VMEM((3 * chunks, 2 * edge, LANES), jnp.float32),
            pltpu.VMEM((6 * chunks, edge * SUBLANES, LANES), jnp.float32),
            pltpu.VMEM((3 * chunks, 2 * edge * SUBLANES, LANES), jnp.float32),
            pltpu.SemaphoreType.DMA((3,)),
        ],
        compiler_params=pltpu.CompilerParams(vmem_limit_bytes=VMEM),
        cost_estimate=pl.CostEstimate(
            flops=2 * clusters * width, bytes_accessed=16 * clusters * width, transcendentals=0
        ),
        name="finish",
    )(rest, *pinned(pos), received, near, far)


def local(
    displacement,
    positions,
    cluster_basis,
    near_pairs,
    near_count,
    far_pairs,
    far_count,
    far_blocks,
    intact,
    stiffness,
):
    cols = lax.axis_size("cols")
    clusters, width, rank = cluster_basis.shape
    spare = LANES - rank
    segments = split_rows(width, spare)
    disp_bf, halo, disp, pos, base, damage, listed = prepare(
        near_count, far_count, near_pairs.T, displacement, positions, intact, stiffness, spare
    )
    coeff = jnp.einsum("kf,kfr->kr", disp_bf, cluster_basis, preferred_element_type=jnp.float32)
    payload = jnp.concatenate([coeff, halo], axis=1)
    gathered = lax.all_gather(payload, "rows", axis=0, tiled=True)
    partial = far_field(
        listed, far_pairs.T, gathered, far_blocks.transpose(1, 2, 0), cols, segments
    )
    received = lax.all_to_all(partial, "cols", split_axis=0, concat_axis=0)
    near, damage = near_field(listed, disp, pos, base, damage)
    owned = jnp.sum(received[:, :, :rank].astype(jnp.float32), axis=0).astype(jnp.bfloat16)
    far = jnp.einsum("kfr,kr->kf", cluster_basis, owned, preferred_element_type=jnp.float32)
    return finish(listed, positions, received, near, far, rank), damage


def solution(mesh):
    both = ("rows", "cols")
    in_specs = (
        P(both, None),
        P(both, None),
        P(both, None, None),
        P(both, None),
        P(both),
        P(both, None),
        P(both),
        P(both, None, None),
        P(both, None),
        P(both, None),
    )
    out_specs = (P(both, None), P(both, None))
    return jax.shard_map(local, mesh=mesh, in_specs=in_specs, out_specs=out_specs, check_vma=False)
```

```python
import functools

import jax
import jax.numpy as jnp
from jax import lax
from jax.experimental import pallas as pl
from jax.experimental.pallas import tpu as pltpu
from jax.sharding import PartitionSpec as P

HALO = 2
LANES = 128
SUBLANES = 8
CHUNK = 32
GROUPS = LANES // CHUNK
core_square = 0.25
softening = 1.5
UNROLL = 8
FEW = 4
FOLD = 256
PIECES = 3
VMEM = 20 * 1024 * 1024


def split_rows(width, lanes):
    return pl.cdiv(width, lanes)


def in_hbm(count):
    return [pl.BlockSpec(memory_space=pltpu.HBM)] * count


def pinned(*arrays):
    return [pltpu.with_memory_space_constraint(x, pltpu.HBM) for x in arrays]


def start_all(sems, moves):
    copies = [
        pltpu.make_async_copy(source, target, sems.at[n])
        for n, (source, target) in enumerate(moves)
    ]
    for copy in copies:
        copy.start()
    return copies


def prepare_kernel(
    near_count_ref,
    far_count_ref,
    pairs_hbm,
    disp_hbm,
    pos_hbm,
    low_ref,
    halo_ref,
    list_ref,
    pairs_ref,
    disp_ref,
    pos_ref,
    sems,
):
    clusters, width = disp_ref.shape
    spare = halo_ref.shape[1]
    segments = split_rows(width, spare)
    inputs = start_all(
        sems,
        (
            (pairs_hbm, pairs_ref),
            (disp_hbm, disp_ref),
            (pos_hbm, pos_ref),
        ),
    )
    halo_ref[...] = jnp.zeros_like(halo_ref)
    for copy in inputs:
        copy.wait()
    list_pairs(pairs_ref, near_count_ref[0], far_count_ref[0], list_ref, clusters)
    low_ref[...] = disp_ref[...].astype(low_ref.dtype)
    row = 0
    for g in range(segments):
        size = min(spare, width - g * spare)
        for start in (0, clusters - HALO):
            for ref in (disp_ref, pos_ref):
                halo_ref[row : row + HALO, 0:size] = ref[
                    start : start + HALO, g * spare : g * spare + size
                ]
                row += HALO


def list_pairs(pairs_ref, near_count, far_count, list_ref, clusters):
    slots = pairs_ref.shape[1]
    target = pairs_ref[0:1, :]
    source = pairs_ref[1:2, :]
    live = lax.broadcasted_iota(jnp.int32, (1, slots), 1) < near_count
    own = jnp.logical_and(source >= HALO, source < clusters + HALO)
    list_ref[0:1, :] = target
    list_ref[1:2, :] = jnp.clip(source - HALO, 0, clusters - 1)
    list_ref[2:3, :] = jnp.where(jnp.logical_and(live, own), target, clusters) * SUBLANES
    list_ref[3:4, :] = jnp.full((1, slots), near_count, jnp.int32)
    others = jnp.where(jnp.logical_and(live, jnp.logical_not(own)), 1.0, 0.0)
    square = (slots, slots)
    upto = lax.broadcasted_iota(jnp.int32, square, 0) <= lax.broadcasted_iota(jnp.int32, square, 1)
    upto = jnp.where(upto, 1.0, 0.0).astype(jnp.bfloat16)
    order = jnp.dot(
        jnp.broadcast_to(others, (SUBLANES, slots)).astype(jnp.bfloat16),
        upto,
        preferred_element_type=jnp.float32,
    )
    place = jnp.where(others > 0.0, order[0:1, :] - 1.0, -1.0).astype(jnp.int32)
    place = lax.broadcasted_iota(jnp.int32, square, 0) == place
    place = jnp.where(place, 1.0, 0.0).astype(jnp.bfloat16)
    row = lax.broadcasted_iota(jnp.int32, (SUBLANES, slots), 0)
    listed = jnp.where(row == 0, target, source).astype(jnp.float32).astype(jnp.bfloat16)
    listed = lax.dot_general(
        listed, place, (((1,), (1,)), ((), ())), preferred_element_type=jnp.float32
    ).astype(jnp.int32)
    list_ref[4:6, :] = listed[0:2, :]
    number = jnp.sum(others, axis=1, keepdims=True).astype(jnp.int32)
    list_ref[6:7, :] = jnp.broadcast_to(number, (1, slots))
    list_ref[7:8, :] = jnp.full((1, slots), far_count, jnp.int32)


def prepare(near_count, far_count, pairs, disp, pos, spare):
    clusters, width = disp.shape
    slots = pairs.shape[1]
    vmem = pl.BlockSpec(memory_space=pltpu.VMEM)
    smem = pl.BlockSpec(memory_space=pltpu.SMEM)
    return pl.pallas_call(
        prepare_kernel,
        out_shape=(
            jax.ShapeDtypeStruct((clusters, width), jnp.bfloat16),
            jax.ShapeDtypeStruct((clusters, spare), jnp.float32),
            jax.ShapeDtypeStruct((SUBLANES, slots), jnp.int32),
        ),
        in_specs=[smem] * 2 + in_hbm(3),
        out_specs=(vmem,) * 3,
        scratch_shapes=[
            pltpu.VMEM(pairs.shape, pairs.dtype),
            pltpu.VMEM(disp.shape, disp.dtype),
            pltpu.VMEM(pos.shape, pos.dtype),
            pltpu.SemaphoreType.DMA((3,)),
        ],
        compiler_params=pltpu.CompilerParams(vmem_limit_bytes=VMEM),
        cost_estimate=pl.CostEstimate(
            flops=20 * clusters * width, bytes_accessed=24 * clusters * width, transcendentals=0
        ),
        name="prepare",
    )(near_count, far_count, *pinned(pairs, disp, pos))


def far_kernel(
    list_hbm,
    pairs_hbm,
    gathered_hbm,
    blocks_ref,
    out_ref,
    list_ref,
    pairs_ref,
    gathered_ref,
    buffer,
    column_scr,
    coeff_scr,
    place_scr,
    sum_scr,
    summed_scr,
    halo_scr,
    sems,
    block_sems,
    *,
    segments,
):
    rank, _, slots = buffer.shape
    cols, clusters, _ = out_ref.shape
    targets = cols * clusters
    rows = gathered_ref.shape[0] // clusters
    sources = rows * clusters
    tiles = slots // FOLD

    def fetch(t):
        here = pl.ds(pl.multiple_of(t * FOLD, FOLD), FOLD)
        return pltpu.make_async_copy(
            blocks_ref.at[:, :, here], buffer.at[:, :, here], block_sems.at[t]
        )

    inputs = start_all(
        sems, ((list_hbm, list_ref), (pairs_hbm, pairs_ref), (gathered_hbm, gathered_ref))
    )
    fetch(0).start()
    summed_scr[...] = jnp.zeros_like(summed_scr)
    inputs[0].wait()
    count = list_ref[7, 0]
    live = (count + FOLD - 1) // FOLD
    for t in range(1, tiles):

        @pl.when(t < live)
        def _(t=t):
            fetch(t).start()

    inputs[1].wait()
    inputs[2].wait()
    column_scr[...] = gathered_ref[...].astype(jnp.bfloat16)

    index = lax.broadcasted_iota(jnp.int32, (sources, slots), 0)
    pick = jnp.where(index == pairs_ref[1:2, :], 1.0, 0.0).astype(jnp.bfloat16)
    coeff = lax.dot_general(
        column_scr[...], pick, (((0,), (0,)), ((), ())), preferred_element_type=jnp.float32
    )
    coeff_scr[...] = coeff[0:rank, :]
    slot = lax.broadcasted_iota(jnp.int32, (1, slots), 1)
    wanted = jnp.where(slot < count, pairs_ref[0:1, :], -1)
    index = lax.broadcasted_iota(jnp.int32, (targets, slots), 0)
    place_scr[...] = jnp.where(index == wanted, 1.0, 0.0).astype(jnp.bfloat16)

    def multiply(t, carry):
        start = pl.multiple_of(t * FOLD, FOLD)
        lanes = pl.ds(start, FOLD)
        fetch(t).wait()
        coeff = coeff_scr[:, lanes]
        for r in range(rank):
            product = buffer[r, :, lanes].astype(jnp.float32) * coeff
            folded = product[0:SUBLANES]
            for s in range(1, rank // SUBLANES):
                folded = folded + product[s * SUBLANES : (s + 1) * SUBLANES]
            for h in range(FOLD // LANES):
                sum_scr[h, r * SUBLANES : (r + 1) * SUBLANES, :] = folded[
                    :, h * LANES : (h + 1) * LANES
                ]
        parts = []
        for h in range(FOLD // LANES):
            total = sum_scr[h, pl.ds(0, rank, stride=SUBLANES), :]
            for s in range(1, SUBLANES):
                total = total + sum_scr[h, pl.ds(s, rank, stride=SUBLANES), :]
            parts.append(total)
        coupled = jnp.concatenate(parts, axis=1)
        high = coupled.astype(jnp.bfloat16)
        low = (coupled - high.astype(jnp.float32)).astype(jnp.bfloat16)
        both = jnp.concatenate([high, low], axis=0)
        summed_scr[...] += lax.dot_general(
            place_scr[:, lanes], both, (((1,), (1,)), ((), ())), preferred_element_type=jnp.float32
        )
        return carry

    lax.fori_loop(0, live, multiply, 0)

    i = lax.axis_index("rows")
    j = lax.axis_index("cols")
    from_last = jnp.where(j < cols - 1, i, i - 1)
    from_first = jnp.where(j > 0, i, i + 1)
    edge = 2 * HALO
    halo_scr[...] = jnp.zeros_like(halo_scr)
    sides = (
        (0, jnp.minimum(from_first, rows - 1), from_first < rows),
        (edge, jnp.maximum(from_last, 0), from_last >= 0),
    )
    for side, (row, owner, there) in enumerate(sides):
        start = pl.multiple_of(owner * clusters, clusters)
        whole = jnp.where(there, gathered_ref[pl.ds(start, clusters), :], 0.0)
        for n in range(PIECES):
            piece = whole.astype(jnp.bfloat16).astype(jnp.float32)
            whole = whole - piece
            for g in range(segments):
                to = (n * segments + g) * edge
                here = g * 2 * edge + row
                halo_scr[side, to : to + edge, :] = piece[here : here + edge, :]
    after = jnp.where(j < cols - 1, j + 1, 0)
    lane = lax.broadcasted_iota(jnp.int32, (clusters, LANES), 1)
    for d in range(cols):
        halo = halo_scr[jnp.where(after == d, 1, 0)]
        mine = summed_scr[d * clusters : (d + 1) * clusters, :]
        mine = mine + pltpu.roll(mine, rank, 1)
        out_ref[d] = jnp.where(lane < rank, mine, halo).astype(out_ref.dtype)


def far_field(listed, pairs, gathered, blocks, cols, segments):
    rank, _, slots = blocks.shape
    rows = lax.axis_size("rows")
    clusters = gathered.shape[0] // rows
    return pl.pallas_call(
        functools.partial(far_kernel, segments=segments),
        out_shape=jax.ShapeDtypeStruct((cols, clusters, LANES), jnp.bfloat16),
        in_specs=in_hbm(3) + [pl.BlockSpec(memory_space=pl.ANY)],
        out_specs=pl.BlockSpec(memory_space=pltpu.VMEM),
        scratch_shapes=[
            pltpu.SMEM(listed.shape, listed.dtype),
            pltpu.VMEM(pairs.shape, pairs.dtype),
            pltpu.VMEM(gathered.shape, gathered.dtype),
            pltpu.VMEM(blocks.shape, blocks.dtype),
            pltpu.VMEM((rows * clusters, LANES), jnp.bfloat16),
            pltpu.VMEM((rank, slots), jnp.float32),
            pltpu.VMEM((cols * clusters, slots), jnp.bfloat16),
            pltpu.VMEM((FOLD // LANES, rank * SUBLANES, LANES), jnp.float32),
            pltpu.VMEM((cols * clusters, LANES), jnp.float32),
            pltpu.VMEM((2, clusters, LANES), jnp.float32),
            pltpu.SemaphoreType.DMA((3,)),
            pltpu.SemaphoreType.DMA((slots // FOLD,)),
        ],
        compiler_params=pltpu.CompilerParams(vmem_limit_bytes=VMEM),
        cost_estimate=pl.CostEstimate(
            flops=2 * rank * rank * slots,
            bytes_accessed=2 * rank * rank * slots,
            transcendentals=0,
        ),
        name="far_field",
    )(listed, *pinned(pairs), gathered, *pinned(blocks))


def replicate(rows, chunks, store, turned=False):
    within = lax.broadcasted_iota(jnp.int32, (rows.shape[0], LANES), 1)
    if turned:
        within = within + (within // CHUNK) * SUBLANES
    within = within % CHUNK
    for m in range(3 * chunks):
        tile = m // GROUPS
        store(
            m,
            jnp.take_along_axis(
                rows[:, tile * LANES : (tile + 1) * LANES],
                within + (m % GROUPS) * CHUNK,
                axis=1,
                mode="promise_in_bounds",
            ),
        )


def row_of(ref, n, row):
    return ref[n, pl.ds(row, SUBLANES, stride=0), :]


def turn(wide):
    return pltpu.roll(wide, 0, 1, stride=1, stride_axis=0)


def pair_sums(tgt, src, chunks):
    sums = [None] * (3 * chunks)
    size = 3 * chunks
    for h in range(chunks):
        x = [tgt(c * chunks + h) for c in range(3)]
        for f in range(chunks):
            r = [x[c] - src(c * chunks + f) for c in range(3)]
            u = [src(size + c * chunks + f) for c in range(3)]
            q = (r[0] * r[0] + core_square) + (r[1] * r[1] + r[2] * r[2])
            s = r[0] * u[0] + (r[1] * u[1] + r[2] * u[2])
            inverse = lax.rsqrt(q)
            square = inverse * inverse
            weight = square * inverse
            s = (3.0 * s) * square
            for c in range(3):
                term = weight * (u[c] - s * r[c])
                m = c * chunks + h
                sums[m] = term if sums[m] is None else sums[m] + term
    return sums


def gather_sums(acc_scr, clusters, chunks, store):
    own_group = lax.broadcasted_iota(jnp.int32, (clusters, LANES), 1) // CHUNK
    for t in range(pl.cdiv(3 * chunks, GROUPS)):
        merged = None
        for g in range(GROUPS):
            m = t * GROUPS + g
            if m >= 3 * chunks:
                break
            total = acc_scr[m, pl.ds(0, clusters, stride=SUBLANES), :]
            for s in range(1, SUBLANES):
                total = total + acc_scr[m, pl.ds(s, clusters, stride=SUBLANES), :]
            total = total + pltpu.roll(total, 2 * CHUNK, 1)
            total = total + pltpu.roll(total, CHUNK, 1)
            merged = total if merged is None else jnp.where(own_group == g, total, merged)
        store(t, merged)


def turn_matrix():
    shape = (PIECES * CHUNK, SUBLANES * LANES)
    column = lax.broadcasted_iota(jnp.int32, shape, 1)
    lane = column % LANES
    entry = (lane + (lane // CHUNK) * SUBLANES + column // LANES) % CHUNK
    row = lax.broadcasted_iota(jnp.int32, shape, 0) % CHUNK
    return jnp.where(entry == row, 1.0, 0.0).astype(jnp.bfloat16)


def exact_pieces(value):
    pieces = []
    for _ in range(PIECES):
        piece = value.astype(jnp.bfloat16)
        pieces.append(piece)
        value = value - piece.astype(jnp.float32)
    return pieces


def near_kernel(
    list_hbm,
    disp_hbm,
    pos_hbm,
    intact_hbm,
    stiff_hbm,
    out_ref,
    damage_hbm,
    list_ref,
    disp_ref,
    pos_ref,
    intact_ref,
    stiff_ref,
    damage_ref,
    wide_scr,
    piece_scr,
    turn_scr,
    tgt_scr,
    src_scr,
    acc_scr,
    sems,
    out_sem,
):
    clusters, width = disp_ref.shape
    elems = width // 3
    chunks = elems // CHUNK
    size = 3 * chunks

    inputs = start_all(
        sems,
        (
            (pos_hbm, pos_ref),
            (disp_hbm, disp_ref),
            (intact_hbm, intact_ref),
            (stiff_hbm, stiff_ref),
            (list_hbm, list_ref),
        ),
    )
    acc_scr[...] = jnp.zeros_like(acc_scr)
    turn_scr[...] = turn_matrix()

    for k, values in enumerate((pos_ref, disp_ref)):
        inputs[k].wait()
        wide_scr[k, :, 0:width] = values[...]
        for m in range(size):
            pieces = exact_pieces(values[:, m * CHUNK : (m + 1) * CHUNK])
            piece_scr[(k * size + m) * clusters : (k * size + m + 1) * clusters, :] = (
                jnp.concatenate(pieces, axis=1)
            )
    columns = 2 * LANES
    for t in range(SUBLANES * LANES // columns):
        for k in range(2):
            rows = size * clusters
            turned = jnp.dot(
                piece_scr[k * rows : (k + 1) * rows, :],
                turn_scr[:, t * columns : (t + 1) * columns],
                preferred_element_type=jnp.float32,
            )
            for m in range(size):
                for h in range(columns // LANES):
                    s = t * (columns // LANES) + h
                    src_scr[k * size + m, pl.ds(s, clusters, stride=SUBLANES), :] = turned[
                        m * clusters : (m + 1) * clusters, h * LANES : (h + 1) * LANES
                    ]

    def store_target(m, value):
        tgt_scr[m] = value

    replicate(wide_scr[0], chunks, store_target)
    for copy in inputs[2:]:
        copy.wait()
    count = list_ref[3, 0]

    disp = [disp_ref[:, c * elems : (c + 1) * elems] for c in range(3)]
    separation = jnp.sqrt(1.0 + (disp[0] * disp[0] + disp[1] * disp[1] + disp[2] * disp[2]))
    softened = 1.0 - jnp.exp(-(separation - 1.0) / softening)
    intact = intact_ref[...].astype(jnp.float32)
    damage = intact * softened + (1.0 - intact)
    damage_ref[...] = damage
    damage_out = pltpu.make_async_copy(damage_ref, damage_hbm, out_sem)
    damage_out.start()
    hold = (1.0 - damage) * stiff_ref[...]
    for c in range(3):
        out_ref[:, c * elems : (c + 1) * elems] = -hold * disp[c]

    def one_pair(slot):
        target = list_ref[0, slot]
        source = pl.multiple_of(list_ref[1, slot] * SUBLANES, SUBLANES)
        into = pl.multiple_of(list_ref[2, slot], SUBLANES)
        sums = pair_sums(
            lambda m: row_of(tgt_scr, m, target),
            lambda n: src_scr[n, pl.ds(source, SUBLANES), :],
            chunks,
        )
        for m in range(size):
            acc_scr[m, pl.ds(into, SUBLANES), :] += sums[m]

    def step(it, carry):
        for k in range(UNROLL):
            one_pair(it * UNROLL + k)
        return carry

    lax.fori_loop(0, (count + UNROLL - 1) // UNROLL, step, 0)

    def store_sum(t, value):
        wide_scr[0, :, t * LANES : (t + 1) * LANES] = value

    gather_sums(acc_scr, clusters, chunks, store_sum)
    out_ref[...] += wide_scr[0, :, 0:width]
    damage_out.wait()


def near_field(listed, disp, pos, intact, stiffness):
    clusters, width = disp.shape
    elems = width // 3
    chunks = elems // CHUNK
    padded = pl.cdiv(width, LANES) * LANES
    slots = listed.shape[1]
    vmem = pl.BlockSpec(memory_space=pltpu.VMEM)
    return pl.pallas_call(
        near_kernel,
        out_shape=(
            jax.ShapeDtypeStruct((clusters, width), jnp.float32),
            jax.ShapeDtypeStruct(stiffness.shape, jnp.float32),
        ),
        in_specs=in_hbm(5),
        out_specs=(vmem, *in_hbm(1)),
        scratch_shapes=[
            pltpu.SMEM(listed.shape, listed.dtype),
            pltpu.VMEM(disp.shape, disp.dtype),
            pltpu.VMEM(pos.shape, pos.dtype),
            pltpu.VMEM(intact.shape, intact.dtype),
            pltpu.VMEM(stiffness.shape, stiffness.dtype),
            pltpu.VMEM(stiffness.shape, jnp.float32),
            pltpu.VMEM((2, clusters, padded), jnp.float32),
            pltpu.VMEM((6 * chunks * clusters, PIECES * CHUNK), jnp.bfloat16),
            pltpu.VMEM((PIECES * CHUNK, SUBLANES * LANES), jnp.bfloat16),
            pltpu.VMEM((3 * chunks, clusters, LANES), jnp.float32),
            pltpu.VMEM((6 * chunks, clusters * SUBLANES, LANES), jnp.float32),
            pltpu.VMEM((3 * chunks, (clusters + 1) * SUBLANES, LANES), jnp.float32),
            pltpu.SemaphoreType.DMA((5,)),
            pltpu.SemaphoreType.DMA(()),
        ],
        compiler_params=pltpu.CompilerParams(vmem_limit_bytes=VMEM),
        cost_estimate=pl.CostEstimate(
            flops=30 * slots * elems * elems,
            bytes_accessed=4 * clusters * width * 6,
            transcendentals=slots * elems * elems,
        ),
        name="near_field",
    )(listed, *pinned(disp, pos, intact, stiffness))


def finish_kernel(
    rest_hbm,
    pos_hbm,
    received_ref,
    near_ref,
    far_ref,
    out_ref,
    rest_ref,
    pos_ref,
    ext_scr,
    halo_scr,
    tgt_scr,
    src_scr,
    acc_scr,
    sems,
    *,
    rank,
):
    clusters, width = near_ref.shape
    cols = received_ref.shape[0]
    elems = width // 3
    chunks = elems // CHUNK
    size = 3 * chunks
    spare = LANES - rank
    segments = split_rows(width, spare)
    edge = 2 * HALO
    tail = pl.ds(clusters - SUBLANES, SUBLANES)

    inputs = start_all(
        sems,
        (
            (rest_hbm, rest_ref),
            (pos_hbm.at[pl.ds(0, SUBLANES)], pos_ref.at[0]),
            (pos_hbm.at[tail], pos_ref.at[1]),
        ),
    )
    acc_scr[...] = jnp.zeros_like(acc_scr)

    j = lax.axis_index("cols")
    before = jnp.where(j > 0, j - 1, cols - 1)
    after = jnp.where(j < cols - 1, j + 1, 0)
    for start, sender in ((0, before), (HALO, after)):
        halo_scr[...] = received_ref[sender].astype(jnp.float32)
        rows = edge * segments
        whole = halo_scr[0:rows, :]
        for n in range(1, PIECES):
            whole = whole + halo_scr[n * rows : (n + 1) * rows, :]
        for g in range(segments):
            count = min(spare, width - g * spare)
            for k in range(2):
                row = (2 * g + k) * HALO
                ext_scr[k, start : start + HALO, g * spare : g * spare + count] = whole[
                    row : row + HALO, rank : rank + count
                ]
    inputs[1].wait()
    inputs[2].wait()
    ext_scr[1, edge : edge + HALO, 0:width] = pos_ref[0, 0:HALO, :]
    ext_scr[1, edge + HALO : 2 * edge, 0:width] = pos_ref[1, SUBLANES - HALO :, :]
    for k in range(2):

        def store(m, value, k=k):
            for b in range(edge):
                wide = jnp.broadcast_to(value[b : b + 1, :], (SUBLANES, LANES))
                src_scr[(1 - k) * size + m, b * SUBLANES : (b + 1) * SUBLANES, :] = turn(wide)

        replicate(ext_scr[k], chunks, store, True)

    def store_target(m, value):
        tgt_scr[m] = value

    replicate(ext_scr[1], chunks, store_target)
    inputs[0].wait()
    number = rest_ref[6, 0]

    def one_pair(n):
        target = rest_ref[4, n]
        source = rest_ref[5, n]
        target = jnp.where(target < HALO, target, target - (clusters - edge))
        source = jnp.where(source < HALO, source, source - clusters)
        live = n < number
        target = jnp.where(live, target, edge)
        source = pl.multiple_of(jnp.where(live, source, 0) * SUBLANES, SUBLANES)
        into = pl.multiple_of(target * SUBLANES, SUBLANES)
        row = edge + jnp.where(live, target, 0)
        sums = pair_sums(
            lambda m: row_of(tgt_scr, m, row),
            lambda k: src_scr[k, pl.ds(source, SUBLANES), :],
            chunks,
        )
        for m in range(size):
            acc_scr[m, pl.ds(into, SUBLANES), :] += sums[m]

    def step(it, carry):
        for k in range(FEW):
            one_pair(it * FEW + k)
        return carry

    lax.fori_loop(0, (number + FEW - 1) // FEW, step, 0)

    def store_sum(t, value):
        ext_scr[0, :, t * LANES : (t + 1) * LANES] = value

    gather_sums(acc_scr, 2 * edge, chunks, store_sum)
    out_ref[...] = near_ref[...] + far_ref[...]
    out_ref[0:HALO, :] += ext_scr[0, 0:HALO, 0:width]
    out_ref[clusters - HALO :, :] += ext_scr[0, HALO:edge, 0:width]


def finish(rest, pos, received, near, far, rank):
    clusters, width = pos.shape
    chunks = width // 3 // CHUNK
    padded = pl.cdiv(width, LANES) * LANES
    edge = 2 * HALO
    vmem = pl.BlockSpec(memory_space=pltpu.VMEM)
    return pl.pallas_call(
        functools.partial(finish_kernel, rank=rank),
        out_shape=jax.ShapeDtypeStruct((clusters, width), jnp.float32),
        in_specs=in_hbm(2) + [vmem] * 3,
        out_specs=vmem,
        scratch_shapes=[
            pltpu.SMEM(rest.shape, rest.dtype),
            pltpu.VMEM((2, SUBLANES, width), pos.dtype),
            pltpu.VMEM((2, 2 * edge, padded), jnp.float32),
            pltpu.VMEM((clusters, LANES), jnp.float32),
            pltpu.VMEM((3 * chunks, 2 * edge, LANES), jnp.float32),
            pltpu.VMEM((6 * chunks, edge * SUBLANES, LANES), jnp.float32),
            pltpu.VMEM((3 * chunks, 2 * edge * SUBLANES, LANES), jnp.float32),
            pltpu.SemaphoreType.DMA((3,)),
        ],
        compiler_params=pltpu.CompilerParams(vmem_limit_bytes=VMEM),
        cost_estimate=pl.CostEstimate(
            flops=2 * clusters * width, bytes_accessed=16 * clusters * width, transcendentals=0
        ),
        name="finish",
    )(rest, *pinned(pos), received, near, far)


def local(
    displacement,
    positions,
    cluster_basis,
    near_pairs,
    near_count,
    far_pairs,
    far_count,
    far_blocks,
    intact,
    stiffness,
):
    cols = lax.axis_size("cols")
    clusters, width, rank = cluster_basis.shape
    spare = LANES - rank
    segments = split_rows(width, spare)
    disp_bf, halo, listed = prepare(
        near_count, far_count, near_pairs.T, displacement, positions, spare
    )
    coeff = jnp.einsum("kf,kfr->kr", disp_bf, cluster_basis, preferred_element_type=jnp.float32)
    payload = jnp.concatenate([coeff, halo], axis=1)
    gathered = lax.all_gather(payload, "rows", axis=0, tiled=True)
    partial = far_field(
        listed, far_pairs.T, gathered, far_blocks.transpose(1, 2, 0), cols, segments
    )
    received = lax.all_to_all(partial, "cols", split_axis=0, concat_axis=0)
    near, damage = near_field(listed, displacement, positions, intact, stiffness)
    owned = jnp.sum(received[:, :, :rank].astype(jnp.float32), axis=0).astype(jnp.bfloat16)
    far = jnp.einsum("kfr,kr->kf", cluster_basis, owned, preferred_element_type=jnp.float32)
    return finish(listed, positions, received, near, far, rank), damage


def solution(mesh):
    both = ("rows", "cols")
    in_specs = (
        P(both, None),
        P(both, None),
        P(both, None, None),
        P(both, None),
        P(both),
        P(both, None),
        P(both),
        P(both, None, None),
        P(both, None),
        P(both, None),
    )
    out_specs = (P(both, None), P(both, None))
    return jax.shard_map(local, mesh=mesh, in_specs=in_specs, out_specs=out_specs, check_vma=False)
```

```python
import functools

import jax
import jax.numpy as jnp
from jax import lax
from jax.experimental import pallas as pl
from jax.experimental.pallas import tpu as pltpu
from jax.sharding import PartitionSpec as P

HALO = 2
LANES = 128
SUBLANES = 8
CHUNK = 32
GROUPS = LANES // CHUNK
core_square = 0.25
softening = 1.5
UNROLL = 8
TOGETHER = 2
FEW = 4
FOLD = 256
PIECES = 3
VMEM = 20 * 1024 * 1024


def split_rows(width, lanes):
    return pl.cdiv(width, lanes)


def in_hbm(count):
    return [pl.BlockSpec(memory_space=pltpu.HBM)] * count


def pinned(*arrays):
    return [pltpu.with_memory_space_constraint(x, pltpu.HBM) for x in arrays]


def start_all(sems, moves):
    copies = [
        pltpu.make_async_copy(source, target, sems.at[n])
        for n, (source, target) in enumerate(moves)
    ]
    for copy in copies:
        copy.start()
    return copies


def prepare_kernel(
    near_count_ref,
    far_count_ref,
    pairs_hbm,
    disp_hbm,
    pos_hbm,
    intact_hbm,
    stiff_hbm,
    low_ref,
    halo_ref,
    fields_ref,
    damage_ref,
    list_ref,
    pairs_ref,
    intact_ref,
    stiff_ref,
    sems,
):
    _, clusters, width = fields_ref.shape
    pos_ref, disp_ref, base_ref = (fields_ref.at[k] for k in range(3))
    elems = width // 3
    spare = halo_ref.shape[1]
    segments = split_rows(width, spare)
    inputs = start_all(
        sems,
        (
            (pairs_hbm, pairs_ref),
            (disp_hbm, disp_ref),
            (pos_hbm, pos_ref),
            (intact_hbm, intact_ref),
            (stiff_hbm, stiff_ref),
        ),
    )
    halo_ref[...] = jnp.zeros_like(halo_ref)
    for copy in inputs:
        copy.wait()
    list_pairs(pairs_ref, near_count_ref[0], far_count_ref[0], list_ref, clusters)
    low_ref[...] = disp_ref[...].astype(low_ref.dtype)
    row = 0
    for g in range(segments):
        size = min(spare, width - g * spare)
        for start in (0, clusters - HALO):
            for ref in (disp_ref, pos_ref):
                halo_ref[row : row + HALO, 0:size] = ref[
                    start : start + HALO, g * spare : g * spare + size
                ]
                row += HALO

    disp = [disp_ref[:, c * elems : (c + 1) * elems] for c in range(3)]
    separation = jnp.sqrt(1.0 + (disp[0] * disp[0] + disp[1] * disp[1] + disp[2] * disp[2]))
    softened = 1.0 - jnp.exp(-(separation - 1.0) / softening)
    intact = intact_ref[...].astype(jnp.float32)
    damage = intact * softened + (1.0 - intact)
    damage_ref[...] = damage
    hold = (1.0 - damage) * stiff_ref[...]
    for c in range(3):
        base_ref[:, c * elems : (c + 1) * elems] = -hold * disp[c]


def list_pairs(pairs_ref, near_count, far_count, list_ref, clusters):
    slots = pairs_ref.shape[1]
    target = pairs_ref[0:1, :]
    source = pairs_ref[1:2, :]
    live = lax.broadcasted_iota(jnp.int32, (1, slots), 1) < near_count
    own = jnp.logical_and(source >= HALO, source < clusters + HALO)
    list_ref[0:1, :] = target
    list_ref[1:2, :] = jnp.clip(source - HALO, 0, clusters - 1)
    list_ref[2:3, :] = jnp.where(jnp.logical_and(live, own), target, clusters) * SUBLANES
    list_ref[3:4, :] = jnp.full((1, slots), near_count, jnp.int32)
    others = jnp.where(jnp.logical_and(live, jnp.logical_not(own)), 1.0, 0.0)
    square = (slots, slots)
    upto = lax.broadcasted_iota(jnp.int32, square, 0) <= lax.broadcasted_iota(jnp.int32, square, 1)
    upto = jnp.where(upto, 1.0, 0.0).astype(jnp.bfloat16)
    order = jnp.dot(
        jnp.broadcast_to(others, (SUBLANES, slots)).astype(jnp.bfloat16),
        upto,
        preferred_element_type=jnp.float32,
    )
    place = jnp.where(others > 0.0, order[0:1, :] - 1.0, -1.0).astype(jnp.int32)
    place = lax.broadcasted_iota(jnp.int32, square, 0) == place
    place = jnp.where(place, 1.0, 0.0).astype(jnp.bfloat16)
    row = lax.broadcasted_iota(jnp.int32, (SUBLANES, slots), 0)
    listed = jnp.where(row == 0, target, source).astype(jnp.float32).astype(jnp.bfloat16)
    listed = lax.dot_general(
        listed, place, (((1,), (1,)), ((), ())), preferred_element_type=jnp.float32
    ).astype(jnp.int32)
    list_ref[4:6, :] = listed[0:2, :]
    number = jnp.sum(others, axis=1, keepdims=True).astype(jnp.int32)
    list_ref[6:7, :] = jnp.broadcast_to(number, (1, slots))
    list_ref[7:8, :] = jnp.full((1, slots), far_count, jnp.int32)


def prepare(near_count, far_count, pairs, disp, pos, intact, stiffness, spare):
    clusters, width = disp.shape
    slots = pairs.shape[1]
    vmem = pl.BlockSpec(memory_space=pltpu.VMEM)
    smem = pl.BlockSpec(memory_space=pltpu.SMEM)
    return pl.pallas_call(
        prepare_kernel,
        out_shape=(
            jax.ShapeDtypeStruct((clusters, width), jnp.bfloat16),
            jax.ShapeDtypeStruct((clusters, spare), jnp.float32),
            jax.ShapeDtypeStruct((3, clusters, width), jnp.float32),
            jax.ShapeDtypeStruct(stiffness.shape, jnp.float32),
            jax.ShapeDtypeStruct((SUBLANES, slots), jnp.int32),
        ),
        in_specs=[smem] * 2 + in_hbm(5),
        out_specs=(vmem,) * 5,
        scratch_shapes=[
            pltpu.VMEM(pairs.shape, pairs.dtype),
            pltpu.VMEM(intact.shape, intact.dtype),
            pltpu.VMEM(stiffness.shape, stiffness.dtype),
            pltpu.SemaphoreType.DMA((5,)),
        ],
        compiler_params=pltpu.CompilerParams(vmem_limit_bytes=VMEM),
        cost_estimate=pl.CostEstimate(
            flops=20 * clusters * width, bytes_accessed=24 * clusters * width, transcendentals=0
        ),
        name="prepare",
    )(near_count, far_count, *pinned(pairs, disp, pos, intact, stiffness))


def far_kernel(
    list_hbm,
    pairs_hbm,
    gathered_hbm,
    blocks_ref,
    out_ref,
    list_ref,
    pairs_ref,
    gathered_ref,
    buffer,
    column_scr,
    coeff_scr,
    place_scr,
    sum_scr,
    summed_scr,
    halo_scr,
    sems,
    block_sems,
    *,
    segments,
):
    rank, _, slots = buffer.shape
    cols, clusters, _ = out_ref.shape
    targets = cols * clusters
    rows = gathered_ref.shape[0] // clusters
    sources = rows * clusters
    tiles = slots // FOLD

    def fetch(t):
        here = pl.ds(pl.multiple_of(t * FOLD, FOLD), FOLD)
        return pltpu.make_async_copy(
            blocks_ref.at[:, :, here], buffer.at[:, :, here], block_sems.at[t]
        )

    inputs = start_all(
        sems, ((list_hbm, list_ref), (pairs_hbm, pairs_ref), (gathered_hbm, gathered_ref))
    )
    fetch(0).start()
    summed_scr[...] = jnp.zeros_like(summed_scr)
    inputs[0].wait()
    count = list_ref[7, 0]
    live = (count + FOLD - 1) // FOLD
    for t in range(1, tiles):

        @pl.when(t < live)
        def _(t=t):
            fetch(t).start()

    inputs[1].wait()
    inputs[2].wait()
    column_scr[...] = gathered_ref[...].astype(jnp.bfloat16)

    index = lax.broadcasted_iota(jnp.int32, (sources, slots), 0)
    pick = jnp.where(index == pairs_ref[1:2, :], 1.0, 0.0).astype(jnp.bfloat16)
    coeff = lax.dot_general(
        column_scr[...], pick, (((0,), (0,)), ((), ())), preferred_element_type=jnp.float32
    )
    coeff_scr[...] = coeff[0:rank, :]
    slot = lax.broadcasted_iota(jnp.int32, (1, slots), 1)
    wanted = jnp.where(slot < count, pairs_ref[0:1, :], -1)
    index = lax.broadcasted_iota(jnp.int32, (targets, slots), 0)
    place_scr[...] = jnp.where(index == wanted, 1.0, 0.0).astype(jnp.bfloat16)

    def multiply(t, carry):
        start = pl.multiple_of(t * FOLD, FOLD)
        lanes = pl.ds(start, FOLD)
        fetch(t).wait()
        coeff = coeff_scr[:, lanes]
        for r in range(rank):
            product = buffer[r, :, lanes].astype(jnp.float32) * coeff
            folded = product[0:SUBLANES]
            for s in range(1, rank // SUBLANES):
                folded = folded + product[s * SUBLANES : (s + 1) * SUBLANES]
            for h in range(FOLD // LANES):
                sum_scr[h, r * SUBLANES : (r + 1) * SUBLANES, :] = folded[
                    :, h * LANES : (h + 1) * LANES
                ]
        parts = []
        for h in range(FOLD // LANES):
            total = sum_scr[h, pl.ds(0, rank, stride=SUBLANES), :]
            for s in range(1, SUBLANES):
                total = total + sum_scr[h, pl.ds(s, rank, stride=SUBLANES), :]
            parts.append(total)
        coupled = jnp.concatenate(parts, axis=1)
        high = coupled.astype(jnp.bfloat16)
        low = (coupled - high.astype(jnp.float32)).astype(jnp.bfloat16)
        both = jnp.concatenate([high, low], axis=0)
        summed_scr[...] += lax.dot_general(
            place_scr[:, lanes], both, (((1,), (1,)), ((), ())), preferred_element_type=jnp.float32
        )
        return carry

    lax.fori_loop(0, live, multiply, 0)

    i = lax.axis_index("rows")
    j = lax.axis_index("cols")
    from_last = jnp.where(j < cols - 1, i, i - 1)
    from_first = jnp.where(j > 0, i, i + 1)
    edge = 2 * HALO
    halo_scr[...] = jnp.zeros_like(halo_scr)
    sides = (
        (0, jnp.minimum(from_first, rows - 1), from_first < rows),
        (edge, jnp.maximum(from_last, 0), from_last >= 0),
    )
    for side, (row, owner, there) in enumerate(sides):
        start = pl.multiple_of(owner * clusters, clusters)
        whole = jnp.where(there, gathered_ref[pl.ds(start, clusters), :], 0.0)
        for n in range(PIECES):
            piece = whole.astype(jnp.bfloat16).astype(jnp.float32)
            whole = whole - piece
            for g in range(segments):
                to = (n * segments + g) * edge
                here = g * 2 * edge + row
                halo_scr[side, to : to + edge, :] = piece[here : here + edge, :]
    after = jnp.where(j < cols - 1, j + 1, 0)
    lane = lax.broadcasted_iota(jnp.int32, (clusters, LANES), 1)
    for d in range(cols):
        halo = halo_scr[jnp.where(after == d, 1, 0)]
        mine = summed_scr[d * clusters : (d + 1) * clusters, :]
        mine = mine + pltpu.roll(mine, rank, 1)
        out_ref[d] = jnp.where(lane < rank, mine, halo).astype(out_ref.dtype)


def far_field(listed, pairs, gathered, blocks, cols, segments):
    rank, _, slots = blocks.shape
    rows = lax.axis_size("rows")
    clusters = gathered.shape[0] // rows
    return pl.pallas_call(
        functools.partial(far_kernel, segments=segments),
        out_shape=jax.ShapeDtypeStruct((cols, clusters, LANES), jnp.bfloat16),
        in_specs=in_hbm(3) + [pl.BlockSpec(memory_space=pl.ANY)],
        out_specs=pl.BlockSpec(memory_space=pltpu.VMEM),
        scratch_shapes=[
            pltpu.SMEM(listed.shape, listed.dtype),
            pltpu.VMEM(pairs.shape, pairs.dtype),
            pltpu.VMEM(gathered.shape, gathered.dtype),
            pltpu.VMEM(blocks.shape, blocks.dtype),
            pltpu.VMEM((rows * clusters, LANES), jnp.bfloat16),
            pltpu.VMEM((rank, slots), jnp.float32),
            pltpu.VMEM((cols * clusters, slots), jnp.bfloat16),
            pltpu.VMEM((FOLD // LANES, rank * SUBLANES, LANES), jnp.float32),
            pltpu.VMEM((cols * clusters, LANES), jnp.float32),
            pltpu.VMEM((2, clusters, LANES), jnp.float32),
            pltpu.SemaphoreType.DMA((3,)),
            pltpu.SemaphoreType.DMA((slots // FOLD,)),
        ],
        compiler_params=pltpu.CompilerParams(vmem_limit_bytes=VMEM),
        cost_estimate=pl.CostEstimate(
            flops=2 * rank * rank * slots,
            bytes_accessed=2 * rank * rank * slots,
            transcendentals=0,
        ),
        name="far_field",
    )(listed, *pinned(pairs), gathered, *pinned(blocks))


def replicate(rows, chunks, store, turned=False):
    within = lax.broadcasted_iota(jnp.int32, (rows.shape[0], LANES), 1)
    if turned:
        within = within + (within // CHUNK) * SUBLANES
    within = within % CHUNK
    for m in range(3 * chunks):
        tile = m // GROUPS
        store(
            m,
            jnp.take_along_axis(
                rows[:, tile * LANES : (tile + 1) * LANES],
                within + (m % GROUPS) * CHUNK,
                axis=1,
                mode="promise_in_bounds",
            ),
        )


def row_of(ref, n, row):
    return ref[n, pl.ds(row, SUBLANES, stride=0), :]


def turn(wide):
    return pltpu.roll(wide, 0, 1, stride=1, stride_axis=0)


def pair_sums(tgt, src, chunks):
    sums = [None] * (3 * chunks)
    size = 3 * chunks
    for h in range(chunks):
        x = [tgt(c * chunks + h) for c in range(3)]
        for f in range(chunks):
            r = [x[c] - src(c * chunks + f) for c in range(3)]
            u = [src(size + c * chunks + f) for c in range(3)]
            q = (r[0] * r[0] + core_square) + (r[1] * r[1] + r[2] * r[2])
            s = r[0] * u[0] + (r[1] * u[1] + r[2] * u[2])
            inverse = lax.rsqrt(q)
            square = inverse * inverse
            weight = square * inverse
            s = (3.0 * s) * square
            for c in range(3):
                term = weight * (u[c] - s * r[c])
                m = c * chunks + h
                sums[m] = term if sums[m] is None else sums[m] + term
    return sums


def gather_sums(acc_scr, clusters, chunks, store):
    own_group = lax.broadcasted_iota(jnp.int32, (clusters, LANES), 1) // CHUNK
    for t in range(pl.cdiv(3 * chunks, GROUPS)):
        merged = None
        for g in range(GROUPS):
            m = t * GROUPS + g
            if m >= 3 * chunks:
                break
            total = acc_scr[m, pl.ds(0, clusters, stride=SUBLANES), :]
            for s in range(1, SUBLANES):
                total = total + acc_scr[m, pl.ds(s, clusters, stride=SUBLANES), :]
            total = total + pltpu.roll(total, 2 * CHUNK, 1)
            total = total + pltpu.roll(total, CHUNK, 1)
            merged = total if merged is None else jnp.where(own_group == g, total, merged)
        store(t, merged)


def turn_matrix():
    shape = (PIECES * CHUNK, SUBLANES * LANES)
    column = lax.broadcasted_iota(jnp.int32, shape, 1)
    lane = column % LANES
    entry = (lane + (lane // CHUNK) * SUBLANES + column // LANES) % CHUNK
    row = lax.broadcasted_iota(jnp.int32, shape, 0) % CHUNK
    return jnp.where(entry == row, 1.0, 0.0).astype(jnp.bfloat16)


def exact_pieces(value):
    pieces = []
    for _ in range(PIECES):
        piece = value.astype(jnp.bfloat16)
        pieces.append(piece)
        value = value - piece.astype(jnp.float32)
    return pieces


def near_kernel(
    list_hbm,
    fields_ref,
    damage_ref,
    out_ref,
    damage_hbm,
    list_ref,
    wide_scr,
    piece_scr,
    turn_scr,
    tgt_scr,
    src_scr,
    acc_scr,
    sems,
):
    _, clusters, width = fields_ref.shape
    elems = width // 3
    chunks = elems // CHUNK
    size = 3 * chunks

    moves = start_all(sems, ((list_hbm, list_ref), (damage_ref, damage_hbm)))
    acc_scr[...] = jnp.zeros_like(acc_scr)
    turn_scr[...] = turn_matrix()

    wide_scr[:, 0:width] = fields_ref[0]
    for k in range(2):
        for m in range(size):
            pieces = exact_pieces(fields_ref[k, :, m * CHUNK : (m + 1) * CHUNK])
            piece_scr[(k * size + m) * clusters : (k * size + m + 1) * clusters, :] = (
                jnp.concatenate(pieces, axis=1)
            )
    columns = 2 * LANES
    for t in range(SUBLANES * LANES // columns):
        for k in range(2):
            rows = size * clusters
            turned = jnp.dot(
                piece_scr[k * rows : (k + 1) * rows, :],
                turn_scr[:, t * columns : (t + 1) * columns],
                preferred_element_type=jnp.float32,
            )
            for m in range(size):
                for h in range(columns // LANES):
                    s = t * (columns // LANES) + h
                    src_scr[k * size + m, pl.ds(s, clusters, stride=SUBLANES), :] = turned[
                        m * clusters : (m + 1) * clusters, h * LANES : (h + 1) * LANES
                    ]

    def store_target(m, value):
        tgt_scr[m] = value

    replicate(wide_scr[...], chunks, store_target)
    moves[0].wait()
    count = list_ref[3, 0]

    def sums_of(slot):
        target = list_ref[0, slot]
        source = pl.multiple_of(list_ref[1, slot] * SUBLANES, SUBLANES)
        return pair_sums(
            lambda m: row_of(tgt_scr, m, target),
            lambda n: src_scr[n, pl.ds(source, SUBLANES), :],
            chunks,
        )

    def step(it, carry):
        for k in range(0, UNROLL, TOGETHER):
            slots = [it * UNROLL + k + n for n in range(TOGETHER)]
            results = [sums_of(slot) for slot in slots]
            for slot, sums in zip(slots, results):
                into = pl.multiple_of(list_ref[2, slot], SUBLANES)
                for m in range(size):
                    acc_scr[m, pl.ds(into, SUBLANES), :] += sums[m]
        return carry

    lax.fori_loop(0, (count + UNROLL - 1) // UNROLL, step, 0)

    def store_sum(t, value):
        wide_scr[:, t * LANES : (t + 1) * LANES] = value

    gather_sums(acc_scr, clusters, chunks, store_sum)
    out_ref[...] = fields_ref[2] + wide_scr[:, 0:width]
    moves[1].wait()


def near_field(listed, fields, damage):
    _, clusters, width = fields.shape
    elems = width // 3
    chunks = elems // CHUNK
    padded = pl.cdiv(width, LANES) * LANES
    slots = listed.shape[1]
    vmem = pl.BlockSpec(memory_space=pltpu.VMEM)
    return pl.pallas_call(
        near_kernel,
        out_shape=(
            jax.ShapeDtypeStruct((clusters, width), jnp.float32),
            jax.ShapeDtypeStruct(damage.shape, jnp.float32),
        ),
        in_specs=in_hbm(1) + [vmem] * 2,
        out_specs=(vmem, *in_hbm(1)),
        scratch_shapes=[
            pltpu.SMEM(listed.shape, listed.dtype),
            pltpu.VMEM((clusters, padded), jnp.float32),
            pltpu.VMEM((6 * chunks * clusters, PIECES * CHUNK), jnp.bfloat16),
            pltpu.VMEM((PIECES * CHUNK, SUBLANES * LANES), jnp.bfloat16),
            pltpu.VMEM((3 * chunks, clusters, LANES), jnp.float32),
            pltpu.VMEM((6 * chunks, clusters * SUBLANES, LANES), jnp.float32),
            pltpu.VMEM((3 * chunks, (clusters + 1) * SUBLANES, LANES), jnp.float32),
            pltpu.SemaphoreType.DMA((2,)),
        ],
        compiler_params=pltpu.CompilerParams(vmem_limit_bytes=VMEM),
        cost_estimate=pl.CostEstimate(
            flops=30 * slots * elems * elems,
            bytes_accessed=4 * clusters * width * 6,
            transcendentals=slots * elems * elems,
        ),
        name="near_field",
    )(listed, fields, damage)


def finish_kernel(
    rest_hbm,
    pos_hbm,
    received_ref,
    near_ref,
    far_ref,
    out_ref,
    rest_ref,
    pos_ref,
    ext_scr,
    halo_scr,
    tgt_scr,
    src_scr,
    acc_scr,
    sems,
    *,
    rank,
):
    clusters, width = near_ref.shape
    cols = received_ref.shape[0]
    elems = width // 3
    chunks = elems // CHUNK
    size = 3 * chunks
    spare = LANES - rank
    segments = split_rows(width, spare)
    edge = 2 * HALO
    tail = pl.ds(clusters - SUBLANES, SUBLANES)

    inputs = start_all(
        sems,
        (
            (rest_hbm, rest_ref),
            (pos_hbm.at[pl.ds(0, SUBLANES)], pos_ref.at[0]),
            (pos_hbm.at[tail], pos_ref.at[1]),
        ),
    )
    acc_scr[...] = jnp.zeros_like(acc_scr)

    j = lax.axis_index("cols")
    before = jnp.where(j > 0, j - 1, cols - 1)
    after = jnp.where(j < cols - 1, j + 1, 0)
    for start, sender in ((0, before), (HALO, after)):
        halo_scr[...] = received_ref[sender].astype(jnp.float32)
        rows = edge * segments
        whole = halo_scr[0:rows, :]
        for n in range(1, PIECES):
            whole = whole + halo_scr[n * rows : (n + 1) * rows, :]
        for g in range(segments):
            count = min(spare, width - g * spare)
            for k in range(2):
                row = (2 * g + k) * HALO
                ext_scr[k, start : start + HALO, g * spare : g * spare + count] = whole[
                    row : row + HALO, rank : rank + count
                ]
    inputs[1].wait()
    inputs[2].wait()
    ext_scr[1, edge : edge + HALO, 0:width] = pos_ref[0, 0:HALO, :]
    ext_scr[1, edge + HALO : 2 * edge, 0:width] = pos_ref[1, SUBLANES - HALO :, :]
    for k in range(2):

        def store(m, value, k=k):
            for b in range(edge):
                wide = jnp.broadcast_to(value[b : b + 1, :], (SUBLANES, LANES))
                src_scr[(1 - k) * size + m, b * SUBLANES : (b + 1) * SUBLANES, :] = turn(wide)

        replicate(ext_scr[k], chunks, store, True)

    def store_target(m, value):
        tgt_scr[m] = value

    replicate(ext_scr[1], chunks, store_target)
    inputs[0].wait()
    number = rest_ref[6, 0]

    def one_pair(n):
        target = rest_ref[4, n]
        source = rest_ref[5, n]
        target = jnp.where(target < HALO, target, target - (clusters - edge))
        source = jnp.where(source < HALO, source, source - clusters)
        live = n < number
        target = jnp.where(live, target, edge)
        source = pl.multiple_of(jnp.where(live, source, 0) * SUBLANES, SUBLANES)
        into = pl.multiple_of(target * SUBLANES, SUBLANES)
        row = edge + jnp.where(live, target, 0)
        sums = pair_sums(
            lambda m: row_of(tgt_scr, m, row),
            lambda k: src_scr[k, pl.ds(source, SUBLANES), :],
            chunks,
        )
        for m in range(size):
            acc_scr[m, pl.ds(into, SUBLANES), :] += sums[m]

    def step(it, carry):
        for k in range(FEW):
            one_pair(it * FEW + k)
        return carry

    lax.fori_loop(0, (number + FEW - 1) // FEW, step, 0)

    def store_sum(t, value):
        ext_scr[0, :, t * LANES : (t + 1) * LANES] = value

    gather_sums(acc_scr, 2 * edge, chunks, store_sum)
    out_ref[...] = near_ref[...] + far_ref[...]
    out_ref[0:HALO, :] += ext_scr[0, 0:HALO, 0:width]
    out_ref[clusters - HALO :, :] += ext_scr[0, HALO:edge, 0:width]


def finish(rest, pos, received, near, far, rank):
    clusters, width = pos.shape
    chunks = width // 3 // CHUNK
    padded = pl.cdiv(width, LANES) * LANES
    edge = 2 * HALO
    vmem = pl.BlockSpec(memory_space=pltpu.VMEM)
    return pl.pallas_call(
        functools.partial(finish_kernel, rank=rank),
        out_shape=jax.ShapeDtypeStruct((clusters, width), jnp.float32),
        in_specs=in_hbm(2) + [vmem] * 3,
        out_specs=vmem,
        scratch_shapes=[
            pltpu.SMEM(rest.shape, rest.dtype),
            pltpu.VMEM((2, SUBLANES, width), pos.dtype),
            pltpu.VMEM((2, 2 * edge, padded), jnp.float32),
            pltpu.VMEM((clusters, LANES), jnp.float32),
            pltpu.VMEM((3 * chunks, 2 * edge, LANES), jnp.float32),
            pltpu.VMEM((6 * chunks, edge * SUBLANES, LANES), jnp.float32),
            pltpu.VMEM((3 * chunks, 2 * edge * SUBLANES, LANES), jnp.float32),
            pltpu.SemaphoreType.DMA((3,)),
        ],
        compiler_params=pltpu.CompilerParams(vmem_limit_bytes=VMEM),
        cost_estimate=pl.CostEstimate(
            flops=2 * clusters * width, bytes_accessed=16 * clusters * width, transcendentals=0
        ),
        name="finish",
    )(rest, *pinned(pos), received, near, far)


def local(
    displacement,
    positions,
    cluster_basis,
    near_pairs,
    near_count,
    far_pairs,
    far_count,
    far_blocks,
    intact,
    stiffness,
):
    cols = lax.axis_size("cols")
    clusters, width, rank = cluster_basis.shape
    spare = LANES - rank
    segments = split_rows(width, spare)
    disp_bf, halo, fields, damage, listed = prepare(
        near_count, far_count, near_pairs.T, displacement, positions, intact, stiffness, spare
    )
    coeff = jnp.einsum("kf,kfr->kr", disp_bf, cluster_basis, preferred_element_type=jnp.float32)
    payload = jnp.concatenate([coeff, halo], axis=1)
    gathered = lax.all_gather(payload, "rows", axis=0, tiled=True)
    partial = far_field(
        listed, far_pairs.T, gathered, far_blocks.transpose(1, 2, 0), cols, segments
    )
    received = lax.all_to_all(partial, "cols", split_axis=0, concat_axis=0)
    near, damage = near_field(listed, fields, damage)
    owned = jnp.sum(received[:, :, :rank].astype(jnp.float32), axis=0).astype(jnp.bfloat16)
    far = jnp.einsum("kfr,kr->kf", cluster_basis, owned, preferred_element_type=jnp.float32)
    return finish(listed, positions, received, near, far, rank), damage


def solution(mesh):
    both = ("rows", "cols")
    in_specs = (
        P(both, None),
        P(both, None),
        P(both, None, None),
        P(both, None),
        P(both),
        P(both, None),
        P(both),
        P(both, None, None),
        P(both, None),
        P(both, None),
    )
    out_specs = (P(both, None), P(both, None))
    return jax.shard_map(local, mesh=mesh, in_specs=in_specs, out_specs=out_specs, check_vma=False)
```

```python
import functools

import jax
import jax.numpy as jnp
from jax import lax
from jax.experimental import pallas as pl
from jax.experimental.pallas import tpu as pltpu
from jax.sharding import PartitionSpec as P

HALO = 2
LANES = 128
SUBLANES = 8
CHUNK = 32
GROUPS = LANES // CHUNK
core_square = 0.25
softening = 1.5
UNROLL = 8
TOGETHER = 2
FEW = 4
FOLD = 256
PIECES = 3
VMEM = 20 * 1024 * 1024


def split_rows(width, lanes):
    return pl.cdiv(width, lanes)


def in_hbm(count):
    return [pl.BlockSpec(memory_space=pltpu.HBM)] * count


def pinned(*arrays):
    return [pltpu.with_memory_space_constraint(x, pltpu.HBM) for x in arrays]


def start_all(sems, moves):
    copies = [
        pltpu.make_async_copy(source, target, sems.at[n])
        for n, (source, target) in enumerate(moves)
    ]
    for copy in copies:
        copy.start()
    return copies


def prepare_kernel(
    near_count_ref,
    far_count_ref,
    pairs_hbm,
    disp_hbm,
    pos_hbm,
    intact_hbm,
    stiff_hbm,
    low_ref,
    halo_ref,
    fields_ref,
    damage_ref,
    list_ref,
    pairs_ref,
    intact_ref,
    stiff_ref,
    sems,
):
    _, clusters, width = fields_ref.shape
    pos_ref, disp_ref, base_ref = (fields_ref.at[k] for k in range(3))
    elems = width // 3
    spare = halo_ref.shape[1]
    segments = split_rows(width, spare)
    inputs = start_all(
        sems,
        (
            (pairs_hbm, pairs_ref),
            (disp_hbm, disp_ref),
            (pos_hbm, pos_ref),
            (intact_hbm, intact_ref),
            (stiff_hbm, stiff_ref),
        ),
    )
    halo_ref[...] = jnp.zeros_like(halo_ref)
    for copy in inputs:
        copy.wait()
    list_pairs(pairs_ref, near_count_ref[0], far_count_ref[0], list_ref, clusters)
    low_ref[...] = disp_ref[...].astype(low_ref.dtype)
    row = 0
    for g in range(segments):
        size = min(spare, width - g * spare)
        for start in (0, clusters - HALO):
            for ref in (disp_ref, pos_ref):
                halo_ref[row : row + HALO, 0:size] = ref[
                    start : start + HALO, g * spare : g * spare + size
                ]
                row += HALO

    disp = [disp_ref[:, c * elems : (c + 1) * elems] for c in range(3)]
    separation = jnp.sqrt(1.0 + (disp[0] * disp[0] + disp[1] * disp[1] + disp[2] * disp[2]))
    softened = 1.0 - jnp.exp(-(separation - 1.0) / softening)
    intact = intact_ref[...].astype(jnp.float32)
    damage = intact * softened + (1.0 - intact)
    damage_ref[...] = damage
    hold = (1.0 - damage) * stiff_ref[...]
    for c in range(3):
        base_ref[:, c * elems : (c + 1) * elems] = -hold * disp[c]


def list_pairs(pairs_ref, near_count, far_count, list_ref, clusters):
    slots = pairs_ref.shape[1]
    target = pairs_ref[0:1, :]
    source = pairs_ref[1:2, :]
    live = lax.broadcasted_iota(jnp.int32, (1, slots), 1) < near_count
    own = jnp.logical_and(source >= HALO, source < clusters + HALO)
    list_ref[0:1, :] = target
    list_ref[1:2, :] = jnp.clip(source - HALO, 0, clusters - 1)
    list_ref[2:3, :] = jnp.where(jnp.logical_and(live, own), target, clusters) * SUBLANES
    list_ref[3:4, :] = jnp.full((1, slots), near_count, jnp.int32)
    others = jnp.where(jnp.logical_and(live, jnp.logical_not(own)), 1.0, 0.0)
    square = (slots, slots)
    upto = lax.broadcasted_iota(jnp.int32, square, 0) <= lax.broadcasted_iota(jnp.int32, square, 1)
    upto = jnp.where(upto, 1.0, 0.0).astype(jnp.bfloat16)
    order = jnp.dot(
        jnp.broadcast_to(others, (SUBLANES, slots)).astype(jnp.bfloat16),
        upto,
        preferred_element_type=jnp.float32,
    )
    place = jnp.where(others > 0.0, order[0:1, :] - 1.0, -1.0).astype(jnp.int32)
    place = lax.broadcasted_iota(jnp.int32, square, 0) == place
    place = jnp.where(place, 1.0, 0.0).astype(jnp.bfloat16)
    row = lax.broadcasted_iota(jnp.int32, (SUBLANES, slots), 0)
    listed = jnp.where(row == 0, target, source).astype(jnp.float32).astype(jnp.bfloat16)
    listed = lax.dot_general(
        listed, place, (((1,), (1,)), ((), ())), preferred_element_type=jnp.float32
    ).astype(jnp.int32)
    list_ref[4:6, :] = listed[0:2, :]
    number = jnp.sum(others, axis=1, keepdims=True).astype(jnp.int32)
    list_ref[6:7, :] = jnp.broadcast_to(number, (1, slots))
    list_ref[7:8, :] = jnp.full((1, slots), far_count, jnp.int32)


def prepare(near_count, far_count, pairs, disp, pos, intact, stiffness, spare):
    clusters, width = disp.shape
    slots = pairs.shape[1]
    vmem = pl.BlockSpec(memory_space=pltpu.VMEM)
    smem = pl.BlockSpec(memory_space=pltpu.SMEM)
    return pl.pallas_call(
        prepare_kernel,
        out_shape=(
            jax.ShapeDtypeStruct((clusters, width), jnp.bfloat16),
            jax.ShapeDtypeStruct((clusters, spare), jnp.float32),
            pltpu.VMEM((3, clusters, width), jnp.float32),
            jax.ShapeDtypeStruct(stiffness.shape, jnp.float32),
            jax.ShapeDtypeStruct((SUBLANES, slots), jnp.int32),
        ),
        in_specs=[smem] * 2 + in_hbm(5),
        out_specs=(vmem,) * 5,
        scratch_shapes=[
            pltpu.VMEM(pairs.shape, pairs.dtype),
            pltpu.VMEM(intact.shape, intact.dtype),
            pltpu.VMEM(stiffness.shape, stiffness.dtype),
            pltpu.SemaphoreType.DMA((5,)),
        ],
        compiler_params=pltpu.CompilerParams(vmem_limit_bytes=VMEM),
        cost_estimate=pl.CostEstimate(
            flops=20 * clusters * width, bytes_accessed=24 * clusters * width, transcendentals=0
        ),
        name="prepare",
    )(near_count, far_count, *pinned(pairs, disp, pos, intact, stiffness))


def far_kernel(
    list_hbm,
    pairs_hbm,
    gathered_hbm,
    blocks_ref,
    out_ref,
    list_ref,
    pairs_ref,
    gathered_ref,
    buffer,
    column_scr,
    coeff_scr,
    place_scr,
    sum_scr,
    summed_scr,
    halo_scr,
    sems,
    block_sems,
    *,
    segments,
):
    rank, _, slots = buffer.shape
    cols, clusters, _ = out_ref.shape
    targets = cols * clusters
    rows = gathered_ref.shape[0] // clusters
    sources = rows * clusters
    tiles = slots // FOLD

    def fetch(t):
        here = pl.ds(pl.multiple_of(t * FOLD, FOLD), FOLD)
        return pltpu.make_async_copy(
            blocks_ref.at[:, :, here], buffer.at[:, :, here], block_sems.at[t]
        )

    inputs = start_all(
        sems, ((list_hbm, list_ref), (pairs_hbm, pairs_ref), (gathered_hbm, gathered_ref))
    )
    fetch(0).start()
    summed_scr[...] = jnp.zeros_like(summed_scr)
    inputs[0].wait()
    count = list_ref[7, 0]
    live = (count + FOLD - 1) // FOLD
    for t in range(1, tiles):

        @pl.when(t < live)
        def _(t=t):
            fetch(t).start()

    inputs[1].wait()
    inputs[2].wait()
    column_scr[...] = gathered_ref[...].astype(jnp.bfloat16)

    index = lax.broadcasted_iota(jnp.int32, (sources, slots), 0)
    pick = jnp.where(index == pairs_ref[1:2, :], 1.0, 0.0).astype(jnp.bfloat16)
    coeff = lax.dot_general(
        column_scr[...], pick, (((0,), (0,)), ((), ())), preferred_element_type=jnp.float32
    )
    coeff_scr[...] = coeff[0:rank, :]
    slot = lax.broadcasted_iota(jnp.int32, (1, slots), 1)
    wanted = jnp.where(slot < count, pairs_ref[0:1, :], -1)
    index = lax.broadcasted_iota(jnp.int32, (targets, slots), 0)
    place_scr[...] = jnp.where(index == wanted, 1.0, 0.0).astype(jnp.bfloat16)

    def multiply(t, carry):
        start = pl.multiple_of(t * FOLD, FOLD)
        lanes = pl.ds(start, FOLD)
        fetch(t).wait()
        coeff = coeff_scr[:, lanes]
        for r in range(rank):
            product = buffer[r, :, lanes].astype(jnp.float32) * coeff
            folded = product[0:SUBLANES]
            for s in range(1, rank // SUBLANES):
                folded = folded + product[s * SUBLANES : (s + 1) * SUBLANES]
            for h in range(FOLD // LANES):
                sum_scr[h, r * SUBLANES : (r + 1) * SUBLANES, :] = folded[
                    :, h * LANES : (h + 1) * LANES
                ]
        parts = []
        for h in range(FOLD // LANES):
            total = sum_scr[h, pl.ds(0, rank, stride=SUBLANES), :]
            for s in range(1, SUBLANES):
                total = total + sum_scr[h, pl.ds(s, rank, stride=SUBLANES), :]
            parts.append(total)
        coupled = jnp.concatenate(parts, axis=1)
        high = coupled.astype(jnp.bfloat16)
        low = (coupled - high.astype(jnp.float32)).astype(jnp.bfloat16)
        both = jnp.concatenate([high, low], axis=0)
        summed_scr[...] += lax.dot_general(
            place_scr[:, lanes], both, (((1,), (1,)), ((), ())), preferred_element_type=jnp.float32
        )
        return carry

    lax.fori_loop(0, live, multiply, 0)

    i = lax.axis_index("rows")
    j = lax.axis_index("cols")
    from_last = jnp.where(j < cols - 1, i, i - 1)
    from_first = jnp.where(j > 0, i, i + 1)
    edge = 2 * HALO
    halo_scr[...] = jnp.zeros_like(halo_scr)
    sides = (
        (0, jnp.minimum(from_first, rows - 1), from_first < rows),
        (edge, jnp.maximum(from_last, 0), from_last >= 0),
    )
    for side, (row, owner, there) in enumerate(sides):
        start = pl.multiple_of(owner * clusters, clusters)
        whole = jnp.where(there, gathered_ref[pl.ds(start, clusters), :], 0.0)
        for n in range(PIECES):
            piece = whole.astype(jnp.bfloat16).astype(jnp.float32)
            whole = whole - piece
            for g in range(segments):
                to = (n * segments + g) * edge
                here = g * 2 * edge + row
                halo_scr[side, to : to + edge, :] = piece[here : here + edge, :]
    after = jnp.where(j < cols - 1, j + 1, 0)
    lane = lax.broadcasted_iota(jnp.int32, (clusters, LANES), 1)
    for d in range(cols):
        halo = halo_scr[jnp.where(after == d, 1, 0)]
        mine = summed_scr[d * clusters : (d + 1) * clusters, :]
        mine = mine + pltpu.roll(mine, rank, 1)
        out_ref[d] = jnp.where(lane < rank, mine, halo).astype(out_ref.dtype)


def far_field(listed, pairs, gathered, blocks, cols, segments):
    rank, _, slots = blocks.shape
    rows = lax.axis_size("rows")
    clusters = gathered.shape[0] // rows
    return pl.pallas_call(
        functools.partial(far_kernel, segments=segments),
        out_shape=jax.ShapeDtypeStruct((cols, clusters, LANES), jnp.bfloat16),
        in_specs=in_hbm(3) + [pl.BlockSpec(memory_space=pl.ANY)],
        out_specs=pl.BlockSpec(memory_space=pltpu.VMEM),
        scratch_shapes=[
            pltpu.SMEM(listed.shape, listed.dtype),
            pltpu.VMEM(pairs.shape, pairs.dtype),
            pltpu.VMEM(gathered.shape, gathered.dtype),
            pltpu.VMEM(blocks.shape, blocks.dtype),
            pltpu.VMEM((rows * clusters, LANES), jnp.bfloat16),
            pltpu.VMEM((rank, slots), jnp.float32),
            pltpu.VMEM((cols * clusters, slots), jnp.bfloat16),
            pltpu.VMEM((FOLD // LANES, rank * SUBLANES, LANES), jnp.float32),
            pltpu.VMEM((cols * clusters, LANES), jnp.float32),
            pltpu.VMEM((2, clusters, LANES), jnp.float32),
            pltpu.SemaphoreType.DMA((3,)),
            pltpu.SemaphoreType.DMA((slots // FOLD,)),
        ],
        compiler_params=pltpu.CompilerParams(vmem_limit_bytes=VMEM),
        cost_estimate=pl.CostEstimate(
            flops=2 * rank * rank * slots,
            bytes_accessed=2 * rank * rank * slots,
            transcendentals=0,
        ),
        name="far_field",
    )(listed, *pinned(pairs), gathered, *pinned(blocks))


def replicate(rows, chunks, store, turned=False):
    within = lax.broadcasted_iota(jnp.int32, (rows.shape[0], LANES), 1)
    if turned:
        within = within + (within // CHUNK) * SUBLANES
    within = within % CHUNK
    for m in range(3 * chunks):
        tile = m // GROUPS
        store(
            m,
            jnp.take_along_axis(
                rows[:, tile * LANES : (tile + 1) * LANES],
                within + (m % GROUPS) * CHUNK,
                axis=1,
                mode="promise_in_bounds",
            ),
        )


def row_of(ref, n, row):
    return ref[n, pl.ds(row, SUBLANES, stride=0), :]


def turn(wide):
    return pltpu.roll(wide, 0, 1, stride=1, stride_axis=0)


def pair_sums(tgt, src, chunks):
    sums = [None] * (3 * chunks)
    size = 3 * chunks
    for h in range(chunks):
        x = [tgt(c * chunks + h) for c in range(3)]
        for f in range(chunks):
            r = [x[c] - src(c * chunks + f) for c in range(3)]
            u = [src(size + c * chunks + f) for c in range(3)]
            q = (r[0] * r[0] + core_square) + (r[1] * r[1] + r[2] * r[2])
            s = r[0] * u[0] + (r[1] * u[1] + r[2] * u[2])
            inverse = lax.rsqrt(q)
            square = inverse * inverse
            weight = square * inverse
            s = (3.0 * s) * square
            for c in range(3):
                term = weight * (u[c] - s * r[c])
                m = c * chunks + h
                sums[m] = term if sums[m] is None else sums[m] + term
    return sums


def gather_sums(acc_scr, clusters, chunks, store):
    own_group = lax.broadcasted_iota(jnp.int32, (clusters, LANES), 1) // CHUNK
    for t in range(pl.cdiv(3 * chunks, GROUPS)):
        merged = None
        for g in range(GROUPS):
            m = t * GROUPS + g
            if m >= 3 * chunks:
                break
            total = acc_scr[m, pl.ds(0, clusters, stride=SUBLANES), :]
            for s in range(1, SUBLANES):
                total = total + acc_scr[m, pl.ds(s, clusters, stride=SUBLANES), :]
            total = total + pltpu.roll(total, 2 * CHUNK, 1)
            total = total + pltpu.roll(total, CHUNK, 1)
            merged = total if merged is None else jnp.where(own_group == g, total, merged)
        store(t, merged)


def turn_matrix():
    shape = (PIECES * CHUNK, SUBLANES * LANES)
    column = lax.broadcasted_iota(jnp.int32, shape, 1)
    lane = column % LANES
    entry = (lane + (lane // CHUNK) * SUBLANES + column // LANES) % CHUNK
    row = lax.broadcasted_iota(jnp.int32, shape, 0) % CHUNK
    return jnp.where(entry == row, 1.0, 0.0).astype(jnp.bfloat16)


def exact_pieces(value):
    pieces = []
    for _ in range(PIECES):
        piece = value.astype(jnp.bfloat16)
        pieces.append(piece)
        value = value - piece.astype(jnp.float32)
    return pieces


def near_kernel(
    list_hbm,
    fields_ref,
    damage_ref,
    out_ref,
    edge_ref,
    damage_hbm,
    list_ref,
    wide_scr,
    piece_scr,
    turn_scr,
    tgt_scr,
    src_scr,
    acc_scr,
    sems,
):
    _, clusters, width = fields_ref.shape
    elems = width // 3
    chunks = elems // CHUNK
    size = 3 * chunks

    moves = start_all(sems, ((list_hbm, list_ref), (damage_ref, damage_hbm)))
    acc_scr[...] = jnp.zeros_like(acc_scr)
    turn_scr[...] = turn_matrix()

    wide_scr[:, 0:width] = fields_ref[0]
    edge_ref[0:HALO, :] = fields_ref[0, 0:HALO, :]
    edge_ref[HALO:, :] = fields_ref[0, clusters - HALO :, :]
    for k in range(2):
        for m in range(size):
            pieces = exact_pieces(fields_ref[k, :, m * CHUNK : (m + 1) * CHUNK])
            piece_scr[(k * size + m) * clusters : (k * size + m + 1) * clusters, :] = (
                jnp.concatenate(pieces, axis=1)
            )
    columns = 2 * LANES
    for t in range(SUBLANES * LANES // columns):
        for k in range(2):
            rows = size * clusters
            turned = jnp.dot(
                piece_scr[k * rows : (k + 1) * rows, :],
                turn_scr[:, t * columns : (t + 1) * columns],
                preferred_element_type=jnp.float32,
            )
            for m in range(size):
                for h in range(columns // LANES):
                    s = t * (columns // LANES) + h
                    src_scr[k * size + m, pl.ds(s, clusters, stride=SUBLANES), :] = turned[
                        m * clusters : (m + 1) * clusters, h * LANES : (h + 1) * LANES
                    ]

    def store_target(m, value):
        tgt_scr[m] = value

    replicate(wide_scr[...], chunks, store_target)
    moves[0].wait()
    count = list_ref[3, 0]

    def sums_of(slot):
        target = list_ref[0, slot]
        source = pl.multiple_of(list_ref[1, slot] * SUBLANES, SUBLANES)
        return pair_sums(
            lambda m: row_of(tgt_scr, m, target),
            lambda n: src_scr[n, pl.ds(source, SUBLANES), :],
            chunks,
        )

    def step(it, carry):
        for k in range(0, UNROLL, TOGETHER):
            slots = [it * UNROLL + k + n for n in range(TOGETHER)]
            results = [sums_of(slot) for slot in slots]
            for slot, sums in zip(slots, results):
                into = pl.multiple_of(list_ref[2, slot], SUBLANES)
                for m in range(size):
                    acc_scr[m, pl.ds(into, SUBLANES), :] += sums[m]
        return carry

    lax.fori_loop(0, (count + UNROLL - 1) // UNROLL, step, 0)

    def store_sum(t, value):
        wide_scr[:, t * LANES : (t + 1) * LANES] = value

    gather_sums(acc_scr, clusters, chunks, store_sum)
    out_ref[...] = fields_ref[2] + wide_scr[:, 0:width]
    moves[1].wait()


def near_field(listed, fields, damage):
    _, clusters, width = fields.shape
    elems = width // 3
    chunks = elems // CHUNK
    padded = pl.cdiv(width, LANES) * LANES
    slots = listed.shape[1]
    vmem = pl.BlockSpec(memory_space=pltpu.VMEM)
    return pl.pallas_call(
        near_kernel,
        out_shape=(
            jax.ShapeDtypeStruct((clusters, width), jnp.float32),
            jax.ShapeDtypeStruct((2 * HALO, width), jnp.float32),
            jax.ShapeDtypeStruct(damage.shape, jnp.float32),
        ),
        in_specs=in_hbm(1) + [vmem] * 2,
        out_specs=(vmem, vmem, *in_hbm(1)),
        scratch_shapes=[
            pltpu.SMEM(listed.shape, listed.dtype),
            pltpu.VMEM((clusters, padded), jnp.float32),
            pltpu.VMEM((6 * chunks * clusters, PIECES * CHUNK), jnp.bfloat16),
            pltpu.VMEM((PIECES * CHUNK, SUBLANES * LANES), jnp.bfloat16),
            pltpu.VMEM((3 * chunks, clusters, LANES), jnp.float32),
            pltpu.VMEM((6 * chunks, clusters * SUBLANES, LANES), jnp.float32),
            pltpu.VMEM((3 * chunks, (clusters + 1) * SUBLANES, LANES), jnp.float32),
            pltpu.SemaphoreType.DMA((2,)),
        ],
        compiler_params=pltpu.CompilerParams(vmem_limit_bytes=VMEM),
        cost_estimate=pl.CostEstimate(
            flops=30 * slots * elems * elems,
            bytes_accessed=4 * clusters * width * 6,
            transcendentals=slots * elems * elems,
        ),
        name="near_field",
    )(listed, pltpu.with_memory_space_constraint(fields, pltpu.VMEM), damage)


def finish_kernel(
    rest_hbm,
    edge_ref,
    received_ref,
    near_ref,
    far_ref,
    out_ref,
    rest_ref,
    ext_scr,
    halo_scr,
    tgt_scr,
    src_scr,
    acc_scr,
    sem,
    *,
    rank,
):
    clusters, width = near_ref.shape
    cols = received_ref.shape[0]
    elems = width // 3
    chunks = elems // CHUNK
    size = 3 * chunks
    spare = LANES - rank
    segments = split_rows(width, spare)
    edge = 2 * HALO

    fetch = pltpu.make_async_copy(rest_hbm, rest_ref, sem)
    fetch.start()
    acc_scr[...] = jnp.zeros_like(acc_scr)

    j = lax.axis_index("cols")
    before = jnp.where(j > 0, j - 1, cols - 1)
    after = jnp.where(j < cols - 1, j + 1, 0)
    for start, sender in ((0, before), (HALO, after)):
        halo_scr[...] = received_ref[sender].astype(jnp.float32)
        rows = edge * segments
        whole = halo_scr[0:rows, :]
        for n in range(1, PIECES):
            whole = whole + halo_scr[n * rows : (n + 1) * rows, :]
        for g in range(segments):
            count = min(spare, width - g * spare)
            for k in range(2):
                row = (2 * g + k) * HALO
                ext_scr[k, start : start + HALO, g * spare : g * spare + count] = whole[
                    row : row + HALO, rank : rank + count
                ]
    ext_scr[1, edge : 2 * edge, 0:width] = edge_ref[...]
    for k in range(2):

        def store(m, value, k=k):
            for b in range(edge):
                wide = jnp.broadcast_to(value[b : b + 1, :], (SUBLANES, LANES))
                src_scr[(1 - k) * size + m, b * SUBLANES : (b + 1) * SUBLANES, :] = turn(wide)

        replicate(ext_scr[k], chunks, store, True)

    def store_target(m, value):
        tgt_scr[m] = value

    replicate(ext_scr[1], chunks, store_target)
    fetch.wait()
    number = rest_ref[6, 0]

    def one_pair(n):
        target = rest_ref[4, n]
        source = rest_ref[5, n]
        target = jnp.where(target < HALO, target, target - (clusters - edge))
        source = jnp.where(source < HALO, source, source - clusters)
        live = n < number
        target = jnp.where(live, target, edge)
        source = pl.multiple_of(jnp.where(live, source, 0) * SUBLANES, SUBLANES)
        into = pl.multiple_of(target * SUBLANES, SUBLANES)
        row = edge + jnp.where(live, target, 0)
        sums = pair_sums(
            lambda m: row_of(tgt_scr, m, row),
            lambda k: src_scr[k, pl.ds(source, SUBLANES), :],
            chunks,
        )
        for m in range(size):
            acc_scr[m, pl.ds(into, SUBLANES), :] += sums[m]

    def step(it, carry):
        for k in range(FEW):
            one_pair(it * FEW + k)
        return carry

    lax.fori_loop(0, (number + FEW - 1) // FEW, step, 0)

    def store_sum(t, value):
        ext_scr[0, :, t * LANES : (t + 1) * LANES] = value

    gather_sums(acc_scr, 2 * edge, chunks, store_sum)
    out_ref[...] = near_ref[...] + far_ref[...]
    out_ref[0:HALO, :] += ext_scr[0, 0:HALO, 0:width]
    out_ref[clusters - HALO :, :] += ext_scr[0, HALO:edge, 0:width]


def finish(rest, edges, received, near, far, rank):
    clusters, width = near.shape
    chunks = width // 3 // CHUNK
    padded = pl.cdiv(width, LANES) * LANES
    edge = 2 * HALO
    vmem = pl.BlockSpec(memory_space=pltpu.VMEM)
    return pl.pallas_call(
        functools.partial(finish_kernel, rank=rank),
        out_shape=jax.ShapeDtypeStruct((clusters, width), jnp.float32),
        in_specs=in_hbm(1) + [vmem] * 4,
        out_specs=vmem,
        scratch_shapes=[
            pltpu.SMEM(rest.shape, rest.dtype),
            pltpu.VMEM((2, 2 * edge, padded), jnp.float32),
            pltpu.VMEM((clusters, LANES), jnp.float32),
            pltpu.VMEM((3 * chunks, 2 * edge, LANES), jnp.float32),
            pltpu.VMEM((6 * chunks, edge * SUBLANES, LANES), jnp.float32),
            pltpu.VMEM((3 * chunks, 2 * edge * SUBLANES, LANES), jnp.float32),
            pltpu.SemaphoreType.DMA(()),
        ],
        compiler_params=pltpu.CompilerParams(vmem_limit_bytes=VMEM),
        cost_estimate=pl.CostEstimate(
            flops=2 * clusters * width, bytes_accessed=16 * clusters * width, transcendentals=0
        ),
        name="finish",
    )(rest, edges, received, near, far)


def local(
    displacement,
    positions,
    cluster_basis,
    near_pairs,
    near_count,
    far_pairs,
    far_count,
    far_blocks,
    intact,
    stiffness,
):
    cols = lax.axis_size("cols")
    clusters, width, rank = cluster_basis.shape
    spare = LANES - rank
    segments = split_rows(width, spare)
    disp_bf, halo, fields, damage, listed = prepare(
        near_count, far_count, near_pairs.T, displacement, positions, intact, stiffness, spare
    )
    coeff = jnp.einsum("kf,kfr->kr", disp_bf, cluster_basis, preferred_element_type=jnp.float32)
    payload = jnp.concatenate([coeff, halo], axis=1)
    gathered = lax.all_gather(payload, "rows", axis=0, tiled=True)
    partial = far_field(
        listed, far_pairs.T, gathered, far_blocks.transpose(1, 2, 0), cols, segments
    )
    received = lax.all_to_all(partial, "cols", split_axis=0, concat_axis=0)
    near, edges, damage = near_field(listed, fields, damage)
    owned = jnp.sum(received[:, :, :rank].astype(jnp.float32), axis=0).astype(jnp.bfloat16)
    far = jnp.einsum("kfr,kr->kf", cluster_basis, owned, preferred_element_type=jnp.float32)
    return finish(listed, edges, received, near, far, rank), damage


def solution(mesh):
    both = ("rows", "cols")
    in_specs = (
        P(both, None),
        P(both, None),
        P(both, None, None),
        P(both, None),
        P(both),
        P(both, None),
        P(both),
        P(both, None, None),
        P(both, None),
        P(both, None),
    )
    out_specs = (P(both, None), P(both, None))
    return jax.shard_map(local, mesh=mesh, in_specs=in_specs, out_specs=out_specs, check_vma=False)
```

```python
import functools

import jax
import jax.numpy as jnp
from jax import lax
from jax.experimental import pallas as pl
from jax.experimental.pallas import tpu as pltpu
from jax.sharding import PartitionSpec as P

HALO = 2
LANES = 128
SUBLANES = 8
CHUNK = 32
GROUPS = LANES // CHUNK
core_square = 0.25
softening = 1.5
UNROLL = 8
TOGETHER = 2
FEW = 4
FOLD = 256
PIECES = 3
VMEM = 20 * 1024 * 1024


def split_rows(width, lanes):
    return pl.cdiv(width, lanes)


def in_hbm(count):
    return [pl.BlockSpec(memory_space=pltpu.HBM)] * count


def pinned(*arrays):
    return [pltpu.with_memory_space_constraint(x, pltpu.HBM) for x in arrays]


def start_all(sems, moves):
    copies = [
        pltpu.make_async_copy(source, target, sems.at[n])
        for n, (source, target) in enumerate(moves)
    ]
    for copy in copies:
        copy.start()
    return copies


def prepare_kernel(
    near_count_ref,
    far_count_ref,
    disp_hbm,
    pos_hbm,
    low_ref,
    halo_ref,
    counts_ref,
    disp_ref,
    pos_ref,
    sems,
):
    clusters, width = disp_ref.shape
    spare = halo_ref.shape[1]
    segments = split_rows(width, spare)
    inputs = start_all(sems, ((disp_hbm, disp_ref), (pos_hbm, pos_ref)))
    halo_ref[...] = jnp.zeros_like(halo_ref)
    row = lax.broadcasted_iota(jnp.int32, counts_ref.shape, 0)
    counts_ref[...] = jnp.where(row == 0, near_count_ref[0], far_count_ref[0])
    for copy in inputs:
        copy.wait()
    low_ref[...] = disp_ref[...].astype(low_ref.dtype)
    row = 0
    for g in range(segments):
        size = min(spare, width - g * spare)
        for start in (0, clusters - HALO):
            for ref in (disp_ref, pos_ref):
                halo_ref[row : row + HALO, 0:size] = ref[
                    start : start + HALO, g * spare : g * spare + size
                ]
                row += HALO


def list_pairs(pairs_ref, near_count, list_ref, clusters):
    slots = pairs_ref.shape[1]
    target = pairs_ref[0:1, :]
    source = pairs_ref[1:2, :]
    live = lax.broadcasted_iota(jnp.int32, (1, slots), 1) < near_count
    own = jnp.logical_and(source >= HALO, source < clusters + HALO)
    list_ref[0:1, :] = target
    list_ref[1:2, :] = jnp.clip(source - HALO, 0, clusters - 1)
    list_ref[2:3, :] = jnp.where(jnp.logical_and(live, own), target, clusters) * SUBLANES
    list_ref[3:4, :] = jnp.full((1, slots), near_count, jnp.int32)
    others = jnp.where(jnp.logical_and(live, jnp.logical_not(own)), 1.0, 0.0)
    square = (slots, slots)
    upto = lax.broadcasted_iota(jnp.int32, square, 0) <= lax.broadcasted_iota(jnp.int32, square, 1)
    upto = jnp.where(upto, 1.0, 0.0).astype(jnp.bfloat16)
    order = jnp.dot(
        jnp.broadcast_to(others, (SUBLANES, slots)).astype(jnp.bfloat16),
        upto,
        preferred_element_type=jnp.float32,
    )
    place = jnp.where(others > 0.0, order[0:1, :] - 1.0, -1.0).astype(jnp.int32)
    place = lax.broadcasted_iota(jnp.int32, square, 0) == place
    place = jnp.where(place, 1.0, 0.0).astype(jnp.bfloat16)
    row = lax.broadcasted_iota(jnp.int32, (SUBLANES, slots), 0)
    listed = jnp.where(row == 0, target, source).astype(jnp.float32).astype(jnp.bfloat16)
    listed = lax.dot_general(
        listed, place, (((1,), (1,)), ((), ())), preferred_element_type=jnp.float32
    ).astype(jnp.int32)
    list_ref[4:6, :] = listed[0:2, :]
    number = jnp.sum(others, axis=1, keepdims=True).astype(jnp.int32)
    list_ref[6:7, :] = jnp.broadcast_to(number, (1, slots))
    list_ref[7:8, :] = jnp.zeros((1, slots), jnp.int32)


def prepare(near_count, far_count, disp, pos, spare):
    clusters, width = disp.shape
    vmem = pl.BlockSpec(memory_space=pltpu.VMEM)
    smem = pl.BlockSpec(memory_space=pltpu.SMEM)
    return pl.pallas_call(
        prepare_kernel,
        out_shape=(
            jax.ShapeDtypeStruct((clusters, width), jnp.bfloat16),
            jax.ShapeDtypeStruct((clusters, spare), jnp.float32),
            jax.ShapeDtypeStruct((SUBLANES, LANES), jnp.int32),
        ),
        in_specs=[smem] * 2 + in_hbm(2),
        out_specs=(vmem,) * 3,
        scratch_shapes=[
            pltpu.VMEM(disp.shape, disp.dtype),
            pltpu.VMEM(pos.shape, pos.dtype),
            pltpu.SemaphoreType.DMA((2,)),
        ],
        compiler_params=pltpu.CompilerParams(vmem_limit_bytes=VMEM),
        cost_estimate=pl.CostEstimate(
            flops=clusters * width, bytes_accessed=12 * clusters * width, transcendentals=0
        ),
        name="prepare",
    )(near_count, far_count, *pinned(disp, pos))


def far_kernel(
    counts_hbm,
    pairs_hbm,
    gathered_hbm,
    near_pairs_hbm,
    pos_hbm,
    disp_hbm,
    intact_hbm,
    stiff_hbm,
    blocks_ref,
    out_ref,
    fields_ref,
    damage_ref,
    list_ref,
    counts_ref,
    pairs_ref,
    gathered_ref,
    near_pairs_ref,
    intact_ref,
    stiff_ref,
    buffer,
    column_scr,
    coeff_scr,
    place_scr,
    sum_scr,
    summed_scr,
    halo_scr,
    sems,
    block_sems,
    *,
    segments,
):
    rank, _, slots = buffer.shape
    cols, clusters, _ = out_ref.shape
    targets = cols * clusters
    rows = gathered_ref.shape[0] // clusters
    sources = rows * clusters
    tiles = slots // FOLD

    def fetch(t):
        here = pl.ds(pl.multiple_of(t * FOLD, FOLD), FOLD)
        return pltpu.make_async_copy(
            blocks_ref.at[:, :, here], buffer.at[:, :, here], block_sems.at[t]
        )

    inputs = start_all(
        sems,
        (
            (counts_hbm, counts_ref),
            (pairs_hbm, pairs_ref),
            (gathered_hbm, gathered_ref),
            (near_pairs_hbm, near_pairs_ref),
            (pos_hbm, fields_ref.at[0]),
            (disp_hbm, fields_ref.at[1]),
            (intact_hbm, intact_ref),
            (stiff_hbm, stiff_ref),
        ),
    )
    fetch(0).start()
    summed_scr[...] = jnp.zeros_like(summed_scr)
    inputs[0].wait()
    count = counts_ref[1, 0]
    live = (count + FOLD - 1) // FOLD
    for t in range(1, tiles):

        @pl.when(t < live)
        def _(t=t):
            fetch(t).start()

    inputs[1].wait()
    inputs[2].wait()
    column_scr[...] = gathered_ref[...].astype(jnp.bfloat16)

    index = lax.broadcasted_iota(jnp.int32, (sources, slots), 0)
    pick = jnp.where(index == pairs_ref[1:2, :], 1.0, 0.0).astype(jnp.bfloat16)
    coeff = lax.dot_general(
        column_scr[...], pick, (((0,), (0,)), ((), ())), preferred_element_type=jnp.float32
    )
    coeff_scr[...] = coeff[0:rank, :]
    slot = lax.broadcasted_iota(jnp.int32, (1, slots), 1)
    wanted = jnp.where(slot < count, pairs_ref[0:1, :], -1)
    index = lax.broadcasted_iota(jnp.int32, (targets, slots), 0)
    place_scr[...] = jnp.where(index == wanted, 1.0, 0.0).astype(jnp.bfloat16)

    for copy in inputs[3:]:
        copy.wait()
    list_pairs(near_pairs_ref, counts_ref[0, 0], list_ref, clusters)
    elems = damage_ref.shape[1]
    disp = [fields_ref[1, :, c * elems : (c + 1) * elems] for c in range(3)]
    separation = jnp.sqrt(1.0 + (disp[0] * disp[0] + disp[1] * disp[1] + disp[2] * disp[2]))
    softened = 1.0 - jnp.exp(-(separation - 1.0) / softening)
    intact = intact_ref[...].astype(jnp.float32)
    damage = intact * softened + (1.0 - intact)
    damage_ref[...] = damage
    hold = (1.0 - damage) * stiff_ref[...]
    for c in range(3):
        fields_ref[2, :, c * elems : (c + 1) * elems] = -hold * disp[c]

    def multiply(t, carry):
        start = pl.multiple_of(t * FOLD, FOLD)
        lanes = pl.ds(start, FOLD)
        fetch(t).wait()
        coeff = coeff_scr[:, lanes]
        for r in range(rank):
            product = buffer[r, :, lanes].astype(jnp.float32) * coeff
            folded = product[0:SUBLANES]
            for s in range(1, rank // SUBLANES):
                folded = folded + product[s * SUBLANES : (s + 1) * SUBLANES]
            for h in range(FOLD // LANES):
                sum_scr[h, r * SUBLANES : (r + 1) * SUBLANES, :] = folded[
                    :, h * LANES : (h + 1) * LANES
                ]
        parts = []
        for h in range(FOLD // LANES):
            total = sum_scr[h, pl.ds(0, rank, stride=SUBLANES), :]
            for s in range(1, SUBLANES):
                total = total + sum_scr[h, pl.ds(s, rank, stride=SUBLANES), :]
            parts.append(total)
        coupled = jnp.concatenate(parts, axis=1)
        high = coupled.astype(jnp.bfloat16)
        low = (coupled - high.astype(jnp.float32)).astype(jnp.bfloat16)
        both = jnp.concatenate([high, low], axis=0)
        summed_scr[...] += lax.dot_general(
            place_scr[:, lanes], both, (((1,), (1,)), ((), ())), preferred_element_type=jnp.float32
        )
        return carry

    lax.fori_loop(0, live, multiply, 0)

    i = lax.axis_index("rows")
    j = lax.axis_index("cols")
    from_last = jnp.where(j < cols - 1, i, i - 1)
    from_first = jnp.where(j > 0, i, i + 1)
    edge = 2 * HALO
    halo_scr[...] = jnp.zeros_like(halo_scr)
    sides = (
        (0, jnp.minimum(from_first, rows - 1), from_first < rows),
        (edge, jnp.maximum(from_last, 0), from_last >= 0),
    )
    for side, (row, owner, there) in enumerate(sides):
        start = pl.multiple_of(owner * clusters, clusters)
        whole = jnp.where(there, gathered_ref[pl.ds(start, clusters), :], 0.0)
        for n in range(PIECES):
            piece = whole.astype(jnp.bfloat16).astype(jnp.float32)
            whole = whole - piece
            for g in range(segments):
                to = (n * segments + g) * edge
                here = g * 2 * edge + row
                halo_scr[side, to : to + edge, :] = piece[here : here + edge, :]
    after = jnp.where(j < cols - 1, j + 1, 0)
    lane = lax.broadcasted_iota(jnp.int32, (clusters, LANES), 1)
    for d in range(cols):
        halo = halo_scr[jnp.where(after == d, 1, 0)]
        mine = summed_scr[d * clusters : (d + 1) * clusters, :]
        mine = mine + pltpu.roll(mine, rank, 1)
        out_ref[d] = jnp.where(lane < rank, mine, halo).astype(out_ref.dtype)


def far_field(counts, pairs, gathered, near_pairs, pos, disp, intact, stiffness, blocks, cols, segments):
    rank, _, slots = blocks.shape
    rows = lax.axis_size("rows")
    clusters = gathered.shape[0] // rows
    return pl.pallas_call(
        functools.partial(far_kernel, segments=segments),
        out_shape=(
            jax.ShapeDtypeStruct((cols, clusters, LANES), jnp.bfloat16),
            jax.ShapeDtypeStruct((3, *pos.shape), jnp.float32),
            jax.ShapeDtypeStruct(stiffness.shape, jnp.float32),
            jax.ShapeDtypeStruct((SUBLANES, near_pairs.shape[1]), jnp.int32),
        ),
        in_specs=in_hbm(9),
        out_specs=(pl.BlockSpec(memory_space=pltpu.VMEM),) * 4,
        scratch_shapes=[
            pltpu.SMEM(counts.shape, counts.dtype),
            pltpu.VMEM(pairs.shape, pairs.dtype),
            pltpu.VMEM(gathered.shape, gathered.dtype),
            pltpu.VMEM(near_pairs.shape, near_pairs.dtype),
            pltpu.VMEM(intact.shape, intact.dtype),
            pltpu.VMEM(stiffness.shape, stiffness.dtype),
            pltpu.VMEM(blocks.shape, blocks.dtype),
            pltpu.VMEM((rows * clusters, LANES), jnp.bfloat16),
            pltpu.VMEM((rank, slots), jnp.float32),
            pltpu.VMEM((cols * clusters, slots), jnp.bfloat16),
            pltpu.VMEM((FOLD // LANES, rank * SUBLANES, LANES), jnp.float32),
            pltpu.VMEM((cols * clusters, LANES), jnp.float32),
            pltpu.VMEM((2, clusters, LANES), jnp.float32),
            pltpu.SemaphoreType.DMA((8,)),
            pltpu.SemaphoreType.DMA((slots // FOLD,)),
        ],
        compiler_params=pltpu.CompilerParams(vmem_limit_bytes=VMEM),
        cost_estimate=pl.CostEstimate(
            flops=2 * rank * rank * slots,
            bytes_accessed=2 * rank * rank * slots,
            transcendentals=0,
        ),
        name="far_field",
    )(
        counts,
        *pinned(pairs),
        gathered,
        *pinned(near_pairs, pos, disp, intact, stiffness, blocks),
    )


def replicate(rows, chunks, store, turned=False):
    within = lax.broadcasted_iota(jnp.int32, (rows.shape[0], LANES), 1)
    if turned:
        within = within + (within // CHUNK) * SUBLANES
    within = within % CHUNK
    for m in range(3 * chunks):
        tile = m // GROUPS
        store(
            m,
            jnp.take_along_axis(
                rows[:, tile * LANES : (tile + 1) * LANES],
                within + (m % GROUPS) * CHUNK,
                axis=1,
                mode="promise_in_bounds",
            ),
        )


def row_of(ref, n, row):
    return ref[n, pl.ds(row, SUBLANES, stride=0), :]


def turn(wide):
    return pltpu.roll(wide, 0, 1, stride=1, stride_axis=0)


def pair_sums(tgt, src, chunks):
    sums = [None] * (3 * chunks)
    size = 3 * chunks
    for h in range(chunks):
        x = [tgt(c * chunks + h) for c in range(3)]
        for f in range(chunks):
            r = [x[c] - src(c * chunks + f) for c in range(3)]
            u = [src(size + c * chunks + f) for c in range(3)]
            q = (r[0] * r[0] + core_square) + (r[1] * r[1] + r[2] * r[2])
            s = r[0] * u[0] + (r[1] * u[1] + r[2] * u[2])
            inverse = lax.rsqrt(q)
            square = inverse * inverse
            weight = square * inverse
            s = (3.0 * s) * square
            for c in range(3):
                term = weight * (u[c] - s * r[c])
                m = c * chunks + h
                sums[m] = term if sums[m] is None else sums[m] + term
    return sums


def gather_sums(acc_scr, clusters, chunks, store):
    own_group = lax.broadcasted_iota(jnp.int32, (clusters, LANES), 1) // CHUNK
    for t in range(pl.cdiv(3 * chunks, GROUPS)):
        merged = None
        for g in range(GROUPS):
            m = t * GROUPS + g
            if m >= 3 * chunks:
                break
            total = acc_scr[m, pl.ds(0, clusters, stride=SUBLANES), :]
            for s in range(1, SUBLANES):
                total = total + acc_scr[m, pl.ds(s, clusters, stride=SUBLANES), :]
            total = total + pltpu.roll(total, 2 * CHUNK, 1)
            total = total + pltpu.roll(total, CHUNK, 1)
            merged = total if merged is None else jnp.where(own_group == g, total, merged)
        store(t, merged)


def turn_matrix():
    shape = (PIECES * CHUNK, SUBLANES * LANES)
    column = lax.broadcasted_iota(jnp.int32, shape, 1)
    lane = column % LANES
    entry = (lane + (lane // CHUNK) * SUBLANES + column // LANES) % CHUNK
    row = lax.broadcasted_iota(jnp.int32, shape, 0) % CHUNK
    return jnp.where(entry == row, 1.0, 0.0).astype(jnp.bfloat16)


def exact_pieces(value):
    pieces = []
    for _ in range(PIECES):
        piece = value.astype(jnp.bfloat16)
        pieces.append(piece)
        value = value - piece.astype(jnp.float32)
    return pieces


def near_kernel(
    list_hbm,
    fields_ref,
    damage_ref,
    out_ref,
    edge_ref,
    damage_hbm,
    list_ref,
    wide_scr,
    piece_scr,
    turn_scr,
    tgt_scr,
    src_scr,
    acc_scr,
    sems,
):
    _, clusters, width = fields_ref.shape
    elems = width // 3
    chunks = elems // CHUNK
    size = 3 * chunks

    moves = start_all(sems, ((list_hbm, list_ref), (damage_ref, damage_hbm)))
    acc_scr[...] = jnp.zeros_like(acc_scr)
    turn_scr[...] = turn_matrix()

    wide_scr[:, 0:width] = fields_ref[0]
    edge_ref[0:HALO, :] = fields_ref[0, 0:HALO, :]
    edge_ref[HALO:, :] = fields_ref[0, clusters - HALO :, :]
    for k in range(2):
        for m in range(size):
            pieces = exact_pieces(fields_ref[k, :, m * CHUNK : (m + 1) * CHUNK])
            piece_scr[(k * size + m) * clusters : (k * size + m + 1) * clusters, :] = (
                jnp.concatenate(pieces, axis=1)
            )
    columns = 2 * LANES
    for t in range(SUBLANES * LANES // columns):
        for k in range(2):
            rows = size * clusters
            turned = jnp.dot(
                piece_scr[k * rows : (k + 1) * rows, :],
                turn_scr[:, t * columns : (t + 1) * columns],
                preferred_element_type=jnp.float32,
            )
            for m in range(size):
                for h in range(columns // LANES):
                    s = t * (columns // LANES) + h
                    src_scr[k * size + m, pl.ds(s, clusters, stride=SUBLANES), :] = turned[
                        m * clusters : (m + 1) * clusters, h * LANES : (h + 1) * LANES
                    ]

    def store_target(m, value):
        tgt_scr[m] = value

    replicate(wide_scr[...], chunks, store_target)
    moves[0].wait()
    count = list_ref[3, 0]

    def sums_of(slot):
        target = list_ref[0, slot]
        source = pl.multiple_of(list_ref[1, slot] * SUBLANES, SUBLANES)
        return pair_sums(
            lambda m: row_of(tgt_scr, m, target),
            lambda n: src_scr[n, pl.ds(source, SUBLANES), :],
            chunks,
        )

    def step(it, carry):
        for k in range(0, UNROLL, TOGETHER):
            slots = [it * UNROLL + k + n for n in range(TOGETHER)]
            results = [sums_of(slot) for slot in slots]
            for slot, sums in zip(slots, results):
                into = pl.multiple_of(list_ref[2, slot], SUBLANES)
                for m in range(size):
                    acc_scr[m, pl.ds(into, SUBLANES), :] += sums[m]
        return carry

    lax.fori_loop(0, (count + UNROLL - 1) // UNROLL, step, 0)

    def store_sum(t, value):
        wide_scr[:, t * LANES : (t + 1) * LANES] = value

    gather_sums(acc_scr, clusters, chunks, store_sum)
    out_ref[...] = fields_ref[2] + wide_scr[:, 0:width]
    moves[1].wait()


def near_field(listed, fields, damage):
    _, clusters, width = fields.shape
    elems = width // 3
    chunks = elems // CHUNK
    padded = pl.cdiv(width, LANES) * LANES
    slots = listed.shape[1]
    vmem = pl.BlockSpec(memory_space=pltpu.VMEM)
    return pl.pallas_call(
        near_kernel,
        out_shape=(
            jax.ShapeDtypeStruct((clusters, width), jnp.float32),
            jax.ShapeDtypeStruct((2 * HALO, width), jnp.float32),
            jax.ShapeDtypeStruct(damage.shape, jnp.float32),
        ),
        in_specs=in_hbm(1) + [vmem] * 2,
        out_specs=(vmem, vmem, *in_hbm(1)),
        scratch_shapes=[
            pltpu.SMEM(listed.shape, listed.dtype),
            pltpu.VMEM((clusters, padded), jnp.float32),
            pltpu.VMEM((6 * chunks * clusters, PIECES * CHUNK), jnp.bfloat16),
            pltpu.VMEM((PIECES * CHUNK, SUBLANES * LANES), jnp.bfloat16),
            pltpu.VMEM((3 * chunks, clusters, LANES), jnp.float32),
            pltpu.VMEM((6 * chunks, clusters * SUBLANES, LANES), jnp.float32),
            pltpu.VMEM((3 * chunks, (clusters + 1) * SUBLANES, LANES), jnp.float32),
            pltpu.SemaphoreType.DMA((2,)),
        ],
        compiler_params=pltpu.CompilerParams(vmem_limit_bytes=VMEM),
        cost_estimate=pl.CostEstimate(
            flops=30 * slots * elems * elems,
            bytes_accessed=4 * clusters * width * 6,
            transcendentals=slots * elems * elems,
        ),
        name="near_field",
    )(listed, fields, damage)


def finish_kernel(
    rest_hbm,
    edge_ref,
    received_ref,
    near_ref,
    far_ref,
    out_ref,
    rest_ref,
    ext_scr,
    halo_scr,
    tgt_scr,
    src_scr,
    acc_scr,
    sem,
    *,
    rank,
):
    clusters, width = near_ref.shape
    cols = received_ref.shape[0]
    elems = width // 3
    chunks = elems // CHUNK
    size = 3 * chunks
    spare = LANES - rank
    segments = split_rows(width, spare)
    edge = 2 * HALO

    fetch = pltpu.make_async_copy(rest_hbm, rest_ref, sem)
    fetch.start()
    acc_scr[...] = jnp.zeros_like(acc_scr)

    j = lax.axis_index("cols")
    before = jnp.where(j > 0, j - 1, cols - 1)
    after = jnp.where(j < cols - 1, j + 1, 0)
    for start, sender in ((0, before), (HALO, after)):
        halo_scr[...] = received_ref[sender].astype(jnp.float32)
        rows = edge * segments
        whole = halo_scr[0:rows, :]
        for n in range(1, PIECES):
            whole = whole + halo_scr[n * rows : (n + 1) * rows, :]
        for g in range(segments):
            count = min(spare, width - g * spare)
            for k in range(2):
                row = (2 * g + k) * HALO
                ext_scr[k, start : start + HALO, g * spare : g * spare + count] = whole[
                    row : row + HALO, rank : rank + count
                ]
    ext_scr[1, edge : 2 * edge, 0:width] = edge_ref[...]
    for k in range(2):

        def store(m, value, k=k):
            for b in range(edge):
                wide = jnp.broadcast_to(value[b : b + 1, :], (SUBLANES, LANES))
                src_scr[(1 - k) * size + m, b * SUBLANES : (b + 1) * SUBLANES, :] = turn(wide)

        replicate(ext_scr[k], chunks, store, True)

    def store_target(m, value):
        tgt_scr[m] = value

    replicate(ext_scr[1], chunks, store_target)
    fetch.wait()
    number = rest_ref[6, 0]

    def one_pair(n):
        target = rest_ref[4, n]
        source = rest_ref[5, n]
        target = jnp.where(target < HALO, target, target - (clusters - edge))
        source = jnp.where(source < HALO, source, source - clusters)
        live = n < number
        target = jnp.where(live, target, edge)
        source = pl.multiple_of(jnp.where(live, source, 0) * SUBLANES, SUBLANES)
        into = pl.multiple_of(target * SUBLANES, SUBLANES)
        row = edge + jnp.where(live, target, 0)
        sums = pair_sums(
            lambda m: row_of(tgt_scr, m, row),
            lambda k: src_scr[k, pl.ds(source, SUBLANES), :],
            chunks,
        )
        for m in range(size):
            acc_scr[m, pl.ds(into, SUBLANES), :] += sums[m]

    def step(it, carry):
        for k in range(FEW):
            one_pair(it * FEW + k)
        return carry

    lax.fori_loop(0, (number + FEW - 1) // FEW, step, 0)

    def store_sum(t, value):
        ext_scr[0, :, t * LANES : (t + 1) * LANES] = value

    gather_sums(acc_scr, 2 * edge, chunks, store_sum)
    out_ref[...] = near_ref[...] + far_ref[...]
    out_ref[0:HALO, :] += ext_scr[0, 0:HALO, 0:width]
    out_ref[clusters - HALO :, :] += ext_scr[0, HALO:edge, 0:width]


def finish(rest, edges, received, near, far, rank):
    clusters, width = near.shape
    chunks = width // 3 // CHUNK
    padded = pl.cdiv(width, LANES) * LANES
    edge = 2 * HALO
    vmem = pl.BlockSpec(memory_space=pltpu.VMEM)
    return pl.pallas_call(
        functools.partial(finish_kernel, rank=rank),
        out_shape=jax.ShapeDtypeStruct((clusters, width), jnp.float32),
        in_specs=in_hbm(1) + [vmem] * 4,
        out_specs=vmem,
        scratch_shapes=[
            pltpu.SMEM(rest.shape, rest.dtype),
            pltpu.VMEM((2, 2 * edge, padded), jnp.float32),
            pltpu.VMEM((clusters, LANES), jnp.float32),
            pltpu.VMEM((3 * chunks, 2 * edge, LANES), jnp.float32),
            pltpu.VMEM((6 * chunks, edge * SUBLANES, LANES), jnp.float32),
            pltpu.VMEM((3 * chunks, 2 * edge * SUBLANES, LANES), jnp.float32),
            pltpu.SemaphoreType.DMA(()),
        ],
        compiler_params=pltpu.CompilerParams(vmem_limit_bytes=VMEM),
        cost_estimate=pl.CostEstimate(
            flops=2 * clusters * width, bytes_accessed=16 * clusters * width, transcendentals=0
        ),
        name="finish",
    )(rest, edges, received, near, far)


def local(
    displacement,
    positions,
    cluster_basis,
    near_pairs,
    near_count,
    far_pairs,
    far_count,
    far_blocks,
    intact,
    stiffness,
):
    cols = lax.axis_size("cols")
    clusters, width, rank = cluster_basis.shape
    spare = LANES - rank
    segments = split_rows(width, spare)
    disp_bf, halo, counts = prepare(near_count, far_count, displacement, positions, spare)
    coeff = jnp.einsum("kf,kfr->kr", disp_bf, cluster_basis, preferred_element_type=jnp.float32)
    payload = jnp.concatenate([coeff, halo], axis=1)
    gathered = lax.all_gather(payload, "rows", axis=0, tiled=True)
    partial, fields, damage, listed = far_field(
        counts,
        far_pairs.T,
        gathered,
        near_pairs.T,
        positions,
        displacement,
        intact,
        stiffness,
        far_blocks.transpose(1, 2, 0),
        cols,
        segments,
    )
    received = lax.all_to_all(partial, "cols", split_axis=0, concat_axis=0)
    near, edges, damage = near_field(listed, fields, damage)
    owned = jnp.sum(received[:, :, :rank].astype(jnp.float32), axis=0).astype(jnp.bfloat16)
    far = jnp.einsum("kfr,kr->kf", cluster_basis, owned, preferred_element_type=jnp.float32)
    return finish(listed, edges, received, near, far, rank), damage


def solution(mesh):
    both = ("rows", "cols")
    in_specs = (
        P(both, None),
        P(both, None),
        P(both, None, None),
        P(both, None),
        P(both),
        P(both, None),
        P(both),
        P(both, None, None),
        P(both, None),
        P(both, None),
    )
    out_specs = (P(both, None), P(both, None))
    return jax.shard_map(local, mesh=mesh, in_specs=in_specs, out_specs=out_specs, check_vma=False)
```

```python
import functools

import jax
import jax.numpy as jnp
from jax import lax
from jax.experimental import pallas as pl
from jax.experimental.pallas import tpu as pltpu
from jax.sharding import PartitionSpec as P

HALO = 2
LANES = 128
SUBLANES = 8
CHUNK = 32
GROUPS = LANES // CHUNK
core_square = 0.25
softening = 1.5
UNROLL = 8
TOGETHER = 2
FEW = 4
FOLD = 256
PIECES = 3
VMEM = 14 * 1024 * 1024


def split_rows(width, lanes):
    return pl.cdiv(width, lanes)


def in_hbm(count):
    return [pl.BlockSpec(memory_space=pltpu.HBM)] * count


def pinned(*arrays):
    return [pltpu.with_memory_space_constraint(x, pltpu.HBM) for x in arrays]


def start_all(sems, moves):
    copies = [
        pltpu.make_async_copy(source, target, sems.at[n])
        for n, (source, target) in enumerate(moves)
    ]
    for copy in copies:
        copy.start()
    return copies


def prepare_kernel(
    near_count_ref,
    far_count_ref,
    disp_hbm,
    pos_hbm,
    low_ref,
    halo_ref,
    counts_ref,
    disp_ref,
    pos_ref,
    sems,
):
    clusters, width = disp_ref.shape
    spare = halo_ref.shape[1]
    segments = split_rows(width, spare)
    inputs = start_all(sems, ((disp_hbm, disp_ref), (pos_hbm, pos_ref)))
    halo_ref[...] = jnp.zeros_like(halo_ref)
    row = lax.broadcasted_iota(jnp.int32, counts_ref.shape, 0)
    counts_ref[...] = jnp.where(row == 0, near_count_ref[0], far_count_ref[0])
    for copy in inputs:
        copy.wait()
    low_ref[...] = disp_ref[...].astype(low_ref.dtype)
    row = 0
    for g in range(segments):
        size = min(spare, width - g * spare)
        for start in (0, clusters - HALO):
            for ref in (disp_ref, pos_ref):
                halo_ref[row : row + HALO, 0:size] = ref[
                    start : start + HALO, g * spare : g * spare + size
                ]
                row += HALO


def list_pairs(pairs_ref, near_count, list_ref, clusters):
    slots = pairs_ref.shape[1]
    target = pairs_ref[0:1, :]
    source = pairs_ref[1:2, :]
    live = lax.broadcasted_iota(jnp.int32, (1, slots), 1) < near_count
    own = jnp.logical_and(source >= HALO, source < clusters + HALO)
    list_ref[0:1, :] = target
    list_ref[1:2, :] = jnp.clip(source - HALO, 0, clusters - 1)
    list_ref[2:3, :] = jnp.where(jnp.logical_and(live, own), target, clusters) * SUBLANES
    list_ref[3:4, :] = jnp.full((1, slots), near_count, jnp.int32)
    others = jnp.where(jnp.logical_and(live, jnp.logical_not(own)), 1.0, 0.0)
    square = (slots, slots)
    upto = lax.broadcasted_iota(jnp.int32, square, 0) <= lax.broadcasted_iota(jnp.int32, square, 1)
    upto = jnp.where(upto, 1.0, 0.0).astype(jnp.bfloat16)
    order = jnp.dot(
        jnp.broadcast_to(others, (SUBLANES, slots)).astype(jnp.bfloat16),
        upto,
        preferred_element_type=jnp.float32,
    )
    place = jnp.where(others > 0.0, order[0:1, :] - 1.0, -1.0).astype(jnp.int32)
    place = lax.broadcasted_iota(jnp.int32, square, 0) == place
    place = jnp.where(place, 1.0, 0.0).astype(jnp.bfloat16)
    row = lax.broadcasted_iota(jnp.int32, (SUBLANES, slots), 0)
    listed = jnp.where(row == 0, target, source).astype(jnp.float32).astype(jnp.bfloat16)
    listed = lax.dot_general(
        listed, place, (((1,), (1,)), ((), ())), preferred_element_type=jnp.float32
    ).astype(jnp.int32)
    list_ref[4:6, :] = listed[0:2, :]
    number = jnp.sum(others, axis=1, keepdims=True).astype(jnp.int32)
    list_ref[6:7, :] = jnp.broadcast_to(number, (1, slots))
    list_ref[7:8, :] = jnp.zeros((1, slots), jnp.int32)


def prepare(near_count, far_count, disp, pos, spare):
    clusters, width = disp.shape
    vmem = pl.BlockSpec(memory_space=pltpu.VMEM)
    smem = pl.BlockSpec(memory_space=pltpu.SMEM)
    return pl.pallas_call(
        prepare_kernel,
        out_shape=(
            jax.ShapeDtypeStruct((clusters, width), jnp.bfloat16),
            jax.ShapeDtypeStruct((clusters, spare), jnp.float32),
            jax.ShapeDtypeStruct((SUBLANES, LANES), jnp.int32),
        ),
        in_specs=[smem] * 2 + in_hbm(2),
        out_specs=(vmem,) * 3,
        scratch_shapes=[
            pltpu.VMEM(disp.shape, disp.dtype),
            pltpu.VMEM(pos.shape, pos.dtype),
            pltpu.SemaphoreType.DMA((2,)),
        ],
        compiler_params=pltpu.CompilerParams(vmem_limit_bytes=VMEM),
        cost_estimate=pl.CostEstimate(
            flops=clusters * width, bytes_accessed=12 * clusters * width, transcendentals=0
        ),
        name="prepare",
    )(near_count, far_count, *pinned(disp, pos))


def far_kernel(
    counts_hbm,
    pairs_hbm,
    gathered_hbm,
    near_pairs_hbm,
    pos_hbm,
    disp_hbm,
    intact_hbm,
    stiff_hbm,
    blocks_ref,
    out_ref,
    fields_ref,
    damage_ref,
    list_ref,
    counts_ref,
    pairs_ref,
    gathered_ref,
    near_pairs_ref,
    intact_ref,
    stiff_ref,
    buffer,
    column_scr,
    coeff_scr,
    place_scr,
    sum_scr,
    summed_scr,
    halo_scr,
    sems,
    block_sems,
    *,
    segments,
):
    rank, _, slots = buffer.shape
    cols, clusters, _ = out_ref.shape
    targets = cols * clusters
    rows = gathered_ref.shape[0] // clusters
    sources = rows * clusters
    tiles = slots // FOLD

    def fetch(t):
        here = pl.ds(pl.multiple_of(t * FOLD, FOLD), FOLD)
        return pltpu.make_async_copy(
            blocks_ref.at[:, :, here], buffer.at[:, :, here], block_sems.at[t]
        )

    inputs = start_all(
        sems,
        (
            (counts_hbm, counts_ref),
            (pairs_hbm, pairs_ref),
            (gathered_hbm, gathered_ref),
            (near_pairs_hbm, near_pairs_ref),
            (pos_hbm, fields_ref.at[0]),
            (disp_hbm, fields_ref.at[1]),
            (intact_hbm, intact_ref),
            (stiff_hbm, stiff_ref),
        ),
    )
    fetch(0).start()
    summed_scr[...] = jnp.zeros_like(summed_scr)
    inputs[0].wait()
    count = counts_ref[1, 0]
    live = (count + FOLD - 1) // FOLD
    for t in range(1, tiles):

        @pl.when(t < live)
        def _(t=t):
            fetch(t).start()

    inputs[1].wait()
    inputs[2].wait()
    column_scr[...] = gathered_ref[...].astype(jnp.bfloat16)

    index = lax.broadcasted_iota(jnp.int32, (sources, slots), 0)
    pick = jnp.where(index == pairs_ref[1:2, :], 1.0, 0.0).astype(jnp.bfloat16)
    coeff = lax.dot_general(
        column_scr[...], pick, (((0,), (0,)), ((), ())), preferred_element_type=jnp.float32
    )
    coeff_scr[...] = coeff[0:rank, :]
    slot = lax.broadcasted_iota(jnp.int32, (1, slots), 1)
    wanted = jnp.where(slot < count, pairs_ref[0:1, :], -1)
    index = lax.broadcasted_iota(jnp.int32, (targets, slots), 0)
    place_scr[...] = jnp.where(index == wanted, 1.0, 0.0).astype(jnp.bfloat16)

    for copy in inputs[3:]:
        copy.wait()
    list_pairs(near_pairs_ref, counts_ref[0, 0], list_ref, clusters)
    elems = damage_ref.shape[1]
    disp = [fields_ref[1, :, c * elems : (c + 1) * elems] for c in range(3)]
    separation = jnp.sqrt(1.0 + (disp[0] * disp[0] + disp[1] * disp[1] + disp[2] * disp[2]))
    softened = 1.0 - jnp.exp(-(separation - 1.0) / softening)
    intact = intact_ref[...].astype(jnp.float32)
    damage = intact * softened + (1.0 - intact)
    damage_ref[...] = damage
    hold = (1.0 - damage) * stiff_ref[...]
    for c in range(3):
        fields_ref[2, :, c * elems : (c + 1) * elems] = -hold * disp[c]

    def multiply(t, carry):
        start = pl.multiple_of(t * FOLD, FOLD)
        lanes = pl.ds(start, FOLD)
        fetch(t).wait()
        coeff = coeff_scr[:, lanes]
        for r in range(rank):
            product = buffer[r, :, lanes].astype(jnp.float32) * coeff
            folded = product[0:SUBLANES]
            for s in range(1, rank // SUBLANES):
                folded = folded + product[s * SUBLANES : (s + 1) * SUBLANES]
            for h in range(FOLD // LANES):
                sum_scr[h, r * SUBLANES : (r + 1) * SUBLANES, :] = folded[
                    :, h * LANES : (h + 1) * LANES
                ]
        parts = []
        for h in range(FOLD // LANES):
            total = sum_scr[h, pl.ds(0, rank, stride=SUBLANES), :]
            for s in range(1, SUBLANES):
                total = total + sum_scr[h, pl.ds(s, rank, stride=SUBLANES), :]
            parts.append(total)
        coupled = jnp.concatenate(parts, axis=1)
        high = coupled.astype(jnp.bfloat16)
        low = (coupled - high.astype(jnp.float32)).astype(jnp.bfloat16)
        both = jnp.concatenate([high, low], axis=0)
        summed_scr[...] += lax.dot_general(
            place_scr[:, lanes], both, (((1,), (1,)), ((), ())), preferred_element_type=jnp.float32
        )
        return carry

    lax.fori_loop(0, live, multiply, 0)

    i = lax.axis_index("rows")
    j = lax.axis_index("cols")
    from_last = jnp.where(j < cols - 1, i, i - 1)
    from_first = jnp.where(j > 0, i, i + 1)
    edge = 2 * HALO
    halo_scr[...] = jnp.zeros_like(halo_scr)
    sides = (
        (0, jnp.minimum(from_first, rows - 1), from_first < rows),
        (edge, jnp.maximum(from_last, 0), from_last >= 0),
    )
    for side, (row, owner, there) in enumerate(sides):
        start = pl.multiple_of(owner * clusters, clusters)
        whole = jnp.where(there, gathered_ref[pl.ds(start, clusters), :], 0.0)
        for n in range(PIECES):
            piece = whole.astype(jnp.bfloat16).astype(jnp.float32)
            whole = whole - piece
            for g in range(segments):
                to = (n * segments + g) * edge
                here = g * 2 * edge + row
                halo_scr[side, to : to + edge, :] = piece[here : here + edge, :]
    after = jnp.where(j < cols - 1, j + 1, 0)
    lane = lax.broadcasted_iota(jnp.int32, (clusters, LANES), 1)
    for d in range(cols):
        halo = halo_scr[jnp.where(after == d, 1, 0)]
        mine = summed_scr[d * clusters : (d + 1) * clusters, :]
        mine = mine + pltpu.roll(mine, rank, 1)
        out_ref[d] = jnp.where(lane < rank, mine, halo).astype(out_ref.dtype)


def far_field(counts, pairs, gathered, near_pairs, pos, disp, intact, stiffness, blocks, cols, segments):
    rank, _, slots = blocks.shape
    rows = lax.axis_size("rows")
    clusters = gathered.shape[0] // rows
    return pl.pallas_call(
        functools.partial(far_kernel, segments=segments),
        out_shape=(
            jax.ShapeDtypeStruct((cols, clusters, LANES), jnp.bfloat16),
            jax.ShapeDtypeStruct((3, *pos.shape), jnp.float32),
            jax.ShapeDtypeStruct(stiffness.shape, jnp.float32),
            jax.ShapeDtypeStruct((SUBLANES, near_pairs.shape[1]), jnp.int32),
        ),
        in_specs=in_hbm(9),
        out_specs=(pl.BlockSpec(memory_space=pltpu.VMEM),) * 4,
        scratch_shapes=[
            pltpu.SMEM(counts.shape, counts.dtype),
            pltpu.VMEM(pairs.shape, pairs.dtype),
            pltpu.VMEM(gathered.shape, gathered.dtype),
            pltpu.VMEM(near_pairs.shape, near_pairs.dtype),
            pltpu.VMEM(intact.shape, intact.dtype),
            pltpu.VMEM(stiffness.shape, stiffness.dtype),
            pltpu.VMEM(blocks.shape, blocks.dtype),
            pltpu.VMEM((rows * clusters, LANES), jnp.bfloat16),
            pltpu.VMEM((rank, slots), jnp.float32),
            pltpu.VMEM((cols * clusters, slots), jnp.bfloat16),
            pltpu.VMEM((FOLD // LANES, rank * SUBLANES, LANES), jnp.float32),
            pltpu.VMEM((cols * clusters, LANES), jnp.float32),
            pltpu.VMEM((2, clusters, LANES), jnp.float32),
            pltpu.SemaphoreType.DMA((8,)),
            pltpu.SemaphoreType.DMA((slots // FOLD,)),
        ],
        compiler_params=pltpu.CompilerParams(vmem_limit_bytes=VMEM),
        cost_estimate=pl.CostEstimate(
            flops=2 * rank * rank * slots,
            bytes_accessed=2 * rank * rank * slots,
            transcendentals=0,
        ),
        name="far_field",
    )(
        counts,
        *pinned(pairs),
        gathered,
        *pinned(near_pairs, pos, disp, intact, stiffness, blocks),
    )


def replicate(rows, chunks, store, turned=False):
    within = lax.broadcasted_iota(jnp.int32, (rows.shape[0], LANES), 1)
    if turned:
        within = within + (within // CHUNK) * SUBLANES
    within = within % CHUNK
    for m in range(3 * chunks):
        tile = m // GROUPS
        store(
            m,
            jnp.take_along_axis(
                rows[:, tile * LANES : (tile + 1) * LANES],
                within + (m % GROUPS) * CHUNK,
                axis=1,
                mode="promise_in_bounds",
            ),
        )


def row_of(ref, n, row):
    return ref[n, pl.ds(row, SUBLANES, stride=0), :]


def turn(wide):
    return pltpu.roll(wide, 0, 1, stride=1, stride_axis=0)


def pair_sums(tgt, src, chunks):
    sums = [None] * (3 * chunks)
    size = 3 * chunks
    for h in range(chunks):
        x = [tgt(c * chunks + h) for c in range(3)]
        for f in range(chunks):
            r = [x[c] - src(c * chunks + f) for c in range(3)]
            u = [src(size + c * chunks + f) for c in range(3)]
            q = (r[0] * r[0] + core_square) + (r[1] * r[1] + r[2] * r[2])
            s = r[0] * u[0] + (r[1] * u[1] + r[2] * u[2])
            inverse = lax.rsqrt(q)
            square = inverse * inverse
            weight = square * inverse
            s = (3.0 * s) * square
            for c in range(3):
                term = weight * (u[c] - s * r[c])
                m = c * chunks + h
                sums[m] = term if sums[m] is None else sums[m] + term
    return sums


def gather_sums(acc_scr, clusters, chunks, store):
    own_group = lax.broadcasted_iota(jnp.int32, (clusters, LANES), 1) // CHUNK
    for t in range(pl.cdiv(3 * chunks, GROUPS)):
        merged = None
        for g in range(GROUPS):
            m = t * GROUPS + g
            if m >= 3 * chunks:
                break
            total = acc_scr[m, pl.ds(0, clusters, stride=SUBLANES), :]
            for s in range(1, SUBLANES):
                total = total + acc_scr[m, pl.ds(s, clusters, stride=SUBLANES), :]
            total = total + pltpu.roll(total, 2 * CHUNK, 1)
            total = total + pltpu.roll(total, CHUNK, 1)
            merged = total if merged is None else jnp.where(own_group == g, total, merged)
        store(t, merged)


def turn_matrix():
    shape = (PIECES * CHUNK, SUBLANES * LANES)
    column = lax.broadcasted_iota(jnp.int32, shape, 1)
    lane = column % LANES
    entry = (lane + (lane // CHUNK) * SUBLANES + column // LANES) % CHUNK
    row = lax.broadcasted_iota(jnp.int32, shape, 0) % CHUNK
    return jnp.where(entry == row, 1.0, 0.0).astype(jnp.bfloat16)


def exact_pieces(value):
    pieces = []
    for _ in range(PIECES):
        piece = value.astype(jnp.bfloat16)
        pieces.append(piece)
        value = value - piece.astype(jnp.float32)
    return pieces


def near_kernel(
    list_hbm,
    fields_ref,
    damage_ref,
    out_ref,
    edge_ref,
    damage_hbm,
    list_ref,
    wide_scr,
    piece_scr,
    turn_scr,
    tgt_scr,
    src_scr,
    acc_scr,
    sems,
):
    _, clusters, width = fields_ref.shape
    elems = width // 3
    chunks = elems // CHUNK
    size = 3 * chunks

    moves = start_all(sems, ((list_hbm, list_ref), (damage_ref, damage_hbm)))
    acc_scr[...] = jnp.zeros_like(acc_scr)
    turn_scr[...] = turn_matrix()

    wide_scr[:, 0:width] = fields_ref[0]
    edge_ref[0:HALO, :] = fields_ref[0, 0:HALO, :]
    edge_ref[HALO:, :] = fields_ref[0, clusters - HALO :, :]
    for k in range(2):
        for m in range(size):
            pieces = exact_pieces(fields_ref[k, :, m * CHUNK : (m + 1) * CHUNK])
            piece_scr[(k * size + m) * clusters : (k * size + m + 1) * clusters, :] = (
                jnp.concatenate(pieces, axis=1)
            )
    columns = 2 * LANES
    for t in range(SUBLANES * LANES // columns):
        for k in range(2):
            rows = size * clusters
            turned = jnp.dot(
                piece_scr[k * rows : (k + 1) * rows, :],
                turn_scr[:, t * columns : (t + 1) * columns],
                preferred_element_type=jnp.float32,
            )
            for m in range(size):
                for h in range(columns // LANES):
                    s = t * (columns // LANES) + h
                    src_scr[k * size + m, pl.ds(s, clusters, stride=SUBLANES), :] = turned[
                        m * clusters : (m + 1) * clusters, h * LANES : (h + 1) * LANES
                    ]

    def store_target(m, value):
        tgt_scr[m] = value

    replicate(wide_scr[...], chunks, store_target)
    moves[0].wait()
    count = list_ref[3, 0]

    def sums_of(slot):
        target = list_ref[0, slot]
        source = pl.multiple_of(list_ref[1, slot] * SUBLANES, SUBLANES)
        return pair_sums(
            lambda m: row_of(tgt_scr, m, target),
            lambda n: src_scr[n, pl.ds(source, SUBLANES), :],
            chunks,
        )

    def step(it, carry):
        for k in range(0, UNROLL, TOGETHER):
            slots = [it * UNROLL + k + n for n in range(TOGETHER)]
            results = [sums_of(slot) for slot in slots]
            for slot, sums in zip(slots, results):
                into = pl.multiple_of(list_ref[2, slot], SUBLANES)
                for m in range(size):
                    acc_scr[m, pl.ds(into, SUBLANES), :] += sums[m]
        return carry

    lax.fori_loop(0, (count + UNROLL - 1) // UNROLL, step, 0)

    def store_sum(t, value):
        wide_scr[:, t * LANES : (t + 1) * LANES] = value

    gather_sums(acc_scr, clusters, chunks, store_sum)
    out_ref[...] = fields_ref[2] + wide_scr[:, 0:width]
    moves[1].wait()


def near_field(listed, fields, damage):
    _, clusters, width = fields.shape
    elems = width // 3
    chunks = elems // CHUNK
    padded = pl.cdiv(width, LANES) * LANES
    slots = listed.shape[1]
    vmem = pl.BlockSpec(memory_space=pltpu.VMEM)
    return pl.pallas_call(
        near_kernel,
        out_shape=(
            jax.ShapeDtypeStruct((clusters, width), jnp.float32),
            jax.ShapeDtypeStruct((2 * HALO, width), jnp.float32),
            jax.ShapeDtypeStruct(damage.shape, jnp.float32),
        ),
        in_specs=in_hbm(1) + [vmem] * 2,
        out_specs=(vmem, vmem, *in_hbm(1)),
        scratch_shapes=[
            pltpu.SMEM(listed.shape, listed.dtype),
            pltpu.VMEM((clusters, padded), jnp.float32),
            pltpu.VMEM((6 * chunks * clusters, PIECES * CHUNK), jnp.bfloat16),
            pltpu.VMEM((PIECES * CHUNK, SUBLANES * LANES), jnp.bfloat16),
            pltpu.VMEM((3 * chunks, clusters, LANES), jnp.float32),
            pltpu.VMEM((6 * chunks, clusters * SUBLANES, LANES), jnp.float32),
            pltpu.VMEM((3 * chunks, (clusters + 1) * SUBLANES, LANES), jnp.float32),
            pltpu.SemaphoreType.DMA((2,)),
        ],
        compiler_params=pltpu.CompilerParams(vmem_limit_bytes=VMEM),
        cost_estimate=pl.CostEstimate(
            flops=30 * slots * elems * elems,
            bytes_accessed=4 * clusters * width * 6,
            transcendentals=slots * elems * elems,
        ),
        name="near_field",
    )(listed, fields, damage)


def finish_kernel(
    rest_hbm,
    edge_ref,
    received_ref,
    near_ref,
    far_ref,
    out_ref,
    rest_ref,
    ext_scr,
    halo_scr,
    tgt_scr,
    src_scr,
    acc_scr,
    sem,
    *,
    rank,
):
    clusters, width = near_ref.shape
    cols = received_ref.shape[0]
    elems = width // 3
    chunks = elems // CHUNK
    size = 3 * chunks
    spare = LANES - rank
    segments = split_rows(width, spare)
    edge = 2 * HALO

    fetch = pltpu.make_async_copy(rest_hbm, rest_ref, sem)
    fetch.start()
    acc_scr[...] = jnp.zeros_like(acc_scr)

    j = lax.axis_index("cols")
    before = jnp.where(j > 0, j - 1, cols - 1)
    after = jnp.where(j < cols - 1, j + 1, 0)
    for start, sender in ((0, before), (HALO, after)):
        halo_scr[...] = received_ref[sender].astype(jnp.float32)
        rows = edge * segments
        whole = halo_scr[0:rows, :]
        for n in range(1, PIECES):
            whole = whole + halo_scr[n * rows : (n + 1) * rows, :]
        for g in range(segments):
            count = min(spare, width - g * spare)
            for k in range(2):
                row = (2 * g + k) * HALO
                ext_scr[k, start : start + HALO, g * spare : g * spare + count] = whole[
                    row : row + HALO, rank : rank + count
                ]
    ext_scr[1, edge : 2 * edge, 0:width] = edge_ref[...]
    for k in range(2):

        def store(m, value, k=k):
            for b in range(edge):
                wide = jnp.broadcast_to(value[b : b + 1, :], (SUBLANES, LANES))
                src_scr[(1 - k) * size + m, b * SUBLANES : (b + 1) * SUBLANES, :] = turn(wide)

        replicate(ext_scr[k], chunks, store, True)

    def store_target(m, value):
        tgt_scr[m] = value

    replicate(ext_scr[1], chunks, store_target)
    fetch.wait()
    number = rest_ref[6, 0]

    def one_pair(n):
        target = rest_ref[4, n]
        source = rest_ref[5, n]
        target = jnp.where(target < HALO, target, target - (clusters - edge))
        source = jnp.where(source < HALO, source, source - clusters)
        live = n < number
        target = jnp.where(live, target, edge)
        source = pl.multiple_of(jnp.where(live, source, 0) * SUBLANES, SUBLANES)
        into = pl.multiple_of(target * SUBLANES, SUBLANES)
        row = edge + jnp.where(live, target, 0)
        sums = pair_sums(
            lambda m: row_of(tgt_scr, m, row),
            lambda k: src_scr[k, pl.ds(source, SUBLANES), :],
            chunks,
        )
        for m in range(size):
            acc_scr[m, pl.ds(into, SUBLANES), :] += sums[m]

    def step(it, carry):
        for k in range(FEW):
            one_pair(it * FEW + k)
        return carry

    lax.fori_loop(0, (number + FEW - 1) // FEW, step, 0)

    def store_sum(t, value):
        ext_scr[0, :, t * LANES : (t + 1) * LANES] = value

    gather_sums(acc_scr, 2 * edge, chunks, store_sum)
    out_ref[...] = near_ref[...] + far_ref[...]
    out_ref[0:HALO, :] += ext_scr[0, 0:HALO, 0:width]
    out_ref[clusters - HALO :, :] += ext_scr[0, HALO:edge, 0:width]


def finish(rest, edges, received, near, far, rank):
    clusters, width = near.shape
    chunks = width // 3 // CHUNK
    padded = pl.cdiv(width, LANES) * LANES
    edge = 2 * HALO
    vmem = pl.BlockSpec(memory_space=pltpu.VMEM)
    return pl.pallas_call(
        functools.partial(finish_kernel, rank=rank),
        out_shape=jax.ShapeDtypeStruct((clusters, width), jnp.float32),
        in_specs=in_hbm(1) + [vmem] * 4,
        out_specs=vmem,
        scratch_shapes=[
            pltpu.SMEM(rest.shape, rest.dtype),
            pltpu.VMEM((2, 2 * edge, padded), jnp.float32),
            pltpu.VMEM((clusters, LANES), jnp.float32),
            pltpu.VMEM((3 * chunks, 2 * edge, LANES), jnp.float32),
            pltpu.VMEM((6 * chunks, edge * SUBLANES, LANES), jnp.float32),
            pltpu.VMEM((3 * chunks, 2 * edge * SUBLANES, LANES), jnp.float32),
            pltpu.SemaphoreType.DMA(()),
        ],
        compiler_params=pltpu.CompilerParams(vmem_limit_bytes=VMEM),
        cost_estimate=pl.CostEstimate(
            flops=2 * clusters * width, bytes_accessed=16 * clusters * width, transcendentals=0
        ),
        name="finish",
    )(rest, edges, received, near, far)


def local(
    displacement,
    positions,
    cluster_basis,
    near_pairs,
    near_count,
    far_pairs,
    far_count,
    far_blocks,
    intact,
    stiffness,
):
    cols = lax.axis_size("cols")
    clusters, width, rank = cluster_basis.shape
    spare = LANES - rank
    segments = split_rows(width, spare)
    disp_bf, halo, counts = prepare(near_count, far_count, displacement, positions, spare)
    coeff = jnp.einsum("kf,kfr->kr", disp_bf, cluster_basis, preferred_element_type=jnp.float32)
    payload = jnp.concatenate([coeff, halo], axis=1)
    gathered = lax.all_gather(payload, "rows", axis=0, tiled=True)
    partial, fields, damage, listed = far_field(
        counts,
        far_pairs.T,
        gathered,
        near_pairs.T,
        positions,
        displacement,
        intact,
        stiffness,
        far_blocks.transpose(1, 2, 0),
        cols,
        segments,
    )
    received = lax.all_to_all(partial, "cols", split_axis=0, concat_axis=0)
    near, edges, damage = near_field(listed, fields, damage)
    owned = jnp.sum(received[:, :, :rank].astype(jnp.float32), axis=0).astype(jnp.bfloat16)
    far = jnp.einsum("kfr,kr->kf", cluster_basis, owned, preferred_element_type=jnp.float32)
    return finish(listed, edges, received, near, far, rank), damage


def solution(mesh):
    both = ("rows", "cols")
    in_specs = (
        P(both, None),
        P(both, None),
        P(both, None, None),
        P(both, None),
        P(both),
        P(both, None),
        P(both),
        P(both, None, None),
        P(both, None),
        P(both, None),
    )
    out_specs = (P(both, None), P(both, None))
    return jax.shard_map(local, mesh=mesh, in_specs=in_specs, out_specs=out_specs, check_vma=False)
```

```python
import functools

import jax
import jax.numpy as jnp
from jax import lax
from jax.experimental import pallas as pl
from jax.experimental.pallas import tpu as pltpu
from jax.sharding import PartitionSpec as P

HALO = 2
LANES = 128
SUBLANES = 8
CHUNK = 32
GROUPS = LANES // CHUNK
core_square = 0.25
softening = 1.5
UNROLL = 8
TOGETHER = 2
FEW = 4
FOLD = 256
PIECES = 3
VMEM = 20 * 1024 * 1024


def split_rows(width, lanes):
    return pl.cdiv(width, lanes)


def in_hbm(count):
    return [pl.BlockSpec(memory_space=pltpu.HBM)] * count


def pinned(*arrays):
    return [pltpu.with_memory_space_constraint(x, pltpu.HBM) for x in arrays]


def start_all(sems, moves):
    copies = [
        pltpu.make_async_copy(source, target, sems.at[n])
        for n, (source, target) in enumerate(moves)
    ]
    for copy in copies:
        copy.start()
    return copies


def prepare_kernel(
    near_count_ref,
    far_count_ref,
    disp_hbm,
    pos_hbm,
    low_ref,
    halo_ref,
    counts_ref,
    disp_ref,
    pos_ref,
    sems,
):
    clusters, width = disp_ref.shape
    spare = halo_ref.shape[1]
    segments = split_rows(width, spare)
    inputs = start_all(sems, ((disp_hbm, disp_ref), (pos_hbm, pos_ref)))
    halo_ref[...] = jnp.zeros_like(halo_ref)
    row = lax.broadcasted_iota(jnp.int32, counts_ref.shape, 0)
    counts_ref[...] = jnp.where(row == 0, near_count_ref[0], far_count_ref[0])
    for copy in inputs:
        copy.wait()
    low_ref[...] = disp_ref[...].astype(low_ref.dtype)
    row = 0
    for g in range(segments):
        size = min(spare, width - g * spare)
        for start in (0, clusters - HALO):
            for ref in (disp_ref, pos_ref):
                halo_ref[row : row + HALO, 0:size] = ref[
                    start : start + HALO, g * spare : g * spare + size
                ]
                row += HALO


def list_pairs(pairs_ref, near_count, list_ref, clusters):
    slots = pairs_ref.shape[1]
    target = pairs_ref[0:1, :]
    source = pairs_ref[1:2, :]
    slot = lax.broadcasted_iota(jnp.int32, (1, slots), 1)
    live = slot < near_count
    own = jnp.logical_and(source >= HALO, source < clusters + HALO)
    square = (slots, slots)
    first = lax.broadcasted_iota(jnp.int32, square, 0)
    upto = first <= lax.broadcasted_iota(jnp.int32, square, 1)
    upto = jnp.where(upto, 1.0, 0.0).astype(jnp.bfloat16)
    row = lax.broadcasted_iota(jnp.int32, (SUBLANES, slots), 0)
    pairs = jnp.where(row == 0, target, source).astype(jnp.float32).astype(jnp.bfloat16)
    results = []
    for wanted in (own, jnp.logical_not(own)):
        chosen = jnp.where(jnp.logical_and(live, wanted), 1.0, 0.0)
        order = jnp.dot(
            jnp.broadcast_to(chosen, (SUBLANES, slots)).astype(jnp.bfloat16),
            upto,
            preferred_element_type=jnp.float32,
        )
        place = first == jnp.where(chosen > 0.0, order[0:1, :] - 1.0, -1.0).astype(jnp.int32)
        place = jnp.where(place, 1.0, 0.0).astype(jnp.bfloat16)
        together = lax.dot_general(
            pairs, place, (((1,), (1,)), ((), ())), preferred_element_type=jnp.float32
        ).astype(jnp.int32)
        number = jnp.sum(chosen, axis=1, keepdims=True).astype(jnp.int32)
        results.append((together, jnp.broadcast_to(number, (1, slots))))
    (pairs, number), (others, others_number) = results
    list_ref[0:1, :] = pairs[0:1, :]
    list_ref[1:2, :] = jnp.clip(pairs[1:2, :] - HALO, 0, clusters - 1)
    list_ref[2:3, :] = jnp.where(slot < number, pairs[0:1, :], clusters) * SUBLANES
    list_ref[3:4, :] = number
    list_ref[4:6, :] = others[0:2, :]
    list_ref[6:7, :] = others_number
    list_ref[7:8, :] = jnp.zeros((1, slots), jnp.int32)


def prepare(near_count, far_count, disp, pos, spare):
    clusters, width = disp.shape
    vmem = pl.BlockSpec(memory_space=pltpu.VMEM)
    smem = pl.BlockSpec(memory_space=pltpu.SMEM)
    return pl.pallas_call(
        prepare_kernel,
        out_shape=(
            jax.ShapeDtypeStruct((clusters, width), jnp.bfloat16),
            jax.ShapeDtypeStruct((clusters, spare), jnp.float32),
            jax.ShapeDtypeStruct((SUBLANES, LANES), jnp.int32),
        ),
        in_specs=[smem] * 2 + in_hbm(2),
        out_specs=(vmem,) * 3,
        scratch_shapes=[
            pltpu.VMEM(disp.shape, disp.dtype),
            pltpu.VMEM(pos.shape, pos.dtype),
            pltpu.SemaphoreType.DMA((2,)),
        ],
        compiler_params=pltpu.CompilerParams(vmem_limit_bytes=VMEM),
        cost_estimate=pl.CostEstimate(
            flops=clusters * width, bytes_accessed=12 * clusters * width, transcendentals=0
        ),
        name="prepare",
    )(near_count, far_count, *pinned(disp, pos))


def far_kernel(
    counts_hbm,
    pairs_hbm,
    gathered_hbm,
    near_pairs_hbm,
    disp_hbm,
    intact_hbm,
    stiff_hbm,
    blocks_ref,
    out_ref,
    base_ref,
    damage_ref,
    list_ref,
    counts_ref,
    pairs_ref,
    gathered_ref,
    near_pairs_ref,
    disp_ref,
    intact_ref,
    stiff_ref,
    buffer,
    column_scr,
    coeff_scr,
    place_scr,
    sum_scr,
    summed_scr,
    halo_scr,
    sems,
    block_sems,
    *,
    segments,
):
    rank, _, slots = buffer.shape
    cols, clusters, _ = out_ref.shape
    targets = cols * clusters
    rows = gathered_ref.shape[0] // clusters
    sources = rows * clusters
    tiles = slots // FOLD

    def fetch(t):
        here = pl.ds(pl.multiple_of(t * FOLD, FOLD), FOLD)
        return pltpu.make_async_copy(
            blocks_ref.at[:, :, here], buffer.at[:, :, here], block_sems.at[t]
        )

    inputs = start_all(
        sems,
        (
            (counts_hbm, counts_ref),
            (pairs_hbm, pairs_ref),
            (gathered_hbm, gathered_ref),
            (near_pairs_hbm, near_pairs_ref),
            (disp_hbm, disp_ref),
            (intact_hbm, intact_ref),
            (stiff_hbm, stiff_ref),
        ),
    )
    fetch(0).start()
    summed_scr[...] = jnp.zeros_like(summed_scr)
    inputs[0].wait()
    count = counts_ref[1, 0]
    live = (count + FOLD - 1) // FOLD
    for t in range(1, tiles):

        @pl.when(t < live)
        def _(t=t):
            fetch(t).start()

    inputs[1].wait()
    inputs[2].wait()
    column_scr[...] = gathered_ref[...].astype(jnp.bfloat16)

    index = lax.broadcasted_iota(jnp.int32, (sources, slots), 0)
    pick = jnp.where(index == pairs_ref[1:2, :], 1.0, 0.0).astype(jnp.bfloat16)
    coeff = lax.dot_general(
        column_scr[...], pick, (((0,), (0,)), ((), ())), preferred_element_type=jnp.float32
    )
    coeff_scr[...] = coeff[0:rank, :]
    slot = lax.broadcasted_iota(jnp.int32, (1, slots), 1)
    wanted = jnp.where(slot < count, pairs_ref[0:1, :], -1)
    index = lax.broadcasted_iota(jnp.int32, (targets, slots), 0)
    place_scr[...] = jnp.where(index == wanted, 1.0, 0.0).astype(jnp.bfloat16)

    for copy in inputs[3:]:
        copy.wait()
    list_pairs(near_pairs_ref, counts_ref[0, 0], list_ref, clusters)
    elems = damage_ref.shape[1]
    disp = [disp_ref[:, c * elems : (c + 1) * elems] for c in range(3)]
    separation = jnp.sqrt(1.0 + (disp[0] * disp[0] + disp[1] * disp[1] + disp[2] * disp[2]))
    softened = 1.0 - jnp.exp(-(separation - 1.0) / softening)
    intact = intact_ref[...].astype(jnp.float32)
    damage = intact * softened + (1.0 - intact)
    damage_ref[...] = damage
    hold = (1.0 - damage) * stiff_ref[...]
    for c in range(3):
        base_ref[:, c * elems : (c + 1) * elems] = -hold * disp[c]

    def multiply(t, carry):
        start = pl.multiple_of(t * FOLD, FOLD)
        lanes = pl.ds(start, FOLD)
        fetch(t).wait()
        coeff = coeff_scr[:, lanes]
        for r in range(rank):
            product = buffer[r, :, lanes].astype(jnp.float32) * coeff
            folded = product[0:SUBLANES]
            for s in range(1, rank // SUBLANES):
                folded = folded + product[s * SUBLANES : (s + 1) * SUBLANES]
            for h in range(FOLD // LANES):
                sum_scr[h, r * SUBLANES : (r + 1) * SUBLANES, :] = folded[
                    :, h * LANES : (h + 1) * LANES
                ]
        parts = []
        for h in range(FOLD // LANES):
            total = sum_scr[h, pl.ds(0, rank, stride=SUBLANES), :]
            for s in range(1, SUBLANES):
                total = total + sum_scr[h, pl.ds(s, rank, stride=SUBLANES), :]
            parts.append(total)
        coupled = jnp.concatenate(parts, axis=1)
        high = coupled.astype(jnp.bfloat16)
        low = (coupled - high.astype(jnp.float32)).astype(jnp.bfloat16)
        both = jnp.concatenate([high, low], axis=0)
        summed_scr[...] += lax.dot_general(
            place_scr[:, lanes], both, (((1,), (1,)), ((), ())), preferred_element_type=jnp.float32
        )
        return carry

    lax.fori_loop(0, live, multiply, 0)

    i = lax.axis_index("rows")
    j = lax.axis_index("cols")
    from_last = jnp.where(j < cols - 1, i, i - 1)
    from_first = jnp.where(j > 0, i, i + 1)
    edge = 2 * HALO
    halo_scr[...] = jnp.zeros_like(halo_scr)
    sides = (
        (0, jnp.minimum(from_first, rows - 1), from_first < rows),
        (edge, jnp.maximum(from_last, 0), from_last >= 0),
    )
    for side, (row, owner, there) in enumerate(sides):
        start = pl.multiple_of(owner * clusters, clusters)
        whole = jnp.where(there, gathered_ref[pl.ds(start, clusters), :], 0.0)
        for n in range(PIECES):
            piece = whole.astype(jnp.bfloat16).astype(jnp.float32)
            whole = whole - piece
            for g in range(segments):
                to = (n * segments + g) * edge
                here = g * 2 * edge + row
                halo_scr[side, to : to + edge, :] = piece[here : here + edge, :]
    after = jnp.where(j < cols - 1, j + 1, 0)
    lane = lax.broadcasted_iota(jnp.int32, (clusters, LANES), 1)
    for d in range(cols):
        halo = halo_scr[jnp.where(after == d, 1, 0)]
        mine = summed_scr[d * clusters : (d + 1) * clusters, :]
        mine = mine + pltpu.roll(mine, rank, 1)
        out_ref[d] = jnp.where(lane < rank, mine, halo).astype(out_ref.dtype)


def far_field(counts, pairs, gathered, near_pairs, disp, intact, stiffness, blocks, cols, segments):
    rank, _, slots = blocks.shape
    rows = lax.axis_size("rows")
    clusters = gathered.shape[0] // rows
    return pl.pallas_call(
        functools.partial(far_kernel, segments=segments),
        out_shape=(
            jax.ShapeDtypeStruct((cols, clusters, LANES), jnp.bfloat16),
            jax.ShapeDtypeStruct(disp.shape, jnp.float32),
            jax.ShapeDtypeStruct(stiffness.shape, jnp.float32),
            jax.ShapeDtypeStruct((SUBLANES, near_pairs.shape[1]), jnp.int32),
        ),
        in_specs=in_hbm(8),
        out_specs=(pl.BlockSpec(memory_space=pltpu.VMEM),) * 4,
        scratch_shapes=[
            pltpu.SMEM(counts.shape, counts.dtype),
            pltpu.VMEM(pairs.shape, pairs.dtype),
            pltpu.VMEM(gathered.shape, gathered.dtype),
            pltpu.VMEM(near_pairs.shape, near_pairs.dtype),
            pltpu.VMEM(disp.shape, disp.dtype),
            pltpu.VMEM(intact.shape, intact.dtype),
            pltpu.VMEM(stiffness.shape, stiffness.dtype),
            pltpu.VMEM(blocks.shape, blocks.dtype),
            pltpu.VMEM((rows * clusters, LANES), jnp.bfloat16),
            pltpu.VMEM((rank, slots), jnp.float32),
            pltpu.VMEM((cols * clusters, slots), jnp.bfloat16),
            pltpu.VMEM((FOLD // LANES, rank * SUBLANES, LANES), jnp.float32),
            pltpu.VMEM((cols * clusters, LANES), jnp.float32),
            pltpu.VMEM((2, clusters, LANES), jnp.float32),
            pltpu.SemaphoreType.DMA((7,)),
            pltpu.SemaphoreType.DMA((slots // FOLD,)),
        ],
        compiler_params=pltpu.CompilerParams(vmem_limit_bytes=VMEM),
        cost_estimate=pl.CostEstimate(
            flops=2 * rank * rank * slots,
            bytes_accessed=2 * rank * rank * slots,
            transcendentals=0,
        ),
        name="far_field",
    )(
        counts,
        *pinned(pairs),
        gathered,
        *pinned(near_pairs, disp, intact, stiffness, blocks),
    )


def replicate(rows, chunks, store, turned=False):
    within = lax.broadcasted_iota(jnp.int32, (rows.shape[0], LANES), 1)
    if turned:
        within = within + (within // CHUNK) * SUBLANES
    within = within % CHUNK
    for m in range(3 * chunks):
        tile = m // GROUPS
        store(
            m,
            jnp.take_along_axis(
                rows[:, tile * LANES : (tile + 1) * LANES],
                within + (m % GROUPS) * CHUNK,
                axis=1,
                mode="promise_in_bounds",
            ),
        )


def row_of(ref, n, row):
    return ref[n, pl.ds(row, SUBLANES, stride=0), :]


def turn(wide):
    return pltpu.roll(wide, 0, 1, stride=1, stride_axis=0)


def pair_sums(tgt, src, chunks):
    sums = [None] * (3 * chunks)
    size = 3 * chunks
    for h in range(chunks):
        x = [tgt(c * chunks + h) for c in range(3)]
        for f in range(chunks):
            r = [x[c] - src(c * chunks + f) for c in range(3)]
            u = [src(size + c * chunks + f) for c in range(3)]
            q = (r[0] * r[0] + core_square) + (r[1] * r[1] + r[2] * r[2])
            s = r[0] * u[0] + (r[1] * u[1] + r[2] * u[2])
            inverse = lax.rsqrt(q)
            square = inverse * inverse
            weight = square * inverse
            s = (3.0 * s) * square
            for c in range(3):
                term = weight * (u[c] - s * r[c])
                m = c * chunks + h
                sums[m] = term if sums[m] is None else sums[m] + term
    return sums


def gather_sums(acc_scr, clusters, chunks, store):
    own_group = lax.broadcasted_iota(jnp.int32, (clusters, LANES), 1) // CHUNK
    for t in range(pl.cdiv(3 * chunks, GROUPS)):
        merged = None
        for g in range(GROUPS):
            m = t * GROUPS + g
            if m >= 3 * chunks:
                break
            total = acc_scr[m, pl.ds(0, clusters, stride=SUBLANES), :]
            for s in range(1, SUBLANES):
                total = total + acc_scr[m, pl.ds(s, clusters, stride=SUBLANES), :]
            total = total + pltpu.roll(total, 2 * CHUNK, 1)
            total = total + pltpu.roll(total, CHUNK, 1)
            merged = total if merged is None else jnp.where(own_group == g, total, merged)
        store(t, merged)


def turn_matrix():
    shape = (PIECES * CHUNK, SUBLANES * LANES)
    column = lax.broadcasted_iota(jnp.int32, shape, 1)
    lane = column % LANES
    entry = (lane + (lane // CHUNK) * SUBLANES + column // LANES) % CHUNK
    row = lax.broadcasted_iota(jnp.int32, shape, 0) % CHUNK
    return jnp.where(entry == row, 1.0, 0.0).astype(jnp.bfloat16)


def exact_pieces(value):
    pieces = []
    for _ in range(PIECES):
        piece = value.astype(jnp.bfloat16)
        pieces.append(piece)
        value = value - piece.astype(jnp.float32)
    return pieces


def near_kernel(
    list_hbm,
    pos_hbm,
    disp_hbm,
    base_ref,
    damage_ref,
    out_ref,
    edge_ref,
    damage_hbm,
    list_ref,
    pos_ref,
    disp_ref,
    wide_scr,
    piece_scr,
    turn_scr,
    tgt_scr,
    src_scr,
    acc_scr,
    sems,
):
    clusters, width = base_ref.shape
    elems = width // 3
    chunks = elems // CHUNK
    size = 3 * chunks

    moves = start_all(
        sems,
        (
            (list_hbm, list_ref),
            (damage_ref, damage_hbm),
            (pos_hbm, pos_ref),
            (disp_hbm, disp_ref),
        ),
    )
    acc_scr[...] = jnp.zeros_like(acc_scr)
    turn_scr[...] = turn_matrix()

    moves[2].wait()
    wide_scr[:, 0:width] = pos_ref[...]
    edge_ref[0:HALO, :] = pos_ref[0:HALO, :]
    edge_ref[HALO:, :] = pos_ref[clusters - HALO :, :]
    moves[3].wait()
    for k, values in enumerate((pos_ref, disp_ref)):
        for m in range(size):
            pieces = exact_pieces(values[:, m * CHUNK : (m + 1) * CHUNK])
            piece_scr[(k * size + m) * clusters : (k * size + m + 1) * clusters, :] = (
                jnp.concatenate(pieces, axis=1)
            )
    columns = 2 * LANES
    for t in range(SUBLANES * LANES // columns):
        for k in range(2):
            rows = size * clusters
            turned = jnp.dot(
                piece_scr[k * rows : (k + 1) * rows, :],
                turn_scr[:, t * columns : (t + 1) * columns],
                preferred_element_type=jnp.float32,
            )
            for m in range(size):
                for h in range(columns // LANES):
                    s = t * (columns // LANES) + h
                    src_scr[k * size + m, pl.ds(s, clusters, stride=SUBLANES), :] = turned[
                        m * clusters : (m + 1) * clusters, h * LANES : (h + 1) * LANES
                    ]

    def store_target(m, value):
        tgt_scr[m] = value

    replicate(wide_scr[...], chunks, store_target)
    moves[0].wait()
    count = list_ref[3, 0]

    def sums_of(slot):
        target = list_ref[0, slot]
        source = pl.multiple_of(list_ref[1, slot] * SUBLANES, SUBLANES)
        return pair_sums(
            lambda m: row_of(tgt_scr, m, target),
            lambda n: src_scr[n, pl.ds(source, SUBLANES), :],
            chunks,
        )

    def step(it, carry):
        for k in range(0, UNROLL, TOGETHER):
            slots = [it * UNROLL + k + n for n in range(TOGETHER)]
            results = [sums_of(slot) for slot in slots]
            for slot, sums in zip(slots, results):
                into = pl.multiple_of(list_ref[2, slot], SUBLANES)
                for m in range(size):
                    acc_scr[m, pl.ds(into, SUBLANES), :] += sums[m]
        return carry

    lax.fori_loop(0, (count + UNROLL - 1) // UNROLL, step, 0)

    def store_sum(t, value):
        wide_scr[:, t * LANES : (t + 1) * LANES] = value

    gather_sums(acc_scr, clusters, chunks, store_sum)
    out_ref[...] = base_ref[...] + wide_scr[:, 0:width]
    moves[1].wait()


def near_field(listed, pos, disp, base, damage):
    clusters, width = pos.shape
    elems = width // 3
    chunks = elems // CHUNK
    padded = pl.cdiv(width, LANES) * LANES
    slots = listed.shape[1]
    vmem = pl.BlockSpec(memory_space=pltpu.VMEM)
    return pl.pallas_call(
        near_kernel,
        out_shape=(
            jax.ShapeDtypeStruct((clusters, width), jnp.float32),
            jax.ShapeDtypeStruct((2 * HALO, width), jnp.float32),
            jax.ShapeDtypeStruct(damage.shape, jnp.float32),
        ),
        in_specs=in_hbm(3) + [vmem] * 2,
        out_specs=(vmem, vmem, *in_hbm(1)),
        scratch_shapes=[
            pltpu.SMEM(listed.shape, listed.dtype),
            pltpu.VMEM(pos.shape, pos.dtype),
            pltpu.VMEM(disp.shape, disp.dtype),
            pltpu.VMEM((clusters, padded), jnp.float32),
            pltpu.VMEM((6 * chunks * clusters, PIECES * CHUNK), jnp.bfloat16),
            pltpu.VMEM((PIECES * CHUNK, SUBLANES * LANES), jnp.bfloat16),
            pltpu.VMEM((3 * chunks, clusters, LANES), jnp.float32),
            pltpu.VMEM((6 * chunks, clusters * SUBLANES, LANES), jnp.float32),
            pltpu.VMEM((3 * chunks, (clusters + 1) * SUBLANES, LANES), jnp.float32),
            pltpu.SemaphoreType.DMA((4,)),
        ],
        compiler_params=pltpu.CompilerParams(vmem_limit_bytes=VMEM),
        cost_estimate=pl.CostEstimate(
            flops=30 * slots * elems * elems,
            bytes_accessed=4 * clusters * width * 6,
            transcendentals=slots * elems * elems,
        ),
        name="near_field",
    )(listed, *pinned(pos, disp), base, damage)


def finish_kernel(
    rest_hbm,
    edge_ref,
    received_ref,
    near_ref,
    far_ref,
    out_ref,
    rest_ref,
    ext_scr,
    halo_scr,
    tgt_scr,
    src_scr,
    acc_scr,
    sem,
    *,
    rank,
):
    clusters, width = near_ref.shape
    cols = received_ref.shape[0]
    elems = width // 3
    chunks = elems // CHUNK
    size = 3 * chunks
    spare = LANES - rank
    segments = split_rows(width, spare)
    edge = 2 * HALO

    fetch = pltpu.make_async_copy(rest_hbm, rest_ref, sem)
    fetch.start()
    acc_scr[...] = jnp.zeros_like(acc_scr)

    j = lax.axis_index("cols")
    before = jnp.where(j > 0, j - 1, cols - 1)
    after = jnp.where(j < cols - 1, j + 1, 0)
    for start, sender in ((0, before), (HALO, after)):
        halo_scr[...] = received_ref[sender].astype(jnp.float32)
        rows = edge * segments
        whole = halo_scr[0:rows, :]
        for n in range(1, PIECES):
            whole = whole + halo_scr[n * rows : (n + 1) * rows, :]
        for g in range(segments):
            count = min(spare, width - g * spare)
            for k in range(2):
                row = (2 * g + k) * HALO
                ext_scr[k, start : start + HALO, g * spare : g * spare + count] = whole[
                    row : row + HALO, rank : rank + count
                ]
    ext_scr[1, edge : 2 * edge, 0:width] = edge_ref[...]
    for k in range(2):

        def store(m, value, k=k):
            for b in range(edge):
                wide = jnp.broadcast_to(value[b : b + 1, :], (SUBLANES, LANES))
                src_scr[(1 - k) * size + m, b * SUBLANES : (b + 1) * SUBLANES, :] = turn(wide)

        replicate(ext_scr[k], chunks, store, True)

    def store_target(m, value):
        tgt_scr[m] = value

    replicate(ext_scr[1], chunks, store_target)
    fetch.wait()
    number = rest_ref[6, 0]

    def one_pair(n):
        target = rest_ref[4, n]
        source = rest_ref[5, n]
        target = jnp.where(target < HALO, target, target - (clusters - edge))
        source = jnp.where(source < HALO, source, source - clusters)
        live = n < number
        target = jnp.where(live, target, edge)
        source = pl.multiple_of(jnp.where(live, source, 0) * SUBLANES, SUBLANES)
        into = pl.multiple_of(target * SUBLANES, SUBLANES)
        row = edge + jnp.where(live, target, 0)
        sums = pair_sums(
            lambda m: row_of(tgt_scr, m, row),
            lambda k: src_scr[k, pl.ds(source, SUBLANES), :],
            chunks,
        )
        for m in range(size):
            acc_scr[m, pl.ds(into, SUBLANES), :] += sums[m]

    def step(it, carry):
        for k in range(FEW):
            one_pair(it * FEW + k)
        return carry

    lax.fori_loop(0, (number + FEW - 1) // FEW, step, 0)

    def store_sum(t, value):
        ext_scr[0, :, t * LANES : (t + 1) * LANES] = value

    gather_sums(acc_scr, 2 * edge, chunks, store_sum)
    out_ref[...] = near_ref[...] + far_ref[...]
    out_ref[0:HALO, :] += ext_scr[0, 0:HALO, 0:width]
    out_ref[clusters - HALO :, :] += ext_scr[0, HALO:edge, 0:width]


def finish(rest, edges, received, near, far, rank):
    clusters, width = near.shape
    chunks = width // 3 // CHUNK
    padded = pl.cdiv(width, LANES) * LANES
    edge = 2 * HALO
    vmem = pl.BlockSpec(memory_space=pltpu.VMEM)
    return pl.pallas_call(
        functools.partial(finish_kernel, rank=rank),
        out_shape=jax.ShapeDtypeStruct((clusters, width), jnp.float32),
        in_specs=in_hbm(1) + [vmem] * 4,
        out_specs=vmem,
        scratch_shapes=[
            pltpu.SMEM(rest.shape, rest.dtype),
            pltpu.VMEM((2, 2 * edge, padded), jnp.float32),
            pltpu.VMEM((clusters, LANES), jnp.float32),
            pltpu.VMEM((3 * chunks, 2 * edge, LANES), jnp.float32),
            pltpu.VMEM((6 * chunks, edge * SUBLANES, LANES), jnp.float32),
            pltpu.VMEM((3 * chunks, 2 * edge * SUBLANES, LANES), jnp.float32),
            pltpu.SemaphoreType.DMA(()),
        ],
        compiler_params=pltpu.CompilerParams(vmem_limit_bytes=VMEM),
        cost_estimate=pl.CostEstimate(
            flops=2 * clusters * width, bytes_accessed=16 * clusters * width, transcendentals=0
        ),
        name="finish",
    )(rest, edges, received, near, far)


def local(
    displacement,
    positions,
    cluster_basis,
    near_pairs,
    near_count,
    far_pairs,
    far_count,
    far_blocks,
    intact,
    stiffness,
):
    cols = lax.axis_size("cols")
    clusters, width, rank = cluster_basis.shape
    spare = LANES - rank
    segments = split_rows(width, spare)
    disp_bf, halo, counts = prepare(near_count, far_count, displacement, positions, spare)
    coeff = jnp.einsum("kf,kfr->kr", disp_bf, cluster_basis, preferred_element_type=jnp.float32)
    payload = jnp.concatenate([coeff, halo], axis=1)
    gathered = lax.all_gather(payload, "rows", axis=0, tiled=True)
    partial, base, damage, listed = far_field(
        counts,
        far_pairs.T,
        gathered,
        near_pairs.T,
        displacement,
        intact,
        stiffness,
        far_blocks.transpose(1, 2, 0),
        cols,
        segments,
    )
    received = lax.all_to_all(partial, "cols", split_axis=0, concat_axis=0)
    near, edges, damage = near_field(listed, positions, displacement, base, damage)
    owned = jnp.sum(received[:, :, :rank].astype(jnp.float32), axis=0).astype(jnp.bfloat16)
    far = jnp.einsum("kfr,kr->kf", cluster_basis, owned, preferred_element_type=jnp.float32)
    return finish(listed, edges, received, near, far, rank), damage


def solution(mesh):
    both = ("rows", "cols")
    in_specs = (
        P(both, None),
        P(both, None),
        P(both, None, None),
        P(both, None),
        P(both),
        P(both, None),
        P(both),
        P(both, None, None),
        P(both, None),
        P(both, None),
    )
    out_specs = (P(both, None), P(both, None))
    return jax.shard_map(local, mesh=mesh, in_specs=in_specs, out_specs=out_specs, check_vma=False)
```

```python
import functools

import jax
import jax.numpy as jnp
from jax import lax
from jax.experimental import pallas as pl
from jax.experimental.pallas import tpu as pltpu
from jax.sharding import PartitionSpec as P

HALO = 2
LANES = 128
SUBLANES = 8
CHUNK = 32
GROUPS = LANES // CHUNK
core_square = 0.25
softening = 1.5
UNROLL = 8
TOGETHER = 2
FEW = 4
FOLD = 256
PIECES = 3
VMEM = 20 * 1024 * 1024


def split_rows(width, lanes):
    return pl.cdiv(width, lanes)


def in_hbm(count):
    return [pl.BlockSpec(memory_space=pltpu.HBM)] * count


def pinned(*arrays):
    return [pltpu.with_memory_space_constraint(x, pltpu.HBM) for x in arrays]


def start_all(sems, moves):
    copies = [
        pltpu.make_async_copy(source, target, sems.at[n])
        for n, (source, target) in enumerate(moves)
    ]
    for copy in copies:
        copy.start()
    return copies


def prepare_kernel(
    near_count_ref,
    far_count_ref,
    disp_hbm,
    pos_hbm,
    low_ref,
    halo_ref,
    counts_ref,
    disp_ref,
    pos_ref,
    sems,
):
    clusters, width = disp_ref.shape
    spare = halo_ref.shape[1]
    segments = split_rows(width, spare)
    inputs = start_all(sems, ((disp_hbm, disp_ref), (pos_hbm, pos_ref)))
    halo_ref[...] = jnp.zeros_like(halo_ref)
    row = lax.broadcasted_iota(jnp.int32, counts_ref.shape, 0)
    counts_ref[...] = jnp.where(row == 0, near_count_ref[0], far_count_ref[0])
    for copy in inputs:
        copy.wait()
    low_ref[...] = disp_ref[...].astype(low_ref.dtype)
    row = 0
    for g in range(segments):
        size = min(spare, width - g * spare)
        for start in (0, clusters - HALO):
            for ref in (disp_ref, pos_ref):
                halo_ref[row : row + HALO, 0:size] = ref[
                    start : start + HALO, g * spare : g * spare + size
                ]
                row += HALO


def list_pairs(pairs_ref, near_count, list_ref, clusters):
    slots = pairs_ref.shape[1]
    target = pairs_ref[0:1, :]
    source = pairs_ref[1:2, :]
    slot = lax.broadcasted_iota(jnp.int32, (1, slots), 1)
    live = slot < near_count
    own = jnp.logical_and(source >= HALO, source < clusters + HALO)
    square = (slots, slots)
    first = lax.broadcasted_iota(jnp.int32, square, 0)
    upto = first <= lax.broadcasted_iota(jnp.int32, square, 1)
    upto = jnp.where(upto, 1.0, 0.0).astype(jnp.bfloat16)
    row = lax.broadcasted_iota(jnp.int32, (SUBLANES, slots), 0)
    pairs = jnp.where(row == 0, target, source).astype(jnp.float32).astype(jnp.bfloat16)
    results = []
    for wanted in (own, jnp.logical_not(own)):
        chosen = jnp.where(jnp.logical_and(live, wanted), 1.0, 0.0)
        order = jnp.dot(
            jnp.broadcast_to(chosen, (SUBLANES, slots)).astype(jnp.bfloat16),
            upto,
            preferred_element_type=jnp.float32,
        )
        place = first == jnp.where(chosen > 0.0, order[0:1, :] - 1.0, -1.0).astype(jnp.int32)
        place = jnp.where(place, 1.0, 0.0).astype(jnp.bfloat16)
        together = lax.dot_general(
            pairs, place, (((1,), (1,)), ((), ())), preferred_element_type=jnp.float32
        ).astype(jnp.int32)
        number = jnp.sum(chosen, axis=1, keepdims=True).astype(jnp.int32)
        results.append((together, jnp.broadcast_to(number, (1, slots))))
    (pairs, number), (others, others_number) = results
    list_ref[0:1, :] = pairs[0:1, :]
    list_ref[1:2, :] = jnp.clip(pairs[1:2, :] - HALO, 0, clusters - 1)
    list_ref[2:3, :] = jnp.where(slot < number, pairs[0:1, :], clusters) * SUBLANES
    list_ref[3:4, :] = number
    list_ref[4:6, :] = others[0:2, :]
    list_ref[6:7, :] = others_number
    list_ref[7:8, :] = jnp.zeros((1, slots), jnp.int32)


def prepare(near_count, far_count, disp, pos, spare):
    clusters, width = disp.shape
    vmem = pl.BlockSpec(memory_space=pltpu.VMEM)
    smem = pl.BlockSpec(memory_space=pltpu.SMEM)
    return pl.pallas_call(
        prepare_kernel,
        out_shape=(
            jax.ShapeDtypeStruct((clusters, width), jnp.bfloat16),
            jax.ShapeDtypeStruct((clusters, spare), jnp.float32),
            jax.ShapeDtypeStruct((SUBLANES, LANES), jnp.int32),
        ),
        in_specs=[smem] * 2 + in_hbm(2),
        out_specs=(vmem,) * 3,
        scratch_shapes=[
            pltpu.VMEM(disp.shape, disp.dtype),
            pltpu.VMEM(pos.shape, pos.dtype),
            pltpu.SemaphoreType.DMA((2,)),
        ],
        compiler_params=pltpu.CompilerParams(vmem_limit_bytes=VMEM),
        cost_estimate=pl.CostEstimate(
            flops=clusters * width, bytes_accessed=12 * clusters * width, transcendentals=0
        ),
        name="prepare",
    )(near_count, far_count, *pinned(disp, pos))


def far_kernel(
    counts_hbm,
    pairs_hbm,
    gathered_hbm,
    near_pairs_hbm,
    pos_hbm,
    disp_hbm,
    intact_hbm,
    stiff_hbm,
    blocks_ref,
    out_ref,
    pos_ref,
    hold_ref,
    list_ref,
    damage_hbm,
    counts_ref,
    pairs_ref,
    gathered_ref,
    near_pairs_ref,
    disp_ref,
    intact_ref,
    stiff_ref,
    damage_ref,
    buffer,
    column_scr,
    coeff_scr,
    place_scr,
    sum_scr,
    summed_scr,
    halo_scr,
    sems,
    block_sems,
    out_sem,
    *,
    segments,
):
    rank, _, slots = buffer.shape
    cols, clusters, _ = out_ref.shape
    targets = cols * clusters
    rows = gathered_ref.shape[0] // clusters
    sources = rows * clusters

    def fetch(t):
        here = pl.ds(pl.multiple_of(t * FOLD, FOLD), FOLD)
        return pltpu.make_async_copy(
            blocks_ref.at[:, :, here], buffer.at[:, :, here], block_sems.at[t]
        )

    inputs = start_all(
        sems,
        (
            (counts_hbm, counts_ref),
            (pairs_hbm, pairs_ref),
            (gathered_hbm, gathered_ref),
            (near_pairs_hbm, near_pairs_ref),
            (pos_hbm, pos_ref),
            (disp_hbm, disp_ref),
            (intact_hbm, intact_ref),
            (stiff_hbm, stiff_ref),
        ),
    )
    fetch(0).start()
    summed_scr[...] = jnp.zeros_like(summed_scr)
    inputs[0].wait()
    count = counts_ref[1, 0]
    live = (count + FOLD - 1) // FOLD

    @pl.when(live > 1)
    def _():
        fetch(1).start()

    inputs[1].wait()
    inputs[2].wait()
    column_scr[...] = gathered_ref[...].astype(jnp.bfloat16)

    index = lax.broadcasted_iota(jnp.int32, (sources, slots), 0)
    pick = jnp.where(index == pairs_ref[1:2, :], 1.0, 0.0).astype(jnp.bfloat16)
    coeff = lax.dot_general(
        column_scr[...], pick, (((0,), (0,)), ((), ())), preferred_element_type=jnp.float32
    )
    coeff_scr[...] = coeff[0:rank, :]
    slot = lax.broadcasted_iota(jnp.int32, (1, slots), 1)
    wanted = jnp.where(slot < count, pairs_ref[0:1, :], -1)
    index = lax.broadcasted_iota(jnp.int32, (targets, slots), 0)
    place_scr[...] = jnp.where(index == wanted, 1.0, 0.0).astype(jnp.bfloat16)

    for copy in inputs[3:]:
        copy.wait()
    list_pairs(near_pairs_ref, counts_ref[0, 0], list_ref, clusters)
    elems = damage_ref.shape[1]
    disp = [disp_ref[:, c * elems : (c + 1) * elems] for c in range(3)]
    separation = jnp.sqrt(1.0 + (disp[0] * disp[0] + disp[1] * disp[1] + disp[2] * disp[2]))
    softened = 1.0 - jnp.exp(-(separation - 1.0) / softening)
    intact = intact_ref[...].astype(jnp.float32)
    damage = intact * softened + (1.0 - intact)
    damage_ref[...] = damage
    damage_out = pltpu.make_async_copy(damage_ref, damage_hbm, out_sem)
    damage_out.start()
    hold_ref[...] = (1.0 - damage) * stiff_ref[...]

    def multiply(t, carry):
        start = pl.multiple_of(t * FOLD, FOLD)
        lanes = pl.ds(start, FOLD)
        fetch(t).wait()

        @pl.when(t + 2 < live)
        def _():
            fetch(t + 2).start()

        coeff = coeff_scr[:, lanes]
        for r in range(rank):
            product = buffer[r, :, lanes].astype(jnp.float32) * coeff
            folded = product[0:SUBLANES]
            for s in range(1, rank // SUBLANES):
                folded = folded + product[s * SUBLANES : (s + 1) * SUBLANES]
            for h in range(FOLD // LANES):
                sum_scr[h, r * SUBLANES : (r + 1) * SUBLANES, :] = folded[
                    :, h * LANES : (h + 1) * LANES
                ]
        parts = []
        for h in range(FOLD // LANES):
            total = sum_scr[h, pl.ds(0, rank, stride=SUBLANES), :]
            for s in range(1, SUBLANES):
                total = total + sum_scr[h, pl.ds(s, rank, stride=SUBLANES), :]
            parts.append(total)
        coupled = jnp.concatenate(parts, axis=1)
        high = coupled.astype(jnp.bfloat16)
        low = (coupled - high.astype(jnp.float32)).astype(jnp.bfloat16)
        both = jnp.concatenate([high, low], axis=0)
        summed_scr[...] += lax.dot_general(
            place_scr[:, lanes], both, (((1,), (1,)), ((), ())), preferred_element_type=jnp.float32
        )
        return carry

    lax.fori_loop(0, live, multiply, 0)
    damage_out.wait()

    i = lax.axis_index("rows")
    j = lax.axis_index("cols")
    from_last = jnp.where(j < cols - 1, i, i - 1)
    from_first = jnp.where(j > 0, i, i + 1)
    edge = 2 * HALO
    halo_scr[...] = jnp.zeros_like(halo_scr)
    sides = (
        (0, jnp.minimum(from_first, rows - 1), from_first < rows),
        (edge, jnp.maximum(from_last, 0), from_last >= 0),
    )
    for side, (row, owner, there) in enumerate(sides):
        start = pl.multiple_of(owner * clusters, clusters)
        whole = jnp.where(there, gathered_ref[pl.ds(start, clusters), :], 0.0)
        for n in range(PIECES):
            piece = whole.astype(jnp.bfloat16).astype(jnp.float32)
            whole = whole - piece
            for g in range(segments):
                to = (n * segments + g) * edge
                here = g * 2 * edge + row
                halo_scr[side, to : to + edge, :] = piece[here : here + edge, :]
    after = jnp.where(j < cols - 1, j + 1, 0)
    lane = lax.broadcasted_iota(jnp.int32, (clusters, LANES), 1)
    for d in range(cols):
        halo = halo_scr[jnp.where(after == d, 1, 0)]
        mine = summed_scr[d * clusters : (d + 1) * clusters, :]
        mine = mine + pltpu.roll(mine, rank, 1)
        out_ref[d] = jnp.where(lane < rank, mine, halo).astype(out_ref.dtype)


def far_field(
    counts, pairs, gathered, near_pairs, pos, disp, intact, stiffness, blocks, cols, segments
):
    rank, _, slots = blocks.shape
    rows = lax.axis_size("rows")
    clusters = gathered.shape[0] // rows
    return pl.pallas_call(
        functools.partial(far_kernel, segments=segments),
        out_shape=(
            jax.ShapeDtypeStruct((cols, clusters, LANES), jnp.bfloat16),
            jax.ShapeDtypeStruct(pos.shape, jnp.float32),
            jax.ShapeDtypeStruct(stiffness.shape, jnp.float32),
            jax.ShapeDtypeStruct((SUBLANES, near_pairs.shape[1]), jnp.int32),
            jax.ShapeDtypeStruct(stiffness.shape, jnp.float32),
        ),
        in_specs=in_hbm(9),
        out_specs=(pl.BlockSpec(memory_space=pltpu.VMEM),) * 4 + tuple(in_hbm(1)),
        scratch_shapes=[
            pltpu.SMEM(counts.shape, counts.dtype),
            pltpu.VMEM(pairs.shape, pairs.dtype),
            pltpu.VMEM(gathered.shape, gathered.dtype),
            pltpu.VMEM(near_pairs.shape, near_pairs.dtype),
            pltpu.VMEM(disp.shape, disp.dtype),
            pltpu.VMEM(intact.shape, intact.dtype),
            pltpu.VMEM(stiffness.shape, stiffness.dtype),
            pltpu.VMEM(stiffness.shape, jnp.float32),
            pltpu.VMEM(blocks.shape, blocks.dtype),
            pltpu.VMEM((rows * clusters, LANES), jnp.bfloat16),
            pltpu.VMEM((rank, slots), jnp.float32),
            pltpu.VMEM((cols * clusters, slots), jnp.bfloat16),
            pltpu.VMEM((FOLD // LANES, rank * SUBLANES, LANES), jnp.float32),
            pltpu.VMEM((cols * clusters, LANES), jnp.float32),
            pltpu.VMEM((2, clusters, LANES), jnp.float32),
            pltpu.SemaphoreType.DMA((8,)),
            pltpu.SemaphoreType.DMA((slots // FOLD,)),
            pltpu.SemaphoreType.DMA(()),
        ],
        compiler_params=pltpu.CompilerParams(vmem_limit_bytes=VMEM),
        cost_estimate=pl.CostEstimate(
            flops=2 * rank * rank * slots,
            bytes_accessed=2 * rank * rank * slots,
            transcendentals=0,
        ),
        name="far_field",
    )(
        counts,
        *pinned(pairs),
        gathered,
        *pinned(near_pairs, pos, disp, intact, stiffness, blocks),
    )


def replicate(rows, chunks, store, turned=False):
    within = lax.broadcasted_iota(jnp.int32, (rows.shape[0], LANES), 1)
    if turned:
        within = within + (within // CHUNK) * SUBLANES
    within = within % CHUNK
    for m in range(3 * chunks):
        tile = m // GROUPS
        store(
            m,
            jnp.take_along_axis(
                rows[:, tile * LANES : (tile + 1) * LANES],
                within + (m % GROUPS) * CHUNK,
                axis=1,
                mode="promise_in_bounds",
            ),
        )


def row_of(ref, n, row):
    return ref[n, pl.ds(row, SUBLANES, stride=0), :]


def turn(wide):
    return pltpu.roll(wide, 0, 1, stride=1, stride_axis=0)


def pair_sums(tgt, src, chunks):
    sums = [None] * (3 * chunks)
    size = 3 * chunks
    for h in range(chunks):
        x = [tgt(c * chunks + h) for c in range(3)]
        for f in range(chunks):
            r = [x[c] - src(c * chunks + f) for c in range(3)]
            u = [src(size + c * chunks + f) for c in range(3)]
            q = (r[0] * r[0] + core_square) + (r[1] * r[1] + r[2] * r[2])
            s = r[0] * u[0] + (r[1] * u[1] + r[2] * u[2])
            inverse = lax.rsqrt(q)
            square = inverse * inverse
            weight = square * inverse
            s = (3.0 * s) * square
            for c in range(3):
                term = weight * (u[c] - s * r[c])
                m = c * chunks + h
                sums[m] = term if sums[m] is None else sums[m] + term
    return sums


def gather_sums(acc_scr, clusters, chunks, store):
    own_group = lax.broadcasted_iota(jnp.int32, (clusters, LANES), 1) // CHUNK
    for t in range(pl.cdiv(3 * chunks, GROUPS)):
        merged = None
        for g in range(GROUPS):
            m = t * GROUPS + g
            if m >= 3 * chunks:
                break
            total = acc_scr[m, pl.ds(0, clusters, stride=SUBLANES), :]
            for s in range(1, SUBLANES):
                total = total + acc_scr[m, pl.ds(s, clusters, stride=SUBLANES), :]
            total = total + pltpu.roll(total, 2 * CHUNK, 1)
            total = total + pltpu.roll(total, CHUNK, 1)
            merged = total if merged is None else jnp.where(own_group == g, total, merged)
        store(t, merged)


def turn_matrix():
    shape = (PIECES * CHUNK, SUBLANES * LANES)
    column = lax.broadcasted_iota(jnp.int32, shape, 1)
    lane = column % LANES
    entry = (lane + (lane // CHUNK) * SUBLANES + column // LANES) % CHUNK
    row = lax.broadcasted_iota(jnp.int32, shape, 0) % CHUNK
    return jnp.where(entry == row, 1.0, 0.0).astype(jnp.bfloat16)


def exact_pieces(value):
    pieces = []
    for _ in range(PIECES):
        piece = value.astype(jnp.bfloat16)
        pieces.append(piece)
        value = value - piece.astype(jnp.float32)
    return pieces


def near_kernel(
    list_hbm,
    disp_hbm,
    pos_ref,
    hold_ref,
    out_ref,
    edge_ref,
    list_ref,
    disp_ref,
    wide_scr,
    piece_scr,
    turn_scr,
    tgt_scr,
    src_scr,
    acc_scr,
    sems,
):
    clusters, width = pos_ref.shape
    elems = width // 3
    chunks = elems // CHUNK
    size = 3 * chunks

    moves = start_all(sems, ((list_hbm, list_ref), (disp_hbm, disp_ref)))
    acc_scr[...] = jnp.zeros_like(acc_scr)
    turn_scr[...] = turn_matrix()

    wide_scr[:, 0:width] = pos_ref[...]
    edge_ref[0:HALO, :] = pos_ref[0:HALO, :]
    edge_ref[HALO:, :] = pos_ref[clusters - HALO :, :]
    columns = 2 * LANES
    for k, values in enumerate((pos_ref, disp_ref)):
        if k == 1:
            moves[1].wait()
        for m in range(size):
            pieces = exact_pieces(values[:, m * CHUNK : (m + 1) * CHUNK])
            piece_scr[m * clusters : (m + 1) * clusters, :] = jnp.concatenate(pieces, axis=1)
        for t in range(SUBLANES * LANES // columns):
            turned = jnp.dot(
                piece_scr[...],
                turn_scr[:, t * columns : (t + 1) * columns],
                preferred_element_type=jnp.float32,
            )
            for m in range(size):
                for h in range(columns // LANES):
                    s = t * (columns // LANES) + h
                    src_scr[k * size + m, pl.ds(s, clusters, stride=SUBLANES), :] = turned[
                        m * clusters : (m + 1) * clusters, h * LANES : (h + 1) * LANES
                    ]

    def store_target(m, value):
        tgt_scr[m] = value

    replicate(wide_scr[...], chunks, store_target)
    moves[0].wait()
    count = list_ref[3, 0]

    def sums_of(slot):
        target = list_ref[0, slot]
        source = pl.multiple_of(list_ref[1, slot] * SUBLANES, SUBLANES)
        return pair_sums(
            lambda m: row_of(tgt_scr, m, target),
            lambda n: src_scr[n, pl.ds(source, SUBLANES), :],
            chunks,
        )

    def step(it, carry):
        for k in range(0, UNROLL, TOGETHER):
            slots = [it * UNROLL + k + n for n in range(TOGETHER)]
            results = [sums_of(slot) for slot in slots]
            for slot, sums in zip(slots, results):
                into = pl.multiple_of(list_ref[2, slot], SUBLANES)
                for m in range(size):
                    acc_scr[m, pl.ds(into, SUBLANES), :] += sums[m]
        return carry

    lax.fori_loop(0, (count + UNROLL - 1) // UNROLL, step, 0)

    def store_sum(t, value):
        wide_scr[:, t * LANES : (t + 1) * LANES] = value

    gather_sums(acc_scr, clusters, chunks, store_sum)
    for c in range(3):
        here = slice(c * elems, (c + 1) * elems)
        out_ref[:, here] = wide_scr[:, here] - hold_ref[...] * disp_ref[:, here]


def near_field(listed, disp, pos, hold):
    clusters, width = pos.shape
    elems = width // 3
    chunks = elems // CHUNK
    padded = pl.cdiv(width, LANES) * LANES
    slots = listed.shape[1]
    vmem = pl.BlockSpec(memory_space=pltpu.VMEM)
    return pl.pallas_call(
        near_kernel,
        out_shape=(
            jax.ShapeDtypeStruct((clusters, width), jnp.float32),
            jax.ShapeDtypeStruct((2 * HALO, width), jnp.float32),
        ),
        in_specs=in_hbm(2) + [vmem] * 2,
        out_specs=(vmem, vmem),
        scratch_shapes=[
            pltpu.SMEM(listed.shape, listed.dtype),
            pltpu.VMEM(disp.shape, disp.dtype),
            pltpu.VMEM((clusters, padded), jnp.float32),
            pltpu.VMEM((3 * chunks * clusters, PIECES * CHUNK), jnp.bfloat16),
            pltpu.VMEM((PIECES * CHUNK, SUBLANES * LANES), jnp.bfloat16),
            pltpu.VMEM((3 * chunks, clusters, LANES), jnp.float32),
            pltpu.VMEM((6 * chunks, clusters * SUBLANES, LANES), jnp.float32),
            pltpu.VMEM((3 * chunks, (clusters + 1) * SUBLANES, LANES), jnp.float32),
            pltpu.SemaphoreType.DMA((2,)),
        ],
        compiler_params=pltpu.CompilerParams(vmem_limit_bytes=VMEM),
        cost_estimate=pl.CostEstimate(
            flops=30 * slots * elems * elems,
            bytes_accessed=4 * clusters * width * 6,
            transcendentals=slots * elems * elems,
        ),
        name="near_field",
    )(listed, *pinned(disp), pos, hold)


def finish_kernel(
    rest_hbm,
    edge_ref,
    received_ref,
    near_ref,
    far_ref,
    out_ref,
    rest_ref,
    ext_scr,
    halo_scr,
    tgt_scr,
    src_scr,
    acc_scr,
    sem,
    *,
    rank,
):
    clusters, width = near_ref.shape
    cols = received_ref.shape[0]
    elems = width // 3
    chunks = elems // CHUNK
    size = 3 * chunks
    spare = LANES - rank
    segments = split_rows(width, spare)
    edge = 2 * HALO

    fetch = pltpu.make_async_copy(rest_hbm, rest_ref, sem)
    fetch.start()
    acc_scr[...] = jnp.zeros_like(acc_scr)

    j = lax.axis_index("cols")
    before = jnp.where(j > 0, j - 1, cols - 1)
    after = jnp.where(j < cols - 1, j + 1, 0)
    for start, sender in ((0, before), (HALO, after)):
        halo_scr[...] = received_ref[sender].astype(jnp.float32)
        rows = edge * segments
        whole = halo_scr[0:rows, :]
        for n in range(1, PIECES):
            whole = whole + halo_scr[n * rows : (n + 1) * rows, :]
        for g in range(segments):
            count = min(spare, width - g * spare)
            for k in range(2):
                row = (2 * g + k) * HALO
                ext_scr[k, start : start + HALO, g * spare : g * spare + count] = whole[
                    row : row + HALO, rank : rank + count
                ]
    ext_scr[1, edge : 2 * edge, 0:width] = edge_ref[...]
    for k in range(2):

        def store(m, value, k=k):
            for b in range(edge):
                wide = jnp.broadcast_to(value[b : b + 1, :], (SUBLANES, LANES))
                src_scr[(1 - k) * size + m, b * SUBLANES : (b + 1) * SUBLANES, :] = turn(wide)

        replicate(ext_scr[k], chunks, store, True)

    def store_target(m, value):
        tgt_scr[m] = value

    replicate(ext_scr[1], chunks, store_target)
    fetch.wait()
    number = rest_ref[6, 0]

    def one_pair(n):
        target = rest_ref[4, n]
        source = rest_ref[5, n]
        target = jnp.where(target < HALO, target, target - (clusters - edge))
        source = jnp.where(source < HALO, source, source - clusters)
        live = n < number
        target = jnp.where(live, target, edge)
        source = pl.multiple_of(jnp.where(live, source, 0) * SUBLANES, SUBLANES)
        into = pl.multiple_of(target * SUBLANES, SUBLANES)
        row = edge + jnp.where(live, target, 0)
        sums = pair_sums(
            lambda m: row_of(tgt_scr, m, row),
            lambda k: src_scr[k, pl.ds(source, SUBLANES), :],
            chunks,
        )
        for m in range(size):
            acc_scr[m, pl.ds(into, SUBLANES), :] += sums[m]

    def step(it, carry):
        for k in range(FEW):
            one_pair(it * FEW + k)
        return carry

    lax.fori_loop(0, (number + FEW - 1) // FEW, step, 0)

    def store_sum(t, value):
        ext_scr[0, :, t * LANES : (t + 1) * LANES] = value

    gather_sums(acc_scr, 2 * edge, chunks, store_sum)
    out_ref[...] = near_ref[...] + far_ref[...]
    out_ref[0:HALO, :] += ext_scr[0, 0:HALO, 0:width]
    out_ref[clusters - HALO :, :] += ext_scr[0, HALO:edge, 0:width]


def finish(rest, edges, received, near, far, rank):
    clusters, width = near.shape
    chunks = width // 3 // CHUNK
    padded = pl.cdiv(width, LANES) * LANES
    edge = 2 * HALO
    vmem = pl.BlockSpec(memory_space=pltpu.VMEM)
    return pl.pallas_call(
        functools.partial(finish_kernel, rank=rank),
        out_shape=jax.ShapeDtypeStruct((clusters, width), jnp.float32),
        in_specs=in_hbm(1) + [vmem] * 4,
        out_specs=vmem,
        scratch_shapes=[
            pltpu.SMEM(rest.shape, rest.dtype),
            pltpu.VMEM((2, 2 * edge, padded), jnp.float32),
            pltpu.VMEM((clusters, LANES), jnp.float32),
            pltpu.VMEM((3 * chunks, 2 * edge, LANES), jnp.float32),
            pltpu.VMEM((6 * chunks, edge * SUBLANES, LANES), jnp.float32),
            pltpu.VMEM((3 * chunks, 2 * edge * SUBLANES, LANES), jnp.float32),
            pltpu.SemaphoreType.DMA(()),
        ],
        compiler_params=pltpu.CompilerParams(vmem_limit_bytes=VMEM),
        cost_estimate=pl.CostEstimate(
            flops=2 * clusters * width, bytes_accessed=16 * clusters * width, transcendentals=0
        ),
        name="finish",
    )(rest, edges, received, near, far)


def local(
    displacement,
    positions,
    cluster_basis,
    near_pairs,
    near_count,
    far_pairs,
    far_count,
    far_blocks,
    intact,
    stiffness,
):
    cols = lax.axis_size("cols")
    clusters, width, rank = cluster_basis.shape
    spare = LANES - rank
    segments = split_rows(width, spare)
    disp_bf, halo, counts = prepare(near_count, far_count, displacement, positions, spare)
    coeff = jnp.einsum("kf,kfr->kr", disp_bf, cluster_basis, preferred_element_type=jnp.float32)
    payload = jnp.concatenate([coeff, halo], axis=1)
    gathered = lax.all_gather(payload, "rows", axis=0, tiled=True)
    partial, pos, hold, listed, damage = far_field(
        counts,
        far_pairs.T,
        gathered,
        near_pairs.T,
        positions,
        displacement,
        intact,
        stiffness,
        far_blocks.transpose(1, 2, 0),
        cols,
        segments,
    )
    received = lax.all_to_all(partial, "cols", split_axis=0, concat_axis=0)
    near, edges = near_field(listed, displacement, pos, hold)
    owned = jnp.sum(received[:, :, :rank].astype(jnp.float32), axis=0).astype(jnp.bfloat16)
    far = jnp.einsum("kfr,kr->kf", cluster_basis, owned, preferred_element_type=jnp.float32)
    return finish(listed, edges, received, near, far, rank), damage


def solution(mesh):
    both = ("rows", "cols")
    in_specs = (
        P(both, None),
        P(both, None),
        P(both, None, None),
        P(both, None),
        P(both),
        P(both, None),
        P(both),
        P(both, None, None),
        P(both, None),
        P(both, None),
    )
    out_specs = (P(both, None), P(both, None))
    return jax.shard_map(local, mesh=mesh, in_specs=in_specs, out_specs=out_specs, check_vma=False)
```

```python
import functools

import jax
import jax.numpy as jnp
from jax import lax
from jax.experimental import pallas as pl
from jax.experimental.pallas import tpu as pltpu
from jax.sharding import PartitionSpec as P

HALO = 2
LANES = 128
SUBLANES = 8
CHUNK = 32
GROUPS = LANES // CHUNK
core_square = 0.25
softening = 1.5
UNROLL = 8
TOGETHER = 2
FEW = 4
FOLD = 256
WIDE = 512
PIECES = 3
VMEM = 20 * 1024 * 1024


def split_rows(width, lanes):
    return pl.cdiv(width, lanes)


def in_hbm(count):
    return [pl.BlockSpec(memory_space=pltpu.HBM)] * count


def pinned(*arrays):
    return [pltpu.with_memory_space_constraint(x, pltpu.HBM) for x in arrays]


def start_all(sems, moves):
    copies = [
        pltpu.make_async_copy(source, target, sems.at[n])
        for n, (source, target) in enumerate(moves)
    ]
    for copy in copies:
        copy.start()
    return copies


def prepare_kernel(
    near_count_ref,
    far_count_ref,
    disp_hbm,
    pos_hbm,
    low_ref,
    halo_ref,
    counts_ref,
    disp_ref,
    pos_ref,
    sems,
):
    clusters, width = disp_ref.shape
    spare = halo_ref.shape[1]
    segments = split_rows(width, spare)
    inputs = start_all(sems, ((disp_hbm, disp_ref), (pos_hbm, pos_ref)))
    halo_ref[...] = jnp.zeros_like(halo_ref)
    row = lax.broadcasted_iota(jnp.int32, counts_ref.shape, 0)
    counts_ref[...] = jnp.where(row == 0, near_count_ref[0], far_count_ref[0])
    for copy in inputs:
        copy.wait()
    low_ref[...] = disp_ref[...].astype(low_ref.dtype)
    row = 0
    for g in range(segments):
        size = min(spare, width - g * spare)
        for start in (0, clusters - HALO):
            for ref in (disp_ref, pos_ref):
                halo_ref[row : row + HALO, 0:size] = ref[
                    start : start + HALO, g * spare : g * spare + size
                ]
                row += HALO


def list_pairs(pairs_ref, near_count, list_ref, clusters):
    slots = pairs_ref.shape[1]
    target = pairs_ref[0:1, :]
    source = pairs_ref[1:2, :]
    slot = lax.broadcasted_iota(jnp.int32, (1, slots), 1)
    live = slot < near_count
    own = jnp.logical_and(source >= HALO, source < clusters + HALO)
    square = (slots, slots)
    first = lax.broadcasted_iota(jnp.int32, square, 0)
    upto = first <= lax.broadcasted_iota(jnp.int32, square, 1)
    upto = jnp.where(upto, 1.0, 0.0).astype(jnp.bfloat16)
    row = lax.broadcasted_iota(jnp.int32, (SUBLANES, slots), 0)
    pairs = jnp.where(row == 0, target, source).astype(jnp.float32).astype(jnp.bfloat16)
    results = []
    for wanted in (own, jnp.logical_not(own)):
        chosen = jnp.where(jnp.logical_and(live, wanted), 1.0, 0.0)
        order = jnp.dot(
            jnp.broadcast_to(chosen, (SUBLANES, slots)).astype(jnp.bfloat16),
            upto,
            preferred_element_type=jnp.float32,
        )
        place = first == jnp.where(chosen > 0.0, order[0:1, :] - 1.0, -1.0).astype(jnp.int32)
        place = jnp.where(place, 1.0, 0.0).astype(jnp.bfloat16)
        together = lax.dot_general(
            pairs, place, (((1,), (1,)), ((), ())), preferred_element_type=jnp.float32
        ).astype(jnp.int32)
        number = jnp.sum(chosen, axis=1, keepdims=True).astype(jnp.int32)
        results.append((together, jnp.broadcast_to(number, (1, slots))))
    (pairs, number), (others, others_number) = results
    list_ref[0:1, :] = pairs[0:1, :]
    list_ref[1:2, :] = jnp.clip(pairs[1:2, :] - HALO, 0, clusters - 1)
    list_ref[2:3, :] = jnp.where(slot < number, pairs[0:1, :], clusters) * SUBLANES
    list_ref[3:4, :] = number
    list_ref[4:6, :] = others[0:2, :]
    list_ref[6:7, :] = others_number
    list_ref[7:8, :] = jnp.zeros((1, slots), jnp.int32)


def prepare(near_count, far_count, disp, pos, spare):
    clusters, width = disp.shape
    vmem = pl.BlockSpec(memory_space=pltpu.VMEM)
    smem = pl.BlockSpec(memory_space=pltpu.SMEM)
    return pl.pallas_call(
        prepare_kernel,
        out_shape=(
            jax.ShapeDtypeStruct((clusters, width), jnp.bfloat16),
            jax.ShapeDtypeStruct((clusters, spare), jnp.float32),
            jax.ShapeDtypeStruct((SUBLANES, LANES), jnp.int32),
        ),
        in_specs=[smem] * 2 + in_hbm(2),
        out_specs=(vmem,) * 3,
        scratch_shapes=[
            pltpu.VMEM(disp.shape, disp.dtype),
            pltpu.VMEM(pos.shape, pos.dtype),
            pltpu.SemaphoreType.DMA((2,)),
        ],
        compiler_params=pltpu.CompilerParams(vmem_limit_bytes=VMEM),
        cost_estimate=pl.CostEstimate(
            flops=clusters * width, bytes_accessed=12 * clusters * width, transcendentals=0
        ),
        name="prepare",
    )(near_count, far_count, *pinned(disp, pos))


def far_kernel(
    counts_hbm,
    pairs_hbm,
    gathered_hbm,
    near_pairs_hbm,
    pos_hbm,
    disp_hbm,
    intact_hbm,
    stiff_hbm,
    blocks_ref,
    out_ref,
    pos_ref,
    hold_ref,
    list_ref,
    damage_hbm,
    counts_ref,
    pairs_ref,
    gathered_ref,
    near_pairs_ref,
    disp_ref,
    intact_ref,
    stiff_ref,
    damage_ref,
    buffer,
    column_scr,
    coeff_scr,
    place_scr,
    sum_scr,
    summed_scr,
    halo_scr,
    sems,
    block_sems,
    out_sem,
    *,
    segments,
):
    rank, _, slots = buffer.shape
    cols, clusters, _ = out_ref.shape
    targets = cols * clusters
    rows = gathered_ref.shape[0] // clusters
    sources = rows * clusters

    def fetch(t):
        here = pl.ds(pl.multiple_of(t * WIDE, WIDE), WIDE)
        return pltpu.make_async_copy(
            blocks_ref.at[:, :, here], buffer.at[:, :, here], block_sems.at[t]
        )

    inputs = start_all(
        sems,
        (
            (counts_hbm, counts_ref),
            (pairs_hbm, pairs_ref),
            (gathered_hbm, gathered_ref),
            (near_pairs_hbm, near_pairs_ref),
            (pos_hbm, pos_ref),
            (disp_hbm, disp_ref),
            (intact_hbm, intact_ref),
            (stiff_hbm, stiff_ref),
        ),
    )
    fetch(0).start()
    summed_scr[...] = jnp.zeros_like(summed_scr)
    inputs[0].wait()
    count = counts_ref[1, 0]
    live = jnp.maximum((count + FOLD - 1) // FOLD, 1)

    for t in range(1, slots // WIDE):

        @pl.when(t * (WIDE // FOLD) < live)
        def _(t=t):
            fetch(t).start()

    inputs[1].wait()
    inputs[2].wait()
    column_scr[...] = gathered_ref[...].astype(jnp.bfloat16)

    index = lax.broadcasted_iota(jnp.int32, (sources, slots), 0)
    pick = jnp.where(index == pairs_ref[1:2, :], 1.0, 0.0).astype(jnp.bfloat16)
    coeff = lax.dot_general(
        column_scr[...], pick, (((0,), (0,)), ((), ())), preferred_element_type=jnp.float32
    )
    coeff_scr[...] = coeff[0:rank, :]
    slot = lax.broadcasted_iota(jnp.int32, (1, slots), 1)
    wanted = jnp.where(slot < count, pairs_ref[0:1, :], -1)
    index = lax.broadcasted_iota(jnp.int32, (targets, slots), 0)
    place_scr[...] = jnp.where(index == wanted, 1.0, 0.0).astype(jnp.bfloat16)

    damage_out = pltpu.make_async_copy(damage_ref, damage_hbm, out_sem)

    def near_work():
        for copy in inputs[3:]:
            copy.wait()
        list_pairs(near_pairs_ref, counts_ref[0, 0], list_ref, clusters)
        elems = damage_ref.shape[1]
        disp = [disp_ref[:, c * elems : (c + 1) * elems] for c in range(3)]
        separation = jnp.sqrt(1.0 + (disp[0] * disp[0] + disp[1] * disp[1] + disp[2] * disp[2]))
        softened = 1.0 - jnp.exp(-(separation - 1.0) / softening)
        intact = intact_ref[...].astype(jnp.float32)
        damage = intact * softened + (1.0 - intact)
        damage_ref[...] = damage
        damage_out.start()
        hold_ref[...] = (1.0 - damage) * stiff_ref[...]

    def multiply(t, carry):
        start = pl.multiple_of(t * FOLD, FOLD)
        lanes = pl.ds(start, FOLD)

        @pl.when(t % (WIDE // FOLD) == 0)
        def _():
            fetch(t // (WIDE // FOLD)).wait()

        coeff = coeff_scr[:, lanes]
        for r in range(rank):
            product = buffer[r, :, lanes].astype(jnp.float32) * coeff
            folded = product[0:SUBLANES]
            for s in range(1, rank // SUBLANES):
                folded = folded + product[s * SUBLANES : (s + 1) * SUBLANES]
            for h in range(FOLD // LANES):
                sum_scr[h, r * SUBLANES : (r + 1) * SUBLANES, :] = folded[
                    :, h * LANES : (h + 1) * LANES
                ]
        parts = []
        for h in range(FOLD // LANES):
            total = sum_scr[h, pl.ds(0, rank, stride=SUBLANES), :]
            for s in range(1, SUBLANES):
                total = total + sum_scr[h, pl.ds(s, rank, stride=SUBLANES), :]
            parts.append(total)
        coupled = jnp.concatenate(parts, axis=1)
        high = coupled.astype(jnp.bfloat16)
        low = (coupled - high.astype(jnp.float32)).astype(jnp.bfloat16)
        both = jnp.concatenate([high, low], axis=0)
        summed_scr[...] += lax.dot_general(
            place_scr[:, lanes], both, (((1,), (1,)), ((), ())), preferred_element_type=jnp.float32
        )

        @pl.when(t == 0)
        def _():
            near_work()

        return carry

    lax.fori_loop(0, live, multiply, 0)
    damage_out.wait()

    i = lax.axis_index("rows")
    j = lax.axis_index("cols")
    from_last = jnp.where(j < cols - 1, i, i - 1)
    from_first = jnp.where(j > 0, i, i + 1)
    edge = 2 * HALO
    halo_scr[...] = jnp.zeros_like(halo_scr)
    sides = (
        (0, jnp.minimum(from_first, rows - 1), from_first < rows),
        (edge, jnp.maximum(from_last, 0), from_last >= 0),
    )
    for side, (row, owner, there) in enumerate(sides):
        start = pl.multiple_of(owner * clusters, clusters)
        whole = jnp.where(there, gathered_ref[pl.ds(start, clusters), :], 0.0)
        for n in range(PIECES):
            piece = whole.astype(jnp.bfloat16).astype(jnp.float32)
            whole = whole - piece
            for g in range(segments):
                to = (n * segments + g) * edge
                here = g * 2 * edge + row
                halo_scr[side, to : to + edge, :] = piece[here : here + edge, :]
    after = jnp.where(j < cols - 1, j + 1, 0)
    lane = lax.broadcasted_iota(jnp.int32, (clusters, LANES), 1)
    for d in range(cols):
        halo = halo_scr[jnp.where(after == d, 1, 0)]
        mine = summed_scr[d * clusters : (d + 1) * clusters, :]
        mine = mine + pltpu.roll(mine, rank, 1)
        out_ref[d] = jnp.where(lane < rank, mine, halo).astype(out_ref.dtype)


def far_field(
    counts, pairs, gathered, near_pairs, pos, disp, intact, stiffness, blocks, cols, segments
):
    rank, _, slots = blocks.shape
    rows = lax.axis_size("rows")
    clusters = gathered.shape[0] // rows
    return pl.pallas_call(
        functools.partial(far_kernel, segments=segments),
        out_shape=(
            jax.ShapeDtypeStruct((cols, clusters, LANES), jnp.bfloat16),
            jax.ShapeDtypeStruct(pos.shape, jnp.float32),
            jax.ShapeDtypeStruct(stiffness.shape, jnp.float32),
            jax.ShapeDtypeStruct((SUBLANES, near_pairs.shape[1]), jnp.int32),
            jax.ShapeDtypeStruct(stiffness.shape, jnp.float32),
        ),
        in_specs=in_hbm(9),
        out_specs=(pl.BlockSpec(memory_space=pltpu.VMEM),) * 4 + tuple(in_hbm(1)),
        scratch_shapes=[
            pltpu.SMEM(counts.shape, counts.dtype),
            pltpu.VMEM(pairs.shape, pairs.dtype),
            pltpu.VMEM(gathered.shape, gathered.dtype),
            pltpu.VMEM(near_pairs.shape, near_pairs.dtype),
            pltpu.VMEM(disp.shape, disp.dtype),
            pltpu.VMEM(intact.shape, intact.dtype),
            pltpu.VMEM(stiffness.shape, stiffness.dtype),
            pltpu.VMEM(stiffness.shape, jnp.float32),
            pltpu.VMEM(blocks.shape, blocks.dtype),
            pltpu.VMEM((rows * clusters, LANES), jnp.bfloat16),
            pltpu.VMEM((rank, slots), jnp.float32),
            pltpu.VMEM((cols * clusters, slots), jnp.bfloat16),
            pltpu.VMEM((FOLD // LANES, rank * SUBLANES, LANES), jnp.float32),
            pltpu.VMEM((cols * clusters, LANES), jnp.float32),
            pltpu.VMEM((2, clusters, LANES), jnp.float32),
            pltpu.SemaphoreType.DMA((8,)),
            pltpu.SemaphoreType.DMA((slots // WIDE,)),
            pltpu.SemaphoreType.DMA(()),
        ],
        compiler_params=pltpu.CompilerParams(vmem_limit_bytes=VMEM),
        cost_estimate=pl.CostEstimate(
            flops=2 * rank * rank * slots,
            bytes_accessed=2 * rank * rank * slots,
            transcendentals=0,
        ),
        name="far_field",
    )(
        counts,
        *pinned(pairs),
        gathered,
        *pinned(near_pairs, pos, disp, intact, stiffness, blocks),
    )


def replicate(rows, chunks, store, turned=False):
    within = lax.broadcasted_iota(jnp.int32, (rows.shape[0], LANES), 1)
    if turned:
        within = within + (within // CHUNK) * SUBLANES
    within = within % CHUNK
    for m in range(3 * chunks):
        tile = m // GROUPS
        store(
            m,
            jnp.take_along_axis(
                rows[:, tile * LANES : (tile + 1) * LANES],
                within + (m % GROUPS) * CHUNK,
                axis=1,
                mode="promise_in_bounds",
            ),
        )


def row_of(ref, n, row):
    return ref[n, pl.ds(row, SUBLANES, stride=0), :]


def turn(wide):
    return pltpu.roll(wide, 0, 1, stride=1, stride_axis=0)


def pair_sums(tgt, src, chunks):
    sums = [None] * (3 * chunks)
    size = 3 * chunks
    for h in range(chunks):
        x = [tgt(c * chunks + h) for c in range(3)]
        for f in range(chunks):
            r = [x[c] - src(c * chunks + f) for c in range(3)]
            u = [src(size + c * chunks + f) for c in range(3)]
            q = (r[0] * r[0] + core_square) + (r[1] * r[1] + r[2] * r[2])
            s = r[0] * u[0] + (r[1] * u[1] + r[2] * u[2])
            inverse = lax.rsqrt(q)
            square = inverse * inverse
            weight = square * inverse
            s = (3.0 * s) * square
            for c in range(3):
                term = weight * (u[c] - s * r[c])
                m = c * chunks + h
                sums[m] = term if sums[m] is None else sums[m] + term
    return sums


def gather_sums(acc_scr, clusters, chunks, store):
    own_group = lax.broadcasted_iota(jnp.int32, (clusters, LANES), 1) // CHUNK
    for t in range(pl.cdiv(3 * chunks, GROUPS)):
        merged = None
        for g in range(GROUPS):
            m = t * GROUPS + g
            if m >= 3 * chunks:
                break
            total = acc_scr[m, pl.ds(0, clusters, stride=SUBLANES), :]
            for s in range(1, SUBLANES):
                total = total + acc_scr[m, pl.ds(s, clusters, stride=SUBLANES), :]
            total = total + pltpu.roll(total, 2 * CHUNK, 1)
            total = total + pltpu.roll(total, CHUNK, 1)
            merged = total if merged is None else jnp.where(own_group == g, total, merged)
        store(t, merged)


def turn_matrix():
    shape = (PIECES * CHUNK, SUBLANES * LANES)
    column = lax.broadcasted_iota(jnp.int32, shape, 1)
    lane = column % LANES
    entry = (lane + (lane // CHUNK) * SUBLANES + column // LANES) % CHUNK
    row = lax.broadcasted_iota(jnp.int32, shape, 0) % CHUNK
    return jnp.where(entry == row, 1.0, 0.0).astype(jnp.bfloat16)


def exact_pieces(value):
    pieces = []
    for _ in range(PIECES):
        piece = value.astype(jnp.bfloat16)
        pieces.append(piece)
        value = value - piece.astype(jnp.float32)
    return pieces


def near_kernel(
    list_hbm,
    disp_hbm,
    pos_ref,
    hold_ref,
    out_ref,
    edge_ref,
    list_ref,
    disp_ref,
    wide_scr,
    piece_scr,
    turn_scr,
    tgt_scr,
    src_scr,
    acc_scr,
    sems,
):
    clusters, width = pos_ref.shape
    elems = width // 3
    chunks = elems // CHUNK
    size = 3 * chunks

    moves = start_all(sems, ((list_hbm, list_ref), (disp_hbm, disp_ref)))
    acc_scr[...] = jnp.zeros_like(acc_scr)
    turn_scr[...] = turn_matrix()

    wide_scr[:, 0:width] = pos_ref[...]
    edge_ref[0:HALO, :] = pos_ref[0:HALO, :]
    edge_ref[HALO:, :] = pos_ref[clusters - HALO :, :]
    columns = 2 * LANES
    for k, values in enumerate((pos_ref, disp_ref)):
        if k == 1:
            moves[1].wait()
        for m in range(size):
            pieces = exact_pieces(values[:, m * CHUNK : (m + 1) * CHUNK])
            piece_scr[m * clusters : (m + 1) * clusters, :] = jnp.concatenate(pieces, axis=1)
        for t in range(SUBLANES * LANES // columns):
            turned = jnp.dot(
                piece_scr[...],
                turn_scr[:, t * columns : (t + 1) * columns],
                preferred_element_type=jnp.float32,
            )
            for m in range(size):
                for h in range(columns // LANES):
                    s = t * (columns // LANES) + h
                    src_scr[k * size + m, pl.ds(s, clusters, stride=SUBLANES), :] = turned[
                        m * clusters : (m + 1) * clusters, h * LANES : (h + 1) * LANES
                    ]

    def store_target(m, value):
        tgt_scr[m] = value

    replicate(wide_scr[...], chunks, store_target)
    moves[0].wait()
    count = list_ref[3, 0]

    def sums_of(slot):
        target = list_ref[0, slot]
        source = pl.multiple_of(list_ref[1, slot] * SUBLANES, SUBLANES)
        return pair_sums(
            lambda m: row_of(tgt_scr, m, target),
            lambda n: src_scr[n, pl.ds(source, SUBLANES), :],
            chunks,
        )

    def step(it, carry):
        for k in range(0, UNROLL, TOGETHER):
            slots = [it * UNROLL + k + n for n in range(TOGETHER)]
            results = [sums_of(slot) for slot in slots]
            for slot, sums in zip(slots, results):
                into = pl.multiple_of(list_ref[2, slot], SUBLANES)
                for m in range(size):
                    acc_scr[m, pl.ds(into, SUBLANES), :] += sums[m]
        return carry

    lax.fori_loop(0, (count + UNROLL - 1) // UNROLL, step, 0)

    def store_sum(t, value):
        wide_scr[:, t * LANES : (t + 1) * LANES] = value

    gather_sums(acc_scr, clusters, chunks, store_sum)
    for c in range(3):
        here = slice(c * elems, (c + 1) * elems)
        out_ref[:, here] = wide_scr[:, here] - hold_ref[...] * disp_ref[:, here]


def near_field(listed, disp, pos, hold):
    clusters, width = pos.shape
    elems = width // 3
    chunks = elems // CHUNK
    padded = pl.cdiv(width, LANES) * LANES
    slots = listed.shape[1]
    vmem = pl.BlockSpec(memory_space=pltpu.VMEM)
    return pl.pallas_call(
        near_kernel,
        out_shape=(
            jax.ShapeDtypeStruct((clusters, width), jnp.float32),
            jax.ShapeDtypeStruct((2 * HALO, width), jnp.float32),
        ),
        in_specs=in_hbm(2) + [vmem] * 2,
        out_specs=(vmem, vmem),
        scratch_shapes=[
            pltpu.SMEM(listed.shape, listed.dtype),
            pltpu.VMEM(disp.shape, disp.dtype),
            pltpu.VMEM((clusters, padded), jnp.float32),
            pltpu.VMEM((3 * chunks * clusters, PIECES * CHUNK), jnp.bfloat16),
            pltpu.VMEM((PIECES * CHUNK, SUBLANES * LANES), jnp.bfloat16),
            pltpu.VMEM((3 * chunks, clusters, LANES), jnp.float32),
            pltpu.VMEM((6 * chunks, clusters * SUBLANES, LANES), jnp.float32),
            pltpu.VMEM((3 * chunks, (clusters + 1) * SUBLANES, LANES), jnp.float32),
            pltpu.SemaphoreType.DMA((2,)),
        ],
        compiler_params=pltpu.CompilerParams(vmem_limit_bytes=VMEM),
        cost_estimate=pl.CostEstimate(
            flops=30 * slots * elems * elems,
            bytes_accessed=4 * clusters * width * 6,
            transcendentals=slots * elems * elems,
        ),
        name="near_field",
    )(listed, *pinned(disp), pos, hold)


def finish_kernel(
    rest_hbm,
    edge_ref,
    received_ref,
    near_ref,
    far_ref,
    out_ref,
    rest_ref,
    ext_scr,
    halo_scr,
    tgt_scr,
    src_scr,
    acc_scr,
    sem,
    *,
    rank,
):
    clusters, width = near_ref.shape
    cols = received_ref.shape[0]
    elems = width // 3
    chunks = elems // CHUNK
    size = 3 * chunks
    spare = LANES - rank
    segments = split_rows(width, spare)
    edge = 2 * HALO

    fetch = pltpu.make_async_copy(rest_hbm, rest_ref, sem)
    fetch.start()
    acc_scr[...] = jnp.zeros_like(acc_scr)

    j = lax.axis_index("cols")
    before = jnp.where(j > 0, j - 1, cols - 1)
    after = jnp.where(j < cols - 1, j + 1, 0)
    for start, sender in ((0, before), (HALO, after)):
        halo_scr[...] = received_ref[sender].astype(jnp.float32)
        rows = edge * segments
        whole = halo_scr[0:rows, :]
        for n in range(1, PIECES):
            whole = whole + halo_scr[n * rows : (n + 1) * rows, :]
        for g in range(segments):
            count = min(spare, width - g * spare)
            for k in range(2):
                row = (2 * g + k) * HALO
                ext_scr[k, start : start + HALO, g * spare : g * spare + count] = whole[
                    row : row + HALO, rank : rank + count
                ]
    ext_scr[1, edge : 2 * edge, 0:width] = edge_ref[...]
    for k in range(2):

        def store(m, value, k=k):
            for b in range(edge):
                wide = jnp.broadcast_to(value[b : b + 1, :], (SUBLANES, LANES))
                src_scr[(1 - k) * size + m, b * SUBLANES : (b + 1) * SUBLANES, :] = turn(wide)

        replicate(ext_scr[k], chunks, store, True)

    def store_target(m, value):
        tgt_scr[m] = value

    replicate(ext_scr[1], chunks, store_target)
    fetch.wait()
    number = rest_ref[6, 0]

    def one_pair(n):
        target = rest_ref[4, n]
        source = rest_ref[5, n]
        target = jnp.where(target < HALO, target, target - (clusters - edge))
        source = jnp.where(source < HALO, source, source - clusters)
        live = n < number
        target = jnp.where(live, target, edge)
        source = pl.multiple_of(jnp.where(live, source, 0) * SUBLANES, SUBLANES)
        into = pl.multiple_of(target * SUBLANES, SUBLANES)
        row = edge + jnp.where(live, target, 0)
        sums = pair_sums(
            lambda m: row_of(tgt_scr, m, row),
            lambda k: src_scr[k, pl.ds(source, SUBLANES), :],
            chunks,
        )
        for m in range(size):
            acc_scr[m, pl.ds(into, SUBLANES), :] += sums[m]

    def step(it, carry):
        for k in range(FEW):
            one_pair(it * FEW + k)
        return carry

    lax.fori_loop(0, (number + FEW - 1) // FEW, step, 0)

    def store_sum(t, value):
        ext_scr[0, :, t * LANES : (t + 1) * LANES] = value

    gather_sums(acc_scr, 2 * edge, chunks, store_sum)
    out_ref[...] = near_ref[...] + far_ref[...]
    out_ref[0:HALO, :] += ext_scr[0, 0:HALO, 0:width]
    out_ref[clusters - HALO :, :] += ext_scr[0, HALO:edge, 0:width]


def finish(rest, edges, received, near, far, rank):
    clusters, width = near.shape
    chunks = width // 3 // CHUNK
    padded = pl.cdiv(width, LANES) * LANES
    edge = 2 * HALO
    vmem = pl.BlockSpec(memory_space=pltpu.VMEM)
    return pl.pallas_call(
        functools.partial(finish_kernel, rank=rank),
        out_shape=jax.ShapeDtypeStruct((clusters, width), jnp.float32),
        in_specs=in_hbm(1) + [vmem] * 4,
        out_specs=vmem,
        scratch_shapes=[
            pltpu.SMEM(rest.shape, rest.dtype),
            pltpu.VMEM((2, 2 * edge, padded), jnp.float32),
            pltpu.VMEM((clusters, LANES), jnp.float32),
            pltpu.VMEM((3 * chunks, 2 * edge, LANES), jnp.float32),
            pltpu.VMEM((6 * chunks, edge * SUBLANES, LANES), jnp.float32),
            pltpu.VMEM((3 * chunks, 2 * edge * SUBLANES, LANES), jnp.float32),
            pltpu.SemaphoreType.DMA(()),
        ],
        compiler_params=pltpu.CompilerParams(vmem_limit_bytes=VMEM),
        cost_estimate=pl.CostEstimate(
            flops=2 * clusters * width, bytes_accessed=16 * clusters * width, transcendentals=0
        ),
        name="finish",
    )(rest, edges, received, near, far)


def local(
    displacement,
    positions,
    cluster_basis,
    near_pairs,
    near_count,
    far_pairs,
    far_count,
    far_blocks,
    intact,
    stiffness,
):
    cols = lax.axis_size("cols")
    clusters, width, rank = cluster_basis.shape
    spare = LANES - rank
    segments = split_rows(width, spare)
    disp_bf, halo, counts = prepare(near_count, far_count, displacement, positions, spare)
    coeff = jnp.einsum("kf,kfr->kr", disp_bf, cluster_basis, preferred_element_type=jnp.float32)
    payload = jnp.concatenate([coeff, halo], axis=1)
    gathered = lax.all_gather(payload, "rows", axis=0, tiled=True)
    partial, pos, hold, listed, damage = far_field(
        counts,
        far_pairs.T,
        gathered,
        near_pairs.T,
        positions,
        displacement,
        intact,
        stiffness,
        far_blocks.transpose(1, 2, 0),
        cols,
        segments,
    )
    received = lax.all_to_all(partial, "cols", split_axis=0, concat_axis=0)
    near, edges = near_field(listed, displacement, pos, hold)
    owned = jnp.sum(received[:, :, :rank].astype(jnp.float32), axis=0).astype(jnp.bfloat16)
    far = jnp.einsum("kfr,kr->kf", cluster_basis, owned, preferred_element_type=jnp.float32)
    return finish(listed, edges, received, near, far, rank), damage


def solution(mesh):
    both = ("rows", "cols")
    in_specs = (
        P(both, None),
        P(both, None),
        P(both, None, None),
        P(both, None),
        P(both),
        P(both, None),
        P(both),
        P(both, None, None),
        P(both, None),
        P(both, None),
    )
    out_specs = (P(both, None), P(both, None))
    return jax.shard_map(local, mesh=mesh, in_specs=in_specs, out_specs=out_specs, check_vma=False)
```

```python
import functools

import jax
import jax.numpy as jnp
from jax import lax
from jax.experimental import pallas as pl
from jax.experimental.pallas import tpu as pltpu
from jax.sharding import PartitionSpec as P

HALO = 2
LANES = 128
SUBLANES = 8
CHUNK = 32
GROUPS = LANES // CHUNK
core_square = 0.25
softening = 1.5
UNROLL = 8
TOGETHER = 2
FEW = 4
FOLD = 256
PIECES = 3
VMEM = 20 * 1024 * 1024


def split_rows(width, lanes):
    return pl.cdiv(width, lanes)


def in_hbm(count):
    return [pl.BlockSpec(memory_space=pltpu.HBM)] * count


def pinned(*arrays):
    return [pltpu.with_memory_space_constraint(x, pltpu.HBM) for x in arrays]


def start_all(sems, moves):
    copies = [
        pltpu.make_async_copy(source, target, sems.at[n])
        for n, (source, target) in enumerate(moves)
    ]
    for copy in copies:
        copy.start()
    return copies


def prepare_kernel(
    near_count_ref,
    far_count_ref,
    disp_hbm,
    pos_hbm,
    low_ref,
    halo_ref,
    counts_ref,
    disp_ref,
    pos_ref,
    sems,
):
    clusters, width = disp_ref.shape
    spare = halo_ref.shape[1]
    segments = split_rows(width, spare)
    inputs = start_all(sems, ((disp_hbm, disp_ref), (pos_hbm, pos_ref)))
    halo_ref[...] = jnp.zeros_like(halo_ref)
    row = lax.broadcasted_iota(jnp.int32, counts_ref.shape, 0)
    counts_ref[...] = jnp.where(row == 0, near_count_ref[0], far_count_ref[0])
    for copy in inputs:
        copy.wait()
    low_ref[...] = disp_ref[...].astype(low_ref.dtype)
    row = 0
    for g in range(segments):
        size = min(spare, width - g * spare)
        for start in (0, clusters - HALO):
            for ref in (disp_ref, pos_ref):
                halo_ref[row : row + HALO, 0:size] = ref[
                    start : start + HALO, g * spare : g * spare + size
                ]
                row += HALO


def list_pairs(pairs_ref, near_count, list_ref, clusters):
    slots = pairs_ref.shape[1]
    target = pairs_ref[0:1, :]
    source = pairs_ref[1:2, :]
    slot = lax.broadcasted_iota(jnp.int32, (1, slots), 1)
    live = slot < near_count
    own = jnp.logical_and(source >= HALO, source < clusters + HALO)
    square = (slots, slots)
    first = lax.broadcasted_iota(jnp.int32, square, 0)
    upto = first <= lax.broadcasted_iota(jnp.int32, square, 1)
    upto = jnp.where(upto, 1.0, 0.0).astype(jnp.bfloat16)
    row = lax.broadcasted_iota(jnp.int32, (SUBLANES, slots), 0)
    pairs = jnp.where(row == 0, target, source).astype(jnp.float32).astype(jnp.bfloat16)
    results = []
    for wanted in (own, jnp.logical_not(own)):
        chosen = jnp.where(jnp.logical_and(live, wanted), 1.0, 0.0)
        order = jnp.dot(
            jnp.broadcast_to(chosen, (SUBLANES, slots)).astype(jnp.bfloat16),
            upto,
            preferred_element_type=jnp.float32,
        )
        place = first == jnp.where(chosen > 0.0, order[0:1, :] - 1.0, -1.0).astype(jnp.int32)
        place = jnp.where(place, 1.0, 0.0).astype(jnp.bfloat16)
        together = lax.dot_general(
            pairs, place, (((1,), (1,)), ((), ())), preferred_element_type=jnp.float32
        ).astype(jnp.int32)
        number = jnp.sum(chosen, axis=1, keepdims=True).astype(jnp.int32)
        results.append((together, jnp.broadcast_to(number, (1, slots))))
    (pairs, number), (others, others_number) = results
    list_ref[0:1, :] = pairs[0:1, :]
    list_ref[1:2, :] = jnp.clip(pairs[1:2, :] - HALO, 0, clusters - 1)
    list_ref[2:3, :] = jnp.where(slot < number, pairs[0:1, :], clusters) * SUBLANES
    list_ref[3:4, :] = number
    list_ref[4:6, :] = others[0:2, :]
    list_ref[6:7, :] = others_number
    list_ref[7:8, :] = jnp.zeros((1, slots), jnp.int32)


def prepare(near_count, far_count, disp, pos, spare):
    clusters, width = disp.shape
    vmem = pl.BlockSpec(memory_space=pltpu.VMEM)
    smem = pl.BlockSpec(memory_space=pltpu.SMEM)
    return pl.pallas_call(
        prepare_kernel,
        out_shape=(
            jax.ShapeDtypeStruct((clusters, width), jnp.bfloat16),
            jax.ShapeDtypeStruct((clusters, spare), jnp.float32),
            jax.ShapeDtypeStruct((SUBLANES, LANES), jnp.int32),
        ),
        in_specs=[smem] * 2 + in_hbm(2),
        out_specs=(vmem,) * 3,
        scratch_shapes=[
            pltpu.VMEM(disp.shape, disp.dtype),
            pltpu.VMEM(pos.shape, pos.dtype),
            pltpu.SemaphoreType.DMA((2,)),
        ],
        compiler_params=pltpu.CompilerParams(vmem_limit_bytes=VMEM),
        cost_estimate=pl.CostEstimate(
            flops=clusters * width, bytes_accessed=12 * clusters * width, transcendentals=0
        ),
        name="prepare",
    )(near_count, far_count, *pinned(disp, pos))


def far_kernel(
    counts_hbm,
    pairs_hbm,
    gathered_hbm,
    near_pairs_hbm,
    pos_hbm,
    disp_hbm,
    intact_hbm,
    stiff_hbm,
    blocks_ref,
    out_ref,
    pos_ref,
    hold_ref,
    list_ref,
    damage_hbm,
    counts_ref,
    pairs_ref,
    gathered_ref,
    near_pairs_ref,
    disp_ref,
    intact_ref,
    stiff_ref,
    damage_ref,
    buffer,
    column_scr,
    coeff_scr,
    place_scr,
    both_scr,
    sum_scr,
    summed_scr,
    halo_scr,
    sems,
    block_sems,
    out_sem,
    *,
    segments,
):
    rank, _, slots = buffer.shape
    cols, clusters, _ = out_ref.shape
    targets = cols * clusters
    rows = gathered_ref.shape[0] // clusters
    sources = rows * clusters

    def fetch(t):
        here = pl.ds(pl.multiple_of(t * FOLD, FOLD), FOLD)
        return pltpu.make_async_copy(
            blocks_ref.at[:, :, here], buffer.at[:, :, here], block_sems.at[t]
        )

    inputs = start_all(
        sems,
        (
            (counts_hbm, counts_ref),
            (pairs_hbm, pairs_ref),
            (gathered_hbm, gathered_ref),
            (near_pairs_hbm, near_pairs_ref),
            (pos_hbm, pos_ref),
            (disp_hbm, disp_ref),
            (intact_hbm, intact_ref),
            (stiff_hbm, stiff_ref),
        ),
    )
    fetch(0).start()
    both_scr[...] = jnp.zeros_like(both_scr)
    inputs[0].wait()
    count = counts_ref[1, 0]
    live = jnp.maximum((count + FOLD - 1) // FOLD, 1)
    for t in range(1, slots // FOLD):

        @pl.when(t < live)
        def _(t=t):
            fetch(t).start()

    inputs[1].wait()
    inputs[2].wait()
    column_scr[...] = gathered_ref[...].astype(jnp.bfloat16)

    index = lax.broadcasted_iota(jnp.int32, (sources, slots), 0)
    pick = jnp.where(index == pairs_ref[1:2, :], 1.0, 0.0).astype(jnp.bfloat16)
    coeff = lax.dot_general(
        column_scr[...], pick, (((0,), (0,)), ((), ())), preferred_element_type=jnp.float32
    )
    coeff_scr[...] = coeff[0:rank, :]
    slot = lax.broadcasted_iota(jnp.int32, (1, slots), 1)
    wanted = jnp.where(slot < count, pairs_ref[0:1, :], -1)
    index = lax.broadcasted_iota(jnp.int32, (targets, slots), 0)
    place_scr[...] = jnp.where(index == wanted, 1.0, 0.0).astype(jnp.bfloat16)

    for copy in inputs[3:]:
        copy.wait()
    list_pairs(near_pairs_ref, counts_ref[0, 0], list_ref, clusters)
    elems = damage_ref.shape[1]
    disp = [disp_ref[:, c * elems : (c + 1) * elems] for c in range(3)]
    separation = jnp.sqrt(1.0 + (disp[0] * disp[0] + disp[1] * disp[1] + disp[2] * disp[2]))
    softened = 1.0 - jnp.exp(-(separation - 1.0) / softening)
    intact = intact_ref[...].astype(jnp.float32)
    damage = intact * softened + (1.0 - intact)
    damage_ref[...] = damage
    damage_out = pltpu.make_async_copy(damage_ref, damage_hbm, out_sem)
    damage_out.start()
    hold_ref[...] = (1.0 - damage) * stiff_ref[...]

    def multiply(t, carry):
        start = pl.multiple_of(t * FOLD, FOLD)
        lanes = pl.ds(start, FOLD)
        fetch(t).wait()
        coeff = coeff_scr[:, lanes]
        for r in range(rank):
            product = buffer[r, :, lanes].astype(jnp.float32) * coeff
            folded = product[0:SUBLANES]
            for s in range(1, rank // SUBLANES):
                folded = folded + product[s * SUBLANES : (s + 1) * SUBLANES]
            for h in range(FOLD // LANES):
                sum_scr[h, r * SUBLANES : (r + 1) * SUBLANES, :] = folded[
                    :, h * LANES : (h + 1) * LANES
                ]
        parts = []
        for h in range(FOLD // LANES):
            total = sum_scr[h, pl.ds(0, rank, stride=SUBLANES), :]
            for s in range(1, SUBLANES):
                total = total + sum_scr[h, pl.ds(s, rank, stride=SUBLANES), :]
            parts.append(total)
        coupled = jnp.concatenate(parts, axis=1)
        high = coupled.astype(jnp.bfloat16)
        low = (coupled - high.astype(jnp.float32)).astype(jnp.bfloat16)
        both_scr[0:rank, lanes] = high
        both_scr[rank : 2 * rank, lanes] = low
        return carry

    lax.fori_loop(0, live, multiply, 0)
    summed_scr[...] = lax.dot_general(
        place_scr[...], both_scr[...], (((1,), (1,)), ((), ())), preferred_element_type=jnp.float32
    )
    damage_out.wait()

    i = lax.axis_index("rows")
    j = lax.axis_index("cols")
    from_last = jnp.where(j < cols - 1, i, i - 1)
    from_first = jnp.where(j > 0, i, i + 1)
    edge = 2 * HALO
    halo_scr[...] = jnp.zeros_like(halo_scr)
    sides = (
        (0, jnp.minimum(from_first, rows - 1), from_first < rows),
        (edge, jnp.maximum(from_last, 0), from_last >= 0),
    )
    for side, (row, owner, there) in enumerate(sides):
        start = pl.multiple_of(owner * clusters, clusters)
        whole = jnp.where(there, gathered_ref[pl.ds(start, clusters), :], 0.0)
        for n in range(PIECES):
            piece = whole.astype(jnp.bfloat16).astype(jnp.float32)
            whole = whole - piece
            for g in range(segments):
                to = (n * segments + g) * edge
                here = g * 2 * edge + row
                halo_scr[side, to : to + edge, :] = piece[here : here + edge, :]
    after = jnp.where(j < cols - 1, j + 1, 0)
    lane = lax.broadcasted_iota(jnp.int32, (clusters, LANES), 1)
    for d in range(cols):
        halo = halo_scr[jnp.where(after == d, 1, 0)]
        mine = summed_scr[d * clusters : (d + 1) * clusters, :]
        mine = mine + pltpu.roll(mine, rank, 1)
        out_ref[d] = jnp.where(lane < rank, mine, halo).astype(out_ref.dtype)


def far_field(
    counts, pairs, gathered, near_pairs, pos, disp, intact, stiffness, blocks, cols, segments
):
    rank, _, slots = blocks.shape
    rows = lax.axis_size("rows")
    clusters = gathered.shape[0] // rows
    return pl.pallas_call(
        functools.partial(far_kernel, segments=segments),
        out_shape=(
            jax.ShapeDtypeStruct((cols, clusters, LANES), jnp.bfloat16),
            jax.ShapeDtypeStruct(pos.shape, jnp.float32),
            jax.ShapeDtypeStruct(stiffness.shape, jnp.float32),
            jax.ShapeDtypeStruct((SUBLANES, near_pairs.shape[1]), jnp.int32),
            jax.ShapeDtypeStruct(stiffness.shape, jnp.float32),
        ),
        in_specs=in_hbm(9),
        out_specs=(pl.BlockSpec(memory_space=pltpu.VMEM),) * 4 + tuple(in_hbm(1)),
        scratch_shapes=[
            pltpu.SMEM(counts.shape, counts.dtype),
            pltpu.VMEM(pairs.shape, pairs.dtype),
            pltpu.VMEM(gathered.shape, gathered.dtype),
            pltpu.VMEM(near_pairs.shape, near_pairs.dtype),
            pltpu.VMEM(disp.shape, disp.dtype),
            pltpu.VMEM(intact.shape, intact.dtype),
            pltpu.VMEM(stiffness.shape, stiffness.dtype),
            pltpu.VMEM(stiffness.shape, jnp.float32),
            pltpu.VMEM(blocks.shape, blocks.dtype),
            pltpu.VMEM((rows * clusters, LANES), jnp.bfloat16),
            pltpu.VMEM((rank, slots), jnp.float32),
            pltpu.VMEM((cols * clusters, slots), jnp.bfloat16),
            pltpu.VMEM((2 * rank, slots), jnp.bfloat16),
            pltpu.VMEM((FOLD // LANES, rank * SUBLANES, LANES), jnp.float32),
            pltpu.VMEM((cols * clusters, LANES), jnp.float32),
            pltpu.VMEM((2, clusters, LANES), jnp.float32),
            pltpu.SemaphoreType.DMA((8,)),
            pltpu.SemaphoreType.DMA((slots // FOLD,)),
            pltpu.SemaphoreType.DMA(()),
        ],
        compiler_params=pltpu.CompilerParams(vmem_limit_bytes=VMEM),
        cost_estimate=pl.CostEstimate(
            flops=2 * rank * rank * slots,
            bytes_accessed=2 * rank * rank * slots,
            transcendentals=0,
        ),
        name="far_field",
    )(
        counts,
        *pinned(pairs),
        gathered,
        *pinned(near_pairs, pos, disp, intact, stiffness, blocks),
    )


def replicate(rows, chunks, store, turned=False):
    within = lax.broadcasted_iota(jnp.int32, (rows.shape[0], LANES), 1)
    if turned:
        within = within + (within // CHUNK) * SUBLANES
    within = within % CHUNK
    for m in range(3 * chunks):
        tile = m // GROUPS
        store(
            m,
            jnp.take_along_axis(
                rows[:, tile * LANES : (tile + 1) * LANES],
                within + (m % GROUPS) * CHUNK,
                axis=1,
                mode="promise_in_bounds",
            ),
        )


def row_of(ref, n, row):
    return ref[n, pl.ds(row, SUBLANES, stride=0), :]


def turn(wide):
    return pltpu.roll(wide, 0, 1, stride=1, stride_axis=0)


def pair_sums(tgt, src, chunks):
    sums = [None] * (3 * chunks)
    size = 3 * chunks
    for h in range(chunks):
        x = [tgt(c * chunks + h) for c in range(3)]
        for f in range(chunks):
            r = [x[c] - src(c * chunks + f) for c in range(3)]
            u = [src(size + c * chunks + f) for c in range(3)]
            q = (r[0] * r[0] + core_square) + (r[1] * r[1] + r[2] * r[2])
            s = r[0] * u[0] + (r[1] * u[1] + r[2] * u[2])
            inverse = lax.rsqrt(q)
            square = inverse * inverse
            weight = square * inverse
            s = (3.0 * s) * square
            for c in range(3):
                term = weight * (u[c] - s * r[c])
                m = c * chunks + h
                sums[m] = term if sums[m] is None else sums[m] + term
    return sums


def gather_sums(acc_scr, clusters, chunks, store):
    own_group = lax.broadcasted_iota(jnp.int32, (clusters, LANES), 1) // CHUNK
    for t in range(pl.cdiv(3 * chunks, GROUPS)):
        merged = None
        for g in range(GROUPS):
            m = t * GROUPS + g
            if m >= 3 * chunks:
                break
            total = acc_scr[m, pl.ds(0, clusters, stride=SUBLANES), :]
            for s in range(1, SUBLANES):
                total = total + acc_scr[m, pl.ds(s, clusters, stride=SUBLANES), :]
            total = total + pltpu.roll(total, 2 * CHUNK, 1)
            total = total + pltpu.roll(total, CHUNK, 1)
            merged = total if merged is None else jnp.where(own_group == g, total, merged)
        store(t, merged)


def turn_matrix():
    shape = (PIECES * CHUNK, SUBLANES * LANES)
    column = lax.broadcasted_iota(jnp.int32, shape, 1)
    lane = column % LANES
    entry = (lane + (lane // CHUNK) * SUBLANES + column // LANES) % CHUNK
    row = lax.broadcasted_iota(jnp.int32, shape, 0) % CHUNK
    return jnp.where(entry == row, 1.0, 0.0).astype(jnp.bfloat16)


def exact_pieces(value):
    pieces = []
    for _ in range(PIECES):
        piece = value.astype(jnp.bfloat16)
        pieces.append(piece)
        value = value - piece.astype(jnp.float32)
    return pieces


def near_kernel(
    list_hbm,
    disp_hbm,
    pos_ref,
    hold_ref,
    out_ref,
    edge_ref,
    list_ref,
    disp_ref,
    wide_scr,
    piece_scr,
    turn_scr,
    tgt_scr,
    src_scr,
    acc_scr,
    sems,
):
    clusters, width = pos_ref.shape
    elems = width // 3
    chunks = elems // CHUNK
    size = 3 * chunks

    moves = start_all(sems, ((list_hbm, list_ref), (disp_hbm, disp_ref)))
    acc_scr[...] = jnp.zeros_like(acc_scr)
    turn_scr[...] = turn_matrix()

    wide_scr[:, 0:width] = pos_ref[...]
    edge_ref[0:HALO, :] = pos_ref[0:HALO, :]
    edge_ref[HALO:, :] = pos_ref[clusters - HALO :, :]
    columns = 2 * LANES
    for k, values in enumerate((pos_ref, disp_ref)):
        if k == 1:
            moves[1].wait()
        for m in range(size):
            pieces = exact_pieces(values[:, m * CHUNK : (m + 1) * CHUNK])
            piece_scr[m * clusters : (m + 1) * clusters, :] = jnp.concatenate(pieces, axis=1)
        for t in range(SUBLANES * LANES // columns):
            turned = jnp.dot(
                piece_scr[...],
                turn_scr[:, t * columns : (t + 1) * columns],
                preferred_element_type=jnp.float32,
            )
            for m in range(size):
                for h in range(columns // LANES):
                    s = t * (columns // LANES) + h
                    src_scr[k * size + m, pl.ds(s, clusters, stride=SUBLANES), :] = turned[
                        m * clusters : (m + 1) * clusters, h * LANES : (h + 1) * LANES
                    ]

    def store_target(m, value):
        tgt_scr[m] = value

    replicate(wide_scr[...], chunks, store_target)
    moves[0].wait()
    count = list_ref[3, 0]

    def sums_of(slot):
        target = list_ref[0, slot]
        source = pl.multiple_of(list_ref[1, slot] * SUBLANES, SUBLANES)
        return pair_sums(
            lambda m: row_of(tgt_scr, m, target),
            lambda n: src_scr[n, pl.ds(source, SUBLANES), :],
            chunks,
        )

    def step(it, carry):
        for k in range(0, UNROLL, TOGETHER):
            slots = [it * UNROLL + k + n for n in range(TOGETHER)]
            results = [sums_of(slot) for slot in slots]
            for slot, sums in zip(slots, results):
                into = pl.multiple_of(list_ref[2, slot], SUBLANES)
                for m in range(size):
                    acc_scr[m, pl.ds(into, SUBLANES), :] += sums[m]
        return carry

    lax.fori_loop(0, (count + UNROLL - 1) // UNROLL, step, 0)

    def store_sum(t, value):
        wide_scr[:, t * LANES : (t + 1) * LANES] = value

    gather_sums(acc_scr, clusters, chunks, store_sum)
    for c in range(3):
        here = slice(c * elems, (c + 1) * elems)
        out_ref[:, here] = wide_scr[:, here] - hold_ref[...] * disp_ref[:, here]


def near_field(listed, disp, pos, hold):
    clusters, width = pos.shape
    elems = width // 3
    chunks = elems // CHUNK
    padded = pl.cdiv(width, LANES) * LANES
    slots = listed.shape[1]
    vmem = pl.BlockSpec(memory_space=pltpu.VMEM)
    return pl.pallas_call(
        near_kernel,
        out_shape=(
            jax.ShapeDtypeStruct((clusters, width), jnp.float32),
            jax.ShapeDtypeStruct((2 * HALO, width), jnp.float32),
        ),
        in_specs=in_hbm(2) + [vmem] * 2,
        out_specs=(vmem, vmem),
        scratch_shapes=[
            pltpu.SMEM(listed.shape, listed.dtype),
            pltpu.VMEM(disp.shape, disp.dtype),
            pltpu.VMEM((clusters, padded), jnp.float32),
            pltpu.VMEM((3 * chunks * clusters, PIECES * CHUNK), jnp.bfloat16),
            pltpu.VMEM((PIECES * CHUNK, SUBLANES * LANES), jnp.bfloat16),
            pltpu.VMEM((3 * chunks, clusters, LANES), jnp.float32),
            pltpu.VMEM((6 * chunks, clusters * SUBLANES, LANES), jnp.float32),
            pltpu.VMEM((3 * chunks, (clusters + 1) * SUBLANES, LANES), jnp.float32),
            pltpu.SemaphoreType.DMA((2,)),
        ],
        compiler_params=pltpu.CompilerParams(vmem_limit_bytes=VMEM),
        cost_estimate=pl.CostEstimate(
            flops=30 * slots * elems * elems,
            bytes_accessed=4 * clusters * width * 6,
            transcendentals=slots * elems * elems,
        ),
        name="near_field",
    )(listed, *pinned(disp), pos, hold)


def finish_kernel(
    rest_hbm,
    edge_ref,
    received_ref,
    near_ref,
    far_ref,
    out_ref,
    rest_ref,
    ext_scr,
    halo_scr,
    tgt_scr,
    src_scr,
    acc_scr,
    sem,
    *,
    rank,
):
    clusters, width = near_ref.shape
    cols = received_ref.shape[0]
    elems = width // 3
    chunks = elems // CHUNK
    size = 3 * chunks
    spare = LANES - rank
    segments = split_rows(width, spare)
    edge = 2 * HALO

    fetch = pltpu.make_async_copy(rest_hbm, rest_ref, sem)
    fetch.start()
    acc_scr[...] = jnp.zeros_like(acc_scr)

    j = lax.axis_index("cols")
    before = jnp.where(j > 0, j - 1, cols - 1)
    after = jnp.where(j < cols - 1, j + 1, 0)
    for start, sender in ((0, before), (HALO, after)):
        halo_scr[...] = received_ref[sender].astype(jnp.float32)
        rows = edge * segments
        whole = halo_scr[0:rows, :]
        for n in range(1, PIECES):
            whole = whole + halo_scr[n * rows : (n + 1) * rows, :]
        for g in range(segments):
            count = min(spare, width - g * spare)
            for k in range(2):
                row = (2 * g + k) * HALO
                ext_scr[k, start : start + HALO, g * spare : g * spare + count] = whole[
                    row : row + HALO, rank : rank + count
                ]
    ext_scr[1, edge : 2 * edge, 0:width] = edge_ref[...]
    for k in range(2):

        def store(m, value, k=k):
            for b in range(edge):
                wide = jnp.broadcast_to(value[b : b + 1, :], (SUBLANES, LANES))
                src_scr[(1 - k) * size + m, b * SUBLANES : (b + 1) * SUBLANES, :] = turn(wide)

        replicate(ext_scr[k], chunks, store, True)

    def store_target(m, value):
        tgt_scr[m] = value

    replicate(ext_scr[1], chunks, store_target)
    fetch.wait()
    number = rest_ref[6, 0]

    def one_pair(n):
        target = rest_ref[4, n]
        source = rest_ref[5, n]
        target = jnp.where(target < HALO, target, target - (clusters - edge))
        source = jnp.where(source < HALO, source, source - clusters)
        live = n < number
        target = jnp.where(live, target, edge)
        source = pl.multiple_of(jnp.where(live, source, 0) * SUBLANES, SUBLANES)
        into = pl.multiple_of(target * SUBLANES, SUBLANES)
        row = edge + jnp.where(live, target, 0)
        sums = pair_sums(
            lambda m: row_of(tgt_scr, m, row),
            lambda k: src_scr[k, pl.ds(source, SUBLANES), :],
            chunks,
        )
        for m in range(size):
            acc_scr[m, pl.ds(into, SUBLANES), :] += sums[m]

    def step(it, carry):
        for k in range(FEW):
            one_pair(it * FEW + k)
        return carry

    lax.fori_loop(0, (number + FEW - 1) // FEW, step, 0)

    def store_sum(t, value):
        ext_scr[0, :, t * LANES : (t + 1) * LANES] = value

    gather_sums(acc_scr, 2 * edge, chunks, store_sum)
    out_ref[...] = near_ref[...] + far_ref[...]
    out_ref[0:HALO, :] += ext_scr[0, 0:HALO, 0:width]
    out_ref[clusters - HALO :, :] += ext_scr[0, HALO:edge, 0:width]


def finish(rest, edges, received, near, far, rank):
    clusters, width = near.shape
    chunks = width // 3 // CHUNK
    padded = pl.cdiv(width, LANES) * LANES
    edge = 2 * HALO
    vmem = pl.BlockSpec(memory_space=pltpu.VMEM)
    return pl.pallas_call(
        functools.partial(finish_kernel, rank=rank),
        out_shape=jax.ShapeDtypeStruct((clusters, width), jnp.float32),
        in_specs=in_hbm(1) + [vmem] * 4,
        out_specs=vmem,
        scratch_shapes=[
            pltpu.SMEM(rest.shape, rest.dtype),
            pltpu.VMEM((2, 2 * edge, padded), jnp.float32),
            pltpu.VMEM((clusters, LANES), jnp.float32),
            pltpu.VMEM((3 * chunks, 2 * edge, LANES), jnp.float32),
            pltpu.VMEM((6 * chunks, edge * SUBLANES, LANES), jnp.float32),
            pltpu.VMEM((3 * chunks, 2 * edge * SUBLANES, LANES), jnp.float32),
            pltpu.SemaphoreType.DMA(()),
        ],
        compiler_params=pltpu.CompilerParams(vmem_limit_bytes=VMEM),
        cost_estimate=pl.CostEstimate(
            flops=2 * clusters * width, bytes_accessed=16 * clusters * width, transcendentals=0
        ),
        name="finish",
    )(rest, edges, received, near, far)


def local(
    displacement,
    positions,
    cluster_basis,
    near_pairs,
    near_count,
    far_pairs,
    far_count,
    far_blocks,
    intact,
    stiffness,
):
    cols = lax.axis_size("cols")
    clusters, width, rank = cluster_basis.shape
    spare = LANES - rank
    segments = split_rows(width, spare)
    disp_bf, halo, counts = prepare(near_count, far_count, displacement, positions, spare)
    coeff = jnp.einsum("kf,kfr->kr", disp_bf, cluster_basis, preferred_element_type=jnp.float32)
    payload = jnp.concatenate([coeff, halo], axis=1)
    gathered = lax.all_gather(payload, "rows", axis=0, tiled=True)
    partial, pos, hold, listed, damage = far_field(
        counts,
        far_pairs.T,
        gathered,
        near_pairs.T,
        positions,
        displacement,
        intact,
        stiffness,
        far_blocks.transpose(1, 2, 0),
        cols,
        segments,
    )
    received = lax.all_to_all(partial, "cols", split_axis=0, concat_axis=0)
    near, edges = near_field(listed, displacement, pos, hold)
    owned = jnp.sum(received[:, :, :rank].astype(jnp.float32), axis=0).astype(jnp.bfloat16)
    far = jnp.einsum("kfr,kr->kf", cluster_basis, owned, preferred_element_type=jnp.float32)
    return finish(listed, edges, received, near, far, rank), damage


def solution(mesh):
    both = ("rows", "cols")
    in_specs = (
        P(both, None),
        P(both, None),
        P(both, None, None),
        P(both, None),
        P(both),
        P(both, None),
        P(both),
        P(both, None, None),
        P(both, None),
        P(both, None),
    )
    out_specs = (P(both, None), P(both, None))
    return jax.shard_map(local, mesh=mesh, in_specs=in_specs, out_specs=out_specs, check_vma=False)
```

```python
import functools

import jax
import jax.numpy as jnp
from jax import lax
from jax.experimental import pallas as pl
from jax.experimental.pallas import tpu as pltpu
from jax.sharding import PartitionSpec as P

HALO = 2
LANES = 128
SUBLANES = 8
CHUNK = 32
GROUPS = LANES // CHUNK
core_square = 0.25
softening = 1.5
UNROLL = 8
TOGETHER = 2
FEW = 4
FOLD = 256
PIECES = 3
VMEM = 20 * 1024 * 1024


def split_rows(width, lanes):
    return pl.cdiv(width, lanes)


def in_hbm(count):
    return [pl.BlockSpec(memory_space=pltpu.HBM)] * count


def pinned(*arrays):
    return [pltpu.with_memory_space_constraint(x, pltpu.HBM) for x in arrays]


def start_all(sems, moves):
    copies = [
        pltpu.make_async_copy(source, target, sems.at[n])
        for n, (source, target) in enumerate(moves)
    ]
    for copy in copies:
        copy.start()
    return copies


def prepare_kernel(
    near_count_ref,
    far_count_ref,
    disp_hbm,
    pos_hbm,
    near_pairs_hbm,
    far_pairs_hbm,
    low_ref,
    halo_ref,
    counts_ref,
    near_pairs_ref,
    far_pairs_ref,
    disp_ref,
    pos_ref,
    sems,
):
    clusters, width = disp_ref.shape
    spare = halo_ref.shape[1]
    segments = split_rows(width, spare)
    inputs = start_all(
        sems,
        (
            (disp_hbm, disp_ref),
            (pos_hbm, pos_ref),
            (near_pairs_hbm, near_pairs_ref),
            (far_pairs_hbm, far_pairs_ref),
        ),
    )
    halo_ref[...] = jnp.zeros_like(halo_ref)
    row = lax.broadcasted_iota(jnp.int32, counts_ref.shape, 0)
    counts_ref[...] = jnp.where(row == 0, near_count_ref[0], far_count_ref[0])
    for copy in inputs:
        copy.wait()
    low_ref[...] = disp_ref[...].astype(low_ref.dtype)
    row = 0
    for g in range(segments):
        size = min(spare, width - g * spare)
        for start in (0, clusters - HALO):
            for ref in (disp_ref, pos_ref):
                halo_ref[row : row + HALO, 0:size] = ref[
                    start : start + HALO, g * spare : g * spare + size
                ]
                row += HALO


def list_pairs(pairs_ref, near_count, list_ref, clusters):
    slots = pairs_ref.shape[1]
    target = pairs_ref[0:1, :]
    source = pairs_ref[1:2, :]
    slot = lax.broadcasted_iota(jnp.int32, (1, slots), 1)
    live = slot < near_count
    own = jnp.logical_and(source >= HALO, source < clusters + HALO)
    square = (slots, slots)
    first = lax.broadcasted_iota(jnp.int32, square, 0)
    upto = first <= lax.broadcasted_iota(jnp.int32, square, 1)
    upto = jnp.where(upto, 1.0, 0.0).astype(jnp.bfloat16)
    row = lax.broadcasted_iota(jnp.int32, (SUBLANES, slots), 0)
    pairs = jnp.where(row == 0, target, source).astype(jnp.float32).astype(jnp.bfloat16)
    results = []
    for wanted in (own, jnp.logical_not(own)):
        chosen = jnp.where(jnp.logical_and(live, wanted), 1.0, 0.0)
        order = jnp.dot(
            jnp.broadcast_to(chosen, (SUBLANES, slots)).astype(jnp.bfloat16),
            upto,
            preferred_element_type=jnp.float32,
        )
        place = first == jnp.where(chosen > 0.0, order[0:1, :] - 1.0, -1.0).astype(jnp.int32)
        place = jnp.where(place, 1.0, 0.0).astype(jnp.bfloat16)
        together = lax.dot_general(
            pairs, place, (((1,), (1,)), ((), ())), preferred_element_type=jnp.float32
        ).astype(jnp.int32)
        number = jnp.sum(chosen, axis=1, keepdims=True).astype(jnp.int32)
        results.append((together, jnp.broadcast_to(number, (1, slots))))
    (pairs, number), (others, others_number) = results
    list_ref[0:1, :] = pairs[0:1, :]
    list_ref[1:2, :] = jnp.clip(pairs[1:2, :] - HALO, 0, clusters - 1)
    list_ref[2:3, :] = jnp.where(slot < number, pairs[0:1, :], clusters) * SUBLANES
    list_ref[3:4, :] = number
    list_ref[4:6, :] = others[0:2, :]
    list_ref[6:7, :] = others_number
    list_ref[7:8, :] = jnp.zeros((1, slots), jnp.int32)


def prepare(near_count, far_count, disp, pos, near_pairs, far_pairs, spare):
    clusters, width = disp.shape
    vmem = pl.BlockSpec(memory_space=pltpu.VMEM)
    smem = pl.BlockSpec(memory_space=pltpu.SMEM)
    return pl.pallas_call(
        prepare_kernel,
        out_shape=(
            jax.ShapeDtypeStruct((clusters, width), jnp.bfloat16),
            jax.ShapeDtypeStruct((clusters, spare), jnp.float32),
            jax.ShapeDtypeStruct((SUBLANES, LANES), jnp.int32),
            jax.ShapeDtypeStruct(near_pairs.shape, near_pairs.dtype),
            jax.ShapeDtypeStruct(far_pairs.shape, far_pairs.dtype),
        ),
        in_specs=[smem] * 2 + in_hbm(4),
        out_specs=(vmem,) * 5,
        scratch_shapes=[
            pltpu.VMEM(disp.shape, disp.dtype),
            pltpu.VMEM(pos.shape, pos.dtype),
            pltpu.SemaphoreType.DMA((4,)),
        ],
        compiler_params=pltpu.CompilerParams(vmem_limit_bytes=VMEM),
        cost_estimate=pl.CostEstimate(
            flops=clusters * width, bytes_accessed=12 * clusters * width, transcendentals=0
        ),
        name="prepare",
    )(near_count, far_count, *pinned(disp, pos, near_pairs, far_pairs))


def far_kernel(
    counts_hbm,
    pairs_ref,
    gathered_hbm,
    near_pairs_ref,
    pos_hbm,
    disp_hbm,
    intact_hbm,
    stiff_hbm,
    blocks_ref,
    out_ref,
    pos_ref,
    hold_ref,
    list_ref,
    damage_hbm,
    counts_ref,
    gathered_ref,
    disp_ref,
    intact_ref,
    stiff_ref,
    damage_ref,
    buffer,
    column_scr,
    coeff_scr,
    place_scr,
    both_scr,
    sum_scr,
    summed_scr,
    halo_scr,
    sems,
    block_sems,
    out_sem,
    *,
    segments,
):
    rank, _, slots = buffer.shape
    cols, clusters, _ = out_ref.shape
    targets = cols * clusters
    rows = gathered_ref.shape[0] // clusters
    sources = rows * clusters

    def fetch(t):
        here = pl.ds(pl.multiple_of(t * FOLD, FOLD), FOLD)
        return pltpu.make_async_copy(
            blocks_ref.at[:, :, here], buffer.at[:, :, here], block_sems.at[t]
        )

    inputs = start_all(
        sems,
        (
            (counts_hbm, counts_ref),
            (gathered_hbm, gathered_ref),
            (pos_hbm, pos_ref),
            (disp_hbm, disp_ref),
            (intact_hbm, intact_ref),
            (stiff_hbm, stiff_ref),
        ),
    )
    fetch(0).start()
    both_scr[...] = jnp.zeros_like(both_scr)
    inputs[0].wait()
    count = counts_ref[1, 0]
    live = jnp.maximum((count + FOLD - 1) // FOLD, 1)
    for t in range(1, slots // FOLD):

        @pl.when(t < live)
        def _(t=t):
            fetch(t).start()

    inputs[1].wait()
    column_scr[...] = gathered_ref[...].astype(jnp.bfloat16)

    index = lax.broadcasted_iota(jnp.int32, (sources, slots), 0)
    pick = jnp.where(index == pairs_ref[1:2, :], 1.0, 0.0).astype(jnp.bfloat16)
    coeff = lax.dot_general(
        column_scr[...], pick, (((0,), (0,)), ((), ())), preferred_element_type=jnp.float32
    )
    coeff_scr[...] = coeff[0:rank, :]
    slot = lax.broadcasted_iota(jnp.int32, (1, slots), 1)
    wanted = jnp.where(slot < count, pairs_ref[0:1, :], -1)
    index = lax.broadcasted_iota(jnp.int32, (targets, slots), 0)
    place_scr[...] = jnp.where(index == wanted, 1.0, 0.0).astype(jnp.bfloat16)

    list_pairs(near_pairs_ref, counts_ref[0, 0], list_ref, clusters)
    for copy in inputs[2:]:
        copy.wait()
    elems = damage_ref.shape[1]
    disp = [disp_ref[:, c * elems : (c + 1) * elems] for c in range(3)]
    separation = jnp.sqrt(1.0 + (disp[0] * disp[0] + disp[1] * disp[1] + disp[2] * disp[2]))
    softened = 1.0 - jnp.exp(-(separation - 1.0) / softening)
    intact = intact_ref[...].astype(jnp.float32)
    damage = intact * softened + (1.0 - intact)
    damage_ref[...] = damage
    damage_out = pltpu.make_async_copy(damage_ref, damage_hbm, out_sem)
    damage_out.start()
    hold_ref[...] = (1.0 - damage) * stiff_ref[...]

    def multiply(t, carry):
        start = pl.multiple_of(t * FOLD, FOLD)
        lanes = pl.ds(start, FOLD)
        fetch(t).wait()
        coeff = coeff_scr[:, lanes]
        for r in range(rank):
            product = buffer[r, :, lanes].astype(jnp.float32) * coeff
            folded = product[0:SUBLANES]
            for s in range(1, rank // SUBLANES):
                folded = folded + product[s * SUBLANES : (s + 1) * SUBLANES]
            for h in range(FOLD // LANES):
                sum_scr[h, r * SUBLANES : (r + 1) * SUBLANES, :] = folded[
                    :, h * LANES : (h + 1) * LANES
                ]
        parts = []
        for h in range(FOLD // LANES):
            total = sum_scr[h, pl.ds(0, rank, stride=SUBLANES), :]
            for s in range(1, SUBLANES):
                total = total + sum_scr[h, pl.ds(s, rank, stride=SUBLANES), :]
            parts.append(total)
        coupled = jnp.concatenate(parts, axis=1)
        high = coupled.astype(jnp.bfloat16)
        low = (coupled - high.astype(jnp.float32)).astype(jnp.bfloat16)
        both_scr[0:rank, lanes] = high
        both_scr[rank : 2 * rank, lanes] = low
        return carry

    lax.fori_loop(0, live, multiply, 0)
    summed_scr[...] = lax.dot_general(
        place_scr[...], both_scr[...], (((1,), (1,)), ((), ())), preferred_element_type=jnp.float32
    )
    damage_out.wait()

    i = lax.axis_index("rows")
    j = lax.axis_index("cols")
    from_last = jnp.where(j < cols - 1, i, i - 1)
    from_first = jnp.where(j > 0, i, i + 1)
    edge = 2 * HALO
    halo_scr[...] = jnp.zeros_like(halo_scr)
    sides = (
        (0, jnp.minimum(from_first, rows - 1), from_first < rows),
        (edge, jnp.maximum(from_last, 0), from_last >= 0),
    )
    for side, (row, owner, there) in enumerate(sides):
        start = pl.multiple_of(owner * clusters, clusters)
        whole = jnp.where(there, gathered_ref[pl.ds(start, clusters), :], 0.0)
        for n in range(PIECES):
            piece = whole.astype(jnp.bfloat16).astype(jnp.float32)
            whole = whole - piece
            for g in range(segments):
                to = (n * segments + g) * edge
                here = g * 2 * edge + row
                halo_scr[side, to : to + edge, :] = piece[here : here + edge, :]
    after = jnp.where(j < cols - 1, j + 1, 0)
    lane = lax.broadcasted_iota(jnp.int32, (clusters, LANES), 1)
    for d in range(cols):
        halo = halo_scr[jnp.where(after == d, 1, 0)]
        mine = summed_scr[d * clusters : (d + 1) * clusters, :]
        mine = mine + pltpu.roll(mine, rank, 1)
        out_ref[d] = jnp.where(lane < rank, mine, halo).astype(out_ref.dtype)


def far_field(
    counts, pairs, gathered, near_pairs, pos, disp, intact, stiffness, blocks, cols, segments
):
    rank, _, slots = blocks.shape
    rows = lax.axis_size("rows")
    vmem = pl.BlockSpec(memory_space=pltpu.VMEM)
    clusters = gathered.shape[0] // rows
    return pl.pallas_call(
        functools.partial(far_kernel, segments=segments),
        out_shape=(
            jax.ShapeDtypeStruct((cols, clusters, LANES), jnp.bfloat16),
            jax.ShapeDtypeStruct(pos.shape, jnp.float32),
            jax.ShapeDtypeStruct(stiffness.shape, jnp.float32),
            jax.ShapeDtypeStruct((SUBLANES, near_pairs.shape[1]), jnp.int32),
            jax.ShapeDtypeStruct(stiffness.shape, jnp.float32),
        ),
        in_specs=in_hbm(1) + [vmem] + in_hbm(1) + [vmem] + in_hbm(5),
        out_specs=(vmem,) * 4 + tuple(in_hbm(1)),
        scratch_shapes=[
            pltpu.SMEM(counts.shape, counts.dtype),
            pltpu.VMEM(gathered.shape, gathered.dtype),
            pltpu.VMEM(disp.shape, disp.dtype),
            pltpu.VMEM(intact.shape, intact.dtype),
            pltpu.VMEM(stiffness.shape, stiffness.dtype),
            pltpu.VMEM(stiffness.shape, jnp.float32),
            pltpu.VMEM(blocks.shape, blocks.dtype),
            pltpu.VMEM((rows * clusters, LANES), jnp.bfloat16),
            pltpu.VMEM((rank, slots), jnp.float32),
            pltpu.VMEM((cols * clusters, slots), jnp.bfloat16),
            pltpu.VMEM((2 * rank, slots), jnp.bfloat16),
            pltpu.VMEM((FOLD // LANES, rank * SUBLANES, LANES), jnp.float32),
            pltpu.VMEM((cols * clusters, LANES), jnp.float32),
            pltpu.VMEM((2, clusters, LANES), jnp.float32),
            pltpu.SemaphoreType.DMA((6,)),
            pltpu.SemaphoreType.DMA((slots // FOLD,)),
            pltpu.SemaphoreType.DMA(()),
        ],
        compiler_params=pltpu.CompilerParams(vmem_limit_bytes=VMEM),
        cost_estimate=pl.CostEstimate(
            flops=2 * rank * rank * slots,
            bytes_accessed=2 * rank * rank * slots,
            transcendentals=0,
        ),
        name="far_field",
    )(
        counts,
        pairs,
        gathered,
        near_pairs,
        *pinned(pos, disp, intact, stiffness, blocks),
    )


def replicate(rows, chunks, store, turned=False):
    within = lax.broadcasted_iota(jnp.int32, (rows.shape[0], LANES), 1)
    if turned:
        within = within + (within // CHUNK) * SUBLANES
    within = within % CHUNK
    for m in range(3 * chunks):
        tile = m // GROUPS
        store(
            m,
            jnp.take_along_axis(
                rows[:, tile * LANES : (tile + 1) * LANES],
                within + (m % GROUPS) * CHUNK,
                axis=1,
                mode="promise_in_bounds",
            ),
        )


def row_of(ref, n, row):
    return ref[n, pl.ds(row, SUBLANES, stride=0), :]


def turn(wide):
    return pltpu.roll(wide, 0, 1, stride=1, stride_axis=0)


def pair_sums(tgt, src, chunks):
    sums = [None] * (3 * chunks)
    size = 3 * chunks
    for h in range(chunks):
        x = [tgt(c * chunks + h) for c in range(3)]
        for f in range(chunks):
            r = [x[c] - src(c * chunks + f) for c in range(3)]
            u = [src(size + c * chunks + f) for c in range(3)]
            q = (r[0] * r[0] + core_square) + (r[1] * r[1] + r[2] * r[2])
            s = r[0] * u[0] + (r[1] * u[1] + r[2] * u[2])
            inverse = lax.rsqrt(q)
            square = inverse * inverse
            weight = square * inverse
            s = (3.0 * s) * square
            for c in range(3):
                term = weight * (u[c] - s * r[c])
                m = c * chunks + h
                sums[m] = term if sums[m] is None else sums[m] + term
    return sums


def gather_sums(acc_scr, clusters, chunks, store):
    own_group = lax.broadcasted_iota(jnp.int32, (clusters, LANES), 1) // CHUNK
    for t in range(pl.cdiv(3 * chunks, GROUPS)):
        merged = None
        for g in range(GROUPS):
            m = t * GROUPS + g
            if m >= 3 * chunks:
                break
            total = acc_scr[m, pl.ds(0, clusters, stride=SUBLANES), :]
            for s in range(1, SUBLANES):
                total = total + acc_scr[m, pl.ds(s, clusters, stride=SUBLANES), :]
            total = total + pltpu.roll(total, 2 * CHUNK, 1)
            total = total + pltpu.roll(total, CHUNK, 1)
            merged = total if merged is None else jnp.where(own_group == g, total, merged)
        store(t, merged)


def turn_matrix():
    shape = (CHUNK, SUBLANES * LANES)
    column = lax.broadcasted_iota(jnp.int32, shape, 1)
    lane = column % LANES
    entry = (lane + (lane // CHUNK) * SUBLANES + column // LANES) % CHUNK
    chosen = jnp.where(entry == lax.broadcasted_iota(jnp.int32, shape, 0), 1.0, 0.0)
    return jnp.concatenate([chosen.astype(jnp.bfloat16)] * PIECES, axis=0)


def exact_pieces(value):
    pieces = []
    for _ in range(PIECES):
        piece = value.astype(jnp.bfloat16)
        pieces.append(piece)
        value = value - piece.astype(jnp.float32)
    return pieces


def near_kernel(
    list_hbm,
    disp_hbm,
    pos_ref,
    hold_ref,
    out_ref,
    edge_ref,
    list_ref,
    disp_ref,
    wide_scr,
    piece_scr,
    turn_scr,
    tgt_scr,
    src_scr,
    acc_scr,
    sems,
):
    clusters, width = pos_ref.shape
    elems = width // 3
    chunks = elems // CHUNK
    size = 3 * chunks

    moves = start_all(sems, ((list_hbm, list_ref), (disp_hbm, disp_ref)))
    acc_scr[...] = jnp.zeros_like(acc_scr)
    turn_scr[...] = turn_matrix()

    wide_scr[:, 0:width] = pos_ref[...]
    edge_ref[0:HALO, :] = pos_ref[0:HALO, :]
    edge_ref[HALO:, :] = pos_ref[clusters - HALO :, :]
    columns = 2 * LANES
    for k, values in enumerate((pos_ref, disp_ref)):
        if k == 1:
            moves[1].wait()
        for m in range(size):
            pieces = exact_pieces(values[:, m * CHUNK : (m + 1) * CHUNK])
            piece_scr[m * clusters : (m + 1) * clusters, :] = jnp.concatenate(pieces, axis=1)
        for t in range(SUBLANES * LANES // columns):
            turned = jnp.dot(
                piece_scr[...],
                turn_scr[:, t * columns : (t + 1) * columns],
                preferred_element_type=jnp.float32,
            )
            for m in range(size):
                for h in range(columns // LANES):
                    s = t * (columns // LANES) + h
                    src_scr[k * size + m, pl.ds(s, clusters, stride=SUBLANES), :] = turned[
                        m * clusters : (m + 1) * clusters, h * LANES : (h + 1) * LANES
                    ]

    def store_target(m, value):
        tgt_scr[m] = value

    replicate(wide_scr[...], chunks, store_target)
    moves[0].wait()
    count = list_ref[3, 0]

    def sums_of(slot):
        target = list_ref[0, slot]
        source = pl.multiple_of(list_ref[1, slot] * SUBLANES, SUBLANES)
        return pair_sums(
            lambda m: row_of(tgt_scr, m, target),
            lambda n: src_scr[n, pl.ds(source, SUBLANES), :],
            chunks,
        )

    def step(it, carry):
        for k in range(0, UNROLL, TOGETHER):
            slots = [it * UNROLL + k + n for n in range(TOGETHER)]
            results = [sums_of(slot) for slot in slots]
            for slot, sums in zip(slots, results):
                into = pl.multiple_of(list_ref[2, slot], SUBLANES)
                for m in range(size):
                    acc_scr[m, pl.ds(into, SUBLANES), :] += sums[m]
        return carry

    lax.fori_loop(0, (count + UNROLL - 1) // UNROLL, step, 0)

    def store_sum(t, value):
        wide_scr[:, t * LANES : (t + 1) * LANES] = value

    gather_sums(acc_scr, clusters, chunks, store_sum)
    for c in range(3):
        here = slice(c * elems, (c + 1) * elems)
        out_ref[:, here] = wide_scr[:, here] - hold_ref[...] * disp_ref[:, here]


def near_field(listed, disp, pos, hold):
    clusters, width = pos.shape
    elems = width // 3
    chunks = elems // CHUNK
    padded = pl.cdiv(width, LANES) * LANES
    slots = listed.shape[1]
    vmem = pl.BlockSpec(memory_space=pltpu.VMEM)
    return pl.pallas_call(
        near_kernel,
        out_shape=(
            jax.ShapeDtypeStruct((clusters, width), jnp.float32),
            jax.ShapeDtypeStruct((2 * HALO, width), jnp.float32),
        ),
        in_specs=in_hbm(2) + [vmem] * 2,
        out_specs=(vmem, vmem),
        scratch_shapes=[
            pltpu.SMEM(listed.shape, listed.dtype),
            pltpu.VMEM(disp.shape, disp.dtype),
            pltpu.VMEM((clusters, padded), jnp.float32),
            pltpu.VMEM((3 * chunks * clusters, PIECES * CHUNK), jnp.bfloat16),
            pltpu.VMEM((PIECES * CHUNK, SUBLANES * LANES), jnp.bfloat16),
            pltpu.VMEM((3 * chunks, clusters, LANES), jnp.float32),
            pltpu.VMEM((6 * chunks, clusters * SUBLANES, LANES), jnp.float32),
            pltpu.VMEM((3 * chunks, (clusters + 1) * SUBLANES, LANES), jnp.float32),
            pltpu.SemaphoreType.DMA((2,)),
        ],
        compiler_params=pltpu.CompilerParams(vmem_limit_bytes=VMEM),
        cost_estimate=pl.CostEstimate(
            flops=30 * slots * elems * elems,
            bytes_accessed=4 * clusters * width * 6,
            transcendentals=slots * elems * elems,
        ),
        name="near_field",
    )(listed, *pinned(disp), pos, hold)


def finish_kernel(
    rest_hbm,
    edge_ref,
    received_ref,
    near_ref,
    far_ref,
    out_ref,
    rest_ref,
    ext_scr,
    halo_scr,
    tgt_scr,
    src_scr,
    acc_scr,
    sem,
    *,
    rank,
):
    clusters, width = near_ref.shape
    cols = received_ref.shape[0]
    elems = width // 3
    chunks = elems // CHUNK
    size = 3 * chunks
    spare = LANES - rank
    segments = split_rows(width, spare)
    edge = 2 * HALO

    fetch = pltpu.make_async_copy(rest_hbm, rest_ref, sem)
    fetch.start()
    acc_scr[...] = jnp.zeros_like(acc_scr)

    j = lax.axis_index("cols")
    before = jnp.where(j > 0, j - 1, cols - 1)
    after = jnp.where(j < cols - 1, j + 1, 0)
    for start, sender in ((0, before), (HALO, after)):
        halo_scr[...] = received_ref[sender].astype(jnp.float32)
        rows = edge * segments
        whole = halo_scr[0:rows, :]
        for n in range(1, PIECES):
            whole = whole + halo_scr[n * rows : (n + 1) * rows, :]
        for g in range(segments):
            count = min(spare, width - g * spare)
            for k in range(2):
                row = (2 * g + k) * HALO
                ext_scr[k, start : start + HALO, g * spare : g * spare + count] = whole[
                    row : row + HALO, rank : rank + count
                ]
    ext_scr[1, edge : 2 * edge, 0:width] = edge_ref[...]
    for k in range(2):

        def store(m, value, k=k):
            for b in range(edge):
                wide = jnp.broadcast_to(value[b : b + 1, :], (SUBLANES, LANES))
                src_scr[(1 - k) * size + m, b * SUBLANES : (b + 1) * SUBLANES, :] = turn(wide)

        replicate(ext_scr[k], chunks, store, True)

    def store_target(m, value):
        tgt_scr[m] = value

    replicate(ext_scr[1], chunks, store_target)
    fetch.wait()
    number = rest_ref[6, 0]

    def one_pair(n):
        target = rest_ref[4, n]
        source = rest_ref[5, n]
        target = jnp.where(target < HALO, target, target - (clusters - edge))
        source = jnp.where(source < HALO, source, source - clusters)
        live = n < number
        target = jnp.where(live, target, edge)
        source = pl.multiple_of(jnp.where(live, source, 0) * SUBLANES, SUBLANES)
        into = pl.multiple_of(target * SUBLANES, SUBLANES)
        row = edge + jnp.where(live, target, 0)
        sums = pair_sums(
            lambda m: row_of(tgt_scr, m, row),
            lambda k: src_scr[k, pl.ds(source, SUBLANES), :],
            chunks,
        )
        for m in range(size):
            acc_scr[m, pl.ds(into, SUBLANES), :] += sums[m]

    def step(it, carry):
        for k in range(FEW):
            one_pair(it * FEW + k)
        return carry

    lax.fori_loop(0, (number + FEW - 1) // FEW, step, 0)

    def store_sum(t, value):
        ext_scr[0, :, t * LANES : (t + 1) * LANES] = value

    gather_sums(acc_scr, 2 * edge, chunks, store_sum)
    out_ref[...] = near_ref[...] + far_ref[...]
    out_ref[0:HALO, :] += ext_scr[0, 0:HALO, 0:width]
    out_ref[clusters - HALO :, :] += ext_scr[0, HALO:edge, 0:width]


def finish(rest, edges, received, near, far, rank):
    clusters, width = near.shape
    chunks = width // 3 // CHUNK
    padded = pl.cdiv(width, LANES) * LANES
    edge = 2 * HALO
    vmem = pl.BlockSpec(memory_space=pltpu.VMEM)
    return pl.pallas_call(
        functools.partial(finish_kernel, rank=rank),
        out_shape=jax.ShapeDtypeStruct((clusters, width), jnp.float32),
        in_specs=in_hbm(1) + [vmem] * 4,
        out_specs=vmem,
        scratch_shapes=[
            pltpu.SMEM(rest.shape, rest.dtype),
            pltpu.VMEM((2, 2 * edge, padded), jnp.float32),
            pltpu.VMEM((clusters, LANES), jnp.float32),
            pltpu.VMEM((3 * chunks, 2 * edge, LANES), jnp.float32),
            pltpu.VMEM((6 * chunks, edge * SUBLANES, LANES), jnp.float32),
            pltpu.VMEM((3 * chunks, 2 * edge * SUBLANES, LANES), jnp.float32),
            pltpu.SemaphoreType.DMA(()),
        ],
        compiler_params=pltpu.CompilerParams(vmem_limit_bytes=VMEM),
        cost_estimate=pl.CostEstimate(
            flops=2 * clusters * width, bytes_accessed=16 * clusters * width, transcendentals=0
        ),
        name="finish",
    )(rest, edges, received, near, far)


def local(
    displacement,
    positions,
    cluster_basis,
    near_pairs,
    near_count,
    far_pairs,
    far_count,
    far_blocks,
    intact,
    stiffness,
):
    cols = lax.axis_size("cols")
    clusters, width, rank = cluster_basis.shape
    spare = LANES - rank
    segments = split_rows(width, spare)
    disp_bf, halo, counts, near_list, far_list = prepare(
        near_count, far_count, displacement, positions, near_pairs.T, far_pairs.T, spare
    )
    coeff = jnp.einsum("kf,kfr->kr", disp_bf, cluster_basis, preferred_element_type=jnp.float32)
    payload = jnp.concatenate([coeff, halo], axis=1)
    gathered = lax.all_gather(payload, "rows", axis=0, tiled=True)
    partial, pos, hold, listed, damage = far_field(
        counts,
        far_list,
        gathered,
        near_list,
        positions,
        displacement,
        intact,
        stiffness,
        far_blocks.transpose(1, 2, 0),
        cols,
        segments,
    )
    received = lax.all_to_all(partial, "cols", split_axis=0, concat_axis=0)
    near, edges = near_field(listed, displacement, pos, hold)
    owned = jnp.sum(received[:, :, :rank].astype(jnp.float32), axis=0).astype(jnp.bfloat16)
    far = jnp.einsum("kfr,kr->kf", cluster_basis, owned, preferred_element_type=jnp.float32)
    return finish(listed, edges, received, near, far, rank), damage


def solution(mesh):
    both = ("rows", "cols")
    in_specs = (
        P(both, None),
        P(both, None),
        P(both, None, None),
        P(both, None),
        P(both),
        P(both, None),
        P(both),
        P(both, None, None),
        P(both, None),
        P(both, None),
    )
    out_specs = (P(both, None), P(both, None))
    return jax.shard_map(local, mesh=mesh, in_specs=in_specs, out_specs=out_specs, check_vma=False)
```

```python
import functools

import jax
import jax.numpy as jnp
from jax import lax
from jax.experimental import pallas as pl
from jax.experimental.pallas import tpu as pltpu
from jax.sharding import PartitionSpec as P

HALO = 2
LANES = 128
SUBLANES = 8
CHUNK = 32
GROUPS = LANES // CHUNK
core_square = 0.25
softening = 1.5
UNROLL = 8
TOGETHER = 2
FEW = 4
FOLD = 256
PIECES = 3
VMEM = 20 * 1024 * 1024


def split_rows(width, lanes):
    return pl.cdiv(width, lanes)


def in_hbm(count):
    return [pl.BlockSpec(memory_space=pltpu.HBM)] * count


def pinned(*arrays):
    return [pltpu.with_memory_space_constraint(x, pltpu.HBM) for x in arrays]


def start_all(sems, moves):
    copies = [
        pltpu.make_async_copy(source, target, sems.at[n])
        for n, (source, target) in enumerate(moves)
    ]
    for copy in copies:
        copy.start()
    return copies


def prepare_kernel(
    near_count_ref,
    far_count_ref,
    disp_hbm,
    pos_hbm,
    near_pairs_hbm,
    far_pairs_hbm,
    low_ref,
    halo_ref,
    counts_ref,
    near_pairs_ref,
    far_pairs_ref,
    disp_ref,
    pos_ref,
    sems,
):
    clusters, width = disp_ref.shape
    spare = halo_ref.shape[1]
    segments = split_rows(width, spare)
    inputs = start_all(
        sems,
        (
            (disp_hbm, disp_ref),
            (pos_hbm, pos_ref),
            (near_pairs_hbm, near_pairs_ref),
            (far_pairs_hbm, far_pairs_ref),
        ),
    )
    halo_ref[...] = jnp.zeros_like(halo_ref)
    row = lax.broadcasted_iota(jnp.int32, counts_ref.shape, 0)
    counts_ref[...] = jnp.where(row == 0, near_count_ref[0], far_count_ref[0])
    for copy in inputs:
        copy.wait()
    low_ref[...] = disp_ref[...].astype(low_ref.dtype)
    row = 0
    for g in range(segments):
        size = min(spare, width - g * spare)
        for start in (0, clusters - HALO):
            for ref in (disp_ref, pos_ref):
                halo_ref[row : row + HALO, 0:size] = ref[
                    start : start + HALO, g * spare : g * spare + size
                ]
                row += HALO


def list_pairs(pairs_ref, near_count, list_ref, clusters):
    slots = pairs_ref.shape[1]
    target = pairs_ref[0:1, :]
    source = pairs_ref[1:2, :]
    slot = lax.broadcasted_iota(jnp.int32, (1, slots), 1)
    live = slot < near_count
    own = jnp.logical_and(source >= HALO, source < clusters + HALO)
    square = (slots, slots)
    first = lax.broadcasted_iota(jnp.int32, square, 0)
    upto = first <= lax.broadcasted_iota(jnp.int32, square, 1)
    upto = jnp.where(upto, 1.0, 0.0).astype(jnp.bfloat16)
    row = lax.broadcasted_iota(jnp.int32, (SUBLANES, slots), 0)
    pairs = jnp.where(row == 0, target, source).astype(jnp.float32).astype(jnp.bfloat16)
    results = []
    for wanted in (own, jnp.logical_not(own)):
        chosen = jnp.where(jnp.logical_and(live, wanted), 1.0, 0.0)
        order = jnp.dot(
            jnp.broadcast_to(chosen, (SUBLANES, slots)).astype(jnp.bfloat16),
            upto,
            preferred_element_type=jnp.float32,
        )
        place = first == jnp.where(chosen > 0.0, order[0:1, :] - 1.0, -1.0).astype(jnp.int32)
        place = jnp.where(place, 1.0, 0.0).astype(jnp.bfloat16)
        together = lax.dot_general(
            pairs, place, (((1,), (1,)), ((), ())), preferred_element_type=jnp.float32
        ).astype(jnp.int32)
        number = jnp.sum(chosen, axis=1, keepdims=True).astype(jnp.int32)
        results.append((together, jnp.broadcast_to(number, (1, slots))))
    (pairs, number), (others, others_number) = results
    list_ref[0:1, :] = pairs[0:1, :]
    list_ref[1:2, :] = jnp.clip(pairs[1:2, :] - HALO, 0, clusters - 1)
    list_ref[2:3, :] = jnp.where(slot < number, pairs[0:1, :], clusters) * SUBLANES
    list_ref[3:4, :] = number
    list_ref[4:6, :] = others[0:2, :]
    list_ref[6:7, :] = others_number
    list_ref[7:8, :] = jnp.zeros((1, slots), jnp.int32)


def prepare(near_count, far_count, disp, pos, near_pairs, far_pairs, spare):
    clusters, width = disp.shape
    vmem = pl.BlockSpec(memory_space=pltpu.VMEM)
    smem = pl.BlockSpec(memory_space=pltpu.SMEM)
    return pl.pallas_call(
        prepare_kernel,
        out_shape=(
            jax.ShapeDtypeStruct((clusters, width), jnp.bfloat16),
            jax.ShapeDtypeStruct((clusters, spare), jnp.float32),
            jax.ShapeDtypeStruct((SUBLANES, LANES), jnp.int32),
            jax.ShapeDtypeStruct(near_pairs.shape, near_pairs.dtype),
            jax.ShapeDtypeStruct(far_pairs.shape, far_pairs.dtype),
        ),
        in_specs=[smem] * 2 + in_hbm(4),
        out_specs=(vmem,) * 5,
        scratch_shapes=[
            pltpu.VMEM(disp.shape, disp.dtype),
            pltpu.VMEM(pos.shape, pos.dtype),
            pltpu.SemaphoreType.DMA((4,)),
        ],
        compiler_params=pltpu.CompilerParams(vmem_limit_bytes=VMEM),
        cost_estimate=pl.CostEstimate(
            flops=clusters * width, bytes_accessed=12 * clusters * width, transcendentals=0
        ),
        name="prepare",
    )(near_count, far_count, *pinned(disp, pos, near_pairs, far_pairs))


def far_kernel(
    counts_hbm,
    pairs_ref,
    gathered_hbm,
    near_pairs_ref,
    pos_hbm,
    disp_hbm,
    intact_hbm,
    stiff_hbm,
    blocks_ref,
    out_ref,
    pos_ref,
    hold_ref,
    list_ref,
    damage_hbm,
    counts_ref,
    gathered_ref,
    disp_ref,
    intact_ref,
    stiff_ref,
    damage_ref,
    buffer,
    column_scr,
    coeff_scr,
    place_scr,
    both_scr,
    sum_scr,
    summed_scr,
    halo_scr,
    sems,
    block_sems,
    out_sem,
    *,
    segments,
):
    rank, _, slots = buffer.shape
    cols, clusters, _ = out_ref.shape
    targets = cols * clusters
    rows = gathered_ref.shape[0] // clusters
    sources = rows * clusters

    part = rank // 2

    def fetch(t, half):
        rows = pl.ds(half * part, part)
        here = pl.ds(pl.multiple_of(t * FOLD, FOLD), FOLD)
        return pltpu.make_async_copy(
            blocks_ref.at[rows, :, here], buffer.at[rows, :, here], block_sems.at[t, half]
        )

    inputs = start_all(
        sems,
        (
            (counts_hbm, counts_ref),
            (gathered_hbm, gathered_ref),
            (pos_hbm, pos_ref),
            (disp_hbm, disp_ref),
            (intact_hbm, intact_ref),
            (stiff_hbm, stiff_ref),
        ),
    )
    fetch(0, 0).start()
    fetch(0, 1).start()
    both_scr[...] = jnp.zeros_like(both_scr)
    inputs[0].wait()
    count = counts_ref[1, 0]
    live = jnp.maximum((count + FOLD - 1) // FOLD, 1)
    for t in range(1, slots // FOLD):

        @pl.when(t < live)
        def _(t=t):
            fetch(t, 0).start()
            fetch(t, 1).start()

    inputs[1].wait()
    column_scr[...] = gathered_ref[...].astype(jnp.bfloat16)

    index = lax.broadcasted_iota(jnp.int32, (sources, slots), 0)
    pick = jnp.where(index == pairs_ref[1:2, :], 1.0, 0.0).astype(jnp.bfloat16)
    coeff = lax.dot_general(
        column_scr[...], pick, (((0,), (0,)), ((), ())), preferred_element_type=jnp.float32
    )
    coeff_scr[...] = coeff[0:rank, :]
    slot = lax.broadcasted_iota(jnp.int32, (1, slots), 1)
    wanted = jnp.where(slot < count, pairs_ref[0:1, :], -1)
    index = lax.broadcasted_iota(jnp.int32, (targets, slots), 0)
    place_scr[...] = jnp.where(index == wanted, 1.0, 0.0).astype(jnp.bfloat16)

    list_pairs(near_pairs_ref, counts_ref[0, 0], list_ref, clusters)
    for copy in inputs[2:]:
        copy.wait()
    elems = damage_ref.shape[1]
    disp = [disp_ref[:, c * elems : (c + 1) * elems] for c in range(3)]
    separation = jnp.sqrt(1.0 + (disp[0] * disp[0] + disp[1] * disp[1] + disp[2] * disp[2]))
    softened = 1.0 - jnp.exp(-(separation - 1.0) / softening)
    intact = intact_ref[...].astype(jnp.float32)
    damage = intact * softened + (1.0 - intact)
    damage_ref[...] = damage
    damage_out = pltpu.make_async_copy(damage_ref, damage_hbm, out_sem)
    damage_out.start()
    hold_ref[...] = (1.0 - damage) * stiff_ref[...]

    def multiply(t, carry):
        start = pl.multiple_of(t * FOLD, FOLD)
        lanes = pl.ds(start, FOLD)
        coeff = coeff_scr[:, lanes]
        for r in range(rank):
            if r % part == 0:
                fetch(t, r // part).wait()
            product = buffer[r, :, lanes].astype(jnp.float32) * coeff
            folded = product[0:SUBLANES]
            for s in range(1, rank // SUBLANES):
                folded = folded + product[s * SUBLANES : (s + 1) * SUBLANES]
            for h in range(FOLD // LANES):
                sum_scr[h, r * SUBLANES : (r + 1) * SUBLANES, :] = folded[
                    :, h * LANES : (h + 1) * LANES
                ]
        parts = []
        for h in range(FOLD // LANES):
            total = sum_scr[h, pl.ds(0, rank, stride=SUBLANES), :]
            for s in range(1, SUBLANES):
                total = total + sum_scr[h, pl.ds(s, rank, stride=SUBLANES), :]
            parts.append(total)
        coupled = jnp.concatenate(parts, axis=1)
        high = coupled.astype(jnp.bfloat16)
        low = (coupled - high.astype(jnp.float32)).astype(jnp.bfloat16)
        both_scr[0:rank, lanes] = high
        both_scr[rank : 2 * rank, lanes] = low
        return carry

    lax.fori_loop(0, live, multiply, 0)
    summed_scr[...] = lax.dot_general(
        place_scr[...], both_scr[...], (((1,), (1,)), ((), ())), preferred_element_type=jnp.float32
    )
    damage_out.wait()

    i = lax.axis_index("rows")
    j = lax.axis_index("cols")
    from_last = jnp.where(j < cols - 1, i, i - 1)
    from_first = jnp.where(j > 0, i, i + 1)
    edge = 2 * HALO
    halo_scr[...] = jnp.zeros_like(halo_scr)
    sides = (
        (0, jnp.minimum(from_first, rows - 1), from_first < rows),
        (edge, jnp.maximum(from_last, 0), from_last >= 0),
    )
    for side, (row, owner, there) in enumerate(sides):
        start = pl.multiple_of(owner * clusters, clusters)
        whole = jnp.where(there, gathered_ref[pl.ds(start, clusters), :], 0.0)
        for n in range(PIECES):
            piece = whole.astype(jnp.bfloat16).astype(jnp.float32)
            whole = whole - piece
            for g in range(segments):
                to = (n * segments + g) * edge
                here = g * 2 * edge + row
                halo_scr[side, to : to + edge, :] = piece[here : here + edge, :]
    after = jnp.where(j < cols - 1, j + 1, 0)
    lane = lax.broadcasted_iota(jnp.int32, (clusters, LANES), 1)
    for d in range(cols):
        halo = halo_scr[jnp.where(after == d, 1, 0)]
        mine = summed_scr[d * clusters : (d + 1) * clusters, :]
        mine = mine + pltpu.roll(mine, rank, 1)
        out_ref[d] = jnp.where(lane < rank, mine, halo).astype(out_ref.dtype)


def far_field(
    counts, pairs, gathered, near_pairs, pos, disp, intact, stiffness, blocks, cols, segments
):
    rank, _, slots = blocks.shape
    rows = lax.axis_size("rows")
    vmem = pl.BlockSpec(memory_space=pltpu.VMEM)
    clusters = gathered.shape[0] // rows
    return pl.pallas_call(
        functools.partial(far_kernel, segments=segments),
        out_shape=(
            jax.ShapeDtypeStruct((cols, clusters, LANES), jnp.bfloat16),
            jax.ShapeDtypeStruct(pos.shape, jnp.float32),
            jax.ShapeDtypeStruct(stiffness.shape, jnp.float32),
            jax.ShapeDtypeStruct((SUBLANES, near_pairs.shape[1]), jnp.int32),
            jax.ShapeDtypeStruct(stiffness.shape, jnp.float32),
        ),
        in_specs=in_hbm(1) + [vmem] + in_hbm(1) + [vmem] + in_hbm(5),
        out_specs=(vmem,) * 4 + tuple(in_hbm(1)),
        scratch_shapes=[
            pltpu.SMEM(counts.shape, counts.dtype),
            pltpu.VMEM(gathered.shape, gathered.dtype),
            pltpu.VMEM(disp.shape, disp.dtype),
            pltpu.VMEM(intact.shape, intact.dtype),
            pltpu.VMEM(stiffness.shape, stiffness.dtype),
            pltpu.VMEM(stiffness.shape, jnp.float32),
            pltpu.VMEM(blocks.shape, blocks.dtype),
            pltpu.VMEM((rows * clusters, LANES), jnp.bfloat16),
            pltpu.VMEM((rank, slots), jnp.float32),
            pltpu.VMEM((cols * clusters, slots), jnp.bfloat16),
            pltpu.VMEM((2 * rank, slots), jnp.bfloat16),
            pltpu.VMEM((FOLD // LANES, rank * SUBLANES, LANES), jnp.float32),
            pltpu.VMEM((cols * clusters, LANES), jnp.float32),
            pltpu.VMEM((2, clusters, LANES), jnp.float32),
            pltpu.SemaphoreType.DMA((6,)),
            pltpu.SemaphoreType.DMA((slots // FOLD, 2)),
            pltpu.SemaphoreType.DMA(()),
        ],
        compiler_params=pltpu.CompilerParams(vmem_limit_bytes=VMEM),
        cost_estimate=pl.CostEstimate(
            flops=2 * rank * rank * slots,
            bytes_accessed=2 * rank * rank * slots,
            transcendentals=0,
        ),
        name="far_field",
    )(
        counts,
        pairs,
        gathered,
        near_pairs,
        *pinned(pos, disp, intact, stiffness, blocks),
    )


def replicate(rows, chunks, store, turned=False):
    within = lax.broadcasted_iota(jnp.int32, (rows.shape[0], LANES), 1)
    if turned:
        within = within + (within // CHUNK) * SUBLANES
    within = within % CHUNK
    for m in range(3 * chunks):
        tile = m // GROUPS
        store(
            m,
            jnp.take_along_axis(
                rows[:, tile * LANES : (tile + 1) * LANES],
                within + (m % GROUPS) * CHUNK,
                axis=1,
                mode="promise_in_bounds",
            ),
        )


def row_of(ref, n, row):
    return ref[n, pl.ds(row, SUBLANES, stride=0), :]


def turn(wide):
    return pltpu.roll(wide, 0, 1, stride=1, stride_axis=0)


def pair_sums(tgt, src, chunks):
    sums = [None] * (3 * chunks)
    size = 3 * chunks
    for h in range(chunks):
        x = [tgt(c * chunks + h) for c in range(3)]
        for f in range(chunks):
            r = [x[c] - src(c * chunks + f) for c in range(3)]
            u = [src(size + c * chunks + f) for c in range(3)]
            q = (r[0] * r[0] + core_square) + (r[1] * r[1] + r[2] * r[2])
            s = r[0] * u[0] + (r[1] * u[1] + r[2] * u[2])
            inverse = lax.rsqrt(q)
            square = inverse * inverse
            weight = square * inverse
            s = (3.0 * s) * square
            for c in range(3):
                term = weight * (u[c] - s * r[c])
                m = c * chunks + h
                sums[m] = term if sums[m] is None else sums[m] + term
    return sums


def gather_sums(acc_scr, clusters, chunks, store):
    own_group = lax.broadcasted_iota(jnp.int32, (clusters, LANES), 1) // CHUNK
    for t in range(pl.cdiv(3 * chunks, GROUPS)):
        merged = None
        for g in range(GROUPS):
            m = t * GROUPS + g
            if m >= 3 * chunks:
                break
            total = acc_scr[m, pl.ds(0, clusters, stride=SUBLANES), :]
            for s in range(1, SUBLANES):
                total = total + acc_scr[m, pl.ds(s, clusters, stride=SUBLANES), :]
            total = total + pltpu.roll(total, 2 * CHUNK, 1)
            total = total + pltpu.roll(total, CHUNK, 1)
            merged = total if merged is None else jnp.where(own_group == g, total, merged)
        store(t, merged)


def turn_matrix():
    shape = (CHUNK, SUBLANES * LANES)
    column = lax.broadcasted_iota(jnp.int32, shape, 1)
    lane = column % LANES
    entry = (lane + (lane // CHUNK) * SUBLANES + column // LANES) % CHUNK
    chosen = jnp.where(entry == lax.broadcasted_iota(jnp.int32, shape, 0), 1.0, 0.0)
    return jnp.concatenate([chosen.astype(jnp.bfloat16)] * PIECES, axis=0)


def exact_pieces(value):
    pieces = []
    for _ in range(PIECES):
        piece = value.astype(jnp.bfloat16)
        pieces.append(piece)
        value = value - piece.astype(jnp.float32)
    return pieces


def near_kernel(
    list_hbm,
    disp_hbm,
    pos_ref,
    hold_ref,
    out_ref,
    edge_ref,
    list_ref,
    disp_ref,
    wide_scr,
    piece_scr,
    turn_scr,
    tgt_scr,
    src_scr,
    acc_scr,
    sems,
):
    clusters, width = pos_ref.shape
    elems = width // 3
    chunks = elems // CHUNK
    size = 3 * chunks

    moves = start_all(sems, ((list_hbm, list_ref), (disp_hbm, disp_ref)))
    acc_scr[...] = jnp.zeros_like(acc_scr)
    turn_scr[...] = turn_matrix()

    wide_scr[:, 0:width] = pos_ref[...]
    edge_ref[0:HALO, :] = pos_ref[0:HALO, :]
    edge_ref[HALO:, :] = pos_ref[clusters - HALO :, :]
    columns = 2 * LANES
    for k, values in enumerate((pos_ref, disp_ref)):
        if k == 1:
            moves[1].wait()
        for m in range(size):
            pieces = exact_pieces(values[:, m * CHUNK : (m + 1) * CHUNK])
            piece_scr[m * clusters : (m + 1) * clusters, :] = jnp.concatenate(pieces, axis=1)
        for t in range(SUBLANES * LANES // columns):
            turned = jnp.dot(
                piece_scr[...],
                turn_scr[:, t * columns : (t + 1) * columns],
                preferred_element_type=jnp.float32,
            )
            for m in range(size):
                for h in range(columns // LANES):
                    s = t * (columns // LANES) + h
                    src_scr[k * size + m, pl.ds(s, clusters, stride=SUBLANES), :] = turned[
                        m * clusters : (m + 1) * clusters, h * LANES : (h + 1) * LANES
                    ]

    def store_target(m, value):
        tgt_scr[m] = value

    replicate(wide_scr[...], chunks, store_target)
    moves[0].wait()
    count = list_ref[3, 0]

    def sums_of(slot):
        target = list_ref[0, slot]
        source = pl.multiple_of(list_ref[1, slot] * SUBLANES, SUBLANES)
        return pair_sums(
            lambda m: row_of(tgt_scr, m, target),
            lambda n: src_scr[n, pl.ds(source, SUBLANES), :],
            chunks,
        )

    def step(it, carry):
        for k in range(0, UNROLL, TOGETHER):
            slots = [it * UNROLL + k + n for n in range(TOGETHER)]
            results = [sums_of(slot) for slot in slots]
            for slot, sums in zip(slots, results):
                into = pl.multiple_of(list_ref[2, slot], SUBLANES)
                for m in range(size):
                    acc_scr[m, pl.ds(into, SUBLANES), :] += sums[m]
        return carry

    lax.fori_loop(0, (count + UNROLL - 1) // UNROLL, step, 0)

    def store_sum(t, value):
        wide_scr[:, t * LANES : (t + 1) * LANES] = value

    gather_sums(acc_scr, clusters, chunks, store_sum)
    for c in range(3):
        here = slice(c * elems, (c + 1) * elems)
        out_ref[:, here] = wide_scr[:, here] - hold_ref[...] * disp_ref[:, here]


def near_field(listed, disp, pos, hold):
    clusters, width = pos.shape
    elems = width // 3
    chunks = elems // CHUNK
    padded = pl.cdiv(width, LANES) * LANES
    slots = listed.shape[1]
    vmem = pl.BlockSpec(memory_space=pltpu.VMEM)
    return pl.pallas_call(
        near_kernel,
        out_shape=(
            jax.ShapeDtypeStruct((clusters, width), jnp.float32),
            jax.ShapeDtypeStruct((2 * HALO, width), jnp.float32),
        ),
        in_specs=in_hbm(2) + [vmem] * 2,
        out_specs=(vmem, vmem),
        scratch_shapes=[
            pltpu.SMEM(listed.shape, listed.dtype),
            pltpu.VMEM(disp.shape, disp.dtype),
            pltpu.VMEM((clusters, padded), jnp.float32),
            pltpu.VMEM((3 * chunks * clusters, PIECES * CHUNK), jnp.bfloat16),
            pltpu.VMEM((PIECES * CHUNK, SUBLANES * LANES), jnp.bfloat16),
            pltpu.VMEM((3 * chunks, clusters, LANES), jnp.float32),
            pltpu.VMEM((6 * chunks, clusters * SUBLANES, LANES), jnp.float32),
            pltpu.VMEM((3 * chunks, (clusters + 1) * SUBLANES, LANES), jnp.float32),
            pltpu.SemaphoreType.DMA((2,)),
        ],
        compiler_params=pltpu.CompilerParams(vmem_limit_bytes=VMEM),
        cost_estimate=pl.CostEstimate(
            flops=30 * slots * elems * elems,
            bytes_accessed=4 * clusters * width * 6,
            transcendentals=slots * elems * elems,
        ),
        name="near_field",
    )(listed, *pinned(disp), pos, hold)


def finish_kernel(
    rest_hbm,
    edge_ref,
    received_ref,
    near_ref,
    far_ref,
    out_ref,
    rest_ref,
    ext_scr,
    halo_scr,
    tgt_scr,
    src_scr,
    acc_scr,
    sem,
    *,
    rank,
):
    clusters, width = near_ref.shape
    cols = received_ref.shape[0]
    elems = width // 3
    chunks = elems // CHUNK
    size = 3 * chunks
    spare = LANES - rank
    segments = split_rows(width, spare)
    edge = 2 * HALO

    fetch = pltpu.make_async_copy(rest_hbm, rest_ref, sem)
    fetch.start()
    acc_scr[...] = jnp.zeros_like(acc_scr)

    j = lax.axis_index("cols")
    before = jnp.where(j > 0, j - 1, cols - 1)
    after = jnp.where(j < cols - 1, j + 1, 0)
    for start, sender in ((0, before), (HALO, after)):
        halo_scr[...] = received_ref[sender].astype(jnp.float32)
        rows = edge * segments
        whole = halo_scr[0:rows, :]
        for n in range(1, PIECES):
            whole = whole + halo_scr[n * rows : (n + 1) * rows, :]
        for g in range(segments):
            count = min(spare, width - g * spare)
            for k in range(2):
                row = (2 * g + k) * HALO
                ext_scr[k, start : start + HALO, g * spare : g * spare + count] = whole[
                    row : row + HALO, rank : rank + count
                ]
    ext_scr[1, edge : 2 * edge, 0:width] = edge_ref[...]
    for k in range(2):

        def store(m, value, k=k):
            for b in range(edge):
                wide = jnp.broadcast_to(value[b : b + 1, :], (SUBLANES, LANES))
                src_scr[(1 - k) * size + m, b * SUBLANES : (b + 1) * SUBLANES, :] = turn(wide)

        replicate(ext_scr[k], chunks, store, True)

    def store_target(m, value):
        tgt_scr[m] = value

    replicate(ext_scr[1], chunks, store_target)
    fetch.wait()
    number = rest_ref[6, 0]

    def one_pair(n):
        target = rest_ref[4, n]
        source = rest_ref[5, n]
        target = jnp.where(target < HALO, target, target - (clusters - edge))
        source = jnp.where(source < HALO, source, source - clusters)
        live = n < number
        target = jnp.where(live, target, edge)
        source = pl.multiple_of(jnp.where(live, source, 0) * SUBLANES, SUBLANES)
        into = pl.multiple_of(target * SUBLANES, SUBLANES)
        row = edge + jnp.where(live, target, 0)
        sums = pair_sums(
            lambda m: row_of(tgt_scr, m, row),
            lambda k: src_scr[k, pl.ds(source, SUBLANES), :],
            chunks,
        )
        for m in range(size):
            acc_scr[m, pl.ds(into, SUBLANES), :] += sums[m]

    def step(it, carry):
        for k in range(FEW):
            one_pair(it * FEW + k)
        return carry

    lax.fori_loop(0, (number + FEW - 1) // FEW, step, 0)

    def store_sum(t, value):
        ext_scr[0, :, t * LANES : (t + 1) * LANES] = value

    gather_sums(acc_scr, 2 * edge, chunks, store_sum)
    out_ref[...] = near_ref[...] + far_ref[...]
    out_ref[0:HALO, :] += ext_scr[0, 0:HALO, 0:width]
    out_ref[clusters - HALO :, :] += ext_scr[0, HALO:edge, 0:width]


def finish(rest, edges, received, near, far, rank):
    clusters, width = near.shape
    chunks = width // 3 // CHUNK
    padded = pl.cdiv(width, LANES) * LANES
    edge = 2 * HALO
    vmem = pl.BlockSpec(memory_space=pltpu.VMEM)
    return pl.pallas_call(
        functools.partial(finish_kernel, rank=rank),
        out_shape=jax.ShapeDtypeStruct((clusters, width), jnp.float32),
        in_specs=in_hbm(1) + [vmem] * 4,
        out_specs=vmem,
        scratch_shapes=[
            pltpu.SMEM(rest.shape, rest.dtype),
            pltpu.VMEM((2, 2 * edge, padded), jnp.float32),
            pltpu.VMEM((clusters, LANES), jnp.float32),
            pltpu.VMEM((3 * chunks, 2 * edge, LANES), jnp.float32),
            pltpu.VMEM((6 * chunks, edge * SUBLANES, LANES), jnp.float32),
            pltpu.VMEM((3 * chunks, 2 * edge * SUBLANES, LANES), jnp.float32),
            pltpu.SemaphoreType.DMA(()),
        ],
        compiler_params=pltpu.CompilerParams(vmem_limit_bytes=VMEM),
        cost_estimate=pl.CostEstimate(
            flops=2 * clusters * width, bytes_accessed=16 * clusters * width, transcendentals=0
        ),
        name="finish",
    )(rest, edges, received, near, far)


def local(
    displacement,
    positions,
    cluster_basis,
    near_pairs,
    near_count,
    far_pairs,
    far_count,
    far_blocks,
    intact,
    stiffness,
):
    cols = lax.axis_size("cols")
    clusters, width, rank = cluster_basis.shape
    spare = LANES - rank
    segments = split_rows(width, spare)
    disp_bf, halo, counts, near_list, far_list = prepare(
        near_count, far_count, displacement, positions, near_pairs.T, far_pairs.T, spare
    )
    coeff = jnp.einsum("kf,kfr->kr", disp_bf, cluster_basis, preferred_element_type=jnp.float32)
    payload = jnp.concatenate([coeff, halo], axis=1)
    gathered = lax.all_gather(payload, "rows", axis=0, tiled=True)
    partial, pos, hold, listed, damage = far_field(
        counts,
        far_list,
        gathered,
        near_list,
        positions,
        displacement,
        intact,
        stiffness,
        far_blocks.transpose(1, 2, 0),
        cols,
        segments,
    )
    received = lax.all_to_all(partial, "cols", split_axis=0, concat_axis=0)
    near, edges = near_field(listed, displacement, pos, hold)
    owned = jnp.sum(received[:, :, :rank].astype(jnp.float32), axis=0).astype(jnp.bfloat16)
    far = jnp.einsum("kfr,kr->kf", cluster_basis, owned, preferred_element_type=jnp.float32)
    return finish(listed, edges, received, near, far, rank), damage


def solution(mesh):
    both = ("rows", "cols")
    in_specs = (
        P(both, None),
        P(both, None),
        P(both, None, None),
        P(both, None),
        P(both),
        P(both, None),
        P(both),
        P(both, None, None),
        P(both, None),
        P(both, None),
    )
    out_specs = (P(both, None), P(both, None))
    return jax.shard_map(local, mesh=mesh, in_specs=in_specs, out_specs=out_specs, check_vma=False)
```
